32 devices in a mesh: row: 8 (over z, x), col: 2 (over y), ch: 2 (over core).
Axes of the slice: x: 2, y: 2, z: 4, core: 2. Of those that a mesh axis runs over, the one named last changes fastest.
Arguments:
- pair: bfloat16 [192, 192, 128], P('row', 'col'), may hold values from -6 to 6
- cotangent: bfloat16 [192, 192, 128], P('row', 'col', 'ch'), may hold values from -6 to 6
- w_gate_a: bfloat16 [128, 128], P(None, 'ch'), may hold values from -0.5 to 0.5
- w_proj_a: bfloat16 [128, 128], P(None, 'ch'), may hold values from -0.5 to 0.5
- w_gate_b: bfloat16 [128, 128], P(None, 'ch'), may hold values from -0.5 to 0.5
- w_proj_b: bfloat16 [128, 128], P(None, 'ch'), may hold values from -0.5 to 0.5
- w_gate_out: bfloat16 [128, 128], P(None, 'ch'), may hold values from -0.5 to 0.5
- w_out: bfloat16 [128, 128], P(None, 'ch'), may hold values from -0.5 to 0.5
Outputs:
- updated: bfloat16 [192, 192, 128], P('row', 'col', 'ch')
- grad_pair: bfloat16 [192, 192, 128], P('row', 'col', 'ch')
- grad_gate_a: float32 [128, 128], P(None, 'ch')
- grad_proj_a: float32 [128, 128], P(None, 'ch')
- grad_gate_b: float32 [128, 128], P(None, 'ch')
- grad_proj_b: float32 [128, 128], P(None, 'ch')
- grad_gate_out: float32 [128, 128], P(None, 'ch')
- grad_out: float32 [128, 128], P(None, 'ch')
The draws below stay inside these ranges and needn't reach their ends.
All inputs are finite; a program needn't handle non-finite values.
Results may differ from the reference program's by a relative error of at most 0.022.
Values may be sent and summed in bfloat16 or wider, within the bound.
No kernel may reach another device: no remote copies, remote signals or barrier semaphores. Data moves between devices by JAX's collectives and lax.ppermute only.
A program may use at most 64 MiB of HBM per device.

```python
import jax
import jax.numpy as jnp
from jax import lax

C = 128
CH = 128
N = 192


def block_scale(key, shape, cuts, low, top_value):
    factor_of = 1.0
    for axis_at, parts in cuts:
        heights = jax.random.uniform(jax.random.fold_in(jax.random.fold_in(key, 6), axis_at), (parts,), jnp.float32, low / len(cuts), top_value / len(cuts))
        factor_of = factor_of * jnp.repeat(jnp.exp(heights), shape[axis_at] // parts).reshape((-1,) + (1,) * (len(shape) - 1 - axis_at))
    return factor_of


def bell_draw(stream_key, dims, deviation, limit, shards=(), dtype=jnp.bfloat16):
    drawn = jax.random.normal(stream_key, dims, jnp.float32) * deviation
    if len(shards) > 0:
        drawn = block_scale(stream_key, dims, shards, -0.22, 0.18) * drawn
    return jnp.clip(drawn, min=-limit, max=limit).astype(dtype)


def setup_inputs(seed: int = 0) -> dict:
    keys = jax.random.split(jax.random.key(seed), 9)
    return {
        "pair": bell_draw(keys[0], (N, N, C), 1.0, 6.0, ((0, 8), (1, 2))),
        "cotangent": bell_draw(keys[1], (N, N, C), 1.0, 6.0, ((0, 8), (1, 2), (2, 2))),
        "w_gate_a": bell_draw(keys[2], (C, CH), C ** -0.5, 0.5, ((1, 2),)),
        "w_proj_a": bell_draw(keys[3], (C, CH), C ** -0.5, 0.5, ((1, 2),)),
        "w_gate_b": bell_draw(keys[4], (C, CH), C ** -0.5, 0.5, ((1, 2),)),
        "w_proj_b": bell_draw(keys[5], (C, CH), C ** -0.5, 0.5, ((1, 2),)),
        "w_gate_out": bell_draw(keys[6], (C, C), C ** -0.5, 0.5, ((1, 2),)),
        "w_out": bell_draw(keys[7], (CH, C), CH ** -0.5, 0.5, ((1, 2),)),
    }


epsilon = 1e-05

def layer_norm(values):
    average = lax.optimization_barrier(jnp.mean(values, -1, keepdims=True))
    centred = values - average
    spread = lax.optimization_barrier(jnp.mean(centred * centred, -1, keepdims=True))
    inverse = lax.rsqrt(spread + epsilon)
    return (centred * inverse, inverse)

def norm_back(grad, hat, inverse):
    return inverse * (grad - lax.optimization_barrier(jnp.mean(grad, -1, keepdims=True)) - hat * lax.optimization_barrier(jnp.mean(grad * hat, -1, keepdims=True)))

def matmul(first, second):
    return jnp.dot(first, second, preferred_element_type=jnp.float32)

def reference(pair, cotangent, w_gate_a, w_proj_a, w_gate_b, w_proj_b, w_gate_out, w_out):
    pair_hat, pair_rstd = layer_norm(pair.astype(jnp.float32))
    flat_norm = pair_hat.astype(jnp.bfloat16).reshape(N * N, C)
    gate_a = jax.nn.sigmoid(matmul(flat_norm, w_gate_a))
    proj_a = matmul(flat_norm, w_proj_a)
    gate_b = jax.nn.sigmoid(matmul(flat_norm, w_gate_b))
    proj_b = matmul(flat_norm, w_proj_b)
    left_edge = (gate_a * proj_a).astype(jnp.bfloat16).reshape(N, N, CH)
    right_edge = (gate_b * proj_b).astype(jnp.bfloat16).reshape(N, N, CH)
    mixed = jnp.einsum('ikh,jkh->ijh', left_edge.astype(jnp.float32), right_edge.astype(jnp.float32))
    hidden_mean = lax.optimization_barrier(jnp.mean(mixed, -1, keepdims=True))
    hidden_var = lax.optimization_barrier(jnp.mean(mixed * mixed, -1, keepdims=True)) - hidden_mean * hidden_mean
    hidden_rstd = lax.rsqrt(hidden_var + epsilon)
    mixed_hat = (mixed - hidden_mean) * hidden_rstd
    mixed_norm = mixed_hat.astype(jnp.bfloat16).reshape(N * N, CH)
    gate_out = jax.nn.sigmoid(matmul(flat_norm, w_gate_out))
    proj_out = matmul(mixed_norm, w_out)
    updated = (gate_out * proj_out).astype(jnp.bfloat16).reshape(N, N, C)
    upstream = cotangent.reshape(N * N, C).astype(jnp.float32)
    d_proj = (upstream * gate_out).astype(jnp.bfloat16)
    d_gate = (upstream * proj_out * gate_out * (1.0 - gate_out)).astype(jnp.bfloat16)
    grad_scale = 1.0 / N
    grad_out = matmul(mixed_norm.T, d_proj) * grad_scale
    grad_gate_out = matmul(flat_norm.T, d_gate) * grad_scale
    d_norm = matmul(d_proj, w_out.T).reshape(N, N, CH)
    d_mixed = norm_back(d_norm, mixed_hat, hidden_rstd).astype(jnp.bfloat16).astype(jnp.float32)
    d_left = jnp.einsum('ijh,jkh->ikh', d_mixed, right_edge.astype(jnp.float32)).reshape(N * N, CH)
    d_right = jnp.einsum('ijh,ikh->jkh', d_mixed, left_edge.astype(jnp.float32)).reshape(N * N, CH)
    grad_pa = (d_left * gate_a).astype(jnp.bfloat16)
    grad_ga = (d_left * proj_a * gate_a * (1.0 - gate_a)).astype(jnp.bfloat16)
    grad_pb = (d_right * gate_b).astype(jnp.bfloat16)
    grad_gb = (d_right * proj_b * gate_b * (1.0 - gate_b)).astype(jnp.bfloat16)
    grad_gate_a = matmul(flat_norm.T, grad_ga) * grad_scale
    grad_proj_a = matmul(flat_norm.T, grad_pa) * grad_scale
    grad_gate_b = matmul(flat_norm.T, grad_gb) * grad_scale
    grad_proj_b = matmul(flat_norm.T, grad_pb) * grad_scale
    d_input = matmul(grad_ga, w_gate_a.T) + matmul(grad_pa, w_proj_a.T)
    d_input = d_input + matmul(grad_gb, w_gate_b.T) + matmul(grad_pb, w_proj_b.T)
    d_input = d_input + matmul(d_gate, w_gate_out.T)
    grad_pair = norm_back(d_input.reshape(N, N, C), pair_hat, pair_rstd).astype(jnp.bfloat16)
    return (updated, grad_pair, grad_gate_a, grad_proj_a, grad_gate_b, grad_proj_b, grad_gate_out, grad_out)
```

```python
import functools

import jax
import jax.numpy as jnp
import numpy as np
from jax import lax
from jax.experimental import pallas as pl
from jax.experimental.pallas import tpu as pltpu
from jax.sharding import PartitionSpec as P

epsilon = 1e-05


def layer_norm(values):
    average = jnp.mean(values, -1, keepdims=True)
    centred = values - average
    spread = jnp.mean(centred * centred, -1, keepdims=True)
    inverse = lax.rsqrt(spread + epsilon)
    return (centred * inverse, inverse)


def matmul(first, second):
    return jnp.dot(first, second, preferred_element_type=jnp.float32)


def by_rows(pair, cotangent, w_gate_a, w_proj_a, w_gate_b, w_proj_b, w_gate_out, w_out):
    row_count, col_count, channels = pair.shape
    hidden = w_gate_a.shape[1]
    total_hidden = hidden * lax.axis_size("ch")
    out_width = cotangent.shape[2]
    length = row_count * lax.axis_size("row")
    grad_scale = 1.0 / length
    pair_hat, pair_rstd = layer_norm(pair.astype(jnp.float32))
    flat_norm = pair_hat.astype(jnp.bfloat16).reshape(row_count * col_count, channels)
    w_four = jnp.concatenate([w_gate_a, w_proj_a, w_gate_b, w_proj_b], axis=1)
    projected = matmul(flat_norm, w_four)
    gate_a = jax.nn.sigmoid(projected[:, :hidden])
    proj_a = projected[:, hidden : 2 * hidden]
    gate_b = jax.nn.sigmoid(projected[:, 2 * hidden : 3 * hidden])
    proj_b = projected[:, 3 * hidden :]
    left_edge = (gate_a * proj_a).astype(jnp.bfloat16).reshape(row_count, col_count, hidden)
    right_edge = (gate_b * proj_b).astype(jnp.bfloat16).reshape(row_count, col_count, hidden)
    right_all = lax.all_gather(right_edge, "row", axis=0, tiled=True)
    mixed_swap = lax.psum_scatter(
        jnp.einsum("jkh,ikh->jih", right_all, left_edge, preferred_element_type=jnp.float32).astype(
            jnp.bfloat16
        ),
        "col",
        scatter_dimension=0,
        tiled=True,
    ).astype(jnp.float32)
    mixed = jnp.swapaxes(mixed_swap, 0, 1).reshape(row_count * col_count, hidden)
    hidden_sums = lax.psum((jnp.sum(mixed, -1), jnp.sum(mixed * mixed, -1)), "ch")
    hidden_mean = (hidden_sums[0] / total_hidden)[:, None]
    hidden_var = (hidden_sums[1] / total_hidden)[:, None] - hidden_mean * hidden_mean
    hidden_rstd = lax.rsqrt(hidden_var + epsilon)
    mixed_hat = (mixed - hidden_mean) * hidden_rstd
    mixed_norm = mixed_hat.astype(jnp.bfloat16)
    norm_full = lax.all_gather(mixed_norm, "ch", axis=1, tiled=True)
    gate_out = jax.nn.sigmoid(matmul(flat_norm, w_gate_out))
    proj_out = matmul(norm_full, w_out)
    updated = (gate_out * proj_out).astype(jnp.bfloat16).reshape(row_count, col_count, out_width)
    upstream = cotangent.reshape(row_count * col_count, out_width).astype(jnp.float32)
    d_proj = (upstream * gate_out).astype(jnp.bfloat16)
    d_gate = (upstream * proj_out * gate_out * (1.0 - gate_out)).astype(jnp.bfloat16)
    head_grads = lax.psum(
        (matmul(norm_full.T, d_proj) * grad_scale, matmul(flat_norm.T, d_gate) * grad_scale),
        ("row", "col"),
    )
    d_norm = lax.psum_scatter(
        matmul(d_proj, w_out.T).astype(jnp.bfloat16), "ch", scatter_dimension=1, tiled=True
    ).astype(jnp.float32)
    back_sums = lax.psum((jnp.sum(d_norm, -1), jnp.sum(d_norm * mixed_hat, -1)), "ch")
    d_mixed = hidden_rstd * (
        d_norm
        - (back_sums[0] / total_hidden)[:, None]
        - mixed_hat * (back_sums[1] / total_hidden)[:, None]
    )
    d_mixed = d_mixed.astype(jnp.bfloat16).reshape(row_count, col_count, hidden)
    d_rows = lax.all_gather(d_mixed, "col", axis=1, tiled=True)
    right_back = lax.all_gather(right_edge, "row", axis=0, tiled=True)
    d_left = jnp.einsum("ijh,jkh->ikh", d_rows, right_back, preferred_element_type=jnp.float32)
    d_left = d_left.reshape(row_count * col_count, hidden)
    left_all = lax.all_gather(left_edge, "row", axis=0, tiled=True)
    d_columns = lax.all_to_all(d_rows, "row", split_axis=1, concat_axis=0, tiled=True)
    d_right = jnp.einsum("ijh,ikh->jkh", d_columns, left_all, preferred_element_type=jnp.float32)
    d_right = d_right.reshape(row_count * col_count, hidden)
    grad_pa = (d_left * gate_a).astype(jnp.bfloat16)
    grad_ga = (d_left * proj_a * gate_a * (1.0 - gate_a)).astype(jnp.bfloat16)
    grad_pb = (d_right * gate_b).astype(jnp.bfloat16)
    grad_gb = (d_right * proj_b * gate_b * (1.0 - gate_b)).astype(jnp.bfloat16)
    d_four = jnp.concatenate([grad_ga, grad_pa, grad_gb, grad_pb], axis=1)
    weight_terms = matmul(flat_norm.T, d_four) * grad_scale
    summed = lax.psum(weight_terms, ("row", "col"))
    d_flat = matmul(d_four, w_four.T) + matmul(d_gate, w_gate_out.T)
    hat_all = pair_hat.reshape(row_count * col_count, channels)
    rstd_flat = pair_rstd.reshape(row_count * col_count, 1)
    offset = lax.axis_index("ch") * out_width
    grad_whole = lax.psum(d_flat.astype(jnp.bfloat16), "ch").astype(jnp.float32)
    grad_full = rstd_flat * (
        grad_whole
        - jnp.mean(grad_whole, -1, keepdims=True)
        - hat_all * jnp.mean(grad_whole * hat_all, -1, keepdims=True)
    )
    grad_pair = lax.dynamic_slice_in_dim(grad_full, offset, out_width, 1)
    grad_pair = grad_pair.astype(jnp.bfloat16).reshape(row_count, col_count, out_width)
    return (
        updated,
        grad_pair,
        summed[:, :hidden],
        summed[:, hidden : 2 * hidden],
        summed[:, 2 * hidden : 3 * hidden],
        summed[:, 3 * hidden :],
        head_grads[1],
        head_grads[0],
    )


everyone = ("col", "row", "ch")
f32, bf16 = jnp.float32, jnp.bfloat16


def dot(first, second, over):
    return lax.dot_general(
        first, second, (((over[0],), (over[1],)), ((), ())), preferred_element_type=f32
    )


def call(kernel, outs, args, scratch=()):
    whole = pl.BlockSpec(memory_space=pltpu.VMEM)
    scalars = pl.BlockSpec(memory_space=pltpu.SMEM)
    return pl.pallas_call(
        kernel,
        out_shape=tuple(jax.ShapeDtypeStruct(*out) for out in outs),
        in_specs=[scalars if arg.dtype == jnp.int32 else whole for arg in args],
        out_specs=tuple(whole for _ in outs),
        scratch_shapes=scratch,
        compiler_params=pltpu.CompilerParams(vmem_limit_bytes=50 * 2**20),
    )(*args)


def grouping(hidden, share):
    rows = np.arange(2 * hidden)
    group, side, rest = rows // (2 * share), (rows // share) % 2, rows % share
    return (np.arange(2 * hidden)[None] == (side * hidden + group * share + rest)[:, None])


def turn_weights(order, ga, pa, gb, pb, go, wo, out):
    width = order.shape[0]
    order = order[...]
    out[:width] = dot(order, jnp.concatenate([ga[...], gb[...]], axis=1), (1, 1)).astype(bf16)
    out[width : 2 * width] = dot(
        order, jnp.concatenate([pa[...], pb[...]], axis=1), (1, 1)
    ).astype(bf16)
    last = jnp.concatenate([go[...], wo[...]], axis=1).astype(f32).T
    out[2 * width :] = last.astype(bf16)


def rows_of(weights, start, count):
    return jnp.concatenate([weights[c, start : start + count] for c in range(weights.shape[0])], 0)


def edges(width, half, pair, weights, send, normed, hat, inverse):
    count, cols, channels = pair.shape
    count = count // weights.shape[0]
    values = pair[pl.ds(half[0] * count, count)].astype(f32).reshape(count * cols, channels).T
    centred = values - jnp.mean(values, 0, keepdims=True)
    rstd = lax.rsqrt(jnp.mean(centred * centred, 0, keepdims=True) + epsilon)
    hat[...] = centred * rstd
    inverse[...] = rstd
    normed[...] = (centred * rstd).astype(bf16)
    gate = jax.nn.sigmoid(dot(rows_of(weights, 0, width), normed[...], (1, 0)))
    value = dot(rows_of(weights, width, width), normed[...], (1, 0))
    send[...] = (gate * value).reshape(send.shape).astype(bf16)


def gates(width, half, normed, weights, own, other, gate_out, upstream):
    parts, total, _ = weights.shape
    hidden = (total - 2 * width) // 2
    count, cols, _ = other.shape
    gate_out[...] = jax.nn.sigmoid(dot(rows_of(weights, 2 * width, hidden), normed[...], (1, 0)))
    mine = own[pl.ds(half[0] * count, count)].astype(f32).reshape(count * cols, hidden).T
    yours = other[...].astype(f32).reshape(count * cols, hidden).T
    upstream[pl.ds(pl.multiple_of(half[0] * hidden, hidden), hidden)] = mine
    upstream[pl.ds(pl.multiple_of((1 - half[0]) * hidden, hidden), hidden)] = yours


def spread_rows(block, cols, arrived, held):
    devices, q, flat = arrived.shape

    def one(s, _):
        tile = arrived[s].astype(f32)
        for i in range(flat // cols):
            start = pl.multiple_of((s * (flat // cols) + i) * block, block)
            held[pl.ds(start, q), 0:cols] = tile[:, i * cols : (i + 1) * cols]
        return 0

    lax.fori_loop(0, devices, one, 0)


def pack_rows(block, cols, held, send):
    devices, q, flat = send.shape

    def one(s, _):
        pieces = []
        for i in range(flat // cols):
            start = pl.multiple_of((s * (flat // cols) + i) * block, block)
            pieces.append(held[pl.ds(start, block), 0:cols])
        send[s] = jnp.concatenate(pieces, axis=1)[:q].astype(bf16)
        return 0

    lax.fori_loop(0, devices, one, 0)


def mix(parts, cols, arrived, send, kept, held, result):
    block = 8
    q = arrived.shape[1]
    tokens = held.shape[0] // (parts * block)
    spread_rows(block, cols, arrived, held)
    for p in range(parts):
        for e in range(q):
            start = p * tokens * block + e
            kept[e, p] = held[pl.ds(start, tokens, stride=block), 0:cols].astype(bf16)
    for e in range(q // 2):
        for p in range(parts):
            total = 0.0
            for k in range(parts):
                total = total + dot(
                    kept[e, k], kept[q // 2 + e, k, p * cols : (p + 1) * cols], (1, 1)
                )
            result[pl.ds(p * tokens * block + e, tokens, stride=block), 0:cols] = total
    pack_rows(block, cols, result, send)


def head(width, arrived, weights, gate_out, upstream, send, hat_rounded, d_proj, d_gate, updated):
    parts, total, _ = weights.shape
    hidden = (total - 2 * width) // 2
    devices, q, flat = arrived.shape
    mixed = jnp.concatenate([arrived[s].astype(f32) for s in range(devices)], 0)
    average = jnp.mean(mixed, 0, keepdims=True)
    spread = jnp.mean(mixed * mixed, 0, keepdims=True) - average * average
    inverse = lax.rsqrt(spread + epsilon)
    hat = (mixed - average) * inverse
    hat_rounded[...] = hat.astype(bf16)
    w_out = rows_of(weights, 2 * width + hidden, hidden)
    proj = dot(w_out, hat_rounded[...], (1, 0))
    gate = gate_out[...]
    up = upstream[...]
    d_proj[...] = (up * gate).astype(bf16)
    d_gate[...] = (up * proj * gate * (1.0 - gate)).astype(bf16)
    updated[...] = (gate * proj).astype(bf16)
    d_norm = dot(w_out, d_proj[...], (0, 0))
    d_mixed = inverse * (
        d_norm
        - jnp.mean(d_norm, 0, keepdims=True)
        - hat * jnp.mean(d_norm * hat, 0, keepdims=True)
    )
    for s in range(devices):
        send[s] = d_mixed[s * q : (s + 1) * q].astype(bf16)


def head_rest(parts, scale, normed, hat_rounded, d_proj, d_gate, updated, terms, updated_rows):
    hidden = d_gate.shape[0] // parts
    by_gate = dot(d_gate[...], normed[...], (1, 1)) * scale
    by_out = dot(d_proj[...], hat_rounded[...], (1, 1)) * scale
    for c in range(parts):
        terms[c, :hidden] = by_gate[c * hidden : (c + 1) * hidden]
        terms[c, hidden:] = by_out[c * hidden : (c + 1) * hidden]
    turned = updated[...].astype(f32).T
    for c in range(parts):
        updated_rows[c] = turned[:, c * hidden : (c + 1) * hidden].reshape(
            updated_rows.shape[1:]
        ).astype(bf16)


def unmix(parts, cols, arrived, kept, send, held, result):
    block = 8
    q = arrived.shape[1]
    tokens = held.shape[0] // (parts * block)
    spread_rows(block, cols, arrived, held)
    for e in range(q):
        d_mixed = [
            held[pl.ds(p * tokens * block + e, tokens, stride=block), 0:cols].astype(bf16)
            for p in range(parts)
        ]
        for k in range(parts):
            total = 0.0
            for p in range(parts):
                total = total + dot(
                    d_mixed[p], kept[q + e, k, p * cols : (p + 1) * cols], (1, 0)
                )
                start = (k * tokens + p * cols) * block + q + e
                result[pl.ds(start, cols, stride=block), 0:cols] = dot(
                    d_mixed[p], kept[e, k], (0, 0)
                )
            result[pl.ds(k * tokens * block + e, tokens, stride=block), 0:cols] = total
    pack_rows(block, cols, result, send)


def tail(width, scale, arrived, weights, normed, hat, inverse, d_gate, head_terms, send, grad_rows):
    parts, total, channels = weights.shape
    hidden = (total - 2 * width) // 2
    devices, q, flat = arrived.shape
    w_gate, w_value = rows_of(weights, 0, width), rows_of(weights, width, width)
    gate = jax.nn.sigmoid(dot(w_gate, normed[...], (1, 0)))
    value = dot(w_value, normed[...], (1, 0))
    grad = arrived[...].astype(f32).reshape(devices * q, flat)
    by_value = grad * gate
    by_gate = (by_value * (value * (1.0 - gate))).astype(bf16)
    by_value = by_value.astype(bf16)
    terms = [
        dot(by_gate, normed[...], (1, 1)) * scale,
        dot(by_value, normed[...], (1, 1)) * scale,
    ]
    per = send.shape[1]
    for c in range(parts):
        whole = jnp.concatenate(
            [term[c * width : (c + 1) * width] for term in terms] + [head_terms[c]], 0
        )
        for s in range(total // per):
            send[c * (total // per) + s] = whole[s * per : (s + 1) * per].astype(bf16)
    d_input = dot(w_gate, by_gate, (0, 0)) + dot(w_value, by_value, (0, 0))
    d_input = d_input + dot(rows_of(weights, 2 * width, hidden), d_gate[...], (0, 0))
    back = inverse[...] * (
        d_input
        - jnp.mean(d_input, 0, keepdims=True)
        - hat[...] * jnp.mean(d_input * hat[...], 0, keepdims=True)
    )
    turned = back.T
    for c in range(parts):
        grad_rows[c] = turned[:, c * hidden : (c + 1) * hidden].reshape(
            grad_rows.shape[1:]
        ).astype(bf16)


def add_up(arrived, out):
    out[...] = jnp.sum(arrived[...].astype(f32), 0).astype(bf16)


def turn_back(order, sums, ga, pa, gb, pb, go, wo):
    width = order.shape[0]
    hidden = width // 2
    order = order[...]
    whole = jnp.concatenate([sums[s].astype(f32) for s in range(sums.shape[0])], 0)
    for at, (left, right) in enumerate(((ga, gb), (pa, pb))):
        both = dot(whole[at * width : (at + 1) * width].astype(bf16), order, (0, 0))
        left[...] = both[:, :hidden]
        right[...] = both[:, hidden:]
    both = whole[2 * width :].T
    go[...] = both[:, :hidden]
    wo[...] = both[:, hidden:]


def by_channels(pair, cotangent, w_gate_a, w_proj_a, w_gate_b, w_proj_b, w_gate_out, w_out):
    row_count, cols, channels = pair.shape
    hidden = w_gate_a.shape[1]
    parts = lax.axis_size("ch")
    col_parts = lax.axis_size("col")
    devices = lax.axis_size(everyone)
    share = hidden * parts // devices
    width = 2 * hidden
    count = row_count // parts
    flat = count * cols
    tokens = cols * col_parts
    scale = 1.0 / tokens
    half = lax.axis_index("ch").astype(jnp.int32).reshape(1)
    order = jnp.asarray(grouping(hidden, share), bf16)
    swap = [(c, parts - 1 - c) for c in range(parts)]

    (weights,) = call(
        turn_weights,
        [((2 * width + 2 * hidden, channels), bf16)],
        (order, w_gate_a, w_proj_a, w_gate_b, w_proj_b, w_gate_out, w_out),
    )
    weights = lax.all_gather(weights, "ch")
    other = lax.dynamic_slice_in_dim(cotangent, (1 - half[0]) * count, count, 0)
    other = lax.ppermute(other, "ch", swap)
    send, normed, hat, inverse = call(
        functools.partial(edges, width),
        [
            ((devices, 2 * share, flat), bf16),
            ((channels, flat), bf16),
            ((channels, flat), f32),
            ((1, flat), f32),
        ],
        (half, pair, weights),
    )
    arrived = lax.all_to_all(send, everyone, 0, 0)
    gate_out, upstream = call(
        functools.partial(gates, width),
        [((hidden * parts, flat), f32)] * 2,
        (half, normed, weights, cotangent, other),
    )
    room = pltpu.VMEM((col_parts * tokens * 8, -(-cols // 128) * 128), f32)
    send, kept = call(
        functools.partial(mix, col_parts, cols),
        [((devices, share, flat), bf16), ((2 * share, col_parts, tokens, cols), bf16)],
        (arrived,),
        (room, room),
    )
    arrived = lax.all_to_all(send, everyone, 0, 0)
    send, hat_rounded, d_proj, d_gate, updated = call(
        functools.partial(head, width),
        [((devices, share, flat), bf16)] + [((hidden * parts, flat), bf16)] * 4,
        (arrived, weights, gate_out, upstream),
    )
    arrived = lax.all_to_all(send, everyone, 0, 0)
    head_terms, updated_rows = call(
        functools.partial(head_rest, parts, scale),
        [((parts, 2 * hidden, channels), f32), ((parts, count, cols, hidden), bf16)],
        (normed, hat_rounded, d_proj, d_gate, updated),
    )
    updated = lax.all_to_all(updated_rows, "ch", 0, 0).reshape(row_count, cols, hidden)
    (send,) = call(
        functools.partial(unmix, col_parts, cols),
        [((devices, 2 * share, flat), bf16)],
        (arrived, kept),
        (room, room),
    )
    arrived = lax.all_to_all(send, everyone, 0, 0)
    per = (2 * width + 2 * hidden) * parts // devices
    send, grad_rows = call(
        functools.partial(tail, width, scale),
        [((devices, per, channels), bf16), ((parts, count, cols, hidden), bf16)],
        (arrived, weights, normed, hat, inverse, d_gate, head_terms),
    )
    arrived = lax.all_to_all(send, ("ch", "row", "col"), 0, 0)
    grad_pair = lax.all_to_all(grad_rows, "ch", 0, 0).reshape(row_count, cols, hidden)
    (sums,) = call(add_up, [((per, channels), bf16)], (arrived,))
    rest = devices // parts
    sums = lax.all_to_all(
        jnp.broadcast_to(sums[None], (rest, per, channels)), ("row", "col"), 0, 0
    )
    ga, pa, gb, pb, go, wo = call(
        turn_back, [((channels, hidden), f32)] * 6, (order, sums)
    )
    return updated, grad_pair, ga, pa, gb, pb, go, wo


def on_device(*arrays):
    row_count, cols, _ = arrays[0].shape
    parts, devices = lax.axis_size("ch"), lax.axis_size(everyone)
    hidden = arrays[2].shape[1]
    share = hidden * parts // devices
    fits = (
        share * devices == hidden * parts
        and parts == 2
        and 2 * share == 8
        and row_count % parts == 0
        and arrays[1].shape[2] == hidden
        and cols % 16 == 0
    )
    return by_channels(*arrays) if fits else by_rows(*arrays)


def solution(mesh):
    in_specs = (
        P("row", "col", None),
        P("row", "col", "ch"),
        P(None, "ch"),
        P(None, "ch"),
        P(None, "ch"),
        P(None, "ch"),
        P(None, "ch"),
        P(None, "ch"),
    )
    out_specs = (
        P("row", "col", "ch"),
        P("row", "col", "ch"),
        P(None, "ch"),
        P(None, "ch"),
        P(None, "ch"),
        P(None, "ch"),
        P(None, "ch"),
        P(None, "ch"),
    )
    return jax.shard_map(
        on_device, mesh=mesh, in_specs=in_specs, out_specs=out_specs, check_vma=False
    )
```

```python
import functools

import jax
import jax.numpy as jnp
import numpy as np
from jax import lax
from jax.experimental import pallas as pl
from jax.experimental.pallas import tpu as pltpu
from jax.sharding import PartitionSpec as P

epsilon = 1e-05


def layer_norm(values):
    average = jnp.mean(values, -1, keepdims=True)
    centred = values - average
    spread = jnp.mean(centred * centred, -1, keepdims=True)
    inverse = lax.rsqrt(spread + epsilon)
    return (centred * inverse, inverse)


def matmul(first, second):
    return jnp.dot(first, second, preferred_element_type=jnp.float32)


def by_rows(pair, cotangent, w_gate_a, w_proj_a, w_gate_b, w_proj_b, w_gate_out, w_out):
    row_count, col_count, channels = pair.shape
    hidden = w_gate_a.shape[1]
    total_hidden = hidden * lax.axis_size("ch")
    out_width = cotangent.shape[2]
    length = row_count * lax.axis_size("row")
    grad_scale = 1.0 / length
    pair_hat, pair_rstd = layer_norm(pair.astype(jnp.float32))
    flat_norm = pair_hat.astype(jnp.bfloat16).reshape(row_count * col_count, channels)
    w_four = jnp.concatenate([w_gate_a, w_proj_a, w_gate_b, w_proj_b], axis=1)
    projected = matmul(flat_norm, w_four)
    gate_a = jax.nn.sigmoid(projected[:, :hidden])
    proj_a = projected[:, hidden : 2 * hidden]
    gate_b = jax.nn.sigmoid(projected[:, 2 * hidden : 3 * hidden])
    proj_b = projected[:, 3 * hidden :]
    left_edge = (gate_a * proj_a).astype(jnp.bfloat16).reshape(row_count, col_count, hidden)
    right_edge = (gate_b * proj_b).astype(jnp.bfloat16).reshape(row_count, col_count, hidden)
    right_all = lax.all_gather(right_edge, "row", axis=0, tiled=True)
    mixed_swap = lax.psum_scatter(
        jnp.einsum("jkh,ikh->jih", right_all, left_edge, preferred_element_type=jnp.float32).astype(
            jnp.bfloat16
        ),
        "col",
        scatter_dimension=0,
        tiled=True,
    ).astype(jnp.float32)
    mixed = jnp.swapaxes(mixed_swap, 0, 1).reshape(row_count * col_count, hidden)
    hidden_sums = lax.psum((jnp.sum(mixed, -1), jnp.sum(mixed * mixed, -1)), "ch")
    hidden_mean = (hidden_sums[0] / total_hidden)[:, None]
    hidden_var = (hidden_sums[1] / total_hidden)[:, None] - hidden_mean * hidden_mean
    hidden_rstd = lax.rsqrt(hidden_var + epsilon)
    mixed_hat = (mixed - hidden_mean) * hidden_rstd
    mixed_norm = mixed_hat.astype(jnp.bfloat16)
    norm_full = lax.all_gather(mixed_norm, "ch", axis=1, tiled=True)
    gate_out = jax.nn.sigmoid(matmul(flat_norm, w_gate_out))
    proj_out = matmul(norm_full, w_out)
    updated = (gate_out * proj_out).astype(jnp.bfloat16).reshape(row_count, col_count, out_width)
    upstream = cotangent.reshape(row_count * col_count, out_width).astype(jnp.float32)
    d_proj = (upstream * gate_out).astype(jnp.bfloat16)
    d_gate = (upstream * proj_out * gate_out * (1.0 - gate_out)).astype(jnp.bfloat16)
    head_grads = lax.psum(
        (matmul(norm_full.T, d_proj) * grad_scale, matmul(flat_norm.T, d_gate) * grad_scale),
        ("row", "col"),
    )
    d_norm = lax.psum_scatter(
        matmul(d_proj, w_out.T).astype(jnp.bfloat16), "ch", scatter_dimension=1, tiled=True
    ).astype(jnp.float32)
    back_sums = lax.psum((jnp.sum(d_norm, -1), jnp.sum(d_norm * mixed_hat, -1)), "ch")
    d_mixed = hidden_rstd * (
        d_norm
        - (back_sums[0] / total_hidden)[:, None]
        - mixed_hat * (back_sums[1] / total_hidden)[:, None]
    )
    d_mixed = d_mixed.astype(jnp.bfloat16).reshape(row_count, col_count, hidden)
    d_rows = lax.all_gather(d_mixed, "col", axis=1, tiled=True)
    right_back = lax.all_gather(right_edge, "row", axis=0, tiled=True)
    d_left = jnp.einsum("ijh,jkh->ikh", d_rows, right_back, preferred_element_type=jnp.float32)
    d_left = d_left.reshape(row_count * col_count, hidden)
    left_all = lax.all_gather(left_edge, "row", axis=0, tiled=True)
    d_columns = lax.all_to_all(d_rows, "row", split_axis=1, concat_axis=0, tiled=True)
    d_right = jnp.einsum("ijh,ikh->jkh", d_columns, left_all, preferred_element_type=jnp.float32)
    d_right = d_right.reshape(row_count * col_count, hidden)
    grad_pa = (d_left * gate_a).astype(jnp.bfloat16)
    grad_ga = (d_left * proj_a * gate_a * (1.0 - gate_a)).astype(jnp.bfloat16)
    grad_pb = (d_right * gate_b).astype(jnp.bfloat16)
    grad_gb = (d_right * proj_b * gate_b * (1.0 - gate_b)).astype(jnp.bfloat16)
    d_four = jnp.concatenate([grad_ga, grad_pa, grad_gb, grad_pb], axis=1)
    weight_terms = matmul(flat_norm.T, d_four) * grad_scale
    summed = lax.psum(weight_terms, ("row", "col"))
    d_flat = matmul(d_four, w_four.T) + matmul(d_gate, w_gate_out.T)
    hat_all = pair_hat.reshape(row_count * col_count, channels)
    rstd_flat = pair_rstd.reshape(row_count * col_count, 1)
    offset = lax.axis_index("ch") * out_width
    grad_whole = lax.psum(d_flat.astype(jnp.bfloat16), "ch").astype(jnp.float32)
    grad_full = rstd_flat * (
        grad_whole
        - jnp.mean(grad_whole, -1, keepdims=True)
        - hat_all * jnp.mean(grad_whole * hat_all, -1, keepdims=True)
    )
    grad_pair = lax.dynamic_slice_in_dim(grad_full, offset, out_width, 1)
    grad_pair = grad_pair.astype(jnp.bfloat16).reshape(row_count, col_count, out_width)
    return (
        updated,
        grad_pair,
        summed[:, :hidden],
        summed[:, hidden : 2 * hidden],
        summed[:, 2 * hidden : 3 * hidden],
        summed[:, 3 * hidden :],
        head_grads[1],
        head_grads[0],
    )


everyone = ("col", "row", "ch")
f32, bf16 = jnp.float32, jnp.bfloat16


def dot(first, second, over):
    return lax.dot_general(
        first, second, (((over[0],), (over[1],)), ((), ())), preferred_element_type=f32
    )


def call(kernel, outs, args, scratch=(), far=()):
    whole = pl.BlockSpec(memory_space=pltpu.VMEM)
    scalars = pl.BlockSpec(memory_space=pltpu.SMEM)
    anywhere = pl.BlockSpec(memory_space=pl.ANY)
    specs = [
        anywhere if at in far else scalars if arg.dtype == jnp.int32 else whole
        for at, arg in enumerate(args)
    ]
    return pl.pallas_call(
        kernel,
        out_shape=tuple(jax.ShapeDtypeStruct(*out) for out in outs),
        in_specs=specs,
        out_specs=tuple(whole for _ in outs),
        scratch_shapes=scratch,
        compiler_params=pltpu.CompilerParams(vmem_limit_bytes=16 * 2**20),
    )(*args)


def grouping(hidden, share):
    rows = np.arange(2 * hidden)
    group, side, rest = rows // (2 * share), (rows // share) % 2, rows % share
    return (np.arange(2 * hidden)[None] == (side * hidden + group * share + rest)[:, None])


def turn_weights(order, ga, pa, gb, pb, go, wo, out):
    width = order.shape[0]
    hidden = go.shape[0]
    order = order[...]
    out[:width] = dot(order, jnp.concatenate([ga[...], gb[...]], 0), (1, 0)).astype(bf16)
    out[width : 2 * width] = dot(order, jnp.concatenate([pa[...], pb[...]], 0), (1, 0)).astype(bf16)
    out[2 * width : 2 * width + hidden] = go[...]
    out[2 * width + hidden :] = wo[...]


def rows_of(weights, start, count):
    return jnp.concatenate([weights[c, start : start + count] for c in range(weights.shape[0])], 0)


def normalized(pair):
    count, cols, channels = pair.shape
    values = pair.astype(f32).reshape(count * cols, channels).T
    centred = values - jnp.mean(values, 0, keepdims=True)
    rstd = lax.rsqrt(jnp.mean(centred * centred, 0, keepdims=True) + epsilon)
    return centred * rstd, rstd


def edges(width, count, place, pair, weights, send, normed):
    hat, _ = normalized(pair[pl.ds(place[0] * count, count)])
    normed[...] = hat.astype(bf16)
    gate = jax.nn.sigmoid(dot(rows_of(weights, 0, width), normed[...], (1, 0)))
    value = dot(rows_of(weights, width, width), normed[...], (1, 0))
    send[...] = (gate * value).reshape(send.shape).astype(bf16)


def spread_rows(block, cols, arrived, held):
    devices, q, flat = arrived.shape
    rows = flat // cols
    for s in range(devices):
        tile = arrived[s].astype(f32)
        for i in range(rows):
            start = (s * rows + i) * block
            held[start : start + q, 0:cols] = tile[:, i * cols : (i + 1) * cols]


def pack_rows(block, cols, held, send):
    devices, q, flat = send.shape
    rows = flat // cols
    for s in range(devices):
        starts = [(s * rows + i) * block for i in range(rows)]
        whole = jnp.concatenate([held[start : start + block, 0:cols] for start in starts], axis=1)
        send[s] = whole[:q].astype(bf16)


def square(block, parts, cols, held, e):
    tokens = parts * cols
    return jnp.concatenate(
        [
            held[pl.ds(p * tokens * block + e, tokens, stride=block), 0:cols]
            for p in range(parts)
        ],
        axis=1,
    ).astype(bf16)


def put_square(block, parts, cols, held, e, values):
    tokens = parts * cols
    for p in range(parts):
        held[pl.ds(p * tokens * block + e, tokens, stride=block), 0:cols] = values[
            :, p * cols : (p + 1) * cols
        ]


def mix(parts, cols, arrived, send, kept, held, result):
    block = 8
    q = arrived.shape[1]
    spread_rows(block, cols, arrived, held)
    for e in range(q // 2):
        left = square(block, parts, cols, held, e)
        right = square(block, parts, cols, held, q // 2 + e)
        kept[e] = left
        kept[q // 2 + e] = right
        put_square(block, parts, cols, result, e, dot(left, right, (1, 1)))
    pack_rows(block, cols, result, send)


def unmix(parts, cols, arrived, kept_far, send, held, result, kept, arrival):
    block = 8
    q = arrived.shape[1]
    copy = pltpu.make_async_copy(kept_far, kept, arrival)
    copy.start()
    spread_rows(block, cols, arrived, held)
    copy.wait()
    for e in range(q):
        d_mixed = square(block, parts, cols, held, e)
        put_square(block, parts, cols, result, e, dot(d_mixed, kept[q + e], (1, 0)))
        put_square(block, parts, cols, result, q + e, dot(d_mixed, kept[e], (0, 0)))
    pack_rows(block, cols, result, send)


def split_rows(place, cols, values, own, other):
    hidden = values.shape[0] // 2
    first = place[0] == 0
    low, high = values[:hidden], values[hidden:]
    mine = jnp.where(first, low, high)
    yours = jnp.where(first, high, low)
    for i in range(own.shape[0]):
        own[i] = mine[:, i * cols : (i + 1) * cols].astype(bf16)
        other[i] = yours[:, i * cols : (i + 1) * cols].astype(bf16)


def head(
    width, scale, place, arrived, weights, normed_far, own_far, other_far,
    send, d_gate, terms, updated_own, updated_other,
    normed, own, other, upstream, arrivals,
):
    parts, total, _ = weights.shape
    hidden = (total - 2 * width) // 2
    devices, q, flat = arrived.shape
    count, _, cols = other.shape
    copies = [
        pltpu.make_async_copy(normed_far, normed, arrivals.at[0]),
        pltpu.make_async_copy(own_far.at[pl.ds(place[0] * count, count)], own, arrivals.at[1]),
        pltpu.make_async_copy(other_far, other, arrivals.at[2]),
    ]
    for copy in copies:
        copy.start()
    mixed = jnp.concatenate([arrived[s].astype(f32) for s in range(devices)], 0)
    average = jnp.mean(mixed, 0, keepdims=True)
    spread = jnp.mean(mixed * mixed, 0, keepdims=True) - average * average
    inverse = lax.rsqrt(spread + epsilon)
    hat = (mixed - average) * inverse
    hat_rounded = hat.astype(bf16)
    w_out = rows_of(weights, 2 * width + hidden, hidden)
    proj = dot(w_out, hat_rounded, (1, 0))
    for copy in copies:
        copy.wait()
    for part, side in ((own, place[0]), (other, 1 - place[0])):
        upstream[pl.ds(pl.multiple_of(side * hidden, hidden), hidden)] = jnp.concatenate(
            [part[i].astype(f32) for i in range(count)], axis=1
        )
    gate = jax.nn.sigmoid(dot(rows_of(weights, 2 * width, hidden), normed[...], (1, 0)))
    up = upstream[...]
    d_proj = (up * gate).astype(bf16)
    d_gate[...] = (up * proj * gate * (1.0 - gate)).astype(bf16)
    d_norm = dot(w_out, d_proj, (0, 0))
    d_mixed = inverse * (
        d_norm
        - jnp.mean(d_norm, 0, keepdims=True)
        - hat * jnp.mean(d_norm * hat, 0, keepdims=True)
    )
    for s in range(devices):
        send[s] = d_mixed[s * q : (s + 1) * q].astype(bf16)
    by_gate = dot(d_gate[...], normed[...], (1, 1)) * scale
    by_out = dot(d_proj, hat_rounded, (1, 1)) * scale
    for c in range(parts):
        terms[c, :hidden] = by_gate[c * hidden : (c + 1) * hidden]
        terms[c, hidden:] = by_out[c * hidden : (c + 1) * hidden]
    split_rows(place, cols, gate * proj, updated_own, updated_other)


def offsets(shape):
    return list(np.ndindex(*shape))


def tail(width, scale, grid, place, arrived, weights, pair_far, d_gate_far, head_terms, *rest):
    parts, total, channels = weights.shape
    hidden = (total - 2 * width) // 2
    devices, q, flat = arrived.shape
    moves = offsets(grid)
    sends, (grad_own, grad_other) = rest[: len(moves)], rest[len(moves) : len(moves) + 2]
    pair, d_gate, whole, arrivals = rest[len(moves) + 2 :]
    count, cols, _ = pair.shape
    copies = [
        pltpu.make_async_copy(pair_far.at[pl.ds(place[0] * count, count)], pair, arrivals.at[0]),
        pltpu.make_async_copy(d_gate_far, d_gate, arrivals.at[1]),
    ]
    for copy in copies:
        copy.start()
    for copy in copies:
        copy.wait()
    hat, inverse = normalized(pair[...])
    normed = hat.astype(bf16)
    w_gate, w_value = rows_of(weights, 0, width), rows_of(weights, width, width)
    gate = jax.nn.sigmoid(dot(w_gate, normed, (1, 0)))
    value = dot(w_value, normed, (1, 0))
    grad = arrived[...].astype(f32).reshape(devices * q, flat)
    by_value = grad * gate
    by_gate = (by_value * (value * (1.0 - gate))).astype(bf16)
    by_value = by_value.astype(bf16)
    terms = [dot(by_gate, normed, (1, 1)) * scale, dot(by_value, normed, (1, 1)) * scale]
    for c in range(parts):
        for at, term in enumerate(terms):
            start = c * total + at * width
            whole[start : start + width] = term[c * width : (c + 1) * width]
        whole[c * total + 2 * width : (c + 1) * total] = head_terms[c]
    per = sends[0].shape[0]
    for send, move in zip(sends, moves):
        at = 0
        for d in range(len(grid)):
            at = at * grid[d] + lax.rem(place[d] + move[d], grid[d])
        send[...] = whole[pl.ds(pl.multiple_of(at * per, 8), per)].astype(bf16)
    d_input = dot(w_gate, by_gate, (0, 0)) + dot(w_value, by_value, (0, 0))
    d_input = d_input + dot(rows_of(weights, 2 * width, hidden), d_gate[...], (0, 0))
    back = inverse * (
        d_input
        - jnp.mean(d_input, 0, keepdims=True)
        - hat * jnp.mean(d_input * hat, 0, keepdims=True)
    )
    split_rows(place, cols, back, grad_own, grad_other)


def add_up(*refs):
    total = 0.0
    for ref in refs[:-1]:
        total = total + ref[...].astype(f32)
    refs[-1][...] = total.astype(bf16)


def add_planes(place, *refs):
    terms, out, held = refs[:-2], refs[-2], refs[-1]
    far = len(terms)
    for m, term in enumerate(terms):
        held[lax.rem(place[3] + far - m, far)] = term[...].astype(f32)
    out[...] = jnp.sum(held[...], 0).astype(bf16)


def turn_back(grid, place, order, *refs):
    width = order.shape[0]
    hidden = width // 2
    moves = offsets(grid[1:])
    pieces, outs, whole = refs[: len(moves)], refs[len(moves) : -1], refs[-1]
    per = pieces[0].shape[0]
    for piece, move in zip(pieces, moves):
        at = 0
        for d in range(len(move)):
            at = at * grid[d + 1] + lax.rem(place[d + 1] + grid[d + 1] - move[d], grid[d + 1])
        whole[pl.ds(pl.multiple_of(at * per, 8), per)] = piece[...].astype(f32)
    order = order[...]
    ga, pa, gb, pb, go, wo = outs
    for at, (left, right) in enumerate(((ga, gb), (pa, pb))):
        both = dot(order, whole[at * width : (at + 1) * width].astype(bf16), (0, 0))
        left[...] = both[:hidden]
        right[...] = both[hidden:]
    go[...] = whole[2 * width : 2 * width + hidden]
    wo[...] = whole[2 * width + hidden :]


def join_rows(place, own, other, out):
    count = own.shape[0]
    out[pl.ds(place[0] * count, count)] = own[...]
    out[pl.ds((1 - place[0]) * count, count)] = other[...]


def by_channels(pair, cotangent, w_gate_a, w_proj_a, w_gate_b, w_proj_b, w_gate_out, w_out):
    row_count, cols, channels = pair.shape
    hidden = w_gate_a.shape[1]
    parts, col_parts, row_parts = lax.axis_size("ch"), lax.axis_size("col"), lax.axis_size("row")
    devices = parts * col_parts * row_parts
    share = hidden * parts // devices
    width = 2 * hidden
    count = row_count // parts
    flat = count * cols
    tokens = cols * col_parts
    scale = 1.0 / tokens
    order = jnp.asarray(grouping(hidden, share), bf16)
    swap = [(c, parts - 1 - c) for c in range(parts)]
    near = 2
    far = row_parts // near
    grid = (parts, near, col_parts)
    row = lax.axis_index("row")
    place = jnp.stack(
        [lax.axis_index("ch"), row % near, lax.axis_index("col"), row // near]
    ).astype(jnp.int32)

    def shift(array, move):
        pairs = []
        for z, x, y, c in np.ndindex(far, near, col_parts, parts):
            to = ((z + move[3]) % far, (x + move[1]) % near, (y + move[2]) % col_parts, (c + move[0]) % parts)
            line = lambda at: ((at[0] * near + at[1]) * col_parts + at[2]) * parts + at[3]
            pairs.append((int(line((z, x, y, c))), int(line(to))))
        return lax.ppermute(array, ("row", "col", "ch"), pairs)

    (weights,) = call(
        turn_weights,
        [((2 * width + 2 * hidden, channels), bf16)],
        (order, w_gate_a.T, w_proj_a.T, w_gate_b.T, w_proj_b.T, w_gate_out.T, w_out.T),
    )
    weights = lax.all_gather(weights, "ch")
    own = jnp.swapaxes(cotangent, 1, 2)
    other = lax.dynamic_slice_in_dim(own, (1 - place[0]) * count, count, 0)
    other = lax.ppermute(other, "ch", swap)
    send, normed = call(
        functools.partial(edges, width, count),
        [((devices, 2 * share, flat), bf16), ((channels, flat), bf16)],
        (place, pair, weights),
    )
    arrived = lax.all_to_all(send, everyone, 0, 0)
    room = pltpu.VMEM((col_parts * tokens * 8, -(-cols // 128) * 128), f32)
    send, kept = call(
        functools.partial(mix, col_parts, cols),
        [((devices, share, flat), bf16), ((2 * share, tokens, tokens), bf16)],
        (arrived,),
        (room, room),
    )
    arrived = lax.all_to_all(send, everyone, 0, 0)
    part = ((count, hidden, cols), bf16)
    send, d_gate, head_terms, updated_own, updated_other = call(
        functools.partial(head, width, scale),
        [
            ((devices, share, flat), bf16),
            ((hidden * parts, flat), bf16),
            ((parts, 2 * hidden, channels), f32),
            part,
            part,
        ],
        (place, arrived, weights, normed, own, other),
        (
            pltpu.VMEM((channels, flat), bf16),
            pltpu.VMEM(*part),
            pltpu.VMEM(*part),
            pltpu.VMEM((hidden * parts, flat), f32),
            pltpu.SemaphoreType.DMA((3,)),
        ),
        far=(3, 4, 5),
    )
    arrived = lax.all_to_all(send, everyone, 0, 0)
    updated_other = lax.ppermute(updated_other, "ch", swap)
    (send,) = call(
        functools.partial(unmix, col_parts, cols),
        [((devices, 2 * share, flat), bf16)],
        (arrived, kept),
        (room, room, pltpu.VMEM(kept.shape, bf16), pltpu.SemaphoreType.DMA),
        far=(1,),
    )
    arrived = lax.all_to_all(send, everyone, 0, 0)
    (updated,) = call(
        join_rows, [((row_count, hidden, cols), bf16)], (place, updated_own, updated_other)
    )
    moves = offsets(grid)
    total = (2 * width + 2 * hidden) * parts
    per = total // len(moves)
    piece = ((per, channels), bf16)
    *sends, grad_own, grad_other = call(
        functools.partial(tail, width, scale, grid),
        [piece] * len(moves) + [part] * 2,
        (place, arrived, weights, pair, d_gate, head_terms),
        (
            pltpu.VMEM((count, cols, channels), bf16),
            pltpu.VMEM((hidden * parts, flat), bf16),
            pltpu.VMEM((total, channels), f32),
            pltpu.SemaphoreType.DMA((2,)),
        ),
        far=(3, 4),
    )
    terms = [shift(send, move + (0,)) if any(move) else send for send, move in zip(sends, moves)]
    grad_other = lax.ppermute(grad_other, "ch", swap)
    (sums,) = call(add_up, [piece], terms)
    terms = [shift(sums, (0, 0, 0, m)) if m else sums for m in range(far)]
    (sums,) = call(
        add_planes, [piece], (place, *terms), (pltpu.VMEM((far, per, channels), f32),)
    )
    terms = [
        shift(sums, (0,) + move + (0,)) if any(move) else sums for move in offsets(grid[1:])
    ]
    (grad_pair,) = call(
        join_rows, [((row_count, hidden, cols), bf16)], (place, grad_own, grad_other)
    )
    grads = call(
        functools.partial(turn_back, grid),
        [((hidden, channels), f32)] * 6,
        (place, order, *terms),
        (pltpu.VMEM((total // parts, channels), f32),),
    )
    return jnp.swapaxes(updated, 1, 2), jnp.swapaxes(grad_pair, 1, 2), *(g.T for g in grads)


def on_device(*arrays):
    row_count, cols, _ = arrays[0].shape
    parts, devices = lax.axis_size("ch"), lax.axis_size(everyone)
    hidden = arrays[2].shape[1]
    share = hidden * parts // devices
    per = 6 * hidden // (2 * lax.axis_size("col"))
    fits = (
        share * devices == hidden * parts
        and parts == 2
        and 2 * share == 8
        and row_count % parts == 0
        and lax.axis_size("row") % 2 == 0
        and per * 2 * lax.axis_size("col") == 6 * hidden
        and per % 16 == 0
        and arrays[1].shape[2] == hidden
        and cols % 16 == 0
    )
    return by_channels(*arrays) if fits else by_rows(*arrays)


def solution(mesh):
    in_specs = (
        P("row", "col", None),
        P("row", "col", "ch"),
        P(None, "ch"),
        P(None, "ch"),
        P(None, "ch"),
        P(None, "ch"),
        P(None, "ch"),
        P(None, "ch"),
    )
    out_specs = (
        P("row", "col", "ch"),
        P("row", "col", "ch"),
        P(None, "ch"),
        P(None, "ch"),
        P(None, "ch"),
        P(None, "ch"),
        P(None, "ch"),
        P(None, "ch"),
    )
    return jax.shard_map(
        on_device, mesh=mesh, in_specs=in_specs, out_specs=out_specs, check_vma=False
    )
```

```python
import functools

import jax
import jax.numpy as jnp
import numpy as np
from jax import lax
from jax.experimental import pallas as pl
from jax.experimental.pallas import tpu as pltpu
from jax.sharding import PartitionSpec as P

epsilon = 1e-05


def layer_norm(values):
    average = jnp.mean(values, -1, keepdims=True)
    centred = values - average
    spread = jnp.mean(centred * centred, -1, keepdims=True)
    inverse = lax.rsqrt(spread + epsilon)
    return (centred * inverse, inverse)


def matmul(first, second):
    return jnp.dot(first, second, preferred_element_type=jnp.float32)


def by_rows(pair, cotangent, w_gate_a, w_proj_a, w_gate_b, w_proj_b, w_gate_out, w_out):
    row_count, col_count, channels = pair.shape
    hidden = w_gate_a.shape[1]
    total_hidden = hidden * lax.axis_size("ch")
    out_width = cotangent.shape[2]
    length = row_count * lax.axis_size("row")
    grad_scale = 1.0 / length
    pair_hat, pair_rstd = layer_norm(pair.astype(jnp.float32))
    flat_norm = pair_hat.astype(jnp.bfloat16).reshape(row_count * col_count, channels)
    w_four = jnp.concatenate([w_gate_a, w_proj_a, w_gate_b, w_proj_b], axis=1)
    projected = matmul(flat_norm, w_four)
    gate_a = jax.nn.sigmoid(projected[:, :hidden])
    proj_a = projected[:, hidden : 2 * hidden]
    gate_b = jax.nn.sigmoid(projected[:, 2 * hidden : 3 * hidden])
    proj_b = projected[:, 3 * hidden :]
    left_edge = (gate_a * proj_a).astype(jnp.bfloat16).reshape(row_count, col_count, hidden)
    right_edge = (gate_b * proj_b).astype(jnp.bfloat16).reshape(row_count, col_count, hidden)
    right_all = lax.all_gather(right_edge, "row", axis=0, tiled=True)
    mixed_swap = lax.psum_scatter(
        jnp.einsum("jkh,ikh->jih", right_all, left_edge, preferred_element_type=jnp.float32).astype(
            jnp.bfloat16
        ),
        "col",
        scatter_dimension=0,
        tiled=True,
    ).astype(jnp.float32)
    mixed = jnp.swapaxes(mixed_swap, 0, 1).reshape(row_count * col_count, hidden)
    hidden_sums = lax.psum((jnp.sum(mixed, -1), jnp.sum(mixed * mixed, -1)), "ch")
    hidden_mean = (hidden_sums[0] / total_hidden)[:, None]
    hidden_var = (hidden_sums[1] / total_hidden)[:, None] - hidden_mean * hidden_mean
    hidden_rstd = lax.rsqrt(hidden_var + epsilon)
    mixed_hat = (mixed - hidden_mean) * hidden_rstd
    mixed_norm = mixed_hat.astype(jnp.bfloat16)
    norm_full = lax.all_gather(mixed_norm, "ch", axis=1, tiled=True)
    gate_out = jax.nn.sigmoid(matmul(flat_norm, w_gate_out))
    proj_out = matmul(norm_full, w_out)
    updated = (gate_out * proj_out).astype(jnp.bfloat16).reshape(row_count, col_count, out_width)
    upstream = cotangent.reshape(row_count * col_count, out_width).astype(jnp.float32)
    d_proj = (upstream * gate_out).astype(jnp.bfloat16)
    d_gate = (upstream * proj_out * gate_out * (1.0 - gate_out)).astype(jnp.bfloat16)
    head_grads = lax.psum(
        (matmul(norm_full.T, d_proj) * grad_scale, matmul(flat_norm.T, d_gate) * grad_scale),
        ("row", "col"),
    )
    d_norm = lax.psum_scatter(
        matmul(d_proj, w_out.T).astype(jnp.bfloat16), "ch", scatter_dimension=1, tiled=True
    ).astype(jnp.float32)
    back_sums = lax.psum((jnp.sum(d_norm, -1), jnp.sum(d_norm * mixed_hat, -1)), "ch")
    d_mixed = hidden_rstd * (
        d_norm
        - (back_sums[0] / total_hidden)[:, None]
        - mixed_hat * (back_sums[1] / total_hidden)[:, None]
    )
    d_mixed = d_mixed.astype(jnp.bfloat16).reshape(row_count, col_count, hidden)
    d_rows = lax.all_gather(d_mixed, "col", axis=1, tiled=True)
    right_back = lax.all_gather(right_edge, "row", axis=0, tiled=True)
    d_left = jnp.einsum("ijh,jkh->ikh", d_rows, right_back, preferred_element_type=jnp.float32)
    d_left = d_left.reshape(row_count * col_count, hidden)
    left_all = lax.all_gather(left_edge, "row", axis=0, tiled=True)
    d_columns = lax.all_to_all(d_rows, "row", split_axis=1, concat_axis=0, tiled=True)
    d_right = jnp.einsum("ijh,ikh->jkh", d_columns, left_all, preferred_element_type=jnp.float32)
    d_right = d_right.reshape(row_count * col_count, hidden)
    grad_pa = (d_left * gate_a).astype(jnp.bfloat16)
    grad_ga = (d_left * proj_a * gate_a * (1.0 - gate_a)).astype(jnp.bfloat16)
    grad_pb = (d_right * gate_b).astype(jnp.bfloat16)
    grad_gb = (d_right * proj_b * gate_b * (1.0 - gate_b)).astype(jnp.bfloat16)
    d_four = jnp.concatenate([grad_ga, grad_pa, grad_gb, grad_pb], axis=1)
    weight_terms = matmul(flat_norm.T, d_four) * grad_scale
    summed = lax.psum(weight_terms, ("row", "col"))
    d_flat = matmul(d_four, w_four.T) + matmul(d_gate, w_gate_out.T)
    hat_all = pair_hat.reshape(row_count * col_count, channels)
    rstd_flat = pair_rstd.reshape(row_count * col_count, 1)
    offset = lax.axis_index("ch") * out_width
    grad_whole = lax.psum(d_flat.astype(jnp.bfloat16), "ch").astype(jnp.float32)
    grad_full = rstd_flat * (
        grad_whole
        - jnp.mean(grad_whole, -1, keepdims=True)
        - hat_all * jnp.mean(grad_whole * hat_all, -1, keepdims=True)
    )
    grad_pair = lax.dynamic_slice_in_dim(grad_full, offset, out_width, 1)
    grad_pair = grad_pair.astype(jnp.bfloat16).reshape(row_count, col_count, out_width)
    return (
        updated,
        grad_pair,
        summed[:, :hidden],
        summed[:, hidden : 2 * hidden],
        summed[:, 2 * hidden : 3 * hidden],
        summed[:, 3 * hidden :],
        head_grads[1],
        head_grads[0],
    )


everyone = ("col", "row", "ch")
f32, bf16 = jnp.float32, jnp.bfloat16


def dot(first, second, over):
    return lax.dot_general(
        first, second, (((over[0],), (over[1],)), ((), ())), preferred_element_type=f32
    )


def call(kernel, outs, args, scratch=(), far=(), outs_far=False, room=16):
    whole = pl.BlockSpec(memory_space=pltpu.VMEM)
    anywhere = pl.BlockSpec(memory_space=pl.ANY)
    return pl.pallas_call(
        kernel,
        out_shape=tuple(jax.ShapeDtypeStruct(*out) for out in outs),
        in_specs=[anywhere if at in far else whole for at in range(len(args))],
        out_specs=tuple(anywhere if outs_far else whole for _ in outs),
        scratch_shapes=scratch,
        compiler_params=pltpu.CompilerParams(vmem_limit_bytes=room * 2**20),
    )(*args)


def grouping(hidden, share):
    shape = (2 * hidden, 2 * hidden)
    rows = lax.broadcasted_iota(jnp.int32, shape, 0)
    columns = lax.broadcasted_iota(jnp.int32, shape, 1)
    group, within = rows // (2 * share), lax.rem(rows, 2 * share)
    side = within // share
    wanted = side * hidden + group * share + within - side * share
    return jnp.where(columns == wanted, 1.0, 0.0).astype(bf16)


def start_all(copies):
    for copy in copies:
        copy.start()


def wait_all(copies):
    for copy in copies:
        copy.wait()


def turn_weights(share, ga, pa, gb, pb, go, wo, out, gates, values, last, arrivals):
    hidden = go.shape[0]
    width = 2 * hidden
    copies = []
    for at, (held, low, high) in enumerate(((gates, ga, gb), (values, pa, pb), (last, go, wo))):
        copies.append(pltpu.make_async_copy(low, held.at[0:hidden], arrivals.at[2 * at]))
        copies.append(pltpu.make_async_copy(high, held.at[hidden:width], arrivals.at[2 * at + 1]))
    start_all(copies)
    order = grouping(hidden, share)
    wait_all(copies)
    out[:width] = dot(order, gates[...], (1, 0)).astype(bf16)
    out[width : 2 * width] = dot(order, values[...], (1, 0)).astype(bf16)
    out[2 * width :] = last[...]


def rows_of(weights, start, count):
    return jnp.concatenate([weights[c, start : start + count] for c in range(weights.shape[0])], 0)


def normalized(pair):
    count, cols, channels = pair.shape
    values = pair.astype(f32).reshape(count * cols, channels).T
    centred = values - jnp.mean(values, 0, keepdims=True)
    rstd = lax.rsqrt(jnp.mean(centred * centred, 0, keepdims=True) + epsilon)
    return centred * rstd, rstd


def edges(width, count, pair, weights, send, normed):
    hat, _ = normalized(pair[pl.ds(lax.axis_index("ch") * count, count)])
    normed[...] = hat.astype(bf16)
    gate = jax.nn.sigmoid(dot(rows_of(weights, 0, width), normed[...], (1, 0)))
    value = dot(rows_of(weights, width, width), normed[...], (1, 0))
    send[...] = (gate * value).reshape(send.shape).astype(bf16)


def spread_rows(block, cols, arrived, held):
    devices, q, flat = arrived.shape
    rows = flat // cols
    for s in range(devices):
        tile = arrived[s].astype(f32)
        for i in range(rows):
            start = (s * rows + i) * block
            held[start : start + q, 0:cols] = tile[:, i * cols : (i + 1) * cols]


def pack_rows(block, cols, held, send):
    devices, q, flat = send.shape
    rows = flat // cols
    for s in range(devices):
        starts = [(s * rows + i) * block for i in range(rows)]
        whole = jnp.concatenate([held[start : start + block, 0:cols] for start in starts], axis=1)
        send[s] = whole[:q].astype(bf16)


def square(block, parts, cols, held, e):
    tokens = parts * cols
    return jnp.concatenate(
        [
            held[pl.ds(p * tokens * block + e, tokens, stride=block), 0:cols]
            for p in range(parts)
        ],
        axis=1,
    ).astype(bf16)


def put_square(block, parts, cols, held, e, values):
    tokens = parts * cols
    for p in range(parts):
        held[pl.ds(p * tokens * block + e, tokens, stride=block), 0:cols] = values[
            :, p * cols : (p + 1) * cols
        ]


def mix(parts, cols, arrived, send, kept, held, result):
    block = 8
    q = arrived.shape[1]
    spread_rows(block, cols, arrived, held)
    for e in range(q // 2):
        left = square(block, parts, cols, held, e)
        right = square(block, parts, cols, held, q // 2 + e)
        kept[e] = left
        kept[q // 2 + e] = right
        put_square(block, parts, cols, result, e, dot(left, right, (1, 1)))
    pack_rows(block, cols, result, send)


def unmix(parts, cols, arrived, kept_far, send, held, result, kept, arrival):
    block = 8
    q = arrived.shape[1]
    copy = pltpu.make_async_copy(kept_far, kept, arrival)
    copy.start()
    spread_rows(block, cols, arrived, held)
    copy.wait()
    for e in range(q):
        d_mixed = square(block, parts, cols, held, e)
        put_square(block, parts, cols, result, e, dot(d_mixed, kept[q + e], (1, 0)))
        put_square(block, parts, cols, result, q + e, dot(d_mixed, kept[e], (0, 0)))
    pack_rows(block, cols, result, send)


def split_rows(cols, values, own, other):
    hidden = values.shape[0] // 2
    first = lax.axis_index("ch") == 0
    low, high = values[:hidden], values[hidden:]
    mine = jnp.where(first, low, high)
    yours = jnp.where(first, high, low)
    for i in range(own.shape[0]):
        own[i] = mine[:, i * cols : (i + 1) * cols].astype(bf16)
        other[i] = yours[:, i * cols : (i + 1) * cols].astype(bf16)


def head(
    width, scale, arrived, weights, normed_far, own_far, other_far,
    send, d_gate, terms, updated_own, updated_other,
    normed, own, other, upstream, arrivals,
):
    parts, total, _ = weights.shape
    hidden = (total - 2 * width) // 2
    devices, q, flat = arrived.shape
    count, _, cols = other.shape
    core = lax.axis_index("ch")
    copies = [
        pltpu.make_async_copy(normed_far, normed, arrivals.at[0]),
        pltpu.make_async_copy(own_far.at[pl.ds(core * count, count)], own, arrivals.at[1]),
        pltpu.make_async_copy(other_far, other, arrivals.at[2]),
    ]
    start_all(copies)
    mixed = jnp.concatenate([arrived[s].astype(f32) for s in range(devices)], 0)
    average = jnp.mean(mixed, 0, keepdims=True)
    spread = jnp.mean(mixed * mixed, 0, keepdims=True) - average * average
    inverse = lax.rsqrt(spread + epsilon)
    hat = (mixed - average) * inverse
    hat_rounded = hat.astype(bf16)
    w_out = rows_of(weights, 2 * width + hidden, hidden)
    proj = dot(w_out, hat_rounded, (1, 0))
    wait_all(copies)
    for part, side in ((own, core), (other, 1 - core)):
        upstream[pl.ds(pl.multiple_of(side * hidden, hidden), hidden)] = jnp.concatenate(
            [part[i].astype(f32) for i in range(count)], axis=1
        )
    gate = jax.nn.sigmoid(dot(rows_of(weights, 2 * width, hidden), normed[...], (1, 0)))
    up = upstream[...]
    d_proj = (up * gate).astype(bf16)
    d_gate[...] = (up * proj * gate * (1.0 - gate)).astype(bf16)
    d_norm = dot(w_out, d_proj, (0, 0))
    d_mixed = inverse * (
        d_norm
        - jnp.mean(d_norm, 0, keepdims=True)
        - hat * jnp.mean(d_norm * hat, 0, keepdims=True)
    )
    for s in range(devices):
        send[s] = d_mixed[s * q : (s + 1) * q].astype(bf16)
    by_gate = dot(d_gate[...], normed[...], (1, 1)) * scale
    by_out = dot(d_proj, hat_rounded, (1, 1)) * scale
    for c in range(parts):
        terms[c, :hidden] = by_gate[c * hidden : (c + 1) * hidden]
        terms[c, hidden:] = by_out[c * hidden : (c + 1) * hidden]
    split_rows(cols, gate * proj, updated_own, updated_other)


def tail(
    width, scale, arrived, weights, pair_far, d_gate_far, head_terms,
    own_terms, parcel, grad_own,
    pair, d_gate, whole, arrivals,
):
    parts, total, channels = weights.shape
    hidden = (total - 2 * width) // 2
    devices, q, flat = arrived.shape
    count, cols, _ = pair.shape
    core = lax.axis_index("ch")
    copies = [
        pltpu.make_async_copy(pair_far.at[pl.ds(core * count, count)], pair, arrivals.at[0]),
        pltpu.make_async_copy(d_gate_far, d_gate, arrivals.at[1]),
    ]
    start_all(copies)
    wait_all(copies)
    hat, inverse = normalized(pair[...])
    normed = hat.astype(bf16)
    w_gate, w_value = rows_of(weights, 0, width), rows_of(weights, width, width)
    gate = jax.nn.sigmoid(dot(w_gate, normed, (1, 0)))
    value = dot(w_value, normed, (1, 0))
    grad = arrived[...].astype(f32).reshape(devices * q, flat)
    by_value = grad * gate
    by_gate = (by_value * (value * (1.0 - gate))).astype(bf16)
    by_value = by_value.astype(bf16)
    terms = [dot(by_gate, normed, (1, 1)) * scale, dot(by_value, normed, (1, 1)) * scale]
    for c in range(parts):
        for at, term in enumerate(terms):
            start = c * total + at * width
            whole[start : start + width] = term[c * width : (c + 1) * width]
        whole[c * total + 2 * width : (c + 1) * total] = head_terms[c]
    own_terms[...] = whole[pl.ds(pl.multiple_of(core * total, total), total)]
    parcel[count * hidden :] = whole[
        pl.ds(pl.multiple_of((1 - core) * total, total), total)
    ].astype(bf16)
    d_input = dot(w_gate, by_gate, (0, 0)) + dot(w_value, by_value, (0, 0))
    d_input = d_input + dot(rows_of(weights, 2 * width, hidden), d_gate[...], (0, 0))
    back = inverse * (
        d_input
        - jnp.mean(d_input, 0, keepdims=True)
        - hat * jnp.mean(d_input * hat, 0, keepdims=True)
    )
    first = core == 0
    mine = jnp.where(first, back[:hidden], back[hidden:])
    yours = jnp.where(first, back[hidden:], back[:hidden])
    for i in range(count):
        grad_own[i] = mine[:, i * cols : (i + 1) * cols].astype(bf16)
        parcel[i * hidden : (i + 1) * hidden] = jnp.pad(
            yours[:, i * cols : (i + 1) * cols], ((0, 0), (0, channels - cols))
        ).astype(bf16)


def halve(side, skip, own, arrived, kept, send):
    total = own[...] + arrived[skip:].astype(f32)
    half = total.shape[0] // 2
    low, high = total[:half], total[half:]
    first = side() == 0
    kept[...] = jnp.where(first, low, high)
    send[...] = jnp.where(first, high, low).astype(bf16)


def add(own, arrived, out):
    out[...] = (own[...].astype(f32) + arrived[...].astype(f32)).astype(bf16)


def join(side, own, arrived, out):
    first = side() == 0
    rows = own.shape[0]
    out[:rows] = jnp.where(first, own[...].astype(f32), arrived[...].astype(f32)).astype(out.dtype)
    out[rows:] = jnp.where(first, arrived[...].astype(f32), own[...].astype(f32)).astype(out.dtype)


def turn_back(side, share, own, arrived, *refs):
    outs, whole, results, leaves = refs[:6], refs[6], refs[7], refs[8]
    _, hidden, channels = results.shape
    width = 2 * hidden
    join(side, own, arrived, whole)
    order = grouping(hidden, share)
    for at in range(2):
        both = dot(order, whole[at * width : (at + 1) * width].astype(bf16), (0, 0))
        results[at] = both[:hidden]
        results[2 + at] = both[hidden:]
    results[4] = whole[2 * width : 2 * width + hidden]
    results[5] = whole[2 * width + hidden :]
    copies = [
        pltpu.make_async_copy(results.at[at], out, leaves.at[at]) for at, out in enumerate(outs)
    ]
    start_all(copies)
    wait_all(copies)


def join_rows(own, other, out, leaves):
    count = own.shape[0]
    core = lax.axis_index("ch")
    copies = [
        pltpu.make_async_copy(own, out.at[pl.ds(core * count, count)], leaves.at[0]),
        pltpu.make_async_copy(other, out.at[pl.ds((1 - core) * count, count)], leaves.at[1]),
    ]
    start_all(copies)
    wait_all(copies)


def join_parcel(own, parcel, out, other, leaves):
    count, hidden, cols = own.shape
    other[...] = parcel[: count * hidden, :cols].reshape(count, hidden, cols)
    join_rows(own, other, out, leaves)


def by_channels(pair, cotangent, w_gate_a, w_proj_a, w_gate_b, w_proj_b, w_gate_out, w_out):
    row_count, cols, channels = pair.shape
    hidden = w_gate_a.shape[1]
    parts, col_parts, row_parts = lax.axis_size("ch"), lax.axis_size("col"), lax.axis_size("row")
    devices = parts * col_parts * row_parts
    share = hidden * parts // devices
    width = 2 * hidden
    count = row_count // parts
    flat = count * cols
    tokens = cols * col_parts
    scale = 1.0 / tokens
    swap = [(c, parts - 1 - c) for c in range(parts)]
    near = 2
    far = row_parts // near

    def across(array, flip):
        return lax.ppermute(array, "row", [(r, r ^ flip) for r in range(row_parts)])

    def col_side():
        return lax.axis_index("col")

    def near_side():
        return lax.rem(lax.axis_index("row"), near)

    whole_weight = pltpu.VMEM((2 * hidden, channels), bf16)
    (weights,) = call(
        functools.partial(turn_weights, share),
        [((2 * width + 2 * hidden, channels), bf16)],
        (w_gate_a.T, w_proj_a.T, w_gate_b.T, w_proj_b.T, w_gate_out.T, w_out.T),
        (whole_weight, whole_weight, whole_weight, pltpu.SemaphoreType.DMA((6,))),
        far=range(6),
        room=60,
    )
    weights = lax.all_gather(weights, "ch")
    own = jnp.swapaxes(cotangent, 1, 2)
    other = lax.dynamic_slice_in_dim(own, (1 - lax.axis_index("ch")) * count, count, 0)
    other = lax.ppermute(other, "ch", swap)
    send, normed = call(
        functools.partial(edges, width, count),
        [((devices, 2 * share, flat), bf16), ((channels, flat), bf16)],
        (pair, weights),
    )
    arrived = lax.all_to_all(send, everyone, 0, 0)
    room = pltpu.VMEM((col_parts * tokens * 8, -(-cols // 128) * 128), f32)
    send, kept = call(
        functools.partial(mix, col_parts, cols),
        [((devices, share, flat), bf16), ((2 * share, tokens, tokens), bf16)],
        (arrived,),
        (room, room),
    )
    arrived = lax.all_to_all(send, everyone, 0, 0)
    part = ((count, hidden, cols), bf16)
    send, d_gate, head_terms, updated_own, updated_other = call(
        functools.partial(head, width, scale),
        [
            ((devices, share, flat), bf16),
            ((hidden * parts, flat), bf16),
            ((parts, 2 * hidden, channels), f32),
            part,
            part,
        ],
        (arrived, weights, normed, own, other),
        (
            pltpu.VMEM((channels, flat), bf16),
            pltpu.VMEM(*part),
            pltpu.VMEM(*part),
            pltpu.VMEM((hidden * parts, flat), f32),
            pltpu.SemaphoreType.DMA((3,)),
        ),
        far=(2, 3, 4),
    )
    arrived = lax.all_to_all(send, everyone, 0, 0)
    updated_other = lax.ppermute(updated_other, "ch", swap)
    (send,) = call(
        functools.partial(unmix, col_parts, cols),
        [((devices, 2 * share, flat), bf16)],
        (arrived, kept),
        (room, room, pltpu.VMEM(kept.shape, bf16), pltpu.SemaphoreType.DMA),
        far=(1,),
    )
    arrived = lax.all_to_all(send, everyone, 0, 0)
    rows = [((row_count, hidden, cols), bf16)]
    two = pltpu.SemaphoreType.DMA((2,))
    (updated,) = call(join_rows, rows, (updated_own, updated_other), (two,), (0, 1), True)
    arrived, updated = lax.optimization_barrier((arrived, updated))
    total = 2 * width + 2 * hidden
    terms, parcel, grad_own = call(
        functools.partial(tail, width, scale),
        [((total, channels), f32), ((count * hidden + total, channels), bf16), part],
        (arrived, weights, pair, d_gate, head_terms),
        (
            pltpu.VMEM((count, cols, channels), bf16),
            pltpu.VMEM((hidden * parts, flat), bf16),
            pltpu.VMEM((total * parts, channels), f32),
            two,
        ),
        far=(2, 3),
    )
    parcel = lax.ppermute(parcel, "ch", swap)
    half = (total // 2, channels)
    quarter = (total // 4, channels)
    terms, send = call(
        functools.partial(halve, col_side, count * hidden), [(half, f32), (half, bf16)], (terms, parcel)
    )
    arrived = lax.ppermute(send, "col", swap)
    (grad_pair,) = call(join_parcel, rows, (grad_own, parcel), (pltpu.VMEM(*part), two), (), True)
    terms, send = call(
        functools.partial(halve, near_side, 0), [(quarter, f32), (quarter, bf16)], (terms, arrived)
    )
    arrived = across(send, 1)
    (sums,) = call(add, [(quarter, bf16)], (terms, arrived))
    flip = near
    while flip < row_parts:
        (sums,) = call(add, [(quarter, bf16)], (sums, across(sums, flip)))
        sums, grad_pair = lax.optimization_barrier((sums, grad_pair))
        flip *= 2
    (sums,) = call(functools.partial(join, near_side), [(half, bf16)], (sums, across(sums, 1)))
    grads = call(
        functools.partial(turn_back, col_side, share),
        [((hidden, channels), f32)] * 6,
        (sums, lax.ppermute(sums, "col", swap)),
        (
            pltpu.VMEM((total, channels), f32),
            pltpu.VMEM((6, hidden, channels), f32),
            pltpu.SemaphoreType.DMA((6,)),
        ),
        outs_far=True,
    )
    return jnp.swapaxes(updated, 1, 2), jnp.swapaxes(grad_pair, 1, 2), *(g.T for g in grads)


def on_device(*arrays):
    row_count, cols, _ = arrays[0].shape
    parts, devices = lax.axis_size("ch"), lax.axis_size(everyone)
    hidden = arrays[2].shape[1]
    share = hidden * parts // devices
    row_axis = lax.axis_size("row")
    fits = (
        share * devices == hidden * parts
        and parts == 2
        and 2 * share == 8
        and row_count % parts == 0
        and lax.axis_size("col") == 2
        and row_axis > 1
        and row_axis & (row_axis - 1) == 0
        and 6 * hidden % 64 == 0
        and cols <= arrays[0].shape[2]
        and arrays[1].shape[2] == hidden
        and cols % 16 == 0
    )
    return by_channels(*arrays) if fits else by_rows(*arrays)


def solution(mesh):
    in_specs = (
        P("row", "col", None),
        P("row", "col", "ch"),
        P(None, "ch"),
        P(None, "ch"),
        P(None, "ch"),
        P(None, "ch"),
        P(None, "ch"),
        P(None, "ch"),
    )
    out_specs = (
        P("row", "col", "ch"),
        P("row", "col", "ch"),
        P(None, "ch"),
        P(None, "ch"),
        P(None, "ch"),
        P(None, "ch"),
        P(None, "ch"),
        P(None, "ch"),
    )
    return jax.shard_map(
        on_device, mesh=mesh, in_specs=in_specs, out_specs=out_specs, check_vma=False
    )
```

```python
import functools

import jax
import jax.numpy as jnp
import numpy as np
from jax import lax
from jax.experimental import pallas as pl
from jax.experimental.pallas import tpu as pltpu
from jax.sharding import PartitionSpec as P

epsilon = 1e-05


def layer_norm(values):
    average = jnp.mean(values, -1, keepdims=True)
    centred = values - average
    spread = jnp.mean(centred * centred, -1, keepdims=True)
    inverse = lax.rsqrt(spread + epsilon)
    return (centred * inverse, inverse)


def matmul(first, second):
    return jnp.dot(first, second, preferred_element_type=jnp.float32)


def by_rows(pair, cotangent, w_gate_a, w_proj_a, w_gate_b, w_proj_b, w_gate_out, w_out):
    row_count, col_count, channels = pair.shape
    hidden = w_gate_a.shape[1]
    total_hidden = hidden * lax.axis_size("ch")
    out_width = cotangent.shape[2]
    length = row_count * lax.axis_size("row")
    grad_scale = 1.0 / length
    pair_hat, pair_rstd = layer_norm(pair.astype(jnp.float32))
    flat_norm = pair_hat.astype(jnp.bfloat16).reshape(row_count * col_count, channels)
    w_four = jnp.concatenate([w_gate_a, w_proj_a, w_gate_b, w_proj_b], axis=1)
    projected = matmul(flat_norm, w_four)
    gate_a = jax.nn.sigmoid(projected[:, :hidden])
    proj_a = projected[:, hidden : 2 * hidden]
    gate_b = jax.nn.sigmoid(projected[:, 2 * hidden : 3 * hidden])
    proj_b = projected[:, 3 * hidden :]
    left_edge = (gate_a * proj_a).astype(jnp.bfloat16).reshape(row_count, col_count, hidden)
    right_edge = (gate_b * proj_b).astype(jnp.bfloat16).reshape(row_count, col_count, hidden)
    right_all = lax.all_gather(right_edge, "row", axis=0, tiled=True)
    mixed_swap = lax.psum_scatter(
        jnp.einsum("jkh,ikh->jih", right_all, left_edge, preferred_element_type=jnp.float32).astype(
            jnp.bfloat16
        ),
        "col",
        scatter_dimension=0,
        tiled=True,
    ).astype(jnp.float32)
    mixed = jnp.swapaxes(mixed_swap, 0, 1).reshape(row_count * col_count, hidden)
    hidden_sums = lax.psum((jnp.sum(mixed, -1), jnp.sum(mixed * mixed, -1)), "ch")
    hidden_mean = (hidden_sums[0] / total_hidden)[:, None]
    hidden_var = (hidden_sums[1] / total_hidden)[:, None] - hidden_mean * hidden_mean
    hidden_rstd = lax.rsqrt(hidden_var + epsilon)
    mixed_hat = (mixed - hidden_mean) * hidden_rstd
    mixed_norm = mixed_hat.astype(jnp.bfloat16)
    norm_full = lax.all_gather(mixed_norm, "ch", axis=1, tiled=True)
    gate_out = jax.nn.sigmoid(matmul(flat_norm, w_gate_out))
    proj_out = matmul(norm_full, w_out)
    updated = (gate_out * proj_out).astype(jnp.bfloat16).reshape(row_count, col_count, out_width)
    upstream = cotangent.reshape(row_count * col_count, out_width).astype(jnp.float32)
    d_proj = (upstream * gate_out).astype(jnp.bfloat16)
    d_gate = (upstream * proj_out * gate_out * (1.0 - gate_out)).astype(jnp.bfloat16)
    head_grads = lax.psum(
        (matmul(norm_full.T, d_proj) * grad_scale, matmul(flat_norm.T, d_gate) * grad_scale),
        ("row", "col"),
    )
    d_norm = lax.psum_scatter(
        matmul(d_proj, w_out.T).astype(jnp.bfloat16), "ch", scatter_dimension=1, tiled=True
    ).astype(jnp.float32)
    back_sums = lax.psum((jnp.sum(d_norm, -1), jnp.sum(d_norm * mixed_hat, -1)), "ch")
    d_mixed = hidden_rstd * (
        d_norm
        - (back_sums[0] / total_hidden)[:, None]
        - mixed_hat * (back_sums[1] / total_hidden)[:, None]
    )
    d_mixed = d_mixed.astype(jnp.bfloat16).reshape(row_count, col_count, hidden)
    d_rows = lax.all_gather(d_mixed, "col", axis=1, tiled=True)
    right_back = lax.all_gather(right_edge, "row", axis=0, tiled=True)
    d_left = jnp.einsum("ijh,jkh->ikh", d_rows, right_back, preferred_element_type=jnp.float32)
    d_left = d_left.reshape(row_count * col_count, hidden)
    left_all = lax.all_gather(left_edge, "row", axis=0, tiled=True)
    d_columns = lax.all_to_all(d_rows, "row", split_axis=1, concat_axis=0, tiled=True)
    d_right = jnp.einsum("ijh,ikh->jkh", d_columns, left_all, preferred_element_type=jnp.float32)
    d_right = d_right.reshape(row_count * col_count, hidden)
    grad_pa = (d_left * gate_a).astype(jnp.bfloat16)
    grad_ga = (d_left * proj_a * gate_a * (1.0 - gate_a)).astype(jnp.bfloat16)
    grad_pb = (d_right * gate_b).astype(jnp.bfloat16)
    grad_gb = (d_right * proj_b * gate_b * (1.0 - gate_b)).astype(jnp.bfloat16)
    d_four = jnp.concatenate([grad_ga, grad_pa, grad_gb, grad_pb], axis=1)
    weight_terms = matmul(flat_norm.T, d_four) * grad_scale
    summed = lax.psum(weight_terms, ("row", "col"))
    d_flat = matmul(d_four, w_four.T) + matmul(d_gate, w_gate_out.T)
    hat_all = pair_hat.reshape(row_count * col_count, channels)
    rstd_flat = pair_rstd.reshape(row_count * col_count, 1)
    offset = lax.axis_index("ch") * out_width
    grad_whole = lax.psum(d_flat.astype(jnp.bfloat16), "ch").astype(jnp.float32)
    grad_full = rstd_flat * (
        grad_whole
        - jnp.mean(grad_whole, -1, keepdims=True)
        - hat_all * jnp.mean(grad_whole * hat_all, -1, keepdims=True)
    )
    grad_pair = lax.dynamic_slice_in_dim(grad_full, offset, out_width, 1)
    grad_pair = grad_pair.astype(jnp.bfloat16).reshape(row_count, col_count, out_width)
    return (
        updated,
        grad_pair,
        summed[:, :hidden],
        summed[:, hidden : 2 * hidden],
        summed[:, 2 * hidden : 3 * hidden],
        summed[:, 3 * hidden :],
        head_grads[1],
        head_grads[0],
    )


everyone = ("col", "row", "ch")
f32, bf16 = jnp.float32, jnp.bfloat16


def dot(first, second, over):
    return lax.dot_general(
        first, second, (((over[0],), (over[1],)), ((), ())), preferred_element_type=f32
    )


def call(kernel, outs, args, scratch=(), far=(), outs_far=False, room=16):
    whole = pl.BlockSpec(memory_space=pltpu.VMEM)
    anywhere = pl.BlockSpec(memory_space=pl.ANY)
    return pl.pallas_call(
        kernel,
        out_shape=tuple(jax.ShapeDtypeStruct(*out) for out in outs),
        in_specs=[anywhere if at in far else whole for at in range(len(args))],
        out_specs=tuple(anywhere if outs_far else whole for _ in outs),
        scratch_shapes=scratch,
        compiler_params=pltpu.CompilerParams(vmem_limit_bytes=room * 2**20),
    )(*args)


def grouping(hidden, share):
    shape = (2 * hidden, 2 * hidden)
    rows = lax.broadcasted_iota(jnp.int32, shape, 0)
    columns = lax.broadcasted_iota(jnp.int32, shape, 1)
    group, within = rows // (2 * share), lax.rem(rows, 2 * share)
    side = within // share
    wanted = side * hidden + group * share + within - side * share
    return jnp.where(columns == wanted, 1.0, 0.0).astype(bf16)


def start_all(copies):
    for copy in copies:
        copy.start()


def wait_all(copies):
    for copy in copies:
        copy.wait()


def prepare(share, ga, pa, gb, pb, go, wo, pair_far, out, normed, gates, values, last, pair, arrivals):
    hidden = go.shape[0]
    count = pair.shape[0]
    rows = pl.ds(lax.axis_index("ch") * count, count)
    fetch = pltpu.make_async_copy(pair_far.at[rows], pair, arrivals.at[6])
    fetch.start()
    width = 2 * hidden
    copies = []
    for at, (held, low, high) in enumerate(((gates, ga, gb), (values, pa, pb), (last, go, wo))):
        copies.append(pltpu.make_async_copy(low, held.at[0:hidden], arrivals.at[2 * at]))
        copies.append(pltpu.make_async_copy(high, held.at[hidden:width], arrivals.at[2 * at + 1]))
    start_all(copies)
    order = grouping(hidden, share)
    wait_all(copies)
    out[:width] = dot(order, gates[...], (1, 0)).astype(bf16)
    out[width : 2 * width] = dot(order, values[...], (1, 0)).astype(bf16)
    out[2 * width :] = last[...]
    fetch.wait()
    normed[...] = normalized(pair[...])[0].astype(bf16)


def rows_of(weights, start, count):
    return jnp.concatenate([weights[c, start : start + count] for c in range(weights.shape[0])], 0)


def normalized(pair):
    count, cols, channels = pair.shape
    values = pair.astype(f32).reshape(count * cols, channels).T
    centred = values - jnp.mean(values, 0, keepdims=True)
    rstd = lax.rsqrt(jnp.mean(centred * centred, 0, keepdims=True) + epsilon)
    return centred * rstd, rstd


def edges(width, normed, weights, send):
    gate = jax.nn.sigmoid(dot(rows_of(weights, 0, width), normed[...], (1, 0)))
    value = dot(rows_of(weights, width, width), normed[...], (1, 0))
    send[...] = (gate * value).reshape(send.shape).astype(bf16)


def spread_rows(block, cols, arrived, held):
    devices, q, flat = arrived.shape
    rows = flat // cols
    for s in range(devices):
        tile = arrived[s].astype(f32)
        for i in range(rows):
            start = (s * rows + i) * block
            held[start : start + q, 0:cols] = tile[:, i * cols : (i + 1) * cols]


def pack_rows(block, cols, held, send):
    devices, q, flat = send.shape
    rows = flat // cols
    for s in range(devices):
        starts = [(s * rows + i) * block for i in range(rows)]
        whole = jnp.concatenate([held[start : start + block, 0:cols] for start in starts], axis=1)
        send[s] = whole[:q].astype(bf16)


def square(block, parts, cols, held, e):
    tokens = parts * cols
    return jnp.concatenate(
        [
            held[pl.ds(p * tokens * block + e, tokens, stride=block), 0:cols]
            for p in range(parts)
        ],
        axis=1,
    ).astype(bf16)


def put_square(block, parts, cols, held, e, values):
    tokens = parts * cols
    for p in range(parts):
        held[pl.ds(p * tokens * block + e, tokens, stride=block), 0:cols] = values[
            :, p * cols : (p + 1) * cols
        ]


def mix(parts, cols, arrived, send, kept, held, result):
    block = 8
    q = arrived.shape[1]
    spread_rows(block, cols, arrived, held)
    for e in range(q // 2):
        left = square(block, parts, cols, held, e)
        right = square(block, parts, cols, held, q // 2 + e)
        kept[e] = left
        kept[q // 2 + e] = right
        put_square(block, parts, cols, result, e, dot(left, right, (1, 1)))
    pack_rows(block, cols, result, send)


def unmix(parts, cols, arrived, kept_far, send, held, result, kept, arrival):
    block = 8
    q = arrived.shape[1]
    copy = pltpu.make_async_copy(kept_far, kept, arrival)
    copy.start()
    spread_rows(block, cols, arrived, held)
    copy.wait()
    for e in range(q):
        d_mixed = square(block, parts, cols, held, e)
        put_square(block, parts, cols, result, e, dot(d_mixed, kept[q + e], (1, 0)))
        put_square(block, parts, cols, result, q + e, dot(d_mixed, kept[e], (0, 0)))
    pack_rows(block, cols, result, send)


def split_rows(cols, values, own, other):
    hidden = values.shape[0] // 2
    first = lax.axis_index("ch") == 0
    low, high = values[:hidden], values[hidden:]
    mine = jnp.where(first, low, high)
    yours = jnp.where(first, high, low)
    for i in range(own.shape[0]):
        own[i] = mine[:, i * cols : (i + 1) * cols].astype(bf16)
        other[i] = yours[:, i * cols : (i + 1) * cols].astype(bf16)


def head(
    width, scale, arrived, weights, normed_far, own_far, other_far,
    send, d_gate, terms, updated_own, updated_other,
    normed, own, other, upstream, arrivals,
):
    parts, total, _ = weights.shape
    hidden = (total - 2 * width) // 2
    devices, q, flat = arrived.shape
    count, _, cols = other.shape
    core = lax.axis_index("ch")
    copies = [
        pltpu.make_async_copy(normed_far, normed, arrivals.at[0]),
        pltpu.make_async_copy(own_far.at[pl.ds(core * count, count)], own, arrivals.at[1]),
        pltpu.make_async_copy(other_far, other, arrivals.at[2]),
    ]
    start_all(copies)
    mixed = jnp.concatenate([arrived[s].astype(f32) for s in range(devices)], 0)
    average = jnp.mean(mixed, 0, keepdims=True)
    spread = jnp.mean(mixed * mixed, 0, keepdims=True) - average * average
    inverse = lax.rsqrt(spread + epsilon)
    hat = (mixed - average) * inverse
    hat_rounded = hat.astype(bf16)
    w_out = rows_of(weights, 2 * width + hidden, hidden)
    proj = dot(w_out, hat_rounded, (1, 0))
    wait_all(copies)
    for part, side in ((own, core), (other, 1 - core)):
        upstream[pl.ds(pl.multiple_of(side * hidden, hidden), hidden)] = jnp.concatenate(
            [part[i].astype(f32) for i in range(count)], axis=1
        )
    gate = jax.nn.sigmoid(dot(rows_of(weights, 2 * width, hidden), normed[...], (1, 0)))
    up = upstream[...]
    d_proj = (up * gate).astype(bf16)
    d_gate[...] = (up * proj * gate * (1.0 - gate)).astype(bf16)
    d_norm = dot(w_out, d_proj, (0, 0))
    d_mixed = inverse * (
        d_norm
        - jnp.mean(d_norm, 0, keepdims=True)
        - hat * jnp.mean(d_norm * hat, 0, keepdims=True)
    )
    for s in range(devices):
        send[s] = d_mixed[s * q : (s + 1) * q].astype(bf16)
    by_gate = dot(d_gate[...], normed[...], (1, 1)) * scale
    by_out = dot(d_proj, hat_rounded, (1, 1)) * scale
    for c in range(parts):
        terms[c, :hidden] = by_gate[c * hidden : (c + 1) * hidden]
        terms[c, hidden:] = by_out[c * hidden : (c + 1) * hidden]
    split_rows(cols, gate * proj, updated_own, updated_other)


def tail(
    width, scale, arrived, weights, pair_far, d_gate_far, head_terms,
    own_terms, parcel, grad_own,
    pair, d_gate, whole, arrivals,
):
    parts, total, channels = weights.shape
    hidden = (total - 2 * width) // 2
    devices, q, flat = arrived.shape
    count, cols, _ = pair.shape
    core = lax.axis_index("ch")
    copies = [
        pltpu.make_async_copy(pair_far.at[pl.ds(core * count, count)], pair, arrivals.at[0]),
        pltpu.make_async_copy(d_gate_far, d_gate, arrivals.at[1]),
    ]
    start_all(copies)
    wait_all(copies)
    hat, inverse = normalized(pair[...])
    normed = hat.astype(bf16)
    w_gate, w_value = rows_of(weights, 0, width), rows_of(weights, width, width)
    gate = jax.nn.sigmoid(dot(w_gate, normed, (1, 0)))
    value = dot(w_value, normed, (1, 0))
    grad = arrived[...].astype(f32).reshape(devices * q, flat)
    by_value = grad * gate
    by_gate = (by_value * (value * (1.0 - gate))).astype(bf16)
    by_value = by_value.astype(bf16)
    terms = [dot(by_gate, normed, (1, 1)) * scale, dot(by_value, normed, (1, 1)) * scale]
    for c in range(parts):
        for at, term in enumerate(terms):
            start = c * total + at * width
            whole[start : start + width] = term[c * width : (c + 1) * width]
        whole[c * total + 2 * width : (c + 1) * total] = head_terms[c]
    own_terms[...] = whole[pl.ds(pl.multiple_of(core * total, total), total)]
    parcel[count * hidden :] = whole[
        pl.ds(pl.multiple_of((1 - core) * total, total), total)
    ].astype(bf16)
    d_input = dot(w_gate, by_gate, (0, 0)) + dot(w_value, by_value, (0, 0))
    d_input = d_input + dot(rows_of(weights, 2 * width, hidden), d_gate[...], (0, 0))
    back = inverse * (
        d_input
        - jnp.mean(d_input, 0, keepdims=True)
        - hat * jnp.mean(d_input * hat, 0, keepdims=True)
    )
    first = core == 0
    mine = jnp.where(first, back[:hidden], back[hidden:])
    yours = jnp.where(first, back[hidden:], back[:hidden])
    for i in range(count):
        grad_own[i] = mine[:, i * cols : (i + 1) * cols].astype(bf16)
        parcel[i * hidden : (i + 1) * hidden] = jnp.pad(
            yours[:, i * cols : (i + 1) * cols], ((0, 0), (0, channels - cols))
        ).astype(bf16)


def halve(side, skip, own, arrived, kept, send):
    total = own[...] + arrived[skip:].astype(f32)
    half = total.shape[0] // 2
    low, high = total[:half], total[half:]
    first = side() == 0
    kept[...] = jnp.where(first, low, high)
    send[...] = jnp.where(first, high, low).astype(bf16)


def add(own, arrived, out):
    out[...] = (own[...].astype(f32) + arrived[...].astype(f32)).astype(bf16)


def add_all(parts, out):
    out[...] = jnp.sum(parts[...].astype(f32), 0).astype(bf16)


def turn_back(share, whole, *refs):
    outs, results, leaves = refs[:6], refs[6], refs[7]
    _, hidden, channels = results.shape
    width = 2 * hidden
    order = grouping(hidden, share)
    for at in range(2):
        both = dot(order, whole[at * width : (at + 1) * width], (0, 0))
        results[at] = both[:hidden]
        results[2 + at] = both[hidden:]
    results[4] = whole[2 * width : 2 * width + hidden].astype(f32)
    results[5] = whole[2 * width + hidden :].astype(f32)
    copies = [
        pltpu.make_async_copy(results.at[at], out, leaves.at[at]) for at, out in enumerate(outs)
    ]
    start_all(copies)
    wait_all(copies)


def join_rows(own, other, out, leaves):
    count = own.shape[0]
    core = lax.axis_index("ch")
    copies = [
        pltpu.make_async_copy(own, out.at[pl.ds(core * count, count)], leaves.at[0]),
        pltpu.make_async_copy(other, out.at[pl.ds((1 - core) * count, count)], leaves.at[1]),
    ]
    start_all(copies)
    wait_all(copies)


def join_parcel(own, parcel, out, other, leaves):
    count, hidden, cols = own.shape
    other[...] = parcel[: count * hidden, :cols].reshape(count, hidden, cols)
    join_rows(own, other, out, leaves)


def by_channels(pair, cotangent, w_gate_a, w_proj_a, w_gate_b, w_proj_b, w_gate_out, w_out):
    row_count, cols, channels = pair.shape
    hidden = w_gate_a.shape[1]
    parts, col_parts, row_parts = lax.axis_size("ch"), lax.axis_size("col"), lax.axis_size("row")
    devices = parts * col_parts * row_parts
    share = hidden * parts // devices
    width = 2 * hidden
    count = row_count // parts
    flat = count * cols
    tokens = cols * col_parts
    scale = 1.0 / tokens
    swap = [(c, parts - 1 - c) for c in range(parts)]
    def col_side():
        return lax.axis_index("col")

    whole_weight = pltpu.VMEM((2 * hidden, channels), bf16)
    weights, normed = call(
        functools.partial(prepare, share),
        [((2 * width + 2 * hidden, channels), bf16), ((channels, flat), bf16)],
        (w_gate_a.T, w_proj_a.T, w_gate_b.T, w_proj_b.T, w_gate_out.T, w_out.T, pair),
        (
            whole_weight,
            whole_weight,
            whole_weight,
            pltpu.VMEM((count, cols, channels), bf16),
            pltpu.SemaphoreType.DMA((7,)),
        ),
        far=range(7),
        room=60,
    )
    weights = lax.all_gather(weights, "ch")
    own = jnp.swapaxes(cotangent, 1, 2)
    other = lax.dynamic_slice_in_dim(own, (1 - lax.axis_index("ch")) * count, count, 0)
    other = lax.ppermute(other, "ch", swap)
    (send,) = call(
        functools.partial(edges, width), [((devices, 2 * share, flat), bf16)], (normed, weights)
    )
    arrived = lax.all_to_all(send, everyone, 0, 0)
    room = pltpu.VMEM((col_parts * tokens * 8, -(-cols // 128) * 128), f32)
    send, kept = call(
        functools.partial(mix, col_parts, cols),
        [((devices, share, flat), bf16), ((2 * share, tokens, tokens), bf16)],
        (arrived,),
        (room, room),
    )
    arrived = lax.all_to_all(send, everyone, 0, 0)
    part = ((count, hidden, cols), bf16)
    send, d_gate, head_terms, updated_own, updated_other = call(
        functools.partial(head, width, scale),
        [
            ((devices, share, flat), bf16),
            ((hidden * parts, flat), bf16),
            ((parts, 2 * hidden, channels), f32),
            part,
            part,
        ],
        (arrived, weights, normed, own, other),
        (
            pltpu.VMEM((channels, flat), bf16),
            pltpu.VMEM(*part),
            pltpu.VMEM(*part),
            pltpu.VMEM((hidden * parts, flat), f32),
            pltpu.SemaphoreType.DMA((3,)),
        ),
        far=(2, 3, 4),
    )
    arrived = lax.all_to_all(send, everyone, 0, 0)
    updated_other = lax.ppermute(updated_other, "ch", swap)
    (send,) = call(
        functools.partial(unmix, col_parts, cols),
        [((devices, 2 * share, flat), bf16)],
        (arrived, kept),
        (room, room, pltpu.VMEM(kept.shape, bf16), pltpu.SemaphoreType.DMA),
        far=(1,),
    )
    arrived = lax.all_to_all(send, everyone, 0, 0)
    rows = [((row_count, hidden, cols), bf16)]
    two = pltpu.SemaphoreType.DMA((2,))
    (updated,) = call(join_rows, rows, (updated_own, updated_other), (two,), (0, 1), True)
    arrived, updated = lax.optimization_barrier((arrived, updated))
    total = 2 * width + 2 * hidden
    terms, parcel, grad_own = call(
        functools.partial(tail, width, scale),
        [((total, channels), f32), ((count * hidden + total, channels), bf16), part],
        (arrived, weights, pair, d_gate, head_terms),
        (
            pltpu.VMEM((count, cols, channels), bf16),
            pltpu.VMEM((hidden * parts, flat), bf16),
            pltpu.VMEM((total * parts, channels), f32),
            two,
        ),
        far=(2, 3),
    )
    parcel = lax.ppermute(parcel, "ch", swap)
    half = (total // 2, channels)
    terms, send = call(
        functools.partial(halve, col_side, count * hidden), [(half, f32), (half, bf16)], (terms, parcel)
    )
    arrived = lax.ppermute(send, "col", swap)
    (grad_pair,) = call(join_parcel, rows, (grad_own, parcel), (pltpu.VMEM(*part), two), (), True)
    (sums,) = call(add, [(half, bf16)], (terms, arrived))
    sums = lax.all_gather(sums, "row")
    sums, grad_pair = lax.optimization_barrier((sums, grad_pair))
    (sums,) = call(add_all, [(half, bf16)], (sums,))
    grads = call(
        functools.partial(turn_back, share),
        [((hidden, channels), f32)] * 6,
        (lax.all_gather(sums, "col", tiled=True),),
        (
            pltpu.VMEM((6, hidden, channels), f32),
            pltpu.SemaphoreType.DMA((6,)),
        ),
        outs_far=True,
    )
    return jnp.swapaxes(updated, 1, 2), jnp.swapaxes(grad_pair, 1, 2), *(g.T for g in grads)


def on_device(*arrays):
    row_count, cols, _ = arrays[0].shape
    parts, devices = lax.axis_size("ch"), lax.axis_size(everyone)
    hidden = arrays[2].shape[1]
    share = hidden * parts // devices
    fits = (
        share * devices == hidden * parts
        and parts == 2
        and 2 * share == 8
        and row_count % parts == 0
        and lax.axis_size("col") == 2
        and 6 * hidden % 64 == 0
        and cols <= arrays[0].shape[2]
        and arrays[1].shape[2] == hidden
        and cols % 16 == 0
    )
    return by_channels(*arrays) if fits else by_rows(*arrays)


def solution(mesh):
    in_specs = (
        P("row", "col", None),
        P("row", "col", "ch"),
        P(None, "ch"),
        P(None, "ch"),
        P(None, "ch"),
        P(None, "ch"),
        P(None, "ch"),
        P(None, "ch"),
    )
    out_specs = (
        P("row", "col", "ch"),
        P("row", "col", "ch"),
        P(None, "ch"),
        P(None, "ch"),
        P(None, "ch"),
        P(None, "ch"),
        P(None, "ch"),
        P(None, "ch"),
    )
    return jax.shard_map(
        on_device, mesh=mesh, in_specs=in_specs, out_specs=out_specs, check_vma=False
    )
```

```python
import functools

import jax
import jax.numpy as jnp
import numpy as np
from jax import lax
from jax.experimental import pallas as pl
from jax.experimental.pallas import tpu as pltpu
from jax.sharding import PartitionSpec as P

epsilon = 1e-05


def layer_norm(values):
    average = jnp.mean(values, -1, keepdims=True)
    centred = values - average
    spread = jnp.mean(centred * centred, -1, keepdims=True)
    inverse = lax.rsqrt(spread + epsilon)
    return (centred * inverse, inverse)


def matmul(first, second):
    return jnp.dot(first, second, preferred_element_type=jnp.float32)


def by_rows(pair, cotangent, w_gate_a, w_proj_a, w_gate_b, w_proj_b, w_gate_out, w_out):
    row_count, col_count, channels = pair.shape
    hidden = w_gate_a.shape[1]
    total_hidden = hidden * lax.axis_size("ch")
    out_width = cotangent.shape[2]
    length = row_count * lax.axis_size("row")
    grad_scale = 1.0 / length
    pair_hat, pair_rstd = layer_norm(pair.astype(jnp.float32))
    flat_norm = pair_hat.astype(jnp.bfloat16).reshape(row_count * col_count, channels)
    w_four = jnp.concatenate([w_gate_a, w_proj_a, w_gate_b, w_proj_b], axis=1)
    projected = matmul(flat_norm, w_four)
    gate_a = jax.nn.sigmoid(projected[:, :hidden])
    proj_a = projected[:, hidden : 2 * hidden]
    gate_b = jax.nn.sigmoid(projected[:, 2 * hidden : 3 * hidden])
    proj_b = projected[:, 3 * hidden :]
    left_edge = (gate_a * proj_a).astype(jnp.bfloat16).reshape(row_count, col_count, hidden)
    right_edge = (gate_b * proj_b).astype(jnp.bfloat16).reshape(row_count, col_count, hidden)
    right_all = lax.all_gather(right_edge, "row", axis=0, tiled=True)
    mixed_swap = lax.psum_scatter(
        jnp.einsum("jkh,ikh->jih", right_all, left_edge, preferred_element_type=jnp.float32).astype(
            jnp.bfloat16
        ),
        "col",
        scatter_dimension=0,
        tiled=True,
    ).astype(jnp.float32)
    mixed = jnp.swapaxes(mixed_swap, 0, 1).reshape(row_count * col_count, hidden)
    hidden_sums = lax.psum((jnp.sum(mixed, -1), jnp.sum(mixed * mixed, -1)), "ch")
    hidden_mean = (hidden_sums[0] / total_hidden)[:, None]
    hidden_var = (hidden_sums[1] / total_hidden)[:, None] - hidden_mean * hidden_mean
    hidden_rstd = lax.rsqrt(hidden_var + epsilon)
    mixed_hat = (mixed - hidden_mean) * hidden_rstd
    mixed_norm = mixed_hat.astype(jnp.bfloat16)
    norm_full = lax.all_gather(mixed_norm, "ch", axis=1, tiled=True)
    gate_out = jax.nn.sigmoid(matmul(flat_norm, w_gate_out))
    proj_out = matmul(norm_full, w_out)
    updated = (gate_out * proj_out).astype(jnp.bfloat16).reshape(row_count, col_count, out_width)
    upstream = cotangent.reshape(row_count * col_count, out_width).astype(jnp.float32)
    d_proj = (upstream * gate_out).astype(jnp.bfloat16)
    d_gate = (upstream * proj_out * gate_out * (1.0 - gate_out)).astype(jnp.bfloat16)
    head_grads = lax.psum(
        (matmul(norm_full.T, d_proj) * grad_scale, matmul(flat_norm.T, d_gate) * grad_scale),
        ("row", "col"),
    )
    d_norm = lax.psum_scatter(
        matmul(d_proj, w_out.T).astype(jnp.bfloat16), "ch", scatter_dimension=1, tiled=True
    ).astype(jnp.float32)
    back_sums = lax.psum((jnp.sum(d_norm, -1), jnp.sum(d_norm * mixed_hat, -1)), "ch")
    d_mixed = hidden_rstd * (
        d_norm
        - (back_sums[0] / total_hidden)[:, None]
        - mixed_hat * (back_sums[1] / total_hidden)[:, None]
    )
    d_mixed = d_mixed.astype(jnp.bfloat16).reshape(row_count, col_count, hidden)
    d_rows = lax.all_gather(d_mixed, "col", axis=1, tiled=True)
    right_back = lax.all_gather(right_edge, "row", axis=0, tiled=True)
    d_left = jnp.einsum("ijh,jkh->ikh", d_rows, right_back, preferred_element_type=jnp.float32)
    d_left = d_left.reshape(row_count * col_count, hidden)
    left_all = lax.all_gather(left_edge, "row", axis=0, tiled=True)
    d_columns = lax.all_to_all(d_rows, "row", split_axis=1, concat_axis=0, tiled=True)
    d_right = jnp.einsum("ijh,ikh->jkh", d_columns, left_all, preferred_element_type=jnp.float32)
    d_right = d_right.reshape(row_count * col_count, hidden)
    grad_pa = (d_left * gate_a).astype(jnp.bfloat16)
    grad_ga = (d_left * proj_a * gate_a * (1.0 - gate_a)).astype(jnp.bfloat16)
    grad_pb = (d_right * gate_b).astype(jnp.bfloat16)
    grad_gb = (d_right * proj_b * gate_b * (1.0 - gate_b)).astype(jnp.bfloat16)
    d_four = jnp.concatenate([grad_ga, grad_pa, grad_gb, grad_pb], axis=1)
    weight_terms = matmul(flat_norm.T, d_four) * grad_scale
    summed = lax.psum(weight_terms, ("row", "col"))
    d_flat = matmul(d_four, w_four.T) + matmul(d_gate, w_gate_out.T)
    hat_all = pair_hat.reshape(row_count * col_count, channels)
    rstd_flat = pair_rstd.reshape(row_count * col_count, 1)
    offset = lax.axis_index("ch") * out_width
    grad_whole = lax.psum(d_flat.astype(jnp.bfloat16), "ch").astype(jnp.float32)
    grad_full = rstd_flat * (
        grad_whole
        - jnp.mean(grad_whole, -1, keepdims=True)
        - hat_all * jnp.mean(grad_whole * hat_all, -1, keepdims=True)
    )
    grad_pair = lax.dynamic_slice_in_dim(grad_full, offset, out_width, 1)
    grad_pair = grad_pair.astype(jnp.bfloat16).reshape(row_count, col_count, out_width)
    return (
        updated,
        grad_pair,
        summed[:, :hidden],
        summed[:, hidden : 2 * hidden],
        summed[:, 2 * hidden : 3 * hidden],
        summed[:, 3 * hidden :],
        head_grads[1],
        head_grads[0],
    )


everyone = ("col", "row", "ch")
f32, bf16 = jnp.float32, jnp.bfloat16


def dot(first, second, over):
    return lax.dot_general(
        first, second, (((over[0],), (over[1],)), ((), ())), preferred_element_type=f32
    )


def call(kernel, outs, args, scratch=(), far=(), outs_far=False, room=16):
    whole = pl.BlockSpec(memory_space=pltpu.VMEM)
    anywhere = pl.BlockSpec(memory_space=pl.ANY)
    return pl.pallas_call(
        kernel,
        out_shape=tuple(jax.ShapeDtypeStruct(*out) for out in outs),
        in_specs=[anywhere if at in far else whole for at in range(len(args))],
        out_specs=tuple(anywhere if outs_far else whole for _ in outs),
        scratch_shapes=scratch,
        compiler_params=pltpu.CompilerParams(vmem_limit_bytes=room * 2**20),
    )(*args)


def grouping(hidden, share):
    shape = (2 * hidden, 2 * hidden)
    rows = lax.broadcasted_iota(jnp.int32, shape, 0)
    columns = lax.broadcasted_iota(jnp.int32, shape, 1)
    group, within = rows // (2 * share), lax.rem(rows, 2 * share)
    side = within // share
    wanted = side * hidden + group * share + within - side * share
    return jnp.where(columns == wanted, 1.0, 0.0).astype(bf16)


def start_all(copies):
    for copy in copies:
        copy.start()


def wait_all(copies):
    for copy in copies:
        copy.wait()


def prepare(share, ga, pa, gb, pb, go, wo, pair_far, out, normed, gates, values, last, pair, arrivals):
    hidden = go.shape[0]
    count = pair.shape[0]
    rows = pl.ds(lax.axis_index("ch") * count, count)
    fetch = pltpu.make_async_copy(pair_far.at[rows], pair, arrivals.at[6])
    fetch.start()
    width = 2 * hidden
    copies = []
    for at, (held, low, high) in enumerate(((gates, ga, gb), (values, pa, pb), (last, go, wo))):
        copies.append(pltpu.make_async_copy(low, held.at[0:hidden], arrivals.at[2 * at]))
        copies.append(pltpu.make_async_copy(high, held.at[hidden:width], arrivals.at[2 * at + 1]))
    start_all(copies)
    order = grouping(hidden, share)
    wait_all(copies)
    out[:width] = dot(order, gates[...], (1, 0)).astype(bf16)
    out[width : 2 * width] = dot(order, values[...], (1, 0)).astype(bf16)
    out[2 * width :] = last[...]
    fetch.wait()
    normed[...] = normalized(pair[...])[0].astype(bf16)


def rows_of(weights, start, count):
    return jnp.concatenate([weights[c, start : start + count] for c in range(weights.shape[0])], 0)


def normalized(pair):
    count, cols, channels = pair.shape
    values = pair.astype(f32).reshape(count * cols, channels).T
    centred = values - jnp.mean(values, 0, keepdims=True)
    rstd = lax.rsqrt(jnp.mean(centred * centred, 0, keepdims=True) + epsilon)
    return centred * rstd, rstd


def edges(width, normed, weights, send):
    gate = jax.nn.sigmoid(dot(rows_of(weights, 0, width), normed[...], (1, 0)))
    value = dot(rows_of(weights, width, width), normed[...], (1, 0))
    send[...] = (gate * value).reshape(send.shape).astype(bf16)


def spread_rows(block, cols, arrived, held):
    devices, q, flat = arrived.shape
    rows = flat // cols
    for s in range(devices):
        tile = arrived[s].astype(f32)
        for i in range(rows):
            start = (s * rows + i) * block
            held[start : start + q, 0:cols] = tile[:, i * cols : (i + 1) * cols]


def pack_rows(block, cols, held, send):
    devices, q, flat = send.shape
    rows = flat // cols
    for s in range(devices):
        starts = [(s * rows + i) * block for i in range(rows)]
        whole = jnp.concatenate([held[start : start + block, 0:cols] for start in starts], axis=1)
        send[s] = whole[:q].astype(bf16)


def square(block, parts, cols, held, e):
    tokens = parts * cols
    return jnp.concatenate(
        [
            held[pl.ds(p * tokens * block + e, tokens, stride=block), 0:cols]
            for p in range(parts)
        ],
        axis=1,
    ).astype(bf16)


def put_square(block, parts, cols, held, e, values):
    tokens = parts * cols
    for p in range(parts):
        held[pl.ds(p * tokens * block + e, tokens, stride=block), 0:cols] = values[
            :, p * cols : (p + 1) * cols
        ]


def mix(parts, cols, arrived, send, kept, held, result):
    block = 8
    q = arrived.shape[1]
    spread_rows(block, cols, arrived, held)
    for e in range(q // 2):
        left = square(block, parts, cols, held, e)
        right = square(block, parts, cols, held, q // 2 + e)
        kept[e] = left
        kept[q // 2 + e] = right
        put_square(block, parts, cols, result, e, dot(left, right, (1, 1)))
    pack_rows(block, cols, result, send)


def unmix(parts, cols, arrived, kept_far, send, held, result, kept, arrival):
    block = 8
    q = arrived.shape[1]
    copy = pltpu.make_async_copy(kept_far, kept, arrival)
    copy.start()
    spread_rows(block, cols, arrived, held)
    copy.wait()
    for e in range(q):
        d_mixed = square(block, parts, cols, held, e)
        put_square(block, parts, cols, result, e, dot(d_mixed, kept[q + e], (1, 0)))
        put_square(block, parts, cols, result, q + e, dot(d_mixed, kept[e], (0, 0)))
    pack_rows(block, cols, result, send)


def split_rows(cols, values, own, other):
    hidden = values.shape[0] // 2
    first = lax.axis_index("ch") == 0
    low, high = values[:hidden], values[hidden:]
    mine = jnp.where(first, low, high)
    yours = jnp.where(first, high, low)
    for i in range(own.shape[0]):
        own[i] = mine[:, i * cols : (i + 1) * cols].astype(bf16)
        other[i] = yours[:, i * cols : (i + 1) * cols].astype(bf16)


def head(
    width, scale, arrived, weights, normed_far, own_far, other_far,
    send, d_gate, terms, updated_own, updated_other,
    normed, own, other, upstream, arrivals,
):
    parts, total, _ = weights.shape
    hidden = (total - 2 * width) // 2
    devices, q, flat = arrived.shape
    count, _, cols = other.shape
    core = lax.axis_index("ch")
    copies = [
        pltpu.make_async_copy(normed_far, normed, arrivals.at[0]),
        pltpu.make_async_copy(own_far.at[pl.ds(core * count, count)], own, arrivals.at[1]),
        pltpu.make_async_copy(other_far, other, arrivals.at[2]),
    ]
    start_all(copies)
    mixed = jnp.concatenate([arrived[s].astype(f32) for s in range(devices)], 0)
    average = jnp.mean(mixed, 0, keepdims=True)
    spread = jnp.mean(mixed * mixed, 0, keepdims=True) - average * average
    inverse = lax.rsqrt(spread + epsilon)
    hat = (mixed - average) * inverse
    hat_rounded = hat.astype(bf16)
    w_out = rows_of(weights, 2 * width + hidden, hidden)
    proj = dot(w_out, hat_rounded, (1, 0))
    wait_all(copies)
    for part, side in ((own, core), (other, 1 - core)):
        upstream[pl.ds(pl.multiple_of(side * hidden, hidden), hidden)] = jnp.concatenate(
            [part[i].astype(f32) for i in range(count)], axis=1
        )
    gate = jax.nn.sigmoid(dot(rows_of(weights, 2 * width, hidden), normed[...], (1, 0)))
    up = upstream[...]
    d_proj = (up * gate).astype(bf16)
    d_gate[...] = (up * proj * gate * (1.0 - gate)).astype(bf16)
    d_norm = dot(w_out, d_proj, (0, 0))
    d_mixed = inverse * (
        d_norm
        - jnp.mean(d_norm, 0, keepdims=True)
        - hat * jnp.mean(d_norm * hat, 0, keepdims=True)
    )
    for s in range(devices):
        send[s] = d_mixed[s * q : (s + 1) * q].astype(bf16)
    by_gate = dot(d_gate[...], normed[...], (1, 1)) * scale
    by_out = dot(d_proj, hat_rounded, (1, 1)) * scale
    for c in range(parts):
        terms[c, :hidden] = by_gate[c * hidden : (c + 1) * hidden]
        terms[c, hidden:] = by_out[c * hidden : (c + 1) * hidden]
    split_rows(cols, gate * proj, updated_own, updated_other)


def tail(
    width, scale, arrived, weights, pair_far, d_gate_far, head_terms,
    send, grad_own, grad_other,
    pair, d_gate, whole, arrivals,
):
    parts, total, channels = weights.shape
    hidden = (total - 2 * width) // 2
    devices, q, flat = arrived.shape
    count, cols, _ = pair.shape
    core = lax.axis_index("ch")
    copies = [
        pltpu.make_async_copy(pair_far.at[pl.ds(core * count, count)], pair, arrivals.at[0]),
        pltpu.make_async_copy(d_gate_far, d_gate, arrivals.at[1]),
    ]
    start_all(copies)
    wait_all(copies)
    hat, inverse = normalized(pair[...])
    normed = hat.astype(bf16)
    w_gate, w_value = rows_of(weights, 0, width), rows_of(weights, width, width)
    gate = jax.nn.sigmoid(dot(w_gate, normed, (1, 0)))
    value = dot(w_value, normed, (1, 0))
    grad = arrived[...].astype(f32).reshape(devices * q, flat)
    by_value = grad * gate
    by_gate = (by_value * (value * (1.0 - gate))).astype(bf16)
    by_value = by_value.astype(bf16)
    terms = [dot(by_gate, normed, (1, 1)) * scale, dot(by_value, normed, (1, 1)) * scale]
    for c in range(parts):
        for at, term in enumerate(terms):
            start = c * total + at * width
            whole[start : start + width] = term[c * width : (c + 1) * width]
        whole[c * total + 2 * width : (c + 1) * total] = head_terms[c]
    per = send.shape[1]
    for s in range(devices):
        send[s] = whole[s * per : (s + 1) * per].astype(bf16)
    d_input = dot(w_gate, by_gate, (0, 0)) + dot(w_value, by_value, (0, 0))
    d_input = d_input + dot(rows_of(weights, 2 * width, hidden), d_gate[...], (0, 0))
    back = inverse * (
        d_input
        - jnp.mean(d_input, 0, keepdims=True)
        - hat * jnp.mean(d_input * hat, 0, keepdims=True)
    )
    split_rows(cols, back, grad_own, grad_other)


def add_up(arrived, out):
    total = jnp.sum(arrived[...].astype(f32), 0).astype(bf16)
    for s in range(out.shape[0]):
        out[s] = total


def turn_back(share, sums, *refs):
    outs, whole, results, leaves = refs[:6], refs[6], refs[7], refs[8]
    _, hidden, channels = results.shape
    width = 2 * hidden
    per = sums.shape[1]
    for s in range(sums.shape[0]):
        whole[s * per : (s + 1) * per] = sums[s].astype(f32)
    order = grouping(hidden, share)
    for at in range(2):
        both = dot(order, whole[at * width : (at + 1) * width].astype(bf16), (0, 0))
        results[at] = both[:hidden]
        results[2 + at] = both[hidden:]
    results[4] = whole[2 * width : 2 * width + hidden]
    results[5] = whole[2 * width + hidden :]
    copies = [
        pltpu.make_async_copy(results.at[at], out, leaves.at[at]) for at, out in enumerate(outs)
    ]
    start_all(copies)
    wait_all(copies)


def join_rows(own, other, out, leaves):
    count = own.shape[0]
    core = lax.axis_index("ch")
    copies = [
        pltpu.make_async_copy(own, out.at[pl.ds(core * count, count)], leaves.at[0]),
        pltpu.make_async_copy(other, out.at[pl.ds((1 - core) * count, count)], leaves.at[1]),
    ]
    start_all(copies)
    wait_all(copies)


def by_channels(pair, cotangent, w_gate_a, w_proj_a, w_gate_b, w_proj_b, w_gate_out, w_out):
    row_count, cols, channels = pair.shape
    hidden = w_gate_a.shape[1]
    parts, col_parts, row_parts = lax.axis_size("ch"), lax.axis_size("col"), lax.axis_size("row")
    devices = parts * col_parts * row_parts
    share = hidden * parts // devices
    width = 2 * hidden
    count = row_count // parts
    flat = count * cols
    tokens = cols * col_parts
    scale = 1.0 / tokens
    swap = [(c, parts - 1 - c) for c in range(parts)]
    whole_weight = pltpu.VMEM((2 * hidden, channels), bf16)
    weights, normed = call(
        functools.partial(prepare, share),
        [((2 * width + 2 * hidden, channels), bf16), ((channels, flat), bf16)],
        (w_gate_a.T, w_proj_a.T, w_gate_b.T, w_proj_b.T, w_gate_out.T, w_out.T, pair),
        (
            whole_weight,
            whole_weight,
            whole_weight,
            pltpu.VMEM((count, cols, channels), bf16),
            pltpu.SemaphoreType.DMA((7,)),
        ),
        far=range(7),
        room=60,
    )
    weights = lax.all_gather(weights, "ch")
    own = jnp.swapaxes(cotangent, 1, 2)
    other = lax.dynamic_slice_in_dim(own, (1 - lax.axis_index("ch")) * count, count, 0)
    other = lax.ppermute(other, "ch", swap)
    (send,) = call(
        functools.partial(edges, width), [((devices, 2 * share, flat), bf16)], (normed, weights)
    )
    arrived = lax.all_to_all(send, everyone, 0, 0)
    room = pltpu.VMEM((col_parts * tokens * 8, -(-cols // 128) * 128), f32)
    send, kept = call(
        functools.partial(mix, col_parts, cols),
        [((devices, share, flat), bf16), ((2 * share, tokens, tokens), bf16)],
        (arrived,),
        (room, room),
    )
    arrived = lax.all_to_all(send, everyone, 0, 0)
    part = ((count, hidden, cols), bf16)
    send, d_gate, head_terms, updated_own, updated_other = call(
        functools.partial(head, width, scale),
        [
            ((devices, share, flat), bf16),
            ((hidden * parts, flat), bf16),
            ((parts, 2 * hidden, channels), f32),
            part,
            part,
        ],
        (arrived, weights, normed, own, other),
        (
            pltpu.VMEM((channels, flat), bf16),
            pltpu.VMEM(*part),
            pltpu.VMEM(*part),
            pltpu.VMEM((hidden * parts, flat), f32),
            pltpu.SemaphoreType.DMA((3,)),
        ),
        far=(2, 3, 4),
    )
    arrived = lax.all_to_all(send, everyone, 0, 0)
    updated_other = lax.ppermute(updated_other, "ch", swap)
    (send,) = call(
        functools.partial(unmix, col_parts, cols),
        [((devices, 2 * share, flat), bf16)],
        (arrived, kept),
        (room, room, pltpu.VMEM(kept.shape, bf16), pltpu.SemaphoreType.DMA),
        far=(1,),
    )
    arrived = lax.all_to_all(send, everyone, 0, 0)
    rows = [((row_count, hidden, cols), bf16)]
    two = pltpu.SemaphoreType.DMA((2,))
    (updated,) = call(join_rows, rows, (updated_own, updated_other), (two,), (0, 1), True)
    arrived, updated = lax.optimization_barrier((arrived, updated))
    total = 2 * width + 2 * hidden
    per = total * parts // devices
    send, grad_own, grad_other = call(
        functools.partial(tail, width, scale),
        [((devices, per, channels), bf16), part, part],
        (arrived, weights, pair, d_gate, head_terms),
        (
            pltpu.VMEM((count, cols, channels), bf16),
            pltpu.VMEM((hidden * parts, flat), bf16),
            pltpu.VMEM((total * parts, channels), f32),
            two,
        ),
        far=(2, 3),
    )
    arrived = lax.all_to_all(send, ("ch", "row", "col"), 0, 0)
    grad_other = lax.ppermute(grad_other, "ch", swap)
    (grad_pair,) = call(join_rows, rows, (grad_own, grad_other), (two,), (0, 1), True)
    rest = devices // parts
    (sums,) = call(add_up, [((rest, per, channels), bf16)], (arrived,))
    sums = lax.all_to_all(sums, ("row", "col"), 0, 0)
    sums, grad_pair = lax.optimization_barrier((sums, grad_pair))
    grads = call(
        functools.partial(turn_back, share),
        [((hidden, channels), f32)] * 6,
        (sums,),
        (
            pltpu.VMEM((total, channels), f32),
            pltpu.VMEM((6, hidden, channels), f32),
            pltpu.SemaphoreType.DMA((6,)),
        ),
        outs_far=True,
    )
    return jnp.swapaxes(updated, 1, 2), jnp.swapaxes(grad_pair, 1, 2), *(g.T for g in grads)


def on_device(*arrays):
    row_count, cols, _ = arrays[0].shape
    parts, devices = lax.axis_size("ch"), lax.axis_size(everyone)
    hidden = arrays[2].shape[1]
    share = hidden * parts // devices
    fits = (
        share * devices == hidden * parts
        and parts == 2
        and 2 * share == 8
        and row_count % parts == 0
        and 6 * hidden * parts % devices == 0
        and arrays[1].shape[2] == hidden
        and cols % 16 == 0
    )
    return by_channels(*arrays) if fits else by_rows(*arrays)


def solution(mesh):
    in_specs = (
        P("row", "col", None),
        P("row", "col", "ch"),
        P(None, "ch"),
        P(None, "ch"),
        P(None, "ch"),
        P(None, "ch"),
        P(None, "ch"),
        P(None, "ch"),
    )
    out_specs = (
        P("row", "col", "ch"),
        P("row", "col", "ch"),
        P(None, "ch"),
        P(None, "ch"),
        P(None, "ch"),
        P(None, "ch"),
        P(None, "ch"),
        P(None, "ch"),
    )
    return jax.shard_map(
        on_device, mesh=mesh, in_specs=in_specs, out_specs=out_specs, check_vma=False
    )
```

```python
import functools

import jax
import jax.numpy as jnp
import numpy as np
from jax import lax
from jax.experimental import pallas as pl
from jax.experimental.pallas import tpu as pltpu
from jax.sharding import PartitionSpec as P

epsilon = 1e-05


def layer_norm(values):
    average = jnp.mean(values, -1, keepdims=True)
    centred = values - average
    spread = jnp.mean(centred * centred, -1, keepdims=True)
    inverse = lax.rsqrt(spread + epsilon)
    return (centred * inverse, inverse)


def matmul(first, second):
    return jnp.dot(first, second, preferred_element_type=jnp.float32)


def by_rows(pair, cotangent, w_gate_a, w_proj_a, w_gate_b, w_proj_b, w_gate_out, w_out):
    row_count, col_count, channels = pair.shape
    hidden = w_gate_a.shape[1]
    total_hidden = hidden * lax.axis_size("ch")
    out_width = cotangent.shape[2]
    length = row_count * lax.axis_size("row")
    grad_scale = 1.0 / length
    pair_hat, pair_rstd = layer_norm(pair.astype(jnp.float32))
    flat_norm = pair_hat.astype(jnp.bfloat16).reshape(row_count * col_count, channels)
    w_four = jnp.concatenate([w_gate_a, w_proj_a, w_gate_b, w_proj_b], axis=1)
    projected = matmul(flat_norm, w_four)
    gate_a = jax.nn.sigmoid(projected[:, :hidden])
    proj_a = projected[:, hidden : 2 * hidden]
    gate_b = jax.nn.sigmoid(projected[:, 2 * hidden : 3 * hidden])
    proj_b = projected[:, 3 * hidden :]
    left_edge = (gate_a * proj_a).astype(jnp.bfloat16).reshape(row_count, col_count, hidden)
    right_edge = (gate_b * proj_b).astype(jnp.bfloat16).reshape(row_count, col_count, hidden)
    right_all = lax.all_gather(right_edge, "row", axis=0, tiled=True)
    mixed_swap = lax.psum_scatter(
        jnp.einsum("jkh,ikh->jih", right_all, left_edge, preferred_element_type=jnp.float32).astype(
            jnp.bfloat16
        ),
        "col",
        scatter_dimension=0,
        tiled=True,
    ).astype(jnp.float32)
    mixed = jnp.swapaxes(mixed_swap, 0, 1).reshape(row_count * col_count, hidden)
    hidden_sums = lax.psum((jnp.sum(mixed, -1), jnp.sum(mixed * mixed, -1)), "ch")
    hidden_mean = (hidden_sums[0] / total_hidden)[:, None]
    hidden_var = (hidden_sums[1] / total_hidden)[:, None] - hidden_mean * hidden_mean
    hidden_rstd = lax.rsqrt(hidden_var + epsilon)
    mixed_hat = (mixed - hidden_mean) * hidden_rstd
    mixed_norm = mixed_hat.astype(jnp.bfloat16)
    norm_full = lax.all_gather(mixed_norm, "ch", axis=1, tiled=True)
    gate_out = jax.nn.sigmoid(matmul(flat_norm, w_gate_out))
    proj_out = matmul(norm_full, w_out)
    updated = (gate_out * proj_out).astype(jnp.bfloat16).reshape(row_count, col_count, out_width)
    upstream = cotangent.reshape(row_count * col_count, out_width).astype(jnp.float32)
    d_proj = (upstream * gate_out).astype(jnp.bfloat16)
    d_gate = (upstream * proj_out * gate_out * (1.0 - gate_out)).astype(jnp.bfloat16)
    head_grads = lax.psum(
        (matmul(norm_full.T, d_proj) * grad_scale, matmul(flat_norm.T, d_gate) * grad_scale),
        ("row", "col"),
    )
    d_norm = lax.psum_scatter(
        matmul(d_proj, w_out.T).astype(jnp.bfloat16), "ch", scatter_dimension=1, tiled=True
    ).astype(jnp.float32)
    back_sums = lax.psum((jnp.sum(d_norm, -1), jnp.sum(d_norm * mixed_hat, -1)), "ch")
    d_mixed = hidden_rstd * (
        d_norm
        - (back_sums[0] / total_hidden)[:, None]
        - mixed_hat * (back_sums[1] / total_hidden)[:, None]
    )
    d_mixed = d_mixed.astype(jnp.bfloat16).reshape(row_count, col_count, hidden)
    d_rows = lax.all_gather(d_mixed, "col", axis=1, tiled=True)
    right_back = lax.all_gather(right_edge, "row", axis=0, tiled=True)
    d_left = jnp.einsum("ijh,jkh->ikh", d_rows, right_back, preferred_element_type=jnp.float32)
    d_left = d_left.reshape(row_count * col_count, hidden)
    left_all = lax.all_gather(left_edge, "row", axis=0, tiled=True)
    d_columns = lax.all_to_all(d_rows, "row", split_axis=1, concat_axis=0, tiled=True)
    d_right = jnp.einsum("ijh,ikh->jkh", d_columns, left_all, preferred_element_type=jnp.float32)
    d_right = d_right.reshape(row_count * col_count, hidden)
    grad_pa = (d_left * gate_a).astype(jnp.bfloat16)
    grad_ga = (d_left * proj_a * gate_a * (1.0 - gate_a)).astype(jnp.bfloat16)
    grad_pb = (d_right * gate_b).astype(jnp.bfloat16)
    grad_gb = (d_right * proj_b * gate_b * (1.0 - gate_b)).astype(jnp.bfloat16)
    d_four = jnp.concatenate([grad_ga, grad_pa, grad_gb, grad_pb], axis=1)
    weight_terms = matmul(flat_norm.T, d_four) * grad_scale
    summed = lax.psum(weight_terms, ("row", "col"))
    d_flat = matmul(d_four, w_four.T) + matmul(d_gate, w_gate_out.T)
    hat_all = pair_hat.reshape(row_count * col_count, channels)
    rstd_flat = pair_rstd.reshape(row_count * col_count, 1)
    offset = lax.axis_index("ch") * out_width
    grad_whole = lax.psum(d_flat.astype(jnp.bfloat16), "ch").astype(jnp.float32)
    grad_full = rstd_flat * (
        grad_whole
        - jnp.mean(grad_whole, -1, keepdims=True)
        - hat_all * jnp.mean(grad_whole * hat_all, -1, keepdims=True)
    )
    grad_pair = lax.dynamic_slice_in_dim(grad_full, offset, out_width, 1)
    grad_pair = grad_pair.astype(jnp.bfloat16).reshape(row_count, col_count, out_width)
    return (
        updated,
        grad_pair,
        summed[:, :hidden],
        summed[:, hidden : 2 * hidden],
        summed[:, 2 * hidden : 3 * hidden],
        summed[:, 3 * hidden :],
        head_grads[1],
        head_grads[0],
    )


everyone = ("col", "row", "ch")
f32, bf16 = jnp.float32, jnp.bfloat16


def dot(first, second, over):
    return lax.dot_general(
        first, second, (((over[0],), (over[1],)), ((), ())), preferred_element_type=f32
    )


def call(kernel, outs, args, scratch=(), far=(), outs_far=False, room=16):
    whole = pl.BlockSpec(memory_space=pltpu.VMEM)
    anywhere = pl.BlockSpec(memory_space=pl.ANY)
    return pl.pallas_call(
        kernel,
        out_shape=tuple(jax.ShapeDtypeStruct(*out) for out in outs),
        in_specs=[anywhere if at in far else whole for at in range(len(args))],
        out_specs=tuple(anywhere if outs_far else whole for _ in outs),
        scratch_shapes=scratch,
        compiler_params=pltpu.CompilerParams(vmem_limit_bytes=room * 2**20),
    )(*args)


def grouping(hidden, share):
    shape = (2 * hidden, 2 * hidden)
    rows = lax.broadcasted_iota(jnp.int32, shape, 0)
    columns = lax.broadcasted_iota(jnp.int32, shape, 1)
    group, within = rows // (2 * share), lax.rem(rows, 2 * share)
    side = within // share
    wanted = side * hidden + group * share + within - side * share
    return jnp.where(columns == wanted, 1.0, 0.0).astype(bf16)


def start_all(copies):
    for copy in copies:
        copy.start()


def wait_all(copies):
    for copy in copies:
        copy.wait()


def prepare(share, ga, pa, gb, pb, go, wo, pair_far, out, normed, gates, values, last, pair, arrivals):
    hidden = go.shape[0]
    count = pair.shape[0]
    rows = pl.ds(lax.axis_index("ch") * count, count)
    fetch = pltpu.make_async_copy(pair_far.at[rows], pair, arrivals.at[6])
    fetch.start()
    width = 2 * hidden
    copies = []
    for at, (held, low, high) in enumerate(((gates, ga, gb), (values, pa, pb), (last, go, wo))):
        copies.append(pltpu.make_async_copy(low, held.at[0:hidden], arrivals.at[2 * at]))
        copies.append(pltpu.make_async_copy(high, held.at[hidden:width], arrivals.at[2 * at + 1]))
    start_all(copies)
    order = grouping(hidden, share)
    wait_all(copies)
    out[:width] = dot(order, gates[...], (1, 0)).astype(bf16)
    out[width : 2 * width] = dot(order, values[...], (1, 0)).astype(bf16)
    out[2 * width :] = last[...]
    fetch.wait()
    normed[...] = normalized(pair[...])[0].astype(bf16)


def rows_of(weights, start, count):
    return jnp.concatenate([weights[c, start : start + count] for c in range(weights.shape[0])], 0)


def normalized(pair):
    count, cols, channels = pair.shape
    values = pair.astype(f32).reshape(count * cols, channels).T
    centred = values - jnp.mean(values, 0, keepdims=True)
    rstd = lax.rsqrt(jnp.mean(centred * centred, 0, keepdims=True) + epsilon)
    return centred * rstd, rstd


def edges(width, normed, weights, *sends):
    for c, send in enumerate(sends):
        gate = jax.nn.sigmoid(dot(weights[c, :width], normed[...], (1, 0)))
        edge = gate * dot(weights[c, width : 2 * width], normed[...], (1, 0))
        q = send.shape[1]
        for s in range(send.shape[0]):
            send[s] = edge[s * q : (s + 1) * q].astype(bf16)


def spread_rows(block, cols, arrived, held):
    devices, q, flat = arrived.shape
    rows = flat // cols
    for s in range(devices):
        tile = arrived[s].astype(f32)
        for i in range(rows):
            start = (s * rows + i) * block
            held[start : start + q, 0:cols] = tile[:, i * cols : (i + 1) * cols]


def pack_rows(block, cols, held, send):
    devices, q, flat = send.shape
    rows = flat // cols
    for s in range(devices):
        starts = [(s * rows + i) * block for i in range(rows)]
        whole = jnp.concatenate([held[start : start + block, 0:cols] for start in starts], axis=1)
        send[s] = whole[:q].astype(bf16)


def square(block, parts, cols, held, e):
    tokens = parts * cols
    return jnp.concatenate(
        [
            held[pl.ds(p * tokens * block + e, tokens, stride=block), 0:cols]
            for p in range(parts)
        ],
        axis=1,
    ).astype(bf16)


def put_square(block, parts, cols, held, e, values):
    tokens = parts * cols
    for p in range(parts):
        held[pl.ds(p * tokens * block + e, tokens, stride=block), 0:cols] = values[
            :, p * cols : (p + 1) * cols
        ]


def mix(parts, cols, arrived, send, kept, held, result):
    block = 8
    q = arrived.shape[1]
    spread_rows(block, cols, arrived, held)
    for e in range(q // 2):
        left = square(block, parts, cols, held, e)
        right = square(block, parts, cols, held, q // 2 + e)
        kept[e] = left
        kept[q // 2 + e] = right
        put_square(block, parts, cols, result, e, dot(left, right, (1, 1)))
    pack_rows(block, cols, result, send)


def unmix(parts, cols, arrived, kept_far, send, held, result, kept, arrival):
    block = 8
    q = arrived.shape[1]
    copy = pltpu.make_async_copy(kept_far, kept, arrival)
    copy.start()
    spread_rows(block, cols, arrived, held)
    copy.wait()
    for e in range(q):
        d_mixed = square(block, parts, cols, held, e)
        put_square(block, parts, cols, result, e, dot(d_mixed, kept[q + e], (1, 0)))
        put_square(block, parts, cols, result, q + e, dot(d_mixed, kept[e], (0, 0)))
    pack_rows(block, cols, result, send)


def split_rows(cols, values, own, other):
    hidden = values.shape[0] // 2
    first = lax.axis_index("ch") == 0
    low, high = values[:hidden], values[hidden:]
    mine = jnp.where(first, low, high)
    yours = jnp.where(first, high, low)
    for i in range(own.shape[0]):
        own[i] = mine[:, i * cols : (i + 1) * cols].astype(bf16)
        other[i] = yours[:, i * cols : (i + 1) * cols].astype(bf16)


def head(
    width, scale, first, second, weights, normed_far, own_far, other_far,
    first_send, second_send, d_gate, terms, updated_own, updated_other,
    normed, own, other, upstream, mixed, arrivals,
):
    parts, total, _ = weights.shape
    hidden = (total - 2 * width) // 2
    devices, q, flat = first.shape
    count, _, cols = other.shape
    core = lax.axis_index("ch")
    copies = [
        pltpu.make_async_copy(normed_far, normed, arrivals.at[0]),
        pltpu.make_async_copy(own_far.at[pl.ds(core * count, count)], own, arrivals.at[1]),
        pltpu.make_async_copy(other_far, other, arrivals.at[2]),
    ]
    start_all(copies)
    for c, arrived in enumerate((first, second)):
        for s in range(devices):
            start = (c * devices + s) * q
            mixed[start : start + q] = arrived[s].astype(f32)
    mixed = mixed[...]
    average = jnp.mean(mixed, 0, keepdims=True)
    spread = jnp.mean(mixed * mixed, 0, keepdims=True) - average * average
    inverse = lax.rsqrt(spread + epsilon)
    hat = (mixed - average) * inverse
    hat_rounded = hat.astype(bf16)
    w_out = rows_of(weights, 2 * width + hidden, hidden)
    proj = dot(w_out, hat_rounded, (1, 0))
    wait_all(copies)
    for part, side in ((own, core), (other, 1 - core)):
        upstream[pl.ds(pl.multiple_of(side * hidden, hidden), hidden)] = jnp.concatenate(
            [part[i].astype(f32) for i in range(count)], axis=1
        )
    gate = jax.nn.sigmoid(dot(rows_of(weights, 2 * width, hidden), normed[...], (1, 0)))
    up = upstream[...]
    d_proj = (up * gate).astype(bf16)
    d_gate[...] = (up * proj * gate * (1.0 - gate)).astype(bf16)
    d_norm = dot(w_out, d_proj, (0, 0))
    d_mixed = inverse * (
        d_norm
        - jnp.mean(d_norm, 0, keepdims=True)
        - hat * jnp.mean(d_norm * hat, 0, keepdims=True)
    )
    for c, send in enumerate((first_send, second_send)):
        for s in range(devices):
            start = (c * devices + s) * q
            send[s] = d_mixed[start : start + q].astype(bf16)
    by_gate = dot(d_gate[...], normed[...], (1, 1)) * scale
    by_out = dot(d_proj, hat_rounded, (1, 1)) * scale
    for c in range(parts):
        terms[c, :hidden] = by_gate[c * hidden : (c + 1) * hidden]
        terms[c, hidden:] = by_out[c * hidden : (c + 1) * hidden]
    split_rows(cols, gate * proj, updated_own, updated_other)


def tail(
    width, scale, first, second, weights, pair_far, d_gate_far, head_terms,
    send, grad_own, grad_other,
    pair, d_gate, whole, arrivals,
):
    parts, total, channels = weights.shape
    hidden = (total - 2 * width) // 2
    devices = first.shape[0]
    count, cols, _ = pair.shape
    core = lax.axis_index("ch")
    copies = [
        pltpu.make_async_copy(pair_far.at[pl.ds(core * count, count)], pair, arrivals.at[0]),
        pltpu.make_async_copy(d_gate_far, d_gate, arrivals.at[1]),
    ]
    start_all(copies)
    wait_all(copies)
    hat, inverse = normalized(pair[...])
    normed = hat.astype(bf16)
    w_gate, w_value = rows_of(weights, 0, width), rows_of(weights, width, width)
    gate = jax.nn.sigmoid(dot(w_gate, normed, (1, 0)))
    value = dot(w_value, normed, (1, 0))
    grad = jnp.concatenate([part[s].astype(f32) for part in (first, second) for s in range(devices)], 0)
    by_value = grad * gate
    by_gate = (by_value * (value * (1.0 - gate))).astype(bf16)
    by_value = by_value.astype(bf16)
    terms = [dot(by_gate, normed, (1, 1)) * scale, dot(by_value, normed, (1, 1)) * scale]
    for c in range(parts):
        for at, term in enumerate(terms):
            start = c * total + at * width
            whole[start : start + width] = term[c * width : (c + 1) * width]
        whole[c * total + 2 * width : (c + 1) * total] = head_terms[c]
    per = send.shape[1]
    for s in range(devices):
        send[s] = whole[s * per : (s + 1) * per].astype(bf16)
    d_input = dot(w_gate, by_gate, (0, 0)) + dot(w_value, by_value, (0, 0))
    d_input = d_input + dot(rows_of(weights, 2 * width, hidden), d_gate[...], (0, 0))
    back = inverse * (
        d_input
        - jnp.mean(d_input, 0, keepdims=True)
        - hat * jnp.mean(d_input * hat, 0, keepdims=True)
    )
    split_rows(cols, back, grad_own, grad_other)


def add_up(arrived, out):
    total = jnp.sum(arrived[...].astype(f32), 0).astype(bf16)
    for s in range(out.shape[0]):
        out[s] = total


def turn_back(share, sums, *refs):
    outs, whole, results, leaves = refs[:6], refs[6], refs[7], refs[8]
    _, hidden, channels = results.shape
    width = 2 * hidden
    per = sums.shape[1]
    for s in range(sums.shape[0]):
        whole[s * per : (s + 1) * per] = sums[s].astype(f32)
    order = grouping(hidden, share)
    for at in range(2):
        both = dot(order, whole[at * width : (at + 1) * width].astype(bf16), (0, 0))
        results[at] = both[:hidden]
        results[2 + at] = both[hidden:]
    results[4] = whole[2 * width : 2 * width + hidden]
    results[5] = whole[2 * width + hidden :]
    copies = [
        pltpu.make_async_copy(results.at[at], out, leaves.at[at]) for at, out in enumerate(outs)
    ]
    start_all(copies)
    wait_all(copies)


def join_rows(own, other, out, leaves):
    count = own.shape[0]
    core = lax.axis_index("ch")
    copies = [
        pltpu.make_async_copy(own, out.at[pl.ds(core * count, count)], leaves.at[0]),
        pltpu.make_async_copy(other, out.at[pl.ds((1 - core) * count, count)], leaves.at[1]),
    ]
    start_all(copies)
    wait_all(copies)


def by_channels(pair, cotangent, w_gate_a, w_proj_a, w_gate_b, w_proj_b, w_gate_out, w_out):
    row_count, cols, channels = pair.shape
    hidden = w_gate_a.shape[1]
    parts, col_parts, row_parts = lax.axis_size("ch"), lax.axis_size("col"), lax.axis_size("row")
    devices = parts * col_parts * row_parts
    share = hidden // devices
    width = 2 * hidden
    count = row_count // parts
    flat = count * cols
    tokens = cols * col_parts
    scale = 1.0 / tokens
    swap = [(c, parts - 1 - c) for c in range(parts)]
    whole_weight = pltpu.VMEM((2 * hidden, channels), bf16)
    weights, normed = call(
        functools.partial(prepare, share),
        [((2 * width + 2 * hidden, channels), bf16), ((channels, flat), bf16)],
        (w_gate_a.T, w_proj_a.T, w_gate_b.T, w_proj_b.T, w_gate_out.T, w_out.T, pair),
        (
            whole_weight,
            whole_weight,
            whole_weight,
            pltpu.VMEM((count, cols, channels), bf16),
            pltpu.SemaphoreType.DMA((7,)),
        ),
        far=range(7),
        room=60,
    )
    weights = lax.all_gather(weights, "ch")
    own = jnp.swapaxes(cotangent, 1, 2)
    other = lax.dynamic_slice_in_dim(own, (1 - lax.axis_index("ch")) * count, count, 0)
    other = lax.ppermute(other, "ch", swap)
    edge = ((devices, 2 * share, flat), bf16)
    block = ((devices, share, flat), bf16)
    sends = call(functools.partial(edges, width), [edge] * parts, (normed, weights))
    arrived = [lax.all_to_all(send, everyone, 0, 0) for send in sends]
    room = pltpu.VMEM((col_parts * tokens * 8, -(-cols // 128) * 128), f32)
    kept = [None] * parts
    for c in range(parts):
        send, kept[c] = call(
            functools.partial(mix, col_parts, cols),
            [block, ((2 * share, tokens, tokens), bf16)],
            (arrived[c],),
            (room, room),
        )
        arrived[c] = lax.all_to_all(send, everyone, 0, 0)
    part = ((count, hidden, cols), bf16)
    *sends, d_gate, head_terms, updated_own, updated_other = call(
        functools.partial(head, width, scale),
        [
            block,
            block,
            ((hidden * parts, flat), bf16),
            ((parts, 2 * hidden, channels), f32),
            part,
            part,
        ],
        (*arrived, weights, normed, own, other),
        (
            pltpu.VMEM((channels, flat), bf16),
            pltpu.VMEM(*part),
            pltpu.VMEM(*part),
            pltpu.VMEM((hidden * parts, flat), f32),
            pltpu.VMEM((hidden * parts, flat), f32),
            pltpu.SemaphoreType.DMA((3,)),
        ),
        far=(3, 4, 5),
    )
    arrived = [lax.all_to_all(send, everyone, 0, 0) for send in sends]
    updated_other = lax.ppermute(updated_other, "ch", swap)
    for c in range(parts):
        (send,) = call(
            functools.partial(unmix, col_parts, cols),
            [edge],
            (arrived[c], kept[c]),
            (room, room, pltpu.VMEM(kept[c].shape, bf16), pltpu.SemaphoreType.DMA),
            far=(1,),
        )
        arrived[c] = lax.all_to_all(send, everyone, 0, 0)
    rows = [((row_count, hidden, cols), bf16)]
    two = pltpu.SemaphoreType.DMA((2,))
    (updated,) = call(join_rows, rows, (updated_own, updated_other), (two,), (0, 1), True)
    arrived[-1], updated = lax.optimization_barrier((arrived[-1], updated))
    total = 2 * width + 2 * hidden
    per = total * parts // devices
    send, grad_own, grad_other = call(
        functools.partial(tail, width, scale),
        [((devices, per, channels), bf16), part, part],
        (*arrived, weights, pair, d_gate, head_terms),
        (
            pltpu.VMEM((count, cols, channels), bf16),
            pltpu.VMEM((hidden * parts, flat), bf16),
            pltpu.VMEM((total * parts, channels), f32),
            two,
        ),
        far=(3, 4),
    )
    arrived = lax.all_to_all(send, ("ch", "row", "col"), 0, 0)
    grad_other = lax.ppermute(grad_other, "ch", swap)
    (grad_pair,) = call(join_rows, rows, (grad_own, grad_other), (two,), (0, 1), True)
    rest = devices // parts
    (sums,) = call(add_up, [((rest, per, channels), bf16)], (arrived,))
    sums = lax.all_to_all(sums, ("row", "col"), 0, 0)
    sums, grad_pair = lax.optimization_barrier((sums, grad_pair))
    grads = call(
        functools.partial(turn_back, share),
        [((hidden, channels), f32)] * 6,
        (sums,),
        (
            pltpu.VMEM((total, channels), f32),
            pltpu.VMEM((6, hidden, channels), f32),
            pltpu.SemaphoreType.DMA((6,)),
        ),
        outs_far=True,
    )
    return jnp.swapaxes(updated, 1, 2), jnp.swapaxes(grad_pair, 1, 2), *(g.T for g in grads)


def on_device(*arrays):
    row_count, cols, _ = arrays[0].shape
    parts, devices = lax.axis_size("ch"), lax.axis_size(everyone)
    hidden = arrays[2].shape[1]
    share = hidden // devices
    fits = (
        share * devices == hidden
        and parts == 2
        and 1 <= share <= 4
        and row_count % parts == 0
        and 6 * hidden * parts % devices == 0
        and arrays[1].shape[2] == hidden
        and cols % 16 == 0
    )
    return by_channels(*arrays) if fits else by_rows(*arrays)


def solution(mesh):
    in_specs = (
        P("row", "col", None),
        P("row", "col", "ch"),
        P(None, "ch"),
        P(None, "ch"),
        P(None, "ch"),
        P(None, "ch"),
        P(None, "ch"),
        P(None, "ch"),
    )
    out_specs = (
        P("row", "col", "ch"),
        P("row", "col", "ch"),
        P(None, "ch"),
        P(None, "ch"),
        P(None, "ch"),
        P(None, "ch"),
        P(None, "ch"),
        P(None, "ch"),
    )
    return jax.shard_map(
        on_device, mesh=mesh, in_specs=in_specs, out_specs=out_specs, check_vma=False
    )
```

```python
import functools

import jax
import jax.numpy as jnp
import numpy as np
from jax import lax
from jax.experimental import pallas as pl
from jax.experimental.pallas import tpu as pltpu
from jax.sharding import PartitionSpec as P

epsilon = 1e-05


def layer_norm(values):
    average = jnp.mean(values, -1, keepdims=True)
    centred = values - average
    spread = jnp.mean(centred * centred, -1, keepdims=True)
    inverse = lax.rsqrt(spread + epsilon)
    return (centred * inverse, inverse)


def matmul(first, second):
    return jnp.dot(first, second, preferred_element_type=jnp.float32)


def by_rows(pair, cotangent, w_gate_a, w_proj_a, w_gate_b, w_proj_b, w_gate_out, w_out):
    row_count, col_count, channels = pair.shape
    hidden = w_gate_a.shape[1]
    total_hidden = hidden * lax.axis_size("ch")
    out_width = cotangent.shape[2]
    length = row_count * lax.axis_size("row")
    grad_scale = 1.0 / length
    pair_hat, pair_rstd = layer_norm(pair.astype(jnp.float32))
    flat_norm = pair_hat.astype(jnp.bfloat16).reshape(row_count * col_count, channels)
    w_four = jnp.concatenate([w_gate_a, w_proj_a, w_gate_b, w_proj_b], axis=1)
    projected = matmul(flat_norm, w_four)
    gate_a = jax.nn.sigmoid(projected[:, :hidden])
    proj_a = projected[:, hidden : 2 * hidden]
    gate_b = jax.nn.sigmoid(projected[:, 2 * hidden : 3 * hidden])
    proj_b = projected[:, 3 * hidden :]
    left_edge = (gate_a * proj_a).astype(jnp.bfloat16).reshape(row_count, col_count, hidden)
    right_edge = (gate_b * proj_b).astype(jnp.bfloat16).reshape(row_count, col_count, hidden)
    right_all = lax.all_gather(right_edge, "row", axis=0, tiled=True)
    mixed_swap = lax.psum_scatter(
        jnp.einsum("jkh,ikh->jih", right_all, left_edge, preferred_element_type=jnp.float32).astype(
            jnp.bfloat16
        ),
        "col",
        scatter_dimension=0,
        tiled=True,
    ).astype(jnp.float32)
    mixed = jnp.swapaxes(mixed_swap, 0, 1).reshape(row_count * col_count, hidden)
    hidden_sums = lax.psum((jnp.sum(mixed, -1), jnp.sum(mixed * mixed, -1)), "ch")
    hidden_mean = (hidden_sums[0] / total_hidden)[:, None]
    hidden_var = (hidden_sums[1] / total_hidden)[:, None] - hidden_mean * hidden_mean
    hidden_rstd = lax.rsqrt(hidden_var + epsilon)
    mixed_hat = (mixed - hidden_mean) * hidden_rstd
    mixed_norm = mixed_hat.astype(jnp.bfloat16)
    norm_full = lax.all_gather(mixed_norm, "ch", axis=1, tiled=True)
    gate_out = jax.nn.sigmoid(matmul(flat_norm, w_gate_out))
    proj_out = matmul(norm_full, w_out)
    updated = (gate_out * proj_out).astype(jnp.bfloat16).reshape(row_count, col_count, out_width)
    upstream = cotangent.reshape(row_count * col_count, out_width).astype(jnp.float32)
    d_proj = (upstream * gate_out).astype(jnp.bfloat16)
    d_gate = (upstream * proj_out * gate_out * (1.0 - gate_out)).astype(jnp.bfloat16)
    head_grads = lax.psum(
        (matmul(norm_full.T, d_proj) * grad_scale, matmul(flat_norm.T, d_gate) * grad_scale),
        ("row", "col"),
    )
    d_norm = lax.psum_scatter(
        matmul(d_proj, w_out.T).astype(jnp.bfloat16), "ch", scatter_dimension=1, tiled=True
    ).astype(jnp.float32)
    back_sums = lax.psum((jnp.sum(d_norm, -1), jnp.sum(d_norm * mixed_hat, -1)), "ch")
    d_mixed = hidden_rstd * (
        d_norm
        - (back_sums[0] / total_hidden)[:, None]
        - mixed_hat * (back_sums[1] / total_hidden)[:, None]
    )
    d_mixed = d_mixed.astype(jnp.bfloat16).reshape(row_count, col_count, hidden)
    d_rows = lax.all_gather(d_mixed, "col", axis=1, tiled=True)
    right_back = lax.all_gather(right_edge, "row", axis=0, tiled=True)
    d_left = jnp.einsum("ijh,jkh->ikh", d_rows, right_back, preferred_element_type=jnp.float32)
    d_left = d_left.reshape(row_count * col_count, hidden)
    left_all = lax.all_gather(left_edge, "row", axis=0, tiled=True)
    d_columns = lax.all_to_all(d_rows, "row", split_axis=1, concat_axis=0, tiled=True)
    d_right = jnp.einsum("ijh,ikh->jkh", d_columns, left_all, preferred_element_type=jnp.float32)
    d_right = d_right.reshape(row_count * col_count, hidden)
    grad_pa = (d_left * gate_a).astype(jnp.bfloat16)
    grad_ga = (d_left * proj_a * gate_a * (1.0 - gate_a)).astype(jnp.bfloat16)
    grad_pb = (d_right * gate_b).astype(jnp.bfloat16)
    grad_gb = (d_right * proj_b * gate_b * (1.0 - gate_b)).astype(jnp.bfloat16)
    d_four = jnp.concatenate([grad_ga, grad_pa, grad_gb, grad_pb], axis=1)
    weight_terms = matmul(flat_norm.T, d_four) * grad_scale
    summed = lax.psum(weight_terms, ("row", "col"))
    d_flat = matmul(d_four, w_four.T) + matmul(d_gate, w_gate_out.T)
    hat_all = pair_hat.reshape(row_count * col_count, channels)
    rstd_flat = pair_rstd.reshape(row_count * col_count, 1)
    offset = lax.axis_index("ch") * out_width
    grad_whole = lax.psum(d_flat.astype(jnp.bfloat16), "ch").astype(jnp.float32)
    grad_full = rstd_flat * (
        grad_whole
        - jnp.mean(grad_whole, -1, keepdims=True)
        - hat_all * jnp.mean(grad_whole * hat_all, -1, keepdims=True)
    )
    grad_pair = lax.dynamic_slice_in_dim(grad_full, offset, out_width, 1)
    grad_pair = grad_pair.astype(jnp.bfloat16).reshape(row_count, col_count, out_width)
    return (
        updated,
        grad_pair,
        summed[:, :hidden],
        summed[:, hidden : 2 * hidden],
        summed[:, 2 * hidden : 3 * hidden],
        summed[:, 3 * hidden :],
        head_grads[1],
        head_grads[0],
    )


everyone = ("ch", "col", "row")
one_core = ("col", "row")
f32, bf16 = jnp.float32, jnp.bfloat16


def dot(first, second, over):
    return lax.dot_general(
        first, second, (((over[0],), (over[1],)), ((), ())), preferred_element_type=f32
    )


def call(kernel, outs, args, scratch=(), far=(), outs_far=False, room=16):
    whole = pl.BlockSpec(memory_space=pltpu.VMEM)
    anywhere = pl.BlockSpec(memory_space=pl.ANY)
    return pl.pallas_call(
        kernel,
        out_shape=tuple(jax.ShapeDtypeStruct(*out) for out in outs),
        in_specs=[anywhere if at in far else whole for at in range(len(args))],
        out_specs=tuple(anywhere if outs_far else whole for _ in outs),
        scratch_shapes=scratch,
        compiler_params=pltpu.CompilerParams(vmem_limit_bytes=room * 2**20),
    )(*args)


def grouping(hidden, share):
    shape = (2 * hidden, 2 * hidden)
    rows = lax.broadcasted_iota(jnp.int32, shape, 0)
    columns = lax.broadcasted_iota(jnp.int32, shape, 1)
    group, within = rows // (2 * share), lax.rem(rows, 2 * share)
    side = within // share
    wanted = side * hidden + group * share + within - side * share
    return jnp.where(columns == wanted, 1.0, 0.0).astype(bf16)


def start_all(copies):
    for copy in copies:
        copy.start()


def wait_all(copies):
    for copy in copies:
        copy.wait()


def rows_of(weights, start, count):
    return jnp.concatenate([weights[c, start : start + count] for c in range(weights.shape[0])], 0)


def normalized(pair):
    count, cols, channels = pair.shape
    values = pair.astype(f32).reshape(count * cols, channels).T
    centred = values - jnp.mean(values, 0, keepdims=True)
    rstd = lax.rsqrt(jnp.mean(centred * centred, 0, keepdims=True) + epsilon)
    return centred * rstd, rstd


def edges(
    share, ga, pa, gb, pb, go, wo, pair_far, weights, normed, send,
    gates, values, last, pair, both, arrivals,
):
    hidden = go.shape[0]
    width = 2 * hidden
    parts = both.shape[0]
    flat = both.shape[2]
    count = pair.shape[0] // parts
    copies = []
    for at, (held, low, high) in enumerate(((gates, ga, gb), (values, pa, pb), (last, go, wo))):
        copies.append(pltpu.make_async_copy(low, held.at[0:hidden], arrivals.at[2 * at]))
        copies.append(pltpu.make_async_copy(high, held.at[hidden:width], arrivals.at[2 * at + 1]))
    rows = [pl.ds(c * count, count) for c in range(parts)]
    fetches = [
        pltpu.make_async_copy(pair_far.at[rows[c]], pair.at[rows[c]], arrivals.at[6 + c])
        for c in range(parts)
    ]
    start_all(copies + fetches)
    order = grouping(hidden, share)
    wait_all(copies)
    w_gate = dot(order, gates[...], (1, 0)).astype(bf16)
    w_value = dot(order, values[...], (1, 0)).astype(bf16)
    weights[:width] = w_gate
    weights[width : 2 * width] = w_value
    weights[2 * width :] = last[...]
    for c, fetch in enumerate(fetches):
        fetch.wait()
        hat = normalized(pair[rows[c]])[0].astype(bf16)
        both[c] = hat
        edge = jax.nn.sigmoid(dot(w_gate, hat, (1, 0))) * dot(w_value, hat, (1, 0))
        send[:, :, c * flat : (c + 1) * flat] = edge.reshape(
            send.shape[0], send.shape[1], flat
        ).astype(bf16)
    normed[...] = both[lax.axis_index("ch")]


def first_row(s, devices, cores, rows):
    line = devices // cores
    return (s % line) * cores * rows + (s // line) * rows


def spread_rows(block, cores, cols, arrived, held):
    devices, q, flat = arrived.shape
    rows = flat // cols
    for s in range(devices):
        tile = arrived[s].astype(f32)
        for i in range(rows):
            start = (first_row(s, devices, cores, rows) + i) * block
            held[start : start + q, 0:cols] = tile[:, i * cols : (i + 1) * cols]


def pack_rows(block, cores, cols, held, send):
    devices, q, flat = send.shape
    rows = flat // cols
    for s in range(devices):
        first = first_row(s, devices, cores, rows)
        starts = [(first + i) * block for i in range(rows)]
        whole = jnp.concatenate([held[start : start + block, 0:cols] for start in starts], axis=1)
        send[s] = whole[:q].astype(bf16)


def square(block, parts, cols, held, e):
    tokens = parts * cols
    return jnp.concatenate(
        [
            held[pl.ds(p * tokens * block + e, tokens, stride=block), 0:cols]
            for p in range(parts)
        ],
        axis=1,
    ).astype(bf16)


def put_square(block, parts, cols, held, e, values):
    tokens = parts * cols
    for p in range(parts):
        held[pl.ds(p * tokens * block + e, tokens, stride=block), 0:cols] = values[
            :, p * cols : (p + 1) * cols
        ]


def mix(parts, cores, cols, arrived, send, kept, held, result):
    block = 8
    q = arrived.shape[1]
    spread_rows(block, 1, cols, arrived, held)
    for e in range(q // 2):
        left = square(block, parts, cols, held, e)
        right = square(block, parts, cols, held, q // 2 + e)
        kept[e] = left
        kept[q // 2 + e] = right
        put_square(block, parts, cols, result, e, dot(left, right, (1, 1)))
    pack_rows(block, cores, cols, result, send)


def unmix(parts, cores, cols, arrived, kept_far, send, held, result, kept, arrival):
    block = 8
    q = arrived.shape[1]
    copy = pltpu.make_async_copy(kept_far, kept, arrival)
    copy.start()
    spread_rows(block, cores, cols, arrived, held)
    copy.wait()
    for e in range(q):
        d_mixed = square(block, parts, cols, held, e)
        put_square(block, parts, cols, result, e, dot(d_mixed, kept[q + e], (1, 0)))
        put_square(block, parts, cols, result, q + e, dot(d_mixed, kept[e], (0, 0)))
    pack_rows(block, cores, cols, result, send)


def order_weights(own, other, weights):
    core = lax.axis_index("ch")
    weights[core] = own[...]
    weights[1 - core] = other[...]


def split_rows(cols, values, own, other):
    hidden = values.shape[0] // 2
    first = lax.axis_index("ch") == 0
    low, high = values[:hidden], values[hidden:]
    mine = jnp.where(first, low, high)
    yours = jnp.where(first, high, low)
    for i in range(own.shape[0]):
        own[i] = mine[:, i * cols : (i + 1) * cols].astype(bf16)
        other[i] = yours[:, i * cols : (i + 1) * cols].astype(bf16)


def head(
    width, scale, arrived, own_weights, other_weights, normed_far, own_far, other_far,
    send, d_gate, terms, updated_own, updated_other,
    normed, own, other, upstream, weights, arrivals,
):
    parts, total, _ = weights.shape
    order_weights(own_weights, other_weights, weights)
    hidden = (total - 2 * width) // 2
    devices, q, flat = arrived.shape
    count, _, cols = other.shape
    core = lax.axis_index("ch")
    copies = [
        pltpu.make_async_copy(normed_far, normed, arrivals.at[0]),
        pltpu.make_async_copy(own_far.at[pl.ds(core * count, count)], own, arrivals.at[1]),
        pltpu.make_async_copy(other_far, other, arrivals.at[2]),
    ]
    start_all(copies)
    mixed = jnp.concatenate([arrived[s].astype(f32) for s in range(devices)], 0)
    average = jnp.mean(mixed, 0, keepdims=True)
    spread = jnp.mean(mixed * mixed, 0, keepdims=True) - average * average
    inverse = lax.rsqrt(spread + epsilon)
    hat = (mixed - average) * inverse
    hat_rounded = hat.astype(bf16)
    w_out = rows_of(weights, 2 * width + hidden, hidden)
    proj = dot(w_out, hat_rounded, (1, 0))
    wait_all(copies)
    for part, side in ((own, core), (other, 1 - core)):
        upstream[pl.ds(pl.multiple_of(side * hidden, hidden), hidden)] = jnp.concatenate(
            [part[i].astype(f32) for i in range(count)], axis=1
        )
    gate = jax.nn.sigmoid(dot(rows_of(weights, 2 * width, hidden), normed[...], (1, 0)))
    up = upstream[...]
    d_proj = (up * gate).astype(bf16)
    d_gate[...] = (up * proj * gate * (1.0 - gate)).astype(bf16)
    d_norm = dot(w_out, d_proj, (0, 0))
    d_mixed = inverse * (
        d_norm
        - jnp.mean(d_norm, 0, keepdims=True)
        - hat * jnp.mean(d_norm * hat, 0, keepdims=True)
    )
    for s in range(devices):
        send[s] = d_mixed[s * q : (s + 1) * q].astype(bf16)
    by_gate = dot(d_gate[...], normed[...], (1, 1)) * scale
    by_out = dot(d_proj, hat_rounded, (1, 1)) * scale
    for c in range(parts):
        terms[c, :hidden] = by_gate[c * hidden : (c + 1) * hidden]
        terms[c, hidden:] = by_out[c * hidden : (c + 1) * hidden]
    split_rows(cols, gate * proj, updated_own, updated_other)


def tail(
    width, scale, arrived, own_weights, other_weights, pair_far, d_gate_far, head_terms,
    send, grad_own, grad_other,
    pair, d_gate, whole, weights, arrivals,
):
    parts, total, channels = weights.shape
    hidden = (total - 2 * width) // 2
    devices, q, flat = arrived.shape
    count, cols, _ = pair.shape
    core = lax.axis_index("ch")
    copies = [
        pltpu.make_async_copy(pair_far.at[pl.ds(core * count, count)], pair, arrivals.at[0]),
        pltpu.make_async_copy(d_gate_far, d_gate, arrivals.at[1]),
    ]
    start_all(copies)
    order_weights(own_weights, other_weights, weights)
    wait_all(copies)
    hat, inverse = normalized(pair[...])
    normed = hat.astype(bf16)
    w_gate, w_value = rows_of(weights, 0, width), rows_of(weights, width, width)
    gate = jax.nn.sigmoid(dot(w_gate, normed, (1, 0)))
    value = dot(w_value, normed, (1, 0))
    grad = arrived[...].astype(f32).reshape(devices * q, flat)
    by_value = grad * gate
    by_gate = (by_value * (value * (1.0 - gate))).astype(bf16)
    by_value = by_value.astype(bf16)
    terms = [dot(by_gate, normed, (1, 1)) * scale, dot(by_value, normed, (1, 1)) * scale]
    for c in range(parts):
        for at, term in enumerate(terms):
            start = c * total + at * width
            whole[start : start + width] = term[c * width : (c + 1) * width]
        whole[c * total + 2 * width : (c + 1) * total] = head_terms[c]
    per = send.shape[1]
    for s in range(devices):
        send[s] = whole[s * per : (s + 1) * per].astype(bf16)
    d_input = dot(w_gate, by_gate, (0, 0)) + dot(w_value, by_value, (0, 0))
    d_input = d_input + dot(rows_of(weights, 2 * width, hidden), d_gate[...], (0, 0))
    back = inverse * (
        d_input
        - jnp.mean(d_input, 0, keepdims=True)
        - hat * jnp.mean(d_input * hat, 0, keepdims=True)
    )
    split_rows(cols, back, grad_own, grad_other)


def add_up(arrived, out):
    total = jnp.sum(arrived[...].astype(f32), 0).astype(bf16)
    for s in range(out.shape[0]):
        out[s] = total


def turn_back(share, sums, *refs):
    outs, whole, results, leaves = refs[:6], refs[6], refs[7], refs[8]
    _, hidden, channels = results.shape
    width = 2 * hidden
    per = sums.shape[1]
    for s in range(sums.shape[0]):
        whole[s * per : (s + 1) * per] = sums[s].astype(f32)
    order = grouping(hidden, share)
    for at in range(2):
        both = dot(order, whole[at * width : (at + 1) * width].astype(bf16), (0, 0))
        results[at] = both[:hidden]
        results[2 + at] = both[hidden:]
    results[4] = whole[2 * width : 2 * width + hidden]
    results[5] = whole[2 * width + hidden :]
    copies = [
        pltpu.make_async_copy(results.at[at], out, leaves.at[at]) for at, out in enumerate(outs)
    ]
    start_all(copies)
    wait_all(copies)


def join_rows(own, other, out, leaves):
    count = own.shape[0]
    core = lax.axis_index("ch")
    copies = [
        pltpu.make_async_copy(own, out.at[pl.ds(core * count, count)], leaves.at[0]),
        pltpu.make_async_copy(other, out.at[pl.ds((1 - core) * count, count)], leaves.at[1]),
    ]
    start_all(copies)
    wait_all(copies)


def by_channels(pair, cotangent, w_gate_a, w_proj_a, w_gate_b, w_proj_b, w_gate_out, w_out):
    row_count, cols, channels = pair.shape
    hidden = w_gate_a.shape[1]
    parts, col_parts, row_parts = lax.axis_size("ch"), lax.axis_size("col"), lax.axis_size("row")
    devices = parts * col_parts * row_parts
    share = hidden * parts // devices
    width = 2 * hidden
    count = row_count // parts
    flat = count * cols
    tokens = cols * col_parts
    scale = 1.0 / tokens
    swap = [(c, parts - 1 - c) for c in range(parts)]
    whole_weight = pltpu.VMEM((2 * hidden, channels), bf16)
    rest = devices // parts
    weight = (2 * width + 2 * hidden, channels)
    weights, normed, send = call(
        functools.partial(edges, share),
        [(weight, bf16), ((channels, flat), bf16), ((rest, 2 * share, row_count * cols), bf16)],
        (w_gate_a.T, w_proj_a.T, w_gate_b.T, w_proj_b.T, w_gate_out.T, w_out.T, pair),
        (
            whole_weight,
            whole_weight,
            whole_weight,
            pltpu.VMEM(pair.shape, bf16),
            pltpu.VMEM((parts, channels, flat), bf16),
            pltpu.SemaphoreType.DMA((6 + parts,)),
        ),
        far=range(7),
        room=60,
    )
    arrived = lax.all_to_all(send, one_core, 0, 0)
    weights = (weights, lax.ppermute(weights, "ch", swap))
    own = jnp.swapaxes(cotangent, 1, 2)
    other = lax.dynamic_slice_in_dim(own, (1 - lax.axis_index("ch")) * count, count, 0)
    other = lax.ppermute(other, "ch", swap)
    room = pltpu.VMEM((col_parts * tokens * 8, -(-cols // 128) * 128), f32)
    send, kept = call(
        functools.partial(mix, col_parts, parts, cols),
        [((devices, share, flat), bf16), ((2 * share, tokens, tokens), bf16)],
        (arrived,),
        (room, room),
    )
    arrived = lax.all_to_all(send, everyone, 0, 0)
    part = ((count, hidden, cols), bf16)
    send, d_gate, head_terms, updated_own, updated_other = call(
        functools.partial(head, width, scale),
        [
            ((devices, share, flat), bf16),
            ((hidden * parts, flat), bf16),
            ((parts, 2 * hidden, channels), f32),
            part,
            part,
        ],
        (arrived, *weights, normed, own, other),
        (
            pltpu.VMEM((channels, flat), bf16),
            pltpu.VMEM(*part),
            pltpu.VMEM(*part),
            pltpu.VMEM((hidden * parts, flat), f32),
            pltpu.VMEM((parts, *weight), bf16),
            pltpu.SemaphoreType.DMA((3,)),
        ),
        far=(3, 4, 5),
    )
    arrived = lax.all_to_all(send, everyone, 0, 0)
    updated_other = lax.ppermute(updated_other, "ch", swap)
    (send,) = call(
        functools.partial(unmix, col_parts, parts, cols),
        [((devices, 2 * share, flat), bf16)],
        (arrived, kept),
        (room, room, pltpu.VMEM(kept.shape, bf16), pltpu.SemaphoreType.DMA),
        far=(1,),
    )
    arrived = lax.all_to_all(send, everyone, 0, 0)
    rows = [((row_count, hidden, cols), bf16)]
    two = pltpu.SemaphoreType.DMA((2,))
    (updated,) = call(join_rows, rows, (updated_own, updated_other), (two,), (0, 1), True)
    arrived, updated = lax.optimization_barrier((arrived, updated))
    total = 2 * width + 2 * hidden
    per = total * parts // devices
    send, grad_own, grad_other = call(
        functools.partial(tail, width, scale),
        [((devices, per, channels), bf16), part, part],
        (arrived, *weights, pair, d_gate, head_terms),
        (
            pltpu.VMEM((count, cols, channels), bf16),
            pltpu.VMEM((hidden * parts, flat), bf16),
            pltpu.VMEM((total * parts, channels), f32),
            pltpu.VMEM((parts, *weight), bf16),
            two,
        ),
        far=(3, 4),
    )
    arrived = lax.all_to_all(send, ("ch", "row", "col"), 0, 0)
    grad_other = lax.ppermute(grad_other, "ch", swap)
    (grad_pair,) = call(join_rows, rows, (grad_own, grad_other), (two,), (0, 1), True)
    (sums,) = call(add_up, [((rest, per, channels), bf16)], (arrived,))
    sums = lax.all_to_all(sums, ("row", "col"), 0, 0)
    sums, grad_pair = lax.optimization_barrier((sums, grad_pair))
    grads = call(
        functools.partial(turn_back, share),
        [((hidden, channels), f32)] * 6,
        (sums,),
        (
            pltpu.VMEM((total, channels), f32),
            pltpu.VMEM((6, hidden, channels), f32),
            pltpu.SemaphoreType.DMA((6,)),
        ),
        outs_far=True,
    )
    return jnp.swapaxes(updated, 1, 2), jnp.swapaxes(grad_pair, 1, 2), *(g.T for g in grads)


def on_device(*arrays):
    row_count, cols, _ = arrays[0].shape
    parts, devices = lax.axis_size("ch"), lax.axis_size(everyone)
    hidden = arrays[2].shape[1]
    share = hidden * parts // devices
    fits = (
        share * devices == hidden * parts
        and parts == 2
        and 2 * share == 8
        and row_count % parts == 0
        and 6 * hidden * parts % devices == 0
        and arrays[1].shape[2] == hidden
        and cols % 16 == 0
    )
    return by_channels(*arrays) if fits else by_rows(*arrays)


def solution(mesh):
    in_specs = (
        P("row", "col", None),
        P("row", "col", "ch"),
        P(None, "ch"),
        P(None, "ch"),
        P(None, "ch"),
        P(None, "ch"),
        P(None, "ch"),
        P(None, "ch"),
    )
    out_specs = (
        P("row", "col", "ch"),
        P("row", "col", "ch"),
        P(None, "ch"),
        P(None, "ch"),
        P(None, "ch"),
        P(None, "ch"),
        P(None, "ch"),
        P(None, "ch"),
    )
    return jax.shard_map(
        on_device, mesh=mesh, in_specs=in_specs, out_specs=out_specs, check_vma=False
    )
```

```python
import functools

import jax
import jax.numpy as jnp
import numpy as np
from jax import lax
from jax.experimental import pallas as pl
from jax.experimental.pallas import tpu as pltpu
from jax.sharding import PartitionSpec as P

epsilon = 1e-05


def layer_norm(values):
    average = jnp.mean(values, -1, keepdims=True)
    centred = values - average
    spread = jnp.mean(centred * centred, -1, keepdims=True)
    inverse = lax.rsqrt(spread + epsilon)
    return (centred * inverse, inverse)


def matmul(first, second):
    return jnp.dot(first, second, preferred_element_type=jnp.float32)


def by_rows(pair, cotangent, w_gate_a, w_proj_a, w_gate_b, w_proj_b, w_gate_out, w_out):
    row_count, col_count, channels = pair.shape
    hidden = w_gate_a.shape[1]
    total_hidden = hidden * lax.axis_size("ch")
    out_width = cotangent.shape[2]
    length = row_count * lax.axis_size("row")
    grad_scale = 1.0 / length
    pair_hat, pair_rstd = layer_norm(pair.astype(jnp.float32))
    flat_norm = pair_hat.astype(jnp.bfloat16).reshape(row_count * col_count, channels)
    w_four = jnp.concatenate([w_gate_a, w_proj_a, w_gate_b, w_proj_b], axis=1)
    projected = matmul(flat_norm, w_four)
    gate_a = jax.nn.sigmoid(projected[:, :hidden])
    proj_a = projected[:, hidden : 2 * hidden]
    gate_b = jax.nn.sigmoid(projected[:, 2 * hidden : 3 * hidden])
    proj_b = projected[:, 3 * hidden :]
    left_edge = (gate_a * proj_a).astype(jnp.bfloat16).reshape(row_count, col_count, hidden)
    right_edge = (gate_b * proj_b).astype(jnp.bfloat16).reshape(row_count, col_count, hidden)
    right_all = lax.all_gather(right_edge, "row", axis=0, tiled=True)
    mixed_swap = lax.psum_scatter(
        jnp.einsum("jkh,ikh->jih", right_all, left_edge, preferred_element_type=jnp.float32).astype(
            jnp.bfloat16
        ),
        "col",
        scatter_dimension=0,
        tiled=True,
    ).astype(jnp.float32)
    mixed = jnp.swapaxes(mixed_swap, 0, 1).reshape(row_count * col_count, hidden)
    hidden_sums = lax.psum((jnp.sum(mixed, -1), jnp.sum(mixed * mixed, -1)), "ch")
    hidden_mean = (hidden_sums[0] / total_hidden)[:, None]
    hidden_var = (hidden_sums[1] / total_hidden)[:, None] - hidden_mean * hidden_mean
    hidden_rstd = lax.rsqrt(hidden_var + epsilon)
    mixed_hat = (mixed - hidden_mean) * hidden_rstd
    mixed_norm = mixed_hat.astype(jnp.bfloat16)
    norm_full = lax.all_gather(mixed_norm, "ch", axis=1, tiled=True)
    gate_out = jax.nn.sigmoid(matmul(flat_norm, w_gate_out))
    proj_out = matmul(norm_full, w_out)
    updated = (gate_out * proj_out).astype(jnp.bfloat16).reshape(row_count, col_count, out_width)
    upstream = cotangent.reshape(row_count * col_count, out_width).astype(jnp.float32)
    d_proj = (upstream * gate_out).astype(jnp.bfloat16)
    d_gate = (upstream * proj_out * gate_out * (1.0 - gate_out)).astype(jnp.bfloat16)
    head_grads = lax.psum(
        (matmul(norm_full.T, d_proj) * grad_scale, matmul(flat_norm.T, d_gate) * grad_scale),
        ("row", "col"),
    )
    d_norm = lax.psum_scatter(
        matmul(d_proj, w_out.T).astype(jnp.bfloat16), "ch", scatter_dimension=1, tiled=True
    ).astype(jnp.float32)
    back_sums = lax.psum((jnp.sum(d_norm, -1), jnp.sum(d_norm * mixed_hat, -1)), "ch")
    d_mixed = hidden_rstd * (
        d_norm
        - (back_sums[0] / total_hidden)[:, None]
        - mixed_hat * (back_sums[1] / total_hidden)[:, None]
    )
    d_mixed = d_mixed.astype(jnp.bfloat16).reshape(row_count, col_count, hidden)
    d_rows = lax.all_gather(d_mixed, "col", axis=1, tiled=True)
    right_back = lax.all_gather(right_edge, "row", axis=0, tiled=True)
    d_left = jnp.einsum("ijh,jkh->ikh", d_rows, right_back, preferred_element_type=jnp.float32)
    d_left = d_left.reshape(row_count * col_count, hidden)
    left_all = lax.all_gather(left_edge, "row", axis=0, tiled=True)
    d_columns = lax.all_to_all(d_rows, "row", split_axis=1, concat_axis=0, tiled=True)
    d_right = jnp.einsum("ijh,ikh->jkh", d_columns, left_all, preferred_element_type=jnp.float32)
    d_right = d_right.reshape(row_count * col_count, hidden)
    grad_pa = (d_left * gate_a).astype(jnp.bfloat16)
    grad_ga = (d_left * proj_a * gate_a * (1.0 - gate_a)).astype(jnp.bfloat16)
    grad_pb = (d_right * gate_b).astype(jnp.bfloat16)
    grad_gb = (d_right * proj_b * gate_b * (1.0 - gate_b)).astype(jnp.bfloat16)
    d_four = jnp.concatenate([grad_ga, grad_pa, grad_gb, grad_pb], axis=1)
    weight_terms = matmul(flat_norm.T, d_four) * grad_scale
    summed = lax.psum(weight_terms, ("row", "col"))
    d_flat = matmul(d_four, w_four.T) + matmul(d_gate, w_gate_out.T)
    hat_all = pair_hat.reshape(row_count * col_count, channels)
    rstd_flat = pair_rstd.reshape(row_count * col_count, 1)
    offset = lax.axis_index("ch") * out_width
    grad_whole = lax.psum(d_flat.astype(jnp.bfloat16), "ch").astype(jnp.float32)
    grad_full = rstd_flat * (
        grad_whole
        - jnp.mean(grad_whole, -1, keepdims=True)
        - hat_all * jnp.mean(grad_whole * hat_all, -1, keepdims=True)
    )
    grad_pair = lax.dynamic_slice_in_dim(grad_full, offset, out_width, 1)
    grad_pair = grad_pair.astype(jnp.bfloat16).reshape(row_count, col_count, out_width)
    return (
        updated,
        grad_pair,
        summed[:, :hidden],
        summed[:, hidden : 2 * hidden],
        summed[:, 2 * hidden : 3 * hidden],
        summed[:, 3 * hidden :],
        head_grads[1],
        head_grads[0],
    )


everyone = ("col", "row", "ch")
f32, bf16 = jnp.float32, jnp.bfloat16


def dot(first, second, over):
    return lax.dot_general(
        first, second, (((over[0],), (over[1],)), ((), ())), preferred_element_type=f32
    )


def call(kernel, outs, args, scratch=(), far=(), outs_far=False, room=16):
    whole = pl.BlockSpec(memory_space=pltpu.VMEM)
    anywhere = pl.BlockSpec(memory_space=pl.ANY)
    return pl.pallas_call(
        kernel,
        out_shape=tuple(jax.ShapeDtypeStruct(*out) for out in outs),
        in_specs=[anywhere if at in far else whole for at in range(len(args))],
        out_specs=tuple(anywhere if outs_far else whole for _ in outs),
        scratch_shapes=scratch,
        compiler_params=pltpu.CompilerParams(vmem_limit_bytes=room * 2**20),
    )(*args)


def grouping(hidden, share):
    shape = (2 * hidden, 2 * hidden)
    rows = lax.broadcasted_iota(jnp.int32, shape, 0)
    columns = lax.broadcasted_iota(jnp.int32, shape, 1)
    group, within = rows // (2 * share), lax.rem(rows, 2 * share)
    side = within // share
    wanted = side * hidden + group * share + within - side * share
    return jnp.where(columns == wanted, 1.0, 0.0).astype(bf16)


def start_all(copies):
    for copy in copies:
        copy.start()


def wait_all(copies):
    for copy in copies:
        copy.wait()


def turn_weights(share, ga, pa, gb, pb, go, wo, out, gates, values, last, arrivals):
    hidden = go.shape[0]
    width = 2 * hidden
    copies = []
    for at, (held, low, high) in enumerate(((gates, ga, gb), (values, pa, pb), (last, go, wo))):
        copies.append(pltpu.make_async_copy(low, held.at[0:hidden], arrivals.at[2 * at]))
        copies.append(pltpu.make_async_copy(high, held.at[hidden:width], arrivals.at[2 * at + 1]))
    start_all(copies)
    order = grouping(hidden, share)
    wait_all(copies)
    out[:width] = dot(order, gates[...], (1, 0)).astype(bf16)
    out[width : 2 * width] = dot(order, values[...], (1, 0)).astype(bf16)
    out[2 * width :] = last[...]


def normalize(pair_far, normed, pair, arrival):
    count = pair.shape[0]
    rows = pl.ds(lax.axis_index("ch") * count, count)
    copy = pltpu.make_async_copy(pair_far.at[rows], pair, arrival)
    copy.start()
    copy.wait()
    normed[...] = normalized(pair[...])[0].astype(bf16)


def order_weights(own, other, weights):
    core = lax.axis_index("ch")
    weights[core] = own[...]
    weights[1 - core] = other[...]


def rows_of(weights, start, count):
    return jnp.concatenate([weights[c, start : start + count] for c in range(weights.shape[0])], 0)


def normalized(pair):
    count, cols, channels = pair.shape
    values = pair.astype(f32).reshape(count * cols, channels).T
    centred = values - jnp.mean(values, 0, keepdims=True)
    rstd = lax.rsqrt(jnp.mean(centred * centred, 0, keepdims=True) + epsilon)
    return centred * rstd, rstd


def edges(width, normed, own_weights, other_weights, send, weights):
    order_weights(own_weights, other_weights, weights)
    gate = jax.nn.sigmoid(dot(rows_of(weights, 0, width), normed[...], (1, 0)))
    value = dot(rows_of(weights, width, width), normed[...], (1, 0))
    send[...] = (gate * value).reshape(send.shape).astype(bf16)


def spread_rows(block, cols, arrived, held):
    devices, q, flat = arrived.shape
    rows = flat // cols
    for s in range(devices):
        tile = arrived[s].astype(f32)
        for i in range(rows):
            start = (s * rows + i) * block
            held[start : start + q, 0:cols] = tile[:, i * cols : (i + 1) * cols]


def pack_rows(block, cols, held, send):
    devices, q, flat = send.shape
    rows = flat // cols
    for s in range(devices):
        starts = [(s * rows + i) * block for i in range(rows)]
        whole = jnp.concatenate([held[start : start + block, 0:cols] for start in starts], axis=1)
        send[s] = whole[:q].astype(bf16)


def square(block, parts, cols, held, e):
    tokens = parts * cols
    return jnp.concatenate(
        [
            held[pl.ds(p * tokens * block + e, tokens, stride=block), 0:cols]
            for p in range(parts)
        ],
        axis=1,
    ).astype(bf16)


def put_square(block, parts, cols, held, e, values):
    tokens = parts * cols
    for p in range(parts):
        held[pl.ds(p * tokens * block + e, tokens, stride=block), 0:cols] = values[
            :, p * cols : (p + 1) * cols
        ]


def mix(parts, cols, arrived, send, kept, held, result):
    block = 8
    q = arrived.shape[1]
    spread_rows(block, cols, arrived, held)
    for e in range(q // 2):
        left = square(block, parts, cols, held, e)
        right = square(block, parts, cols, held, q // 2 + e)
        kept[e] = left
        kept[q // 2 + e] = right
        put_square(block, parts, cols, result, e, dot(left, right, (1, 1)))
    pack_rows(block, cols, result, send)


def unmix(parts, cols, arrived, kept_far, send, held, result, kept, arrival):
    block = 8
    q = arrived.shape[1]
    copy = pltpu.make_async_copy(kept_far, kept, arrival)
    copy.start()
    spread_rows(block, cols, arrived, held)
    copy.wait()
    for e in range(q):
        d_mixed = square(block, parts, cols, held, e)
        put_square(block, parts, cols, result, e, dot(d_mixed, kept[q + e], (1, 0)))
        put_square(block, parts, cols, result, q + e, dot(d_mixed, kept[e], (0, 0)))
    pack_rows(block, cols, result, send)


def split_rows(cols, values, own, other):
    hidden = values.shape[0] // 2
    first = lax.axis_index("ch") == 0
    low, high = values[:hidden], values[hidden:]
    mine = jnp.where(first, low, high)
    yours = jnp.where(first, high, low)
    for i in range(own.shape[0]):
        own[i] = mine[:, i * cols : (i + 1) * cols].astype(bf16)
        other[i] = yours[:, i * cols : (i + 1) * cols].astype(bf16)


def head(
    width, scale, arrived, own_weights, other_weights, normed_far, own_far, other_far,
    send, d_gate, terms, updated_own, updated_other,
    normed, own, other, upstream, weights, arrivals,
):
    parts, total, _ = weights.shape
    hidden = (total - 2 * width) // 2
    devices, q, flat = arrived.shape
    count, _, cols = other.shape
    core = lax.axis_index("ch")
    copies = [
        pltpu.make_async_copy(normed_far, normed, arrivals.at[0]),
        pltpu.make_async_copy(own_far.at[pl.ds(core * count, count)], own, arrivals.at[1]),
        pltpu.make_async_copy(other_far, other, arrivals.at[2]),
    ]
    start_all(copies)
    order_weights(own_weights, other_weights, weights)
    mixed = jnp.concatenate([arrived[s].astype(f32) for s in range(devices)], 0)
    average = jnp.mean(mixed, 0, keepdims=True)
    spread = jnp.mean(mixed * mixed, 0, keepdims=True) - average * average
    inverse = lax.rsqrt(spread + epsilon)
    hat = (mixed - average) * inverse
    hat_rounded = hat.astype(bf16)
    w_out = rows_of(weights, 2 * width + hidden, hidden)
    proj = dot(w_out, hat_rounded, (1, 0))
    wait_all(copies)
    for part, side in ((own, core), (other, 1 - core)):
        upstream[pl.ds(pl.multiple_of(side * hidden, hidden), hidden)] = jnp.concatenate(
            [part[i].astype(f32) for i in range(count)], axis=1
        )
    gate = jax.nn.sigmoid(dot(rows_of(weights, 2 * width, hidden), normed[...], (1, 0)))
    up = upstream[...]
    d_proj = (up * gate).astype(bf16)
    d_gate[...] = (up * proj * gate * (1.0 - gate)).astype(bf16)
    d_norm = dot(w_out, d_proj, (0, 0))
    d_mixed = inverse * (
        d_norm
        - jnp.mean(d_norm, 0, keepdims=True)
        - hat * jnp.mean(d_norm * hat, 0, keepdims=True)
    )
    for s in range(devices):
        send[s] = d_mixed[s * q : (s + 1) * q].astype(bf16)
    by_gate = dot(d_gate[...], normed[...], (1, 1)) * scale
    by_out = dot(d_proj, hat_rounded, (1, 1)) * scale
    for c in range(parts):
        terms[c, :hidden] = by_gate[c * hidden : (c + 1) * hidden]
        terms[c, hidden:] = by_out[c * hidden : (c + 1) * hidden]
    split_rows(cols, gate * proj, updated_own, updated_other)


def tail(
    width, scale, arrived, own_weights, other_weights, pair_far, d_gate_far, head_terms, updated_other,
    send, grad_own, others,
    pair, d_gate, whole, weights, arrivals,
):
    parts, total, channels = weights.shape
    hidden = (total - 2 * width) // 2
    devices, q, flat = arrived.shape
    count, cols, _ = pair.shape
    core = lax.axis_index("ch")
    copies = [
        pltpu.make_async_copy(pair_far.at[pl.ds(core * count, count)], pair, arrivals.at[0]),
        pltpu.make_async_copy(d_gate_far, d_gate, arrivals.at[1]),
    ]
    start_all(copies)
    order_weights(own_weights, other_weights, weights)
    others[0] = updated_other[...]
    wait_all(copies)
    hat, inverse = normalized(pair[...])
    normed = hat.astype(bf16)
    w_gate, w_value = rows_of(weights, 0, width), rows_of(weights, width, width)
    gate = jax.nn.sigmoid(dot(w_gate, normed, (1, 0)))
    value = dot(w_value, normed, (1, 0))
    grad = arrived[...].astype(f32).reshape(devices * q, flat)
    by_value = grad * gate
    by_gate = (by_value * (value * (1.0 - gate))).astype(bf16)
    by_value = by_value.astype(bf16)
    terms = [dot(by_gate, normed, (1, 1)) * scale, dot(by_value, normed, (1, 1)) * scale]
    for c in range(parts):
        for at, term in enumerate(terms):
            start = c * total + at * width
            whole[start : start + width] = term[c * width : (c + 1) * width]
        whole[c * total + 2 * width : (c + 1) * total] = head_terms[c]
    per = send.shape[1]
    for s in range(devices):
        send[s] = whole[s * per : (s + 1) * per].astype(bf16)
    d_input = dot(w_gate, by_gate, (0, 0)) + dot(w_value, by_value, (0, 0))
    d_input = d_input + dot(rows_of(weights, 2 * width, hidden), d_gate[...], (0, 0))
    back = inverse * (
        d_input
        - jnp.mean(d_input, 0, keepdims=True)
        - hat * jnp.mean(d_input * hat, 0, keepdims=True)
    )
    split_rows(cols, back, grad_own, others.at[1])


def add_up(arrived, out):
    total = jnp.sum(arrived[...].astype(f32), 0).astype(bf16)
    for s in range(out.shape[0]):
        out[s] = total


def turn_back(share, sums, *refs):
    outs, whole, results, leaves = refs[:6], refs[6], refs[7], refs[8]
    _, hidden, channels = results.shape
    width = 2 * hidden
    per = sums.shape[1]
    for s in range(sums.shape[0]):
        whole[s * per : (s + 1) * per] = sums[s].astype(f32)
    order = grouping(hidden, share)
    for at in range(2):
        both = dot(order, whole[at * width : (at + 1) * width].astype(bf16), (0, 0))
        results[at] = both[:hidden]
        results[2 + at] = both[hidden:]
    results[4] = whole[2 * width : 2 * width + hidden]
    results[5] = whole[2 * width + hidden :]
    copies = [
        pltpu.make_async_copy(results.at[at], out, leaves.at[at]) for at, out in enumerate(outs)
    ]
    start_all(copies)
    wait_all(copies)


def join_rows(updated_own, grad_own, others, updated, grad, leaves):
    count = updated_own.shape[0]
    core = lax.axis_index("ch")
    here, there = pl.ds(core * count, count), pl.ds((1 - core) * count, count)
    copies = []
    for at, (own, out) in enumerate(((updated_own, updated), (grad_own, grad))):
        copies.append(pltpu.make_async_copy(own, out.at[here], leaves.at[2 * at]))
        copies.append(pltpu.make_async_copy(others.at[at], out.at[there], leaves.at[2 * at + 1]))
    start_all(copies)
    wait_all(copies)


def by_channels(pair, cotangent, w_gate_a, w_proj_a, w_gate_b, w_proj_b, w_gate_out, w_out):
    row_count, cols, channels = pair.shape
    hidden = w_gate_a.shape[1]
    parts, col_parts, row_parts = lax.axis_size("ch"), lax.axis_size("col"), lax.axis_size("row")
    devices = parts * col_parts * row_parts
    share = hidden * parts // devices
    width = 2 * hidden
    count = row_count // parts
    flat = count * cols
    tokens = cols * col_parts
    scale = 1.0 / tokens
    swap = [(c, parts - 1 - c) for c in range(parts)]
    whole_weight = pltpu.VMEM((2 * hidden, channels), bf16)
    weight = ((2 * width + 2 * hidden, channels), bf16)
    own = jnp.swapaxes(cotangent, 1, 2)
    other = lax.dynamic_slice_in_dim(own, (1 - lax.axis_index("ch")) * count, count, 0)
    other = lax.ppermute(other, "ch", swap)
    (weights,) = call(
        functools.partial(turn_weights, share),
        [weight],
        (w_gate_a.T, w_proj_a.T, w_gate_b.T, w_proj_b.T, w_gate_out.T, w_out.T),
        (whole_weight, whole_weight, whole_weight, pltpu.SemaphoreType.DMA((6,))),
        far=range(6),
        room=60,
    )
    weights = (weights, lax.ppermute(weights, "ch", swap))
    (normed,) = call(
        normalize,
        [((channels, flat), bf16)],
        (pair,),
        (pltpu.VMEM((count, cols, channels), bf16), pltpu.SemaphoreType.DMA),
        far=(0,),
        room=60,
    )
    normed, other = lax.optimization_barrier((normed, other))
    (send,) = call(
        functools.partial(edges, width), [((devices, 2 * share, flat), bf16)], (normed, *weights),
        (pltpu.VMEM((parts, *weight[0]), bf16),),
    )
    arrived = lax.all_to_all(send, everyone, 0, 0)
    room = pltpu.VMEM((col_parts * tokens * 8, -(-cols // 128) * 128), f32)
    send, kept = call(
        functools.partial(mix, col_parts, cols),
        [((devices, share, flat), bf16), ((2 * share, tokens, tokens), bf16)],
        (arrived,),
        (room, room),
    )
    arrived = lax.all_to_all(send, everyone, 0, 0)
    part = ((count, hidden, cols), bf16)
    send, d_gate, head_terms, updated_own, updated_other = call(
        functools.partial(head, width, scale),
        [
            ((devices, share, flat), bf16),
            ((hidden * parts, flat), bf16),
            ((parts, 2 * hidden, channels), f32),
            part,
            part,
        ],
        (arrived, *weights, normed, own, other),
        (
            pltpu.VMEM((channels, flat), bf16),
            pltpu.VMEM(*part),
            pltpu.VMEM(*part),
            pltpu.VMEM((hidden * parts, flat), f32),
            pltpu.VMEM((parts, *weight[0]), bf16),
            pltpu.SemaphoreType.DMA((3,)),
        ),
        far=(3, 4, 5),
    )
    arrived = lax.all_to_all(send, everyone, 0, 0)
    (send,) = call(
        functools.partial(unmix, col_parts, cols),
        [((devices, 2 * share, flat), bf16)],
        (arrived, kept),
        (room, room, pltpu.VMEM(kept.shape, bf16), pltpu.SemaphoreType.DMA),
        far=(1,),
    )
    arrived = lax.all_to_all(send, everyone, 0, 0)
    total = 2 * width + 2 * hidden
    per = total * parts // devices
    send, grad_own, others = call(
        functools.partial(tail, width, scale),
        [((devices, per, channels), bf16), part, ((2, *part[0]), bf16)],
        (arrived, *weights, pair, d_gate, head_terms, updated_other),
        (
            pltpu.VMEM((count, cols, channels), bf16),
            pltpu.VMEM((hidden * parts, flat), bf16),
            pltpu.VMEM((total * parts, channels), f32),
            pltpu.VMEM((parts, *weight[0]), bf16),
            pltpu.SemaphoreType.DMA((2,)),
        ),
        far=(3, 4),
    )
    arrived = lax.all_to_all(send, ("ch", "row", "col"), 0, 0)
    rest = devices // parts
    (sums,) = call(add_up, [((rest, per, channels), bf16)], (arrived,))
    sums, others = lax.optimization_barrier((sums, others))
    sums = lax.all_to_all(sums, ("row", "col"), 0, 0)
    updated, grad_pair = call(
        join_rows,
        [((row_count, hidden, cols), bf16)] * 2,
        (updated_own, grad_own, lax.ppermute(others, "ch", swap)),
        (pltpu.SemaphoreType.DMA((4,)),),
        (0, 1, 2),
        True,
    )
    sums, updated, grad_pair = lax.optimization_barrier((sums, updated, grad_pair))
    grads = call(
        functools.partial(turn_back, share),
        [((hidden, channels), f32)] * 6,
        (sums,),
        (
            pltpu.VMEM((total, channels), f32),
            pltpu.VMEM((6, hidden, channels), f32),
            pltpu.SemaphoreType.DMA((6,)),
        ),
        outs_far=True,
    )
    return jnp.swapaxes(updated, 1, 2), jnp.swapaxes(grad_pair, 1, 2), *(g.T for g in grads)


def on_device(*arrays):
    row_count, cols, _ = arrays[0].shape
    parts, devices = lax.axis_size("ch"), lax.axis_size(everyone)
    hidden = arrays[2].shape[1]
    share = hidden * parts // devices
    fits = (
        share * devices == hidden * parts
        and parts == 2
        and 2 * share == 8
        and row_count % parts == 0
        and 6 * hidden * parts % devices == 0
        and arrays[1].shape[2] == hidden
        and cols % 16 == 0
    )
    return by_channels(*arrays) if fits else by_rows(*arrays)


def solution(mesh):
    in_specs = (
        P("row", "col", None),
        P("row", "col", "ch"),
        P(None, "ch"),
        P(None, "ch"),
        P(None, "ch"),
        P(None, "ch"),
        P(None, "ch"),
        P(None, "ch"),
    )
    out_specs = (
        P("row", "col", "ch"),
        P("row", "col", "ch"),
        P(None, "ch"),
        P(None, "ch"),
        P(None, "ch"),
        P(None, "ch"),
        P(None, "ch"),
        P(None, "ch"),
    )
    return jax.shard_map(
        on_device, mesh=mesh, in_specs=in_specs, out_specs=out_specs, check_vma=False
    )
```

```python
import functools

import jax
import jax.numpy as jnp
import numpy as np
from jax import lax
from jax.experimental import pallas as pl
from jax.experimental.pallas import tpu as pltpu
from jax.sharding import PartitionSpec as P

epsilon = 1e-05


def layer_norm(values):
    average = jnp.mean(values, -1, keepdims=True)
    centred = values - average
    spread = jnp.mean(centred * centred, -1, keepdims=True)
    inverse = lax.rsqrt(spread + epsilon)
    return (centred * inverse, inverse)


def matmul(first, second):
    return jnp.dot(first, second, preferred_element_type=jnp.float32)


def by_rows(pair, cotangent, w_gate_a, w_proj_a, w_gate_b, w_proj_b, w_gate_out, w_out):
    row_count, col_count, channels = pair.shape
    hidden = w_gate_a.shape[1]
    total_hidden = hidden * lax.axis_size("ch")
    out_width = cotangent.shape[2]
    length = row_count * lax.axis_size("row")
    grad_scale = 1.0 / length
    pair_hat, pair_rstd = layer_norm(pair.astype(jnp.float32))
    flat_norm = pair_hat.astype(jnp.bfloat16).reshape(row_count * col_count, channels)
    w_four = jnp.concatenate([w_gate_a, w_proj_a, w_gate_b, w_proj_b], axis=1)
    projected = matmul(flat_norm, w_four)
    gate_a = jax.nn.sigmoid(projected[:, :hidden])
    proj_a = projected[:, hidden : 2 * hidden]
    gate_b = jax.nn.sigmoid(projected[:, 2 * hidden : 3 * hidden])
    proj_b = projected[:, 3 * hidden :]
    left_edge = (gate_a * proj_a).astype(jnp.bfloat16).reshape(row_count, col_count, hidden)
    right_edge = (gate_b * proj_b).astype(jnp.bfloat16).reshape(row_count, col_count, hidden)
    right_all = lax.all_gather(right_edge, "row", axis=0, tiled=True)
    mixed_swap = lax.psum_scatter(
        jnp.einsum("jkh,ikh->jih", right_all, left_edge, preferred_element_type=jnp.float32).astype(
            jnp.bfloat16
        ),
        "col",
        scatter_dimension=0,
        tiled=True,
    ).astype(jnp.float32)
    mixed = jnp.swapaxes(mixed_swap, 0, 1).reshape(row_count * col_count, hidden)
    hidden_sums = lax.psum((jnp.sum(mixed, -1), jnp.sum(mixed * mixed, -1)), "ch")
    hidden_mean = (hidden_sums[0] / total_hidden)[:, None]
    hidden_var = (hidden_sums[1] / total_hidden)[:, None] - hidden_mean * hidden_mean
    hidden_rstd = lax.rsqrt(hidden_var + epsilon)
    mixed_hat = (mixed - hidden_mean) * hidden_rstd
    mixed_norm = mixed_hat.astype(jnp.bfloat16)
    norm_full = lax.all_gather(mixed_norm, "ch", axis=1, tiled=True)
    gate_out = jax.nn.sigmoid(matmul(flat_norm, w_gate_out))
    proj_out = matmul(norm_full, w_out)
    updated = (gate_out * proj_out).astype(jnp.bfloat16).reshape(row_count, col_count, out_width)
    upstream = cotangent.reshape(row_count * col_count, out_width).astype(jnp.float32)
    d_proj = (upstream * gate_out).astype(jnp.bfloat16)
    d_gate = (upstream * proj_out * gate_out * (1.0 - gate_out)).astype(jnp.bfloat16)
    head_grads = lax.psum(
        (matmul(norm_full.T, d_proj) * grad_scale, matmul(flat_norm.T, d_gate) * grad_scale),
        ("row", "col"),
    )
    d_norm = lax.psum_scatter(
        matmul(d_proj, w_out.T).astype(jnp.bfloat16), "ch", scatter_dimension=1, tiled=True
    ).astype(jnp.float32)
    back_sums = lax.psum((jnp.sum(d_norm, -1), jnp.sum(d_norm * mixed_hat, -1)), "ch")
    d_mixed = hidden_rstd * (
        d_norm
        - (back_sums[0] / total_hidden)[:, None]
        - mixed_hat * (back_sums[1] / total_hidden)[:, None]
    )
    d_mixed = d_mixed.astype(jnp.bfloat16).reshape(row_count, col_count, hidden)
    d_rows = lax.all_gather(d_mixed, "col", axis=1, tiled=True)
    right_back = lax.all_gather(right_edge, "row", axis=0, tiled=True)
    d_left = jnp.einsum("ijh,jkh->ikh", d_rows, right_back, preferred_element_type=jnp.float32)
    d_left = d_left.reshape(row_count * col_count, hidden)
    left_all = lax.all_gather(left_edge, "row", axis=0, tiled=True)
    d_columns = lax.all_to_all(d_rows, "row", split_axis=1, concat_axis=0, tiled=True)
    d_right = jnp.einsum("ijh,ikh->jkh", d_columns, left_all, preferred_element_type=jnp.float32)
    d_right = d_right.reshape(row_count * col_count, hidden)
    grad_pa = (d_left * gate_a).astype(jnp.bfloat16)
    grad_ga = (d_left * proj_a * gate_a * (1.0 - gate_a)).astype(jnp.bfloat16)
    grad_pb = (d_right * gate_b).astype(jnp.bfloat16)
    grad_gb = (d_right * proj_b * gate_b * (1.0 - gate_b)).astype(jnp.bfloat16)
    d_four = jnp.concatenate([grad_ga, grad_pa, grad_gb, grad_pb], axis=1)
    weight_terms = matmul(flat_norm.T, d_four) * grad_scale
    summed = lax.psum(weight_terms, ("row", "col"))
    d_flat = matmul(d_four, w_four.T) + matmul(d_gate, w_gate_out.T)
    hat_all = pair_hat.reshape(row_count * col_count, channels)
    rstd_flat = pair_rstd.reshape(row_count * col_count, 1)
    offset = lax.axis_index("ch") * out_width
    grad_whole = lax.psum(d_flat.astype(jnp.bfloat16), "ch").astype(jnp.float32)
    grad_full = rstd_flat * (
        grad_whole
        - jnp.mean(grad_whole, -1, keepdims=True)
        - hat_all * jnp.mean(grad_whole * hat_all, -1, keepdims=True)
    )
    grad_pair = lax.dynamic_slice_in_dim(grad_full, offset, out_width, 1)
    grad_pair = grad_pair.astype(jnp.bfloat16).reshape(row_count, col_count, out_width)
    return (
        updated,
        grad_pair,
        summed[:, :hidden],
        summed[:, hidden : 2 * hidden],
        summed[:, 2 * hidden : 3 * hidden],
        summed[:, 3 * hidden :],
        head_grads[1],
        head_grads[0],
    )


everyone = ("col", "row", "ch")
f32, bf16 = jnp.float32, jnp.bfloat16


def dot(first, second, over):
    return lax.dot_general(
        first, second, (((over[0],), (over[1],)), ((), ())), preferred_element_type=f32
    )


def call(kernel, outs, args, scratch=(), far=(), outs_far=False, room=16):
    whole = pl.BlockSpec(memory_space=pltpu.VMEM)
    anywhere = pl.BlockSpec(memory_space=pl.ANY)
    return pl.pallas_call(
        kernel,
        out_shape=tuple(jax.ShapeDtypeStruct(*out) for out in outs),
        in_specs=[anywhere if at in far else whole for at in range(len(args))],
        out_specs=tuple(anywhere if outs_far else whole for _ in outs),
        scratch_shapes=scratch,
        compiler_params=pltpu.CompilerParams(vmem_limit_bytes=room * 2**20),
    )(*args)


def grouping(hidden, share):
    shape = (2 * hidden, 2 * hidden)
    rows = lax.broadcasted_iota(jnp.int32, shape, 0)
    columns = lax.broadcasted_iota(jnp.int32, shape, 1)
    group, within = rows // (2 * share), lax.rem(rows, 2 * share)
    side = within // share
    wanted = side * hidden + group * share + within - side * share
    return jnp.where(columns == wanted, 1.0, 0.0).astype(bf16)


def start_all(copies):
    for copy in copies:
        copy.start()


def wait_all(copies):
    for copy in copies:
        copy.wait()


def normalize(pair_far, cotangent_far, normed, other, pair, arrivals):
    count = pair.shape[0]
    core = lax.axis_index("ch")
    fetch = pltpu.make_async_copy(pair_far.at[pl.ds(core * count, count)], pair, arrivals.at[0])
    cut = pltpu.make_async_copy(
        cotangent_far.at[pl.ds((1 - core) * count, count)], other, arrivals.at[1]
    )
    start_all([fetch, cut])
    fetch.wait()
    normed[...] = normalized(pair[...])[0].astype(bf16)
    cut.wait()


def stack_up(*refs):
    parts, out, arrivals = refs[:-2], refs[-2], refs[-1]
    rows = parts[0].shape[0]
    copies = [
        pltpu.make_async_copy(part, out.at[at * rows : (at + 1) * rows], arrivals.at[at])
        for at, part in enumerate(parts)
    ]
    start_all(copies)
    wait_all(copies)


def group_weights(share, stack, weights):
    hidden = stack.shape[0] // 6
    width = 2 * hidden
    ga, pa, gb, pb = [stack[at * hidden : (at + 1) * hidden] for at in range(4)]
    order = grouping(hidden, share)
    weights[:width] = dot(order, jnp.concatenate([ga, gb], 0), (1, 0)).astype(bf16)
    weights[width : 2 * width] = dot(order, jnp.concatenate([pa, pb], 0), (1, 0)).astype(bf16)
    weights[2 * width :] = stack[4 * hidden :]


def rows_of(weights, start, count):
    return jnp.concatenate([weights[c, start : start + count] for c in range(weights.shape[0])], 0)


def normalized(pair):
    count, cols, channels = pair.shape
    values = pair.astype(f32).reshape(count * cols, channels).T
    centred = values - jnp.mean(values, 0, keepdims=True)
    rstd = lax.rsqrt(jnp.mean(centred * centred, 0, keepdims=True) + epsilon)
    return centred * rstd, rstd


def edges(width, share, normed, own_stack, other_stack, send, weights):
    core = lax.axis_index("ch")
    group_weights(share, own_stack, weights.at[core])
    group_weights(share, other_stack, weights.at[1 - core])
    gate = jax.nn.sigmoid(dot(rows_of(weights, 0, width), normed[...], (1, 0)))
    value = dot(rows_of(weights, width, width), normed[...], (1, 0))
    send[...] = (gate * value).reshape(send.shape).astype(bf16)


def spread_rows(block, cols, arrived, held):
    devices, q, flat = arrived.shape
    rows = flat // cols
    for s in range(devices):
        tile = arrived[s].astype(f32)
        for i in range(rows):
            start = (s * rows + i) * block
            held[start : start + q, 0:cols] = tile[:, i * cols : (i + 1) * cols]


def pack_rows(block, cols, held, send):
    devices, q, flat = send.shape
    rows = flat // cols
    for s in range(devices):
        starts = [(s * rows + i) * block for i in range(rows)]
        whole = jnp.concatenate([held[start : start + block, 0:cols] for start in starts], axis=1)
        send[s] = whole[:q].astype(bf16)


def square(block, parts, cols, held, e):
    tokens = parts * cols
    return jnp.concatenate(
        [
            held[pl.ds(p * tokens * block + e, tokens, stride=block), 0:cols]
            for p in range(parts)
        ],
        axis=1,
    ).astype(bf16)


def put_square(block, parts, cols, held, e, values):
    tokens = parts * cols
    for p in range(parts):
        held[pl.ds(p * tokens * block + e, tokens, stride=block), 0:cols] = values[
            :, p * cols : (p + 1) * cols
        ]


def mix(parts, cols, arrived, send, kept, held, result):
    block = 8
    q = arrived.shape[1]
    spread_rows(block, cols, arrived, held)
    for e in range(q // 2):
        left = square(block, parts, cols, held, e)
        right = square(block, parts, cols, held, q // 2 + e)
        kept[e] = left
        kept[q // 2 + e] = right
        put_square(block, parts, cols, result, e, dot(left, right, (1, 1)))
    pack_rows(block, cols, result, send)


def unmix(parts, cols, arrived, kept_far, send, held, result, kept, arrival):
    block = 8
    q = arrived.shape[1]
    copy = pltpu.make_async_copy(kept_far, kept, arrival)
    copy.start()
    spread_rows(block, cols, arrived, held)
    copy.wait()
    for e in range(q):
        d_mixed = square(block, parts, cols, held, e)
        put_square(block, parts, cols, result, e, dot(d_mixed, kept[q + e], (1, 0)))
        put_square(block, parts, cols, result, q + e, dot(d_mixed, kept[e], (0, 0)))
    pack_rows(block, cols, result, send)


def split_rows(cols, values, own, other):
    hidden = values.shape[0] // 2
    first = lax.axis_index("ch") == 0
    low, high = values[:hidden], values[hidden:]
    mine = jnp.where(first, low, high)
    yours = jnp.where(first, high, low)
    for i in range(own.shape[0]):
        own[i] = mine[:, i * cols : (i + 1) * cols].astype(bf16)
        other[i] = yours[:, i * cols : (i + 1) * cols].astype(bf16)


def head(
    width, scale, arrived, weights, normed_far, own_far, other_far,
    send, d_gate, terms, updated_own, updated_other,
    normed, own, other, upstream, arrivals,
):
    parts, total, _ = weights.shape
    hidden = (total - 2 * width) // 2
    devices, q, flat = arrived.shape
    count, _, cols = other.shape
    core = lax.axis_index("ch")
    copies = [
        pltpu.make_async_copy(normed_far, normed, arrivals.at[0]),
        pltpu.make_async_copy(own_far.at[pl.ds(core * count, count)], own, arrivals.at[1]),
        pltpu.make_async_copy(other_far, other, arrivals.at[2]),
    ]
    start_all(copies)
    mixed = jnp.concatenate([arrived[s].astype(f32) for s in range(devices)], 0)
    average = jnp.mean(mixed, 0, keepdims=True)
    spread = jnp.mean(mixed * mixed, 0, keepdims=True) - average * average
    inverse = lax.rsqrt(spread + epsilon)
    hat = (mixed - average) * inverse
    hat_rounded = hat.astype(bf16)
    w_out = rows_of(weights, 2 * width + hidden, hidden)
    proj = dot(w_out, hat_rounded, (1, 0))
    wait_all(copies)
    for part, side in ((own, core), (other, 1 - core)):
        upstream[pl.ds(pl.multiple_of(side * hidden, hidden), hidden)] = jnp.concatenate(
            [part[i].astype(f32) for i in range(count)], axis=1
        )
    gate = jax.nn.sigmoid(dot(rows_of(weights, 2 * width, hidden), normed[...], (1, 0)))
    up = upstream[...]
    d_proj = (up * gate).astype(bf16)
    d_gate[...] = (up * proj * gate * (1.0 - gate)).astype(bf16)
    d_norm = dot(w_out, d_proj, (0, 0))
    d_mixed = inverse * (
        d_norm
        - jnp.mean(d_norm, 0, keepdims=True)
        - hat * jnp.mean(d_norm * hat, 0, keepdims=True)
    )
    for s in range(devices):
        send[s] = d_mixed[s * q : (s + 1) * q].astype(bf16)
    by_gate = dot(d_gate[...], normed[...], (1, 1)) * scale
    by_out = dot(d_proj, hat_rounded, (1, 1)) * scale
    for c in range(parts):
        terms[c, :hidden] = by_gate[c * hidden : (c + 1) * hidden]
        terms[c, hidden:] = by_out[c * hidden : (c + 1) * hidden]
    split_rows(cols, gate * proj, updated_own, updated_other)


def tail(
    width, scale, arrived, weights, pair_far, d_gate_far, head_terms, updated_other,
    send, grad_own, others,
    pair, d_gate, whole, arrivals,
):
    parts, total, channels = weights.shape
    hidden = (total - 2 * width) // 2
    devices, q, flat = arrived.shape
    count, cols, _ = pair.shape
    core = lax.axis_index("ch")
    copies = [
        pltpu.make_async_copy(pair_far.at[pl.ds(core * count, count)], pair, arrivals.at[0]),
        pltpu.make_async_copy(d_gate_far, d_gate, arrivals.at[1]),
    ]
    start_all(copies)
    others[0] = updated_other[...]
    wait_all(copies)
    hat, inverse = normalized(pair[...])
    normed = hat.astype(bf16)
    w_gate, w_value = rows_of(weights, 0, width), rows_of(weights, width, width)
    gate = jax.nn.sigmoid(dot(w_gate, normed, (1, 0)))
    value = dot(w_value, normed, (1, 0))
    grad = arrived[...].astype(f32).reshape(devices * q, flat)
    by_value = grad * gate
    by_gate = (by_value * (value * (1.0 - gate))).astype(bf16)
    by_value = by_value.astype(bf16)
    terms = [dot(by_gate, normed, (1, 1)) * scale, dot(by_value, normed, (1, 1)) * scale]
    for c in range(parts):
        for at, term in enumerate(terms):
            start = c * total + at * width
            whole[start : start + width] = term[c * width : (c + 1) * width]
        whole[c * total + 2 * width : (c + 1) * total] = head_terms[c]
    per = send.shape[1]
    for s in range(devices):
        send[s] = whole[s * per : (s + 1) * per].astype(bf16)
    d_input = dot(w_gate, by_gate, (0, 0)) + dot(w_value, by_value, (0, 0))
    d_input = d_input + dot(rows_of(weights, 2 * width, hidden), d_gate[...], (0, 0))
    back = inverse * (
        d_input
        - jnp.mean(d_input, 0, keepdims=True)
        - hat * jnp.mean(d_input * hat, 0, keepdims=True)
    )
    split_rows(cols, back, grad_own, others.at[1])


def add_up(arrived, out):
    total = jnp.sum(arrived[...].astype(f32), 0).astype(bf16)
    for s in range(out.shape[0]):
        out[s] = total


def turn_back(share, sums, *refs):
    outs, whole, results, leaves = refs[:6], refs[6], refs[7], refs[8]
    _, hidden, channels = results.shape
    width = 2 * hidden
    per = sums.shape[1]
    for s in range(sums.shape[0]):
        whole[s * per : (s + 1) * per] = sums[s].astype(f32)
    order = grouping(hidden, share)
    for at in range(2):
        both = dot(order, whole[at * width : (at + 1) * width].astype(bf16), (0, 0))
        results[at] = both[:hidden]
        results[2 + at] = both[hidden:]
    results[4] = whole[2 * width : 2 * width + hidden]
    results[5] = whole[2 * width + hidden :]
    copies = [
        pltpu.make_async_copy(results.at[at], out, leaves.at[at]) for at, out in enumerate(outs)
    ]
    start_all(copies)
    wait_all(copies)


def join_rows(updated_own, grad_own, others, updated, grad, leaves):
    count = updated_own.shape[0]
    core = lax.axis_index("ch")
    here, there = pl.ds(core * count, count), pl.ds((1 - core) * count, count)
    copies = []
    for at, (own, out) in enumerate(((updated_own, updated), (grad_own, grad))):
        copies.append(pltpu.make_async_copy(own, out.at[here], leaves.at[2 * at]))
        copies.append(pltpu.make_async_copy(others.at[at], out.at[there], leaves.at[2 * at + 1]))
    start_all(copies)
    wait_all(copies)


def by_channels(pair, cotangent, w_gate_a, w_proj_a, w_gate_b, w_proj_b, w_gate_out, w_out):
    row_count, cols, channels = pair.shape
    hidden = w_gate_a.shape[1]
    parts, col_parts, row_parts = lax.axis_size("ch"), lax.axis_size("col"), lax.axis_size("row")
    devices = parts * col_parts * row_parts
    share = hidden * parts // devices
    width = 2 * hidden
    count = row_count // parts
    flat = count * cols
    tokens = cols * col_parts
    scale = 1.0 / tokens
    swap = [(c, parts - 1 - c) for c in range(parts)]
    weight = ((2 * width + 2 * hidden, channels), bf16)
    part = ((count, hidden, cols), bf16)
    own = jnp.swapaxes(cotangent, 1, 2)
    (stack,) = call(
        stack_up,
        [weight],
        (w_gate_a.T, w_proj_a.T, w_gate_b.T, w_proj_b.T, w_gate_out.T, w_out.T),
        (pltpu.SemaphoreType.DMA((6,)),),
        far=range(6),
        outs_far=True,
        room=60,
    )
    other_stack = lax.ppermute(stack, "ch", swap)
    normed, other = call(
        normalize,
        [((channels, flat), bf16), part],
        (pair, own),
        (pltpu.VMEM((count, cols, channels), bf16), pltpu.SemaphoreType.DMA((2,))),
        far=(0, 1),
    )
    send, weights = call(
        functools.partial(edges, width, share),
        [((devices, 2 * share, flat), bf16), ((parts, *weight[0]), bf16)],
        (normed, stack, other_stack),
    )
    arrived = lax.all_to_all(send, everyone, 0, 0)
    arrived, other = lax.optimization_barrier((arrived, other))
    other = lax.ppermute(other, "ch", swap)
    room = pltpu.VMEM((col_parts * tokens * 8, -(-cols // 128) * 128), f32)
    send, kept = call(
        functools.partial(mix, col_parts, cols),
        [((devices, share, flat), bf16), ((2 * share, tokens, tokens), bf16)],
        (arrived,),
        (room, room),
    )
    send, other = lax.optimization_barrier((send, other))
    arrived = lax.all_to_all(send, everyone, 0, 0)
    send, d_gate, head_terms, updated_own, updated_other = call(
        functools.partial(head, width, scale),
        [
            ((devices, share, flat), bf16),
            ((hidden * parts, flat), bf16),
            ((parts, 2 * hidden, channels), f32),
            part,
            part,
        ],
        (arrived, weights, normed, own, other),
        (
            pltpu.VMEM((channels, flat), bf16),
            pltpu.VMEM(*part),
            pltpu.VMEM(*part),
            pltpu.VMEM((hidden * parts, flat), f32),
            pltpu.SemaphoreType.DMA((3,)),
        ),
        far=(2, 3, 4),
    )
    arrived = lax.all_to_all(send, everyone, 0, 0)
    (send,) = call(
        functools.partial(unmix, col_parts, cols),
        [((devices, 2 * share, flat), bf16)],
        (arrived, kept),
        (room, room, pltpu.VMEM(kept.shape, bf16), pltpu.SemaphoreType.DMA),
        far=(1,),
    )
    arrived = lax.all_to_all(send, everyone, 0, 0)
    total = 2 * width + 2 * hidden
    per = total * parts // devices
    send, grad_own, others = call(
        functools.partial(tail, width, scale),
        [((devices, per, channels), bf16), part, ((2, *part[0]), bf16)],
        (arrived, weights, pair, d_gate, head_terms, updated_other),
        (
            pltpu.VMEM((count, cols, channels), bf16),
            pltpu.VMEM((hidden * parts, flat), bf16),
            pltpu.VMEM((total * parts, channels), f32),
            pltpu.SemaphoreType.DMA((2,)),
        ),
        far=(2, 3),
    )
    arrived = lax.all_to_all(send, ("ch", "row", "col"), 0, 0)
    rest = devices // parts
    (sums,) = call(add_up, [((rest, per, channels), bf16)], (arrived,))
    sums, others = lax.optimization_barrier((sums, others))
    sums = lax.all_to_all(sums, ("row", "col"), 0, 0)
    updated, grad_pair = call(
        join_rows,
        [((row_count, hidden, cols), bf16)] * 2,
        (updated_own, grad_own, lax.ppermute(others, "ch", swap)),
        (pltpu.SemaphoreType.DMA((4,)),),
        (0, 1, 2),
        True,
    )
    sums, updated, grad_pair = lax.optimization_barrier((sums, updated, grad_pair))
    grads = call(
        functools.partial(turn_back, share),
        [((hidden, channels), f32)] * 6,
        (sums,),
        (
            pltpu.VMEM((total, channels), f32),
            pltpu.VMEM((6, hidden, channels), f32),
            pltpu.SemaphoreType.DMA((6,)),
        ),
        outs_far=True,
    )
    return jnp.swapaxes(updated, 1, 2), jnp.swapaxes(grad_pair, 1, 2), *(g.T for g in grads)


def on_device(*arrays):
    row_count, cols, _ = arrays[0].shape
    parts, devices = lax.axis_size("ch"), lax.axis_size(everyone)
    hidden = arrays[2].shape[1]
    share = hidden * parts // devices
    fits = (
        share * devices == hidden * parts
        and parts == 2
        and 2 * share == 8
        and row_count % parts == 0
        and 6 * hidden * parts % devices == 0
        and arrays[1].shape[2] == hidden
        and cols % 16 == 0
    )
    return by_channels(*arrays) if fits else by_rows(*arrays)


def solution(mesh):
    in_specs = (
        P("row", "col", None),
        P("row", "col", "ch"),
        P(None, "ch"),
        P(None, "ch"),
        P(None, "ch"),
        P(None, "ch"),
        P(None, "ch"),
        P(None, "ch"),
    )
    out_specs = (
        P("row", "col", "ch"),
        P("row", "col", "ch"),
        P(None, "ch"),
        P(None, "ch"),
        P(None, "ch"),
        P(None, "ch"),
        P(None, "ch"),
        P(None, "ch"),
    )
    return jax.shard_map(
        on_device, mesh=mesh, in_specs=in_specs, out_specs=out_specs, check_vma=False
    )
```

```python
import functools

import jax
import jax.numpy as jnp
import numpy as np
from jax import lax
from jax.experimental import pallas as pl
from jax.experimental.pallas import tpu as pltpu
from jax.sharding import PartitionSpec as P

epsilon = 1e-05


def layer_norm(values):
    average = jnp.mean(values, -1, keepdims=True)
    centred = values - average
    spread = jnp.mean(centred * centred, -1, keepdims=True)
    inverse = lax.rsqrt(spread + epsilon)
    return (centred * inverse, inverse)


def matmul(first, second):
    return jnp.dot(first, second, preferred_element_type=jnp.float32)


def by_rows(pair, cotangent, w_gate_a, w_proj_a, w_gate_b, w_proj_b, w_gate_out, w_out):
    row_count, col_count, channels = pair.shape
    hidden = w_gate_a.shape[1]
    total_hidden = hidden * lax.axis_size("ch")
    out_width = cotangent.shape[2]
    length = row_count * lax.axis_size("row")
    grad_scale = 1.0 / length
    pair_hat, pair_rstd = layer_norm(pair.astype(jnp.float32))
    flat_norm = pair_hat.astype(jnp.bfloat16).reshape(row_count * col_count, channels)
    w_four = jnp.concatenate([w_gate_a, w_proj_a, w_gate_b, w_proj_b], axis=1)
    projected = matmul(flat_norm, w_four)
    gate_a = jax.nn.sigmoid(projected[:, :hidden])
    proj_a = projected[:, hidden : 2 * hidden]
    gate_b = jax.nn.sigmoid(projected[:, 2 * hidden : 3 * hidden])
    proj_b = projected[:, 3 * hidden :]
    left_edge = (gate_a * proj_a).astype(jnp.bfloat16).reshape(row_count, col_count, hidden)
    right_edge = (gate_b * proj_b).astype(jnp.bfloat16).reshape(row_count, col_count, hidden)
    right_all = lax.all_gather(right_edge, "row", axis=0, tiled=True)
    mixed_swap = lax.psum_scatter(
        jnp.einsum("jkh,ikh->jih", right_all, left_edge, preferred_element_type=jnp.float32).astype(
            jnp.bfloat16
        ),
        "col",
        scatter_dimension=0,
        tiled=True,
    ).astype(jnp.float32)
    mixed = jnp.swapaxes(mixed_swap, 0, 1).reshape(row_count * col_count, hidden)
    hidden_sums = lax.psum((jnp.sum(mixed, -1), jnp.sum(mixed * mixed, -1)), "ch")
    hidden_mean = (hidden_sums[0] / total_hidden)[:, None]
    hidden_var = (hidden_sums[1] / total_hidden)[:, None] - hidden_mean * hidden_mean
    hidden_rstd = lax.rsqrt(hidden_var + epsilon)
    mixed_hat = (mixed - hidden_mean) * hidden_rstd
    mixed_norm = mixed_hat.astype(jnp.bfloat16)
    norm_full = lax.all_gather(mixed_norm, "ch", axis=1, tiled=True)
    gate_out = jax.nn.sigmoid(matmul(flat_norm, w_gate_out))
    proj_out = matmul(norm_full, w_out)
    updated = (gate_out * proj_out).astype(jnp.bfloat16).reshape(row_count, col_count, out_width)
    upstream = cotangent.reshape(row_count * col_count, out_width).astype(jnp.float32)
    d_proj = (upstream * gate_out).astype(jnp.bfloat16)
    d_gate = (upstream * proj_out * gate_out * (1.0 - gate_out)).astype(jnp.bfloat16)
    head_grads = lax.psum(
        (matmul(norm_full.T, d_proj) * grad_scale, matmul(flat_norm.T, d_gate) * grad_scale),
        ("row", "col"),
    )
    d_norm = lax.psum_scatter(
        matmul(d_proj, w_out.T).astype(jnp.bfloat16), "ch", scatter_dimension=1, tiled=True
    ).astype(jnp.float32)
    back_sums = lax.psum((jnp.sum(d_norm, -1), jnp.sum(d_norm * mixed_hat, -1)), "ch")
    d_mixed = hidden_rstd * (
        d_norm
        - (back_sums[0] / total_hidden)[:, None]
        - mixed_hat * (back_sums[1] / total_hidden)[:, None]
    )
    d_mixed = d_mixed.astype(jnp.bfloat16).reshape(row_count, col_count, hidden)
    d_rows = lax.all_gather(d_mixed, "col", axis=1, tiled=True)
    right_back = lax.all_gather(right_edge, "row", axis=0, tiled=True)
    d_left = jnp.einsum("ijh,jkh->ikh", d_rows, right_back, preferred_element_type=jnp.float32)
    d_left = d_left.reshape(row_count * col_count, hidden)
    left_all = lax.all_gather(left_edge, "row", axis=0, tiled=True)
    d_columns = lax.all_to_all(d_rows, "row", split_axis=1, concat_axis=0, tiled=True)
    d_right = jnp.einsum("ijh,ikh->jkh", d_columns, left_all, preferred_element_type=jnp.float32)
    d_right = d_right.reshape(row_count * col_count, hidden)
    grad_pa = (d_left * gate_a).astype(jnp.bfloat16)
    grad_ga = (d_left * proj_a * gate_a * (1.0 - gate_a)).astype(jnp.bfloat16)
    grad_pb = (d_right * gate_b).astype(jnp.bfloat16)
    grad_gb = (d_right * proj_b * gate_b * (1.0 - gate_b)).astype(jnp.bfloat16)
    d_four = jnp.concatenate([grad_ga, grad_pa, grad_gb, grad_pb], axis=1)
    weight_terms = matmul(flat_norm.T, d_four) * grad_scale
    summed = lax.psum(weight_terms, ("row", "col"))
    d_flat = matmul(d_four, w_four.T) + matmul(d_gate, w_gate_out.T)
    hat_all = pair_hat.reshape(row_count * col_count, channels)
    rstd_flat = pair_rstd.reshape(row_count * col_count, 1)
    offset = lax.axis_index("ch") * out_width
    grad_whole = lax.psum(d_flat.astype(jnp.bfloat16), "ch").astype(jnp.float32)
    grad_full = rstd_flat * (
        grad_whole
        - jnp.mean(grad_whole, -1, keepdims=True)
        - hat_all * jnp.mean(grad_whole * hat_all, -1, keepdims=True)
    )
    grad_pair = lax.dynamic_slice_in_dim(grad_full, offset, out_width, 1)
    grad_pair = grad_pair.astype(jnp.bfloat16).reshape(row_count, col_count, out_width)
    return (
        updated,
        grad_pair,
        summed[:, :hidden],
        summed[:, hidden : 2 * hidden],
        summed[:, 2 * hidden : 3 * hidden],
        summed[:, 3 * hidden :],
        head_grads[1],
        head_grads[0],
    )


everyone = ("col", "row", "ch")
f32, bf16 = jnp.float32, jnp.bfloat16


def dot(first, second, over):
    return lax.dot_general(
        first, second, (((over[0],), (over[1],)), ((), ())), preferred_element_type=f32
    )


def call(kernel, outs, args, scratch=(), far=(), outs_far=False, room=16):
    whole = pl.BlockSpec(memory_space=pltpu.VMEM)
    anywhere = pl.BlockSpec(memory_space=pl.ANY)
    return pl.pallas_call(
        kernel,
        out_shape=tuple(jax.ShapeDtypeStruct(*out) for out in outs),
        in_specs=[anywhere if at in far else whole for at in range(len(args))],
        out_specs=tuple(anywhere if outs_far else whole for _ in outs),
        scratch_shapes=scratch,
        compiler_params=pltpu.CompilerParams(vmem_limit_bytes=room * 2**20),
    )(*args)


def grouping(hidden, share):
    shape = (2 * hidden, 2 * hidden)
    rows = lax.broadcasted_iota(jnp.int32, shape, 0)
    columns = lax.broadcasted_iota(jnp.int32, shape, 1)
    group, within = rows // (2 * share), lax.rem(rows, 2 * share)
    side = within // share
    wanted = side * hidden + group * share + within - side * share
    return jnp.where(columns == wanted, 1.0, 0.0).astype(bf16)


def start_all(copies):
    for copy in copies:
        copy.start()


def wait_all(copies):
    for copy in copies:
        copy.wait()


def prepare(
    share, ga, pa, gb, pb, go, wo, pair_far, cotangent_far, out, normed, other,
    gates, values, last, pair, arrivals,
):
    hidden = go.shape[0]
    width = 2 * hidden
    count = pair.shape[0]
    core = lax.axis_index("ch")
    copies = []
    for at, (held, low, high) in enumerate(((gates, ga, gb), (values, pa, pb), (last, go, wo))):
        copies.append(pltpu.make_async_copy(low, held.at[0:hidden], arrivals.at[2 * at]))
        copies.append(pltpu.make_async_copy(high, held.at[hidden:width], arrivals.at[2 * at + 1]))
    fetch = pltpu.make_async_copy(pair_far.at[pl.ds(core * count, count)], pair, arrivals.at[6])
    cut = pltpu.make_async_copy(
        cotangent_far.at[pl.ds((1 - core) * count, count)], other, arrivals.at[7]
    )
    start_all(copies + [fetch, cut])
    order = grouping(hidden, share)
    wait_all(copies)
    out[:width] = dot(order, gates[...], (1, 0)).astype(bf16)
    out[width : 2 * width] = dot(order, values[...], (1, 0)).astype(bf16)
    out[2 * width :] = last[...]
    fetch.wait()
    normed[...] = normalized(pair[...])[0].astype(bf16)
    cut.wait()


def rows_of(weights, start, count):
    return jnp.concatenate([weights[c, start : start + count] for c in range(weights.shape[0])], 0)


def normalized(pair):
    count, cols, channels = pair.shape
    values = pair.astype(f32).reshape(count * cols, channels).T
    centred = values - jnp.mean(values, 0, keepdims=True)
    rstd = lax.rsqrt(jnp.mean(centred * centred, 0, keepdims=True) + epsilon)
    return centred * rstd, rstd


def edges(width, normed, weights, send):
    gate = jax.nn.sigmoid(dot(rows_of(weights, 0, width), normed[...], (1, 0)))
    value = dot(rows_of(weights, width, width), normed[...], (1, 0))
    send[...] = (gate * value).reshape(send.shape).astype(bf16)


def spread_rows(block, cols, arrived, held):
    devices, q, flat = arrived.shape
    rows = flat // cols
    for s in range(devices):
        tile = arrived[s].astype(f32)
        for i in range(rows):
            start = (s * rows + i) * block
            held[start : start + q, 0:cols] = tile[:, i * cols : (i + 1) * cols]


def pack_rows(block, cols, held, send):
    devices, q, flat = send.shape
    rows = flat // cols
    for s in range(devices):
        starts = [(s * rows + i) * block for i in range(rows)]
        whole = jnp.concatenate([held[start : start + block, 0:cols] for start in starts], axis=1)
        send[s] = whole[:q].astype(bf16)


def square(block, parts, cols, held, e):
    tokens = parts * cols
    return jnp.concatenate(
        [
            held[pl.ds(p * tokens * block + e, tokens, stride=block), 0:cols]
            for p in range(parts)
        ],
        axis=1,
    ).astype(bf16)


def put_square(block, parts, cols, held, e, values):
    tokens = parts * cols
    for p in range(parts):
        held[pl.ds(p * tokens * block + e, tokens, stride=block), 0:cols] = values[
            :, p * cols : (p + 1) * cols
        ]


def mix(parts, cols, arrived, send, kept, held, result):
    block = 8
    q = arrived.shape[1]
    spread_rows(block, cols, arrived, held)
    for e in range(q // 2):
        left = square(block, parts, cols, held, e)
        right = square(block, parts, cols, held, q // 2 + e)
        kept[e] = left
        kept[q // 2 + e] = right
        put_square(block, parts, cols, result, e, dot(left, right, (1, 1)))
    pack_rows(block, cols, result, send)


def unmix(parts, cols, arrived, kept_far, send, held, result, kept, arrival):
    block = 8
    q = arrived.shape[1]
    copy = pltpu.make_async_copy(kept_far, kept, arrival)
    copy.start()
    spread_rows(block, cols, arrived, held)
    copy.wait()
    for e in range(q):
        d_mixed = square(block, parts, cols, held, e)
        put_square(block, parts, cols, result, e, dot(d_mixed, kept[q + e], (1, 0)))
        put_square(block, parts, cols, result, q + e, dot(d_mixed, kept[e], (0, 0)))
    pack_rows(block, cols, result, send)


def split_rows(cols, values, own, other):
    hidden = values.shape[0] // 2
    first = lax.axis_index("ch") == 0
    low, high = values[:hidden], values[hidden:]
    mine = jnp.where(first, low, high)
    yours = jnp.where(first, high, low)
    for i in range(own.shape[0]):
        own[i] = mine[:, i * cols : (i + 1) * cols].astype(bf16)
        other[i] = yours[:, i * cols : (i + 1) * cols].astype(bf16)


def head(
    width, scale, arrived, weights, normed_far, own_far, other_far,
    send, d_gate, terms, updated_own, updated_other,
    normed, own, other, upstream, arrivals,
):
    parts, total, _ = weights.shape
    hidden = (total - 2 * width) // 2
    devices, q, flat = arrived.shape
    count, _, cols = other.shape
    core = lax.axis_index("ch")
    copies = [
        pltpu.make_async_copy(normed_far, normed, arrivals.at[0]),
        pltpu.make_async_copy(own_far.at[pl.ds(core * count, count)], own, arrivals.at[1]),
        pltpu.make_async_copy(other_far, other, arrivals.at[2]),
    ]
    start_all(copies)
    mixed = jnp.concatenate([arrived[s].astype(f32) for s in range(devices)], 0)
    average = jnp.mean(mixed, 0, keepdims=True)
    spread = jnp.mean(mixed * mixed, 0, keepdims=True) - average * average
    inverse = lax.rsqrt(spread + epsilon)
    hat = (mixed - average) * inverse
    hat_rounded = hat.astype(bf16)
    w_out = rows_of(weights, 2 * width + hidden, hidden)
    proj = dot(w_out, hat_rounded, (1, 0))
    wait_all(copies)
    for part, side in ((own, core), (other, 1 - core)):
        upstream[pl.ds(pl.multiple_of(side * hidden, hidden), hidden)] = jnp.concatenate(
            [part[i].astype(f32) for i in range(count)], axis=1
        )
    gate = jax.nn.sigmoid(dot(rows_of(weights, 2 * width, hidden), normed[...], (1, 0)))
    up = upstream[...]
    d_proj = (up * gate).astype(bf16)
    d_gate[...] = (up * proj * gate * (1.0 - gate)).astype(bf16)
    d_norm = dot(w_out, d_proj, (0, 0))
    d_mixed = inverse * (
        d_norm
        - jnp.mean(d_norm, 0, keepdims=True)
        - hat * jnp.mean(d_norm * hat, 0, keepdims=True)
    )
    for s in range(devices):
        send[s] = d_mixed[s * q : (s + 1) * q].astype(bf16)
    by_gate = dot(d_gate[...], normed[...], (1, 1)) * scale
    by_out = dot(d_proj, hat_rounded, (1, 1)) * scale
    for c in range(parts):
        terms[c, :hidden] = by_gate[c * hidden : (c + 1) * hidden]
        terms[c, hidden:] = by_out[c * hidden : (c + 1) * hidden]
    split_rows(cols, gate * proj, updated_own, updated_other)


def tail(
    width, scale, arrived, weights, pair_far, d_gate_far, head_terms, updated_other,
    send, grad_own, others,
    pair, d_gate, whole, arrivals,
):
    parts, total, channels = weights.shape
    hidden = (total - 2 * width) // 2
    devices, q, flat = arrived.shape
    count, cols, _ = pair.shape
    core = lax.axis_index("ch")
    copies = [
        pltpu.make_async_copy(pair_far.at[pl.ds(core * count, count)], pair, arrivals.at[0]),
        pltpu.make_async_copy(d_gate_far, d_gate, arrivals.at[1]),
    ]
    start_all(copies)
    others[0] = updated_other[...]
    wait_all(copies)
    hat, inverse = normalized(pair[...])
    normed = hat.astype(bf16)
    w_gate, w_value = rows_of(weights, 0, width), rows_of(weights, width, width)
    gate = jax.nn.sigmoid(dot(w_gate, normed, (1, 0)))
    value = dot(w_value, normed, (1, 0))
    grad = arrived[...].astype(f32).reshape(devices * q, flat)
    by_value = grad * gate
    by_gate = (by_value * (value * (1.0 - gate))).astype(bf16)
    by_value = by_value.astype(bf16)
    terms = [dot(by_gate, normed, (1, 1)) * scale, dot(by_value, normed, (1, 1)) * scale]
    for c in range(parts):
        for at, term in enumerate(terms):
            start = c * total + at * width
            whole[start : start + width] = term[c * width : (c + 1) * width]
        whole[c * total + 2 * width : (c + 1) * total] = head_terms[c]
    per = send.shape[1]
    for s in range(devices):
        send[s] = whole[s * per : (s + 1) * per].astype(bf16)
    d_input = dot(w_gate, by_gate, (0, 0)) + dot(w_value, by_value, (0, 0))
    d_input = d_input + dot(rows_of(weights, 2 * width, hidden), d_gate[...], (0, 0))
    back = inverse * (
        d_input
        - jnp.mean(d_input, 0, keepdims=True)
        - hat * jnp.mean(d_input * hat, 0, keepdims=True)
    )
    split_rows(cols, back, grad_own, others.at[1])


def add_up(arrived, out):
    total = jnp.sum(arrived[...].astype(f32), 0).astype(bf16)
    for s in range(out.shape[0]):
        out[s] = total


def turn_back(share, sums, *refs):
    outs, whole, results, leaves = refs[:6], refs[6], refs[7], refs[8]
    _, hidden, channels = results.shape
    width = 2 * hidden
    per = sums.shape[1]
    for s in range(sums.shape[0]):
        whole[s * per : (s + 1) * per] = sums[s].astype(f32)
    order = grouping(hidden, share)
    for at in range(2):
        both = dot(order, whole[at * width : (at + 1) * width].astype(bf16), (0, 0))
        results[at] = both[:hidden]
        results[2 + at] = both[hidden:]
    results[4] = whole[2 * width : 2 * width + hidden]
    results[5] = whole[2 * width + hidden :]
    copies = [
        pltpu.make_async_copy(results.at[at], out, leaves.at[at]) for at, out in enumerate(outs)
    ]
    start_all(copies)
    wait_all(copies)


def join_rows(updated_own, grad_own, others, updated, grad, leaves):
    count = updated_own.shape[0]
    core = lax.axis_index("ch")
    here, there = pl.ds(core * count, count), pl.ds((1 - core) * count, count)
    copies = []
    for at, (own, out) in enumerate(((updated_own, updated), (grad_own, grad))):
        copies.append(pltpu.make_async_copy(own, out.at[here], leaves.at[2 * at]))
        copies.append(pltpu.make_async_copy(others.at[at], out.at[there], leaves.at[2 * at + 1]))
    start_all(copies)
    wait_all(copies)


def by_channels(pair, cotangent, w_gate_a, w_proj_a, w_gate_b, w_proj_b, w_gate_out, w_out):
    row_count, cols, channels = pair.shape
    hidden = w_gate_a.shape[1]
    parts, col_parts, row_parts = lax.axis_size("ch"), lax.axis_size("col"), lax.axis_size("row")
    devices = parts * col_parts * row_parts
    share = hidden * parts // devices
    width = 2 * hidden
    count = row_count // parts
    flat = count * cols
    tokens = cols * col_parts
    scale = 1.0 / tokens
    swap = [(c, parts - 1 - c) for c in range(parts)]
    weight = ((2 * width + 2 * hidden, channels), bf16)
    part = ((count, hidden, cols), bf16)
    own = jnp.swapaxes(cotangent, 1, 2)
    whole_weight = pltpu.VMEM((2 * hidden, channels), bf16)
    weights, normed, other = call(
        functools.partial(prepare, share),
        [weight, ((channels, flat), bf16), part],
        (w_gate_a.T, w_proj_a.T, w_gate_b.T, w_proj_b.T, w_gate_out.T, w_out.T, pair, own),
        (
            whole_weight,
            whole_weight,
            whole_weight,
            pltpu.VMEM((count, cols, channels), bf16),
            pltpu.SemaphoreType.DMA((8,)),
        ),
        far=range(8),
        room=60,
    )
    weights = lax.all_gather(weights, "ch")
    (send,) = call(
        functools.partial(edges, width), [((devices, 2 * share, flat), bf16)], (normed, weights)
    )
    arrived = lax.all_to_all(send, everyone, 0, 0)
    arrived, other = lax.optimization_barrier((arrived, other))
    other = lax.ppermute(other, "ch", swap)
    room = pltpu.VMEM((col_parts * tokens * 8, -(-cols // 128) * 128), f32)
    send, kept = call(
        functools.partial(mix, col_parts, cols),
        [((devices, share, flat), bf16), ((2 * share, tokens, tokens), bf16)],
        (arrived,),
        (room, room),
    )
    send, other = lax.optimization_barrier((send, other))
    arrived = lax.all_to_all(send, everyone, 0, 0)
    send, d_gate, head_terms, updated_own, updated_other = call(
        functools.partial(head, width, scale),
        [
            ((devices, share, flat), bf16),
            ((hidden * parts, flat), bf16),
            ((parts, 2 * hidden, channels), f32),
            part,
            part,
        ],
        (arrived, weights, normed, own, other),
        (
            pltpu.VMEM((channels, flat), bf16),
            pltpu.VMEM(*part),
            pltpu.VMEM(*part),
            pltpu.VMEM((hidden * parts, flat), f32),
            pltpu.SemaphoreType.DMA((3,)),
        ),
        far=(2, 3, 4),
    )
    arrived = lax.all_to_all(send, everyone, 0, 0)
    (send,) = call(
        functools.partial(unmix, col_parts, cols),
        [((devices, 2 * share, flat), bf16)],
        (arrived, kept),
        (room, room, pltpu.VMEM(kept.shape, bf16), pltpu.SemaphoreType.DMA),
        far=(1,),
    )
    arrived = lax.all_to_all(send, everyone, 0, 0)
    total = 2 * width + 2 * hidden
    per = total * parts // devices
    send, grad_own, others = call(
        functools.partial(tail, width, scale),
        [((devices, per, channels), bf16), part, ((2, *part[0]), bf16)],
        (arrived, weights, pair, d_gate, head_terms, updated_other),
        (
            pltpu.VMEM((count, cols, channels), bf16),
            pltpu.VMEM((hidden * parts, flat), bf16),
            pltpu.VMEM((total * parts, channels), f32),
            pltpu.SemaphoreType.DMA((2,)),
        ),
        far=(2, 3),
    )
    arrived = lax.all_to_all(send, ("ch", "row", "col"), 0, 0)
    rest = devices // parts
    (sums,) = call(add_up, [((rest, per, channels), bf16)], (arrived,))
    sums, others = lax.optimization_barrier((sums, others))
    sums = lax.all_to_all(sums, ("row", "col"), 0, 0)
    updated, grad_pair = call(
        join_rows,
        [((row_count, hidden, cols), bf16)] * 2,
        (updated_own, grad_own, lax.ppermute(others, "ch", swap)),
        (pltpu.SemaphoreType.DMA((4,)),),
        (0, 1, 2),
        True,
    )
    sums, updated, grad_pair = lax.optimization_barrier((sums, updated, grad_pair))
    grads = call(
        functools.partial(turn_back, share),
        [((hidden, channels), f32)] * 6,
        (sums,),
        (
            pltpu.VMEM((total, channels), f32),
            pltpu.VMEM((6, hidden, channels), f32),
            pltpu.SemaphoreType.DMA((6,)),
        ),
        outs_far=True,
    )
    return jnp.swapaxes(updated, 1, 2), jnp.swapaxes(grad_pair, 1, 2), *(g.T for g in grads)


def on_device(*arrays):
    row_count, cols, _ = arrays[0].shape
    parts, devices = lax.axis_size("ch"), lax.axis_size(everyone)
    hidden = arrays[2].shape[1]
    share = hidden * parts // devices
    fits = (
        share * devices == hidden * parts
        and parts == 2
        and 2 * share == 8
        and row_count % parts == 0
        and 6 * hidden * parts % devices == 0
        and arrays[1].shape[2] == hidden
        and cols % 16 == 0
    )
    return by_channels(*arrays) if fits else by_rows(*arrays)


def solution(mesh):
    in_specs = (
        P("row", "col", None),
        P("row", "col", "ch"),
        P(None, "ch"),
        P(None, "ch"),
        P(None, "ch"),
        P(None, "ch"),
        P(None, "ch"),
        P(None, "ch"),
    )
    out_specs = (
        P("row", "col", "ch"),
        P("row", "col", "ch"),
        P(None, "ch"),
        P(None, "ch"),
        P(None, "ch"),
        P(None, "ch"),
        P(None, "ch"),
        P(None, "ch"),
    )
    return jax.shard_map(
        on_device, mesh=mesh, in_specs=in_specs, out_specs=out_specs, check_vma=False
    )
```

```python
import functools

import jax
import jax.numpy as jnp
import numpy as np
from jax import lax
from jax.experimental import pallas as pl
from jax.experimental.pallas import tpu as pltpu
from jax.sharding import PartitionSpec as P

epsilon = 1e-05


def layer_norm(values):
    average = jnp.mean(values, -1, keepdims=True)
    centred = values - average
    spread = jnp.mean(centred * centred, -1, keepdims=True)
    inverse = lax.rsqrt(spread + epsilon)
    return (centred * inverse, inverse)


def matmul(first, second):
    return jnp.dot(first, second, preferred_element_type=jnp.float32)


def by_rows(pair, cotangent, w_gate_a, w_proj_a, w_gate_b, w_proj_b, w_gate_out, w_out):
    row_count, col_count, channels = pair.shape
    hidden = w_gate_a.shape[1]
    total_hidden = hidden * lax.axis_size("ch")
    out_width = cotangent.shape[2]
    length = row_count * lax.axis_size("row")
    grad_scale = 1.0 / length
    pair_hat, pair_rstd = layer_norm(pair.astype(jnp.float32))
    flat_norm = pair_hat.astype(jnp.bfloat16).reshape(row_count * col_count, channels)
    w_four = jnp.concatenate([w_gate_a, w_proj_a, w_gate_b, w_proj_b], axis=1)
    projected = matmul(flat_norm, w_four)
    gate_a = jax.nn.sigmoid(projected[:, :hidden])
    proj_a = projected[:, hidden : 2 * hidden]
    gate_b = jax.nn.sigmoid(projected[:, 2 * hidden : 3 * hidden])
    proj_b = projected[:, 3 * hidden :]
    left_edge = (gate_a * proj_a).astype(jnp.bfloat16).reshape(row_count, col_count, hidden)
    right_edge = (gate_b * proj_b).astype(jnp.bfloat16).reshape(row_count, col_count, hidden)
    right_all = lax.all_gather(right_edge, "row", axis=0, tiled=True)
    mixed_swap = lax.psum_scatter(
        jnp.einsum("jkh,ikh->jih", right_all, left_edge, preferred_element_type=jnp.float32).astype(
            jnp.bfloat16
        ),
        "col",
        scatter_dimension=0,
        tiled=True,
    ).astype(jnp.float32)
    mixed = jnp.swapaxes(mixed_swap, 0, 1).reshape(row_count * col_count, hidden)
    hidden_sums = lax.psum((jnp.sum(mixed, -1), jnp.sum(mixed * mixed, -1)), "ch")
    hidden_mean = (hidden_sums[0] / total_hidden)[:, None]
    hidden_var = (hidden_sums[1] / total_hidden)[:, None] - hidden_mean * hidden_mean
    hidden_rstd = lax.rsqrt(hidden_var + epsilon)
    mixed_hat = (mixed - hidden_mean) * hidden_rstd
    mixed_norm = mixed_hat.astype(jnp.bfloat16)
    norm_full = lax.all_gather(mixed_norm, "ch", axis=1, tiled=True)
    gate_out = jax.nn.sigmoid(matmul(flat_norm, w_gate_out))
    proj_out = matmul(norm_full, w_out)
    updated = (gate_out * proj_out).astype(jnp.bfloat16).reshape(row_count, col_count, out_width)
    upstream = cotangent.reshape(row_count * col_count, out_width).astype(jnp.float32)
    d_proj = (upstream * gate_out).astype(jnp.bfloat16)
    d_gate = (upstream * proj_out * gate_out * (1.0 - gate_out)).astype(jnp.bfloat16)
    head_grads = lax.psum(
        (matmul(norm_full.T, d_proj) * grad_scale, matmul(flat_norm.T, d_gate) * grad_scale),
        ("row", "col"),
    )
    d_norm = lax.psum_scatter(
        matmul(d_proj, w_out.T).astype(jnp.bfloat16), "ch", scatter_dimension=1, tiled=True
    ).astype(jnp.float32)
    back_sums = lax.psum((jnp.sum(d_norm, -1), jnp.sum(d_norm * mixed_hat, -1)), "ch")
    d_mixed = hidden_rstd * (
        d_norm
        - (back_sums[0] / total_hidden)[:, None]
        - mixed_hat * (back_sums[1] / total_hidden)[:, None]
    )
    d_mixed = d_mixed.astype(jnp.bfloat16).reshape(row_count, col_count, hidden)
    d_rows = lax.all_gather(d_mixed, "col", axis=1, tiled=True)
    right_back = lax.all_gather(right_edge, "row", axis=0, tiled=True)
    d_left = jnp.einsum("ijh,jkh->ikh", d_rows, right_back, preferred_element_type=jnp.float32)
    d_left = d_left.reshape(row_count * col_count, hidden)
    left_all = lax.all_gather(left_edge, "row", axis=0, tiled=True)
    d_columns = lax.all_to_all(d_rows, "row", split_axis=1, concat_axis=0, tiled=True)
    d_right = jnp.einsum("ijh,ikh->jkh", d_columns, left_all, preferred_element_type=jnp.float32)
    d_right = d_right.reshape(row_count * col_count, hidden)
    grad_pa = (d_left * gate_a).astype(jnp.bfloat16)
    grad_ga = (d_left * proj_a * gate_a * (1.0 - gate_a)).astype(jnp.bfloat16)
    grad_pb = (d_right * gate_b).astype(jnp.bfloat16)
    grad_gb = (d_right * proj_b * gate_b * (1.0 - gate_b)).astype(jnp.bfloat16)
    d_four = jnp.concatenate([grad_ga, grad_pa, grad_gb, grad_pb], axis=1)
    weight_terms = matmul(flat_norm.T, d_four) * grad_scale
    summed = lax.psum(weight_terms, ("row", "col"))
    d_flat = matmul(d_four, w_four.T) + matmul(d_gate, w_gate_out.T)
    hat_all = pair_hat.reshape(row_count * col_count, channels)
    rstd_flat = pair_rstd.reshape(row_count * col_count, 1)
    offset = lax.axis_index("ch") * out_width
    grad_whole = lax.psum(d_flat.astype(jnp.bfloat16), "ch").astype(jnp.float32)
    grad_full = rstd_flat * (
        grad_whole
        - jnp.mean(grad_whole, -1, keepdims=True)
        - hat_all * jnp.mean(grad_whole * hat_all, -1, keepdims=True)
    )
    grad_pair = lax.dynamic_slice_in_dim(grad_full, offset, out_width, 1)
    grad_pair = grad_pair.astype(jnp.bfloat16).reshape(row_count, col_count, out_width)
    return (
        updated,
        grad_pair,
        summed[:, :hidden],
        summed[:, hidden : 2 * hidden],
        summed[:, 2 * hidden : 3 * hidden],
        summed[:, 3 * hidden :],
        head_grads[1],
        head_grads[0],
    )


everyone = ("col", "row", "ch")
f32, bf16 = jnp.float32, jnp.bfloat16


def dot(first, second, over):
    return lax.dot_general(
        first, second, (((over[0],), (over[1],)), ((), ())), preferred_element_type=f32
    )


def call(kernel, outs, args, scratch=(), far=(), outs_far=False, room=16):
    whole = pl.BlockSpec(memory_space=pltpu.VMEM)
    anywhere = pl.BlockSpec(memory_space=pl.ANY)
    return pl.pallas_call(
        kernel,
        out_shape=tuple(jax.ShapeDtypeStruct(*out) for out in outs),
        in_specs=[anywhere if at in far else whole for at in range(len(args))],
        out_specs=tuple(anywhere if outs_far else whole for _ in outs),
        scratch_shapes=scratch,
        compiler_params=pltpu.CompilerParams(vmem_limit_bytes=room * 2**20),
    )(*args)


def grouping(hidden, share):
    shape = (2 * hidden, 2 * hidden)
    rows = lax.broadcasted_iota(jnp.int32, shape, 0)
    columns = lax.broadcasted_iota(jnp.int32, shape, 1)
    group, within = rows // (2 * share), lax.rem(rows, 2 * share)
    side = within // share
    wanted = side * hidden + group * share + within - side * share
    return jnp.where(columns == wanted, 1.0, 0.0).astype(bf16)


def start_all(copies):
    for copy in copies:
        copy.start()


def wait_all(copies):
    for copy in copies:
        copy.wait()


def prepare(
    share, ga, pa, gb, pb, go, wo, pair_far, cotangent_far, out, normed, other,
    gates, values, last, pair, arrivals,
):
    hidden = go.shape[0]
    width = 2 * hidden
    count = pair.shape[0]
    core = lax.axis_index("ch")
    copies = []
    for at, (held, low, high) in enumerate(((gates, ga, gb), (values, pa, pb), (last, go, wo))):
        copies.append(pltpu.make_async_copy(low, held.at[0:hidden], arrivals.at[2 * at]))
        copies.append(pltpu.make_async_copy(high, held.at[hidden:width], arrivals.at[2 * at + 1]))
    fetch = pltpu.make_async_copy(pair_far.at[pl.ds(core * count, count)], pair, arrivals.at[6])
    cut = pltpu.make_async_copy(
        cotangent_far.at[pl.ds((1 - core) * count, count)], other, arrivals.at[7]
    )
    start_all(copies + [fetch, cut])
    order = grouping(hidden, share)
    wait_all(copies)
    out[:width] = dot(order, gates[...], (1, 0)).astype(bf16)
    out[width : 2 * width] = dot(order, values[...], (1, 0)).astype(bf16)
    out[2 * width :] = last[...]
    fetch.wait()
    normed[...] = normalized(pair[...])[0].astype(bf16)
    cut.wait()


def rows_of(weights, start, count):
    return jnp.concatenate([weights[c, start : start + count] for c in range(weights.shape[0])], 0)


def normalized(pair):
    count, cols, channels = pair.shape
    values = pair.astype(f32).reshape(count * cols, channels).T
    centred = values - jnp.mean(values, 0, keepdims=True)
    rstd = lax.rsqrt(jnp.mean(centred * centred, 0, keepdims=True) + epsilon)
    return centred * rstd, rstd


def edges(width, normed, own, other, send, weights):
    core = lax.axis_index("ch")
    weights[core] = own[...]
    weights[1 - core] = other[...]
    gate = jax.nn.sigmoid(dot(rows_of(weights, 0, width), normed[...], (1, 0)))
    value = dot(rows_of(weights, width, width), normed[...], (1, 0))
    send[...] = (gate * value).reshape(send.shape).astype(bf16)


def spread_rows(block, cols, arrived, held):
    devices, q, flat = arrived.shape
    rows = flat // cols
    for s in range(devices):
        tile = arrived[s].astype(f32)
        for i in range(rows):
            start = (s * rows + i) * block
            held[start : start + q, 0:cols] = tile[:, i * cols : (i + 1) * cols]


def pack_rows(block, cols, held, send):
    devices, q, flat = send.shape
    rows = flat // cols
    for s in range(devices):
        starts = [(s * rows + i) * block for i in range(rows)]
        whole = jnp.concatenate([held[start : start + block, 0:cols] for start in starts], axis=1)
        send[s] = whole[:q].astype(bf16)


def square(block, parts, cols, held, e):
    tokens = parts * cols
    return jnp.concatenate(
        [
            held[pl.ds(p * tokens * block + e, tokens, stride=block), 0:cols]
            for p in range(parts)
        ],
        axis=1,
    ).astype(bf16)


def put_square(block, parts, cols, held, e, values):
    tokens = parts * cols
    for p in range(parts):
        held[pl.ds(p * tokens * block + e, tokens, stride=block), 0:cols] = values[
            :, p * cols : (p + 1) * cols
        ]


def mix(parts, cols, arrived, send, kept, held, result):
    block = 8
    q = arrived.shape[1]
    spread_rows(block, cols, arrived, held)
    for e in range(q // 2):
        left = square(block, parts, cols, held, e)
        right = square(block, parts, cols, held, q // 2 + e)
        kept[e] = left
        kept[q // 2 + e] = right
        put_square(block, parts, cols, result, e, dot(left, right, (1, 1)))
    pack_rows(block, cols, result, send)


def unmix(parts, cols, arrived, kept_far, send, held, result, kept, arrival):
    block = 8
    q = arrived.shape[1]
    copy = pltpu.make_async_copy(kept_far, kept, arrival)
    copy.start()
    spread_rows(block, cols, arrived, held)
    copy.wait()
    for e in range(q):
        d_mixed = square(block, parts, cols, held, e)
        put_square(block, parts, cols, result, e, dot(d_mixed, kept[q + e], (1, 0)))
        put_square(block, parts, cols, result, q + e, dot(d_mixed, kept[e], (0, 0)))
    pack_rows(block, cols, result, send)


def split_rows(cols, values, own, other):
    hidden = values.shape[0] // 2
    first = lax.axis_index("ch") == 0
    low, high = values[:hidden], values[hidden:]
    mine = jnp.where(first, low, high)
    yours = jnp.where(first, high, low)
    for i in range(own.shape[0]):
        own[i] = mine[:, i * cols : (i + 1) * cols].astype(bf16)
        other[i] = yours[:, i * cols : (i + 1) * cols].astype(bf16)


def head(
    width, scale, arrived, weights, normed_far, own_far, other_far,
    send, d_gate, terms, updated_own, updated_other,
    normed, own, other, upstream, arrivals,
):
    parts, total, _ = weights.shape
    hidden = (total - 2 * width) // 2
    devices, q, flat = arrived.shape
    count, _, cols = other.shape
    core = lax.axis_index("ch")
    copies = [
        pltpu.make_async_copy(normed_far, normed, arrivals.at[0]),
        pltpu.make_async_copy(own_far.at[pl.ds(core * count, count)], own, arrivals.at[1]),
        pltpu.make_async_copy(other_far, other, arrivals.at[2]),
    ]
    start_all(copies)
    mixed = jnp.concatenate([arrived[s].astype(f32) for s in range(devices)], 0)
    average = jnp.mean(mixed, 0, keepdims=True)
    spread = jnp.mean(mixed * mixed, 0, keepdims=True) - average * average
    inverse = lax.rsqrt(spread + epsilon)
    hat = (mixed - average) * inverse
    hat_rounded = hat.astype(bf16)
    w_out = rows_of(weights, 2 * width + hidden, hidden)
    proj = dot(w_out, hat_rounded, (1, 0))
    wait_all(copies)
    for part, side in ((own, core), (other, 1 - core)):
        upstream[pl.ds(pl.multiple_of(side * hidden, hidden), hidden)] = jnp.concatenate(
            [part[i].astype(f32) for i in range(count)], axis=1
        )
    gate = jax.nn.sigmoid(dot(rows_of(weights, 2 * width, hidden), normed[...], (1, 0)))
    up = upstream[...]
    d_proj = (up * gate).astype(bf16)
    d_gate[...] = (up * proj * gate * (1.0 - gate)).astype(bf16)
    d_norm = dot(w_out, d_proj, (0, 0))
    d_mixed = inverse * (
        d_norm
        - jnp.mean(d_norm, 0, keepdims=True)
        - hat * jnp.mean(d_norm * hat, 0, keepdims=True)
    )
    for s in range(devices):
        send[s] = d_mixed[s * q : (s + 1) * q].astype(bf16)
    by_gate = dot(d_gate[...], normed[...], (1, 1)) * scale
    by_out = dot(d_proj, hat_rounded, (1, 1)) * scale
    for c in range(parts):
        terms[c, :hidden] = by_gate[c * hidden : (c + 1) * hidden]
        terms[c, hidden:] = by_out[c * hidden : (c + 1) * hidden]
    split_rows(cols, gate * proj, updated_own, updated_other)


def tail(
    width, scale, arrived, weights, pair_far, d_gate_far, head_terms, updated_other,
    send, grad_own, others,
    pair, d_gate, whole, arrivals,
):
    parts, total, channels = weights.shape
    hidden = (total - 2 * width) // 2
    devices, q, flat = arrived.shape
    count, cols, _ = pair.shape
    core = lax.axis_index("ch")
    copies = [
        pltpu.make_async_copy(pair_far.at[pl.ds(core * count, count)], pair, arrivals.at[0]),
        pltpu.make_async_copy(d_gate_far, d_gate, arrivals.at[1]),
    ]
    start_all(copies)
    others[0] = updated_other[...]
    wait_all(copies)
    hat, inverse = normalized(pair[...])
    normed = hat.astype(bf16)
    w_gate, w_value = rows_of(weights, 0, width), rows_of(weights, width, width)
    gate = jax.nn.sigmoid(dot(w_gate, normed, (1, 0)))
    value = dot(w_value, normed, (1, 0))
    grad = arrived[...].astype(f32).reshape(devices * q, flat)
    by_value = grad * gate
    by_gate = (by_value * (value * (1.0 - gate))).astype(bf16)
    by_value = by_value.astype(bf16)
    terms = [dot(by_gate, normed, (1, 1)) * scale, dot(by_value, normed, (1, 1)) * scale]
    for c in range(parts):
        for at, term in enumerate(terms):
            start = c * total + at * width
            whole[start : start + width] = term[c * width : (c + 1) * width]
        whole[c * total + 2 * width : (c + 1) * total] = head_terms[c]
    per = send.shape[1]
    for s in range(devices):
        send[s] = whole[s * per : (s + 1) * per].astype(bf16)
    d_input = dot(w_gate, by_gate, (0, 0)) + dot(w_value, by_value, (0, 0))
    d_input = d_input + dot(rows_of(weights, 2 * width, hidden), d_gate[...], (0, 0))
    back = inverse * (
        d_input
        - jnp.mean(d_input, 0, keepdims=True)
        - hat * jnp.mean(d_input * hat, 0, keepdims=True)
    )
    split_rows(cols, back, grad_own, others.at[1])


def add_up(arrived, out):
    total = jnp.sum(arrived[...].astype(f32), 0).astype(bf16)
    for s in range(out.shape[0]):
        out[s] = total


def finish(share, sums, updated_own, grad_own, others, *refs):
    (updated, grad), outs, (whole, results, leaves) = refs[:2], refs[2:8], refs[8:]
    count = updated_own.shape[0]
    core = lax.axis_index("ch")
    here, there = pl.ds(core * count, count), pl.ds((1 - core) * count, count)
    joins = []
    for at, (own, out) in enumerate(((updated_own, updated), (grad_own, grad))):
        joins.append(pltpu.make_async_copy(own, out.at[here], leaves.at[2 * at]))
        joins.append(pltpu.make_async_copy(others.at[at], out.at[there], leaves.at[2 * at + 1]))
    start_all(joins)
    _, hidden, channels = results.shape
    width = 2 * hidden
    per = sums.shape[1]
    for s in range(sums.shape[0]):
        whole[s * per : (s + 1) * per] = sums[s].astype(f32)
    order = grouping(hidden, share)
    for at in range(2):
        both = dot(order, whole[at * width : (at + 1) * width].astype(bf16), (0, 0))
        results[at] = both[:hidden]
        results[2 + at] = both[hidden:]
    results[4] = whole[2 * width : 2 * width + hidden]
    results[5] = whole[2 * width + hidden :]
    copies = [
        pltpu.make_async_copy(results.at[at], out, leaves.at[4 + at]) for at, out in enumerate(outs)
    ]
    start_all(copies)
    wait_all(joins + copies)


def by_channels(pair, cotangent, w_gate_a, w_proj_a, w_gate_b, w_proj_b, w_gate_out, w_out):
    row_count, cols, channels = pair.shape
    hidden = w_gate_a.shape[1]
    parts, col_parts, row_parts = lax.axis_size("ch"), lax.axis_size("col"), lax.axis_size("row")
    devices = parts * col_parts * row_parts
    share = hidden * parts // devices
    width = 2 * hidden
    count = row_count // parts
    flat = count * cols
    tokens = cols * col_parts
    scale = 1.0 / tokens
    swap = [(c, parts - 1 - c) for c in range(parts)]
    weight = ((2 * width + 2 * hidden, channels), bf16)
    part = ((count, hidden, cols), bf16)
    own = jnp.swapaxes(cotangent, 1, 2)
    whole_weight = pltpu.VMEM((2 * hidden, channels), bf16)
    weights, normed, other = call(
        functools.partial(prepare, share),
        [weight, ((channels, flat), bf16), part],
        (w_gate_a.T, w_proj_a.T, w_gate_b.T, w_proj_b.T, w_gate_out.T, w_out.T, pair, own),
        (
            whole_weight,
            whole_weight,
            whole_weight,
            pltpu.VMEM((count, cols, channels), bf16),
            pltpu.SemaphoreType.DMA((8,)),
        ),
        far=range(8),
        room=60,
    )
    send, weights = call(
        functools.partial(edges, width),
        [((devices, 2 * share, flat), bf16), ((parts, *weight[0]), bf16)],
        (normed, weights, lax.ppermute(weights, "ch", swap)),
    )
    arrived = lax.all_to_all(send, everyone, 0, 0)
    arrived, other = lax.optimization_barrier((arrived, other))
    other = lax.ppermute(other, "ch", swap)
    room = pltpu.VMEM((col_parts * tokens * 8, -(-cols // 128) * 128), f32)
    send, kept = call(
        functools.partial(mix, col_parts, cols),
        [((devices, share, flat), bf16), ((2 * share, tokens, tokens), bf16)],
        (arrived,),
        (room, room),
    )
    send, other = lax.optimization_barrier((send, other))
    arrived = lax.all_to_all(send, everyone, 0, 0)
    send, d_gate, head_terms, updated_own, updated_other = call(
        functools.partial(head, width, scale),
        [
            ((devices, share, flat), bf16),
            ((hidden * parts, flat), bf16),
            ((parts, 2 * hidden, channels), f32),
            part,
            part,
        ],
        (arrived, weights, normed, own, other),
        (
            pltpu.VMEM((channels, flat), bf16),
            pltpu.VMEM(*part),
            pltpu.VMEM(*part),
            pltpu.VMEM((hidden * parts, flat), f32),
            pltpu.SemaphoreType.DMA((3,)),
        ),
        far=(2, 3, 4),
    )
    arrived = lax.all_to_all(send, everyone, 0, 0)
    (send,) = call(
        functools.partial(unmix, col_parts, cols),
        [((devices, 2 * share, flat), bf16)],
        (arrived, kept),
        (room, room, pltpu.VMEM(kept.shape, bf16), pltpu.SemaphoreType.DMA),
        far=(1,),
    )
    arrived = lax.all_to_all(send, everyone, 0, 0)
    total = 2 * width + 2 * hidden
    per = total * parts // devices
    send, grad_own, others = call(
        functools.partial(tail, width, scale),
        [((devices, per, channels), bf16), part, ((2, *part[0]), bf16)],
        (arrived, weights, pair, d_gate, head_terms, updated_other),
        (
            pltpu.VMEM((count, cols, channels), bf16),
            pltpu.VMEM((hidden * parts, flat), bf16),
            pltpu.VMEM((total * parts, channels), f32),
            pltpu.SemaphoreType.DMA((2,)),
        ),
        far=(2, 3),
    )
    arrived = lax.all_to_all(send, ("ch", "row", "col"), 0, 0)
    rest = devices // parts
    (sums,) = call(add_up, [((rest, per, channels), bf16)], (arrived,))
    sums = lax.all_to_all(sums, ("row", "col"), 0, 0)
    updated, grad_pair, *grads = call(
        functools.partial(finish, share),
        [((row_count, hidden, cols), bf16)] * 2 + [((hidden, channels), f32)] * 6,
        (sums, updated_own, grad_own, lax.ppermute(others, "ch", swap)),
        (
            pltpu.VMEM((total, channels), f32),
            pltpu.VMEM((6, hidden, channels), f32),
            pltpu.SemaphoreType.DMA((10,)),
        ),
        (1, 2, 3),
        True,
    )
    return jnp.swapaxes(updated, 1, 2), jnp.swapaxes(grad_pair, 1, 2), *(g.T for g in grads)


def on_device(*arrays):
    row_count, cols, _ = arrays[0].shape
    parts, devices = lax.axis_size("ch"), lax.axis_size(everyone)
    hidden = arrays[2].shape[1]
    share = hidden * parts // devices
    fits = (
        share * devices == hidden * parts
        and parts == 2
        and 2 * share == 8
        and row_count % parts == 0
        and 6 * hidden * parts % devices == 0
        and arrays[1].shape[2] == hidden
        and cols % 16 == 0
    )
    return by_channels(*arrays) if fits else by_rows(*arrays)


def solution(mesh):
    in_specs = (
        P("row", "col", None),
        P("row", "col", "ch"),
        P(None, "ch"),
        P(None, "ch"),
        P(None, "ch"),
        P(None, "ch"),
        P(None, "ch"),
        P(None, "ch"),
    )
    out_specs = (
        P("row", "col", "ch"),
        P("row", "col", "ch"),
        P(None, "ch"),
        P(None, "ch"),
        P(None, "ch"),
        P(None, "ch"),
        P(None, "ch"),
        P(None, "ch"),
    )
    return jax.shard_map(
        on_device, mesh=mesh, in_specs=in_specs, out_specs=out_specs, check_vma=False
    )
```

```python
import functools

import jax
import jax.numpy as jnp
import numpy as np
from jax import lax
from jax.experimental import pallas as pl
from jax.experimental.pallas import tpu as pltpu
from jax.sharding import PartitionSpec as P

epsilon = 1e-05


def layer_norm(values):
    average = jnp.mean(values, -1, keepdims=True)
    centred = values - average
    spread = jnp.mean(centred * centred, -1, keepdims=True)
    inverse = lax.rsqrt(spread + epsilon)
    return (centred * inverse, inverse)


def matmul(first, second):
    return jnp.dot(first, second, preferred_element_type=jnp.float32)


def by_rows(pair, cotangent, w_gate_a, w_proj_a, w_gate_b, w_proj_b, w_gate_out, w_out):
    row_count, col_count, channels = pair.shape
    hidden = w_gate_a.shape[1]
    total_hidden = hidden * lax.axis_size("ch")
    out_width = cotangent.shape[2]
    length = row_count * lax.axis_size("row")
    grad_scale = 1.0 / length
    pair_hat, pair_rstd = layer_norm(pair.astype(jnp.float32))
    flat_norm = pair_hat.astype(jnp.bfloat16).reshape(row_count * col_count, channels)
    w_four = jnp.concatenate([w_gate_a, w_proj_a, w_gate_b, w_proj_b], axis=1)
    projected = matmul(flat_norm, w_four)
    gate_a = jax.nn.sigmoid(projected[:, :hidden])
    proj_a = projected[:, hidden : 2 * hidden]
    gate_b = jax.nn.sigmoid(projected[:, 2 * hidden : 3 * hidden])
    proj_b = projected[:, 3 * hidden :]
    left_edge = (gate_a * proj_a).astype(jnp.bfloat16).reshape(row_count, col_count, hidden)
    right_edge = (gate_b * proj_b).astype(jnp.bfloat16).reshape(row_count, col_count, hidden)
    right_all = lax.all_gather(right_edge, "row", axis=0, tiled=True)
    mixed_swap = lax.psum_scatter(
        jnp.einsum("jkh,ikh->jih", right_all, left_edge, preferred_element_type=jnp.float32).astype(
            jnp.bfloat16
        ),
        "col",
        scatter_dimension=0,
        tiled=True,
    ).astype(jnp.float32)
    mixed = jnp.swapaxes(mixed_swap, 0, 1).reshape(row_count * col_count, hidden)
    hidden_sums = lax.psum((jnp.sum(mixed, -1), jnp.sum(mixed * mixed, -1)), "ch")
    hidden_mean = (hidden_sums[0] / total_hidden)[:, None]
    hidden_var = (hidden_sums[1] / total_hidden)[:, None] - hidden_mean * hidden_mean
    hidden_rstd = lax.rsqrt(hidden_var + epsilon)
    mixed_hat = (mixed - hidden_mean) * hidden_rstd
    mixed_norm = mixed_hat.astype(jnp.bfloat16)
    norm_full = lax.all_gather(mixed_norm, "ch", axis=1, tiled=True)
    gate_out = jax.nn.sigmoid(matmul(flat_norm, w_gate_out))
    proj_out = matmul(norm_full, w_out)
    updated = (gate_out * proj_out).astype(jnp.bfloat16).reshape(row_count, col_count, out_width)
    upstream = cotangent.reshape(row_count * col_count, out_width).astype(jnp.float32)
    d_proj = (upstream * gate_out).astype(jnp.bfloat16)
    d_gate = (upstream * proj_out * gate_out * (1.0 - gate_out)).astype(jnp.bfloat16)
    head_grads = lax.psum(
        (matmul(norm_full.T, d_proj) * grad_scale, matmul(flat_norm.T, d_gate) * grad_scale),
        ("row", "col"),
    )
    d_norm = lax.psum_scatter(
        matmul(d_proj, w_out.T).astype(jnp.bfloat16), "ch", scatter_dimension=1, tiled=True
    ).astype(jnp.float32)
    back_sums = lax.psum((jnp.sum(d_norm, -1), jnp.sum(d_norm * mixed_hat, -1)), "ch")
    d_mixed = hidden_rstd * (
        d_norm
        - (back_sums[0] / total_hidden)[:, None]
        - mixed_hat * (back_sums[1] / total_hidden)[:, None]
    )
    d_mixed = d_mixed.astype(jnp.bfloat16).reshape(row_count, col_count, hidden)
    d_rows = lax.all_gather(d_mixed, "col", axis=1, tiled=True)
    right_back = lax.all_gather(right_edge, "row", axis=0, tiled=True)
    d_left = jnp.einsum("ijh,jkh->ikh", d_rows, right_back, preferred_element_type=jnp.float32)
    d_left = d_left.reshape(row_count * col_count, hidden)
    left_all = lax.all_gather(left_edge, "row", axis=0, tiled=True)
    d_columns = lax.all_to_all(d_rows, "row", split_axis=1, concat_axis=0, tiled=True)
    d_right = jnp.einsum("ijh,ikh->jkh", d_columns, left_all, preferred_element_type=jnp.float32)
    d_right = d_right.reshape(row_count * col_count, hidden)
    grad_pa = (d_left * gate_a).astype(jnp.bfloat16)
    grad_ga = (d_left * proj_a * gate_a * (1.0 - gate_a)).astype(jnp.bfloat16)
    grad_pb = (d_right * gate_b).astype(jnp.bfloat16)
    grad_gb = (d_right * proj_b * gate_b * (1.0 - gate_b)).astype(jnp.bfloat16)
    d_four = jnp.concatenate([grad_ga, grad_pa, grad_gb, grad_pb], axis=1)
    weight_terms = matmul(flat_norm.T, d_four) * grad_scale
    summed = lax.psum(weight_terms, ("row", "col"))
    d_flat = matmul(d_four, w_four.T) + matmul(d_gate, w_gate_out.T)
    hat_all = pair_hat.reshape(row_count * col_count, channels)
    rstd_flat = pair_rstd.reshape(row_count * col_count, 1)
    offset = lax.axis_index("ch") * out_width
    grad_whole = lax.psum(d_flat.astype(jnp.bfloat16), "ch").astype(jnp.float32)
    grad_full = rstd_flat * (
        grad_whole
        - jnp.mean(grad_whole, -1, keepdims=True)
        - hat_all * jnp.mean(grad_whole * hat_all, -1, keepdims=True)
    )
    grad_pair = lax.dynamic_slice_in_dim(grad_full, offset, out_width, 1)
    grad_pair = grad_pair.astype(jnp.bfloat16).reshape(row_count, col_count, out_width)
    return (
        updated,
        grad_pair,
        summed[:, :hidden],
        summed[:, hidden : 2 * hidden],
        summed[:, 2 * hidden : 3 * hidden],
        summed[:, 3 * hidden :],
        head_grads[1],
        head_grads[0],
    )


everyone = ("col", "row", "ch")
f32, bf16 = jnp.float32, jnp.bfloat16


def dot(first, second, over):
    return lax.dot_general(
        first, second, (((over[0],), (over[1],)), ((), ())), preferred_element_type=f32
    )


def call(kernel, outs, args, scratch=(), far=(), outs_far=False, room=16):
    whole = pl.BlockSpec(memory_space=pltpu.VMEM)
    anywhere = pl.BlockSpec(memory_space=pl.ANY)
    return pl.pallas_call(
        kernel,
        out_shape=tuple(jax.ShapeDtypeStruct(*out) for out in outs),
        in_specs=[anywhere if at in far else whole for at in range(len(args))],
        out_specs=tuple(anywhere if outs_far else whole for _ in outs),
        scratch_shapes=scratch,
        compiler_params=pltpu.CompilerParams(vmem_limit_bytes=room * 2**20),
    )(*args)


def grouping(hidden, share):
    shape = (2 * hidden, 2 * hidden)
    rows = lax.broadcasted_iota(jnp.int32, shape, 0)
    columns = lax.broadcasted_iota(jnp.int32, shape, 1)
    group, within = rows // (2 * share), lax.rem(rows, 2 * share)
    side = within // share
    wanted = side * hidden + group * share + within - side * share
    return jnp.where(columns == wanted, 1.0, 0.0).astype(bf16)


def start_all(copies):
    for copy in copies:
        copy.start()


def wait_all(copies):
    for copy in copies:
        copy.wait()


def prepare(
    share, ga, pa, gb, pb, go, wo, pair_far, cotangent_far, out, normed, other,
    gates, values, last, pair, arrivals,
):
    hidden = go.shape[0]
    width = 2 * hidden
    count = pair.shape[0]
    core = lax.axis_index("ch")
    copies = []
    for at, (held, low, high) in enumerate(((gates, ga, gb), (values, pa, pb), (last, go, wo))):
        copies.append(pltpu.make_async_copy(low, held.at[0:hidden], arrivals.at[2 * at]))
        copies.append(pltpu.make_async_copy(high, held.at[hidden:width], arrivals.at[2 * at + 1]))
    fetch = pltpu.make_async_copy(pair_far.at[pl.ds(core * count, count)], pair, arrivals.at[6])
    cut = pltpu.make_async_copy(
        cotangent_far.at[pl.ds((1 - core) * count, count)], other, arrivals.at[7]
    )
    start_all(copies + [fetch, cut])
    order = grouping(hidden, share)
    wait_all(copies)
    out[:width] = dot(order, gates[...], (1, 0)).astype(bf16)
    out[width : 2 * width] = dot(order, values[...], (1, 0)).astype(bf16)
    out[2 * width :] = last[...]
    fetch.wait()
    normed[...] = normalized(pair[...])[0].astype(bf16)
    cut.wait()


def rows_of(weights, start, count):
    return jnp.concatenate([weights[c, start : start + count] for c in range(weights.shape[0])], 0)


def normalized(pair):
    count, cols, channels = pair.shape
    values = pair.astype(f32).reshape(count * cols, channels).T
    centred = values - jnp.mean(values, 0, keepdims=True)
    rstd = lax.rsqrt(jnp.mean(centred * centred, 0, keepdims=True) + epsilon)
    return centred * rstd, rstd


def edges(width, normed, weights, send):
    gate = jax.nn.sigmoid(dot(rows_of(weights, 0, width), normed[...], (1, 0)))
    value = dot(rows_of(weights, width, width), normed[...], (1, 0))
    send[...] = (gate * value).reshape(send.shape).astype(bf16)


def spread_rows(block, cols, arrived, held):
    devices, q, flat = arrived.shape
    rows = flat // cols
    for s in range(devices):
        tile = arrived[s].astype(f32)
        for i in range(rows):
            start = (s * rows + i) * block
            held[start : start + q, 0:cols] = tile[:, i * cols : (i + 1) * cols]


def pack_rows(block, cols, held, send):
    devices, q, flat = send.shape
    rows = flat // cols
    for s in range(devices):
        starts = [(s * rows + i) * block for i in range(rows)]
        whole = jnp.concatenate([held[start : start + block, 0:cols] for start in starts], axis=1)
        send[s] = whole[:q].astype(bf16)


def square(block, parts, cols, held, e):
    tokens = parts * cols
    return jnp.concatenate(
        [
            held[pl.ds(p * tokens * block + e, tokens, stride=block), 0:cols]
            for p in range(parts)
        ],
        axis=1,
    ).astype(bf16)


def put_square(block, parts, cols, held, e, values):
    tokens = parts * cols
    for p in range(parts):
        held[pl.ds(p * tokens * block + e, tokens, stride=block), 0:cols] = values[
            :, p * cols : (p + 1) * cols
        ]


def mix(parts, cols, arrived, send, kept, held, result):
    block = 8
    q = arrived.shape[1]
    spread_rows(block, cols, arrived, held)
    for e in range(q // 2):
        left = square(block, parts, cols, held, e)
        right = square(block, parts, cols, held, q // 2 + e)
        kept[e] = left
        kept[q // 2 + e] = right
        put_square(block, parts, cols, result, e, dot(left, right, (1, 1)))
    pack_rows(block, cols, result, send)


def unmix(parts, cols, arrived, kept_far, send, held, result, kept, arrival):
    block = 8
    q = arrived.shape[1]
    copy = pltpu.make_async_copy(kept_far, kept, arrival)
    copy.start()
    spread_rows(block, cols, arrived, held)
    copy.wait()
    for e in range(q):
        d_mixed = square(block, parts, cols, held, e)
        put_square(block, parts, cols, result, e, dot(d_mixed, kept[q + e], (1, 0)))
        put_square(block, parts, cols, result, q + e, dot(d_mixed, kept[e], (0, 0)))
    pack_rows(block, cols, result, send)


def split_rows(cols, values, own, other):
    hidden = values.shape[0] // 2
    first = lax.axis_index("ch") == 0
    low, high = values[:hidden], values[hidden:]
    mine = jnp.where(first, low, high)
    yours = jnp.where(first, high, low)
    for i in range(own.shape[0]):
        own[i] = mine[:, i * cols : (i + 1) * cols].astype(bf16)
        other[i] = yours[:, i * cols : (i + 1) * cols].astype(bf16)


def head(
    width, scale, arrived, weights, normed_far, own_far, other_far,
    send, d_gate, terms, updated_own, updated_other,
    normed, own, other, upstream, arrivals,
):
    parts, total, _ = weights.shape
    hidden = (total - 2 * width) // 2
    devices, q, flat = arrived.shape
    count, _, cols = other.shape
    core = lax.axis_index("ch")
    copies = [
        pltpu.make_async_copy(normed_far, normed, arrivals.at[0]),
        pltpu.make_async_copy(own_far.at[pl.ds(core * count, count)], own, arrivals.at[1]),
        pltpu.make_async_copy(other_far, other, arrivals.at[2]),
    ]
    start_all(copies)
    mixed = jnp.concatenate([arrived[s].astype(f32) for s in range(devices)], 0)
    average = jnp.mean(mixed, 0, keepdims=True)
    spread = jnp.mean(mixed * mixed, 0, keepdims=True) - average * average
    inverse = lax.rsqrt(spread + epsilon)
    hat = (mixed - average) * inverse
    hat_rounded = hat.astype(bf16)
    w_out = rows_of(weights, 2 * width + hidden, hidden)
    proj = dot(w_out, hat_rounded, (1, 0))
    wait_all(copies)
    for part, side in ((own, core), (other, 1 - core)):
        upstream[pl.ds(pl.multiple_of(side * hidden, hidden), hidden)] = jnp.concatenate(
            [part[i].astype(f32) for i in range(count)], axis=1
        )
    gate = jax.nn.sigmoid(dot(rows_of(weights, 2 * width, hidden), normed[...], (1, 0)))
    up = upstream[...]
    d_proj = (up * gate).astype(bf16)
    d_gate[...] = (up * proj * gate * (1.0 - gate)).astype(bf16)
    d_norm = dot(w_out, d_proj, (0, 0))
    d_mixed = inverse * (
        d_norm
        - jnp.mean(d_norm, 0, keepdims=True)
        - hat * jnp.mean(d_norm * hat, 0, keepdims=True)
    )
    for s in range(devices):
        send[s] = d_mixed[s * q : (s + 1) * q].astype(bf16)
    by_gate = dot(d_gate[...], normed[...], (1, 1)) * scale
    by_out = dot(d_proj, hat_rounded, (1, 1)) * scale
    for c in range(parts):
        terms[c, :hidden] = by_gate[c * hidden : (c + 1) * hidden]
        terms[c, hidden:] = by_out[c * hidden : (c + 1) * hidden]
    split_rows(cols, gate * proj, updated_own, updated_other)


def tail(
    width, scale, arrived, weights, pair_far, d_gate_far, head_terms, updated_other,
    send, grad_own, others,
    pair, d_gate, whole, arrivals,
):
    parts, total, channels = weights.shape
    hidden = (total - 2 * width) // 2
    devices, q, flat = arrived.shape
    count, cols, _ = pair.shape
    core = lax.axis_index("ch")
    copies = [
        pltpu.make_async_copy(pair_far.at[pl.ds(core * count, count)], pair, arrivals.at[0]),
        pltpu.make_async_copy(d_gate_far, d_gate, arrivals.at[1]),
    ]
    start_all(copies)
    others[0] = updated_other[...]
    wait_all(copies)
    hat, inverse = normalized(pair[...])
    normed = hat.astype(bf16)
    w_gate, w_value = rows_of(weights, 0, width), rows_of(weights, width, width)
    gate = jax.nn.sigmoid(dot(w_gate, normed, (1, 0)))
    value = dot(w_value, normed, (1, 0))
    grad = arrived[...].astype(f32).reshape(devices * q, flat)
    by_value = grad * gate
    by_gate = (by_value * (value * (1.0 - gate))).astype(bf16)
    by_value = by_value.astype(bf16)
    terms = [dot(by_gate, normed, (1, 1)) * scale, dot(by_value, normed, (1, 1)) * scale]
    for c in range(parts):
        for at, term in enumerate(terms):
            start = c * total + at * width
            whole[start : start + width] = term[c * width : (c + 1) * width]
        whole[c * total + 2 * width : (c + 1) * total] = head_terms[c]
    per = send.shape[1]
    for s in range(devices):
        send[s] = whole[s * per : (s + 1) * per].astype(bf16)
    d_input = dot(w_gate, by_gate, (0, 0)) + dot(w_value, by_value, (0, 0))
    d_input = d_input + dot(rows_of(weights, 2 * width, hidden), d_gate[...], (0, 0))
    back = inverse * (
        d_input
        - jnp.mean(d_input, 0, keepdims=True)
        - hat * jnp.mean(d_input * hat, 0, keepdims=True)
    )
    split_rows(cols, back, grad_own, others.at[1])


def add_up(arrived, out):
    total = jnp.sum(arrived[...].astype(f32), 0).astype(bf16)
    for s in range(out.shape[0]):
        out[s] = total


def finish(share, sums, updated_own, grad_own, others, *refs):
    (updated, grad), outs, (whole, results, leaves) = refs[:2], refs[2:8], refs[8:]
    count = updated_own.shape[0]
    core = lax.axis_index("ch")
    here, there = pl.ds(core * count, count), pl.ds((1 - core) * count, count)
    joins = []
    for at, (own, out) in enumerate(((updated_own, updated), (grad_own, grad))):
        joins.append(pltpu.make_async_copy(own, out.at[here], leaves.at[2 * at]))
        joins.append(pltpu.make_async_copy(others.at[at], out.at[there], leaves.at[2 * at + 1]))
    start_all(joins)
    _, hidden, channels = results.shape
    width = 2 * hidden
    per = sums.shape[1]
    for s in range(sums.shape[0]):
        whole[s * per : (s + 1) * per] = sums[s].astype(f32)
    order = grouping(hidden, share)
    for at in range(2):
        both = dot(order, whole[at * width : (at + 1) * width].astype(bf16), (0, 0))
        results[at] = both[:hidden]
        results[2 + at] = both[hidden:]
    results[4] = whole[2 * width : 2 * width + hidden]
    results[5] = whole[2 * width + hidden :]
    copies = [
        pltpu.make_async_copy(results.at[at], out, leaves.at[4 + at]) for at, out in enumerate(outs)
    ]
    start_all(copies)
    wait_all(joins + copies)


def by_channels(pair, cotangent, w_gate_a, w_proj_a, w_gate_b, w_proj_b, w_gate_out, w_out):
    row_count, cols, channels = pair.shape
    hidden = w_gate_a.shape[1]
    parts, col_parts, row_parts = lax.axis_size("ch"), lax.axis_size("col"), lax.axis_size("row")
    devices = parts * col_parts * row_parts
    share = hidden * parts // devices
    width = 2 * hidden
    count = row_count // parts
    flat = count * cols
    tokens = cols * col_parts
    scale = 1.0 / tokens
    swap = [(c, parts - 1 - c) for c in range(parts)]
    weight = ((2 * width + 2 * hidden, channels), bf16)
    part = ((count, hidden, cols), bf16)
    own = jnp.swapaxes(cotangent, 1, 2)
    whole_weight = pltpu.VMEM((2 * hidden, channels), bf16)
    weights, normed, other = call(
        functools.partial(prepare, share),
        [weight, ((channels, flat), bf16), part],
        (w_gate_a.T, w_proj_a.T, w_gate_b.T, w_proj_b.T, w_gate_out.T, w_out.T, pair, own),
        (
            whole_weight,
            whole_weight,
            whole_weight,
            pltpu.VMEM((count, cols, channels), bf16),
            pltpu.SemaphoreType.DMA((8,)),
        ),
        far=range(8),
        room=60,
    )
    weights = lax.all_gather(weights, "ch")
    (send,) = call(
        functools.partial(edges, width), [((devices, 2 * share, flat), bf16)], (normed, weights)
    )
    arrived = lax.all_to_all(send, everyone, 0, 0)
    arrived, other = lax.optimization_barrier((arrived, other))
    other = lax.ppermute(other, "ch", swap)
    room = pltpu.VMEM((col_parts * tokens * 8, -(-cols // 128) * 128), f32)
    send, kept = call(
        functools.partial(mix, col_parts, cols),
        [((devices, share, flat), bf16), ((2 * share, tokens, tokens), bf16)],
        (arrived,),
        (room, room),
    )
    send, other = lax.optimization_barrier((send, other))
    arrived = lax.all_to_all(send, everyone, 0, 0)
    send, d_gate, head_terms, updated_own, updated_other = call(
        functools.partial(head, width, scale),
        [
            ((devices, share, flat), bf16),
            ((hidden * parts, flat), bf16),
            ((parts, 2 * hidden, channels), f32),
            part,
            part,
        ],
        (arrived, weights, normed, own, other),
        (
            pltpu.VMEM((channels, flat), bf16),
            pltpu.VMEM(*part),
            pltpu.VMEM(*part),
            pltpu.VMEM((hidden * parts, flat), f32),
            pltpu.SemaphoreType.DMA((3,)),
        ),
        far=(2, 3, 4),
    )
    arrived = lax.all_to_all(send, everyone, 0, 0)
    (send,) = call(
        functools.partial(unmix, col_parts, cols),
        [((devices, 2 * share, flat), bf16)],
        (arrived, kept),
        (room, room, pltpu.VMEM(kept.shape, bf16), pltpu.SemaphoreType.DMA),
        far=(1,),
    )
    arrived = lax.all_to_all(send, everyone, 0, 0)
    total = 2 * width + 2 * hidden
    per = total * parts // devices
    send, grad_own, others = call(
        functools.partial(tail, width, scale),
        [((devices, per, channels), bf16), part, ((2, *part[0]), bf16)],
        (arrived, weights, pair, d_gate, head_terms, updated_other),
        (
            pltpu.VMEM((count, cols, channels), bf16),
            pltpu.VMEM((hidden * parts, flat), bf16),
            pltpu.VMEM((total * parts, channels), f32),
            pltpu.SemaphoreType.DMA((2,)),
        ),
        far=(2, 3),
    )
    arrived = lax.all_to_all(send, ("ch", "row", "col"), 0, 0)
    rest = devices // parts
    arrived, others = lax.optimization_barrier((arrived, others))
    (sums,) = call(add_up, [((rest, per, channels), bf16)], (arrived,))
    sums = lax.all_to_all(sums, ("row", "col"), 0, 0)
    updated, grad_pair, *grads = call(
        functools.partial(finish, share),
        [((row_count, hidden, cols), bf16)] * 2 + [((hidden, channels), f32)] * 6,
        (sums, updated_own, grad_own, lax.ppermute(others, "ch", swap)),
        (
            pltpu.VMEM((total, channels), f32),
            pltpu.VMEM((6, hidden, channels), f32),
            pltpu.SemaphoreType.DMA((10,)),
        ),
        (1, 2, 3),
        True,
    )
    return jnp.swapaxes(updated, 1, 2), jnp.swapaxes(grad_pair, 1, 2), *(g.T for g in grads)


def on_device(*arrays):
    row_count, cols, _ = arrays[0].shape
    parts, devices = lax.axis_size("ch"), lax.axis_size(everyone)
    hidden = arrays[2].shape[1]
    share = hidden * parts // devices
    fits = (
        share * devices == hidden * parts
        and parts == 2
        and 2 * share == 8
        and row_count % parts == 0
        and 6 * hidden * parts % devices == 0
        and arrays[1].shape[2] == hidden
        and cols % 16 == 0
    )
    return by_channels(*arrays) if fits else by_rows(*arrays)


def solution(mesh):
    in_specs = (
        P("row", "col", None),
        P("row", "col", "ch"),
        P(None, "ch"),
        P(None, "ch"),
        P(None, "ch"),
        P(None, "ch"),
        P(None, "ch"),
        P(None, "ch"),
    )
    out_specs = (
        P("row", "col", "ch"),
        P("row", "col", "ch"),
        P(None, "ch"),
        P(None, "ch"),
        P(None, "ch"),
        P(None, "ch"),
        P(None, "ch"),
        P(None, "ch"),
    )
    return jax.shard_map(
        on_device, mesh=mesh, in_specs=in_specs, out_specs=out_specs, check_vma=False
    )
```

```python
import functools

import jax
import jax.numpy as jnp
import numpy as np
from jax import lax
from jax.experimental import pallas as pl
from jax.experimental.pallas import tpu as pltpu
from jax.sharding import PartitionSpec as P

epsilon = 1e-05


def layer_norm(values):
    average = jnp.mean(values, -1, keepdims=True)
    centred = values - average
    spread = jnp.mean(centred * centred, -1, keepdims=True)
    inverse = lax.rsqrt(spread + epsilon)
    return (centred * inverse, inverse)


def matmul(first, second):
    return jnp.dot(first, second, preferred_element_type=jnp.float32)


def by_rows(pair, cotangent, w_gate_a, w_proj_a, w_gate_b, w_proj_b, w_gate_out, w_out):
    row_count, col_count, channels = pair.shape
    hidden = w_gate_a.shape[1]
    total_hidden = hidden * lax.axis_size("ch")
    out_width = cotangent.shape[2]
    length = row_count * lax.axis_size("row")
    grad_scale = 1.0 / length
    pair_hat, pair_rstd = layer_norm(pair.astype(jnp.float32))
    flat_norm = pair_hat.astype(jnp.bfloat16).reshape(row_count * col_count, channels)
    w_four = jnp.concatenate([w_gate_a, w_proj_a, w_gate_b, w_proj_b], axis=1)
    projected = matmul(flat_norm, w_four)
    gate_a = jax.nn.sigmoid(projected[:, :hidden])
    proj_a = projected[:, hidden : 2 * hidden]
    gate_b = jax.nn.sigmoid(projected[:, 2 * hidden : 3 * hidden])
    proj_b = projected[:, 3 * hidden :]
    left_edge = (gate_a * proj_a).astype(jnp.bfloat16).reshape(row_count, col_count, hidden)
    right_edge = (gate_b * proj_b).astype(jnp.bfloat16).reshape(row_count, col_count, hidden)
    right_all = lax.all_gather(right_edge, "row", axis=0, tiled=True)
    mixed_swap = lax.psum_scatter(
        jnp.einsum("jkh,ikh->jih", right_all, left_edge, preferred_element_type=jnp.float32).astype(
            jnp.bfloat16
        ),
        "col",
        scatter_dimension=0,
        tiled=True,
    ).astype(jnp.float32)
    mixed = jnp.swapaxes(mixed_swap, 0, 1).reshape(row_count * col_count, hidden)
    hidden_sums = lax.psum((jnp.sum(mixed, -1), jnp.sum(mixed * mixed, -1)), "ch")
    hidden_mean = (hidden_sums[0] / total_hidden)[:, None]
    hidden_var = (hidden_sums[1] / total_hidden)[:, None] - hidden_mean * hidden_mean
    hidden_rstd = lax.rsqrt(hidden_var + epsilon)
    mixed_hat = (mixed - hidden_mean) * hidden_rstd
    mixed_norm = mixed_hat.astype(jnp.bfloat16)
    norm_full = lax.all_gather(mixed_norm, "ch", axis=1, tiled=True)
    gate_out = jax.nn.sigmoid(matmul(flat_norm, w_gate_out))
    proj_out = matmul(norm_full, w_out)
    updated = (gate_out * proj_out).astype(jnp.bfloat16).reshape(row_count, col_count, out_width)
    upstream = cotangent.reshape(row_count * col_count, out_width).astype(jnp.float32)
    d_proj = (upstream * gate_out).astype(jnp.bfloat16)
    d_gate = (upstream * proj_out * gate_out * (1.0 - gate_out)).astype(jnp.bfloat16)
    head_grads = lax.psum(
        (matmul(norm_full.T, d_proj) * grad_scale, matmul(flat_norm.T, d_gate) * grad_scale),
        ("row", "col"),
    )
    d_norm = lax.psum_scatter(
        matmul(d_proj, w_out.T).astype(jnp.bfloat16), "ch", scatter_dimension=1, tiled=True
    ).astype(jnp.float32)
    back_sums = lax.psum((jnp.sum(d_norm, -1), jnp.sum(d_norm * mixed_hat, -1)), "ch")
    d_mixed = hidden_rstd * (
        d_norm
        - (back_sums[0] / total_hidden)[:, None]
        - mixed_hat * (back_sums[1] / total_hidden)[:, None]
    )
    d_mixed = d_mixed.astype(jnp.bfloat16).reshape(row_count, col_count, hidden)
    d_rows = lax.all_gather(d_mixed, "col", axis=1, tiled=True)
    right_back = lax.all_gather(right_edge, "row", axis=0, tiled=True)
    d_left = jnp.einsum("ijh,jkh->ikh", d_rows, right_back, preferred_element_type=jnp.float32)
    d_left = d_left.reshape(row_count * col_count, hidden)
    left_all = lax.all_gather(left_edge, "row", axis=0, tiled=True)
    d_columns = lax.all_to_all(d_rows, "row", split_axis=1, concat_axis=0, tiled=True)
    d_right = jnp.einsum("ijh,ikh->jkh", d_columns, left_all, preferred_element_type=jnp.float32)
    d_right = d_right.reshape(row_count * col_count, hidden)
    grad_pa = (d_left * gate_a).astype(jnp.bfloat16)
    grad_ga = (d_left * proj_a * gate_a * (1.0 - gate_a)).astype(jnp.bfloat16)
    grad_pb = (d_right * gate_b).astype(jnp.bfloat16)
    grad_gb = (d_right * proj_b * gate_b * (1.0 - gate_b)).astype(jnp.bfloat16)
    d_four = jnp.concatenate([grad_ga, grad_pa, grad_gb, grad_pb], axis=1)
    weight_terms = matmul(flat_norm.T, d_four) * grad_scale
    summed = lax.psum(weight_terms, ("row", "col"))
    d_flat = matmul(d_four, w_four.T) + matmul(d_gate, w_gate_out.T)
    hat_all = pair_hat.reshape(row_count * col_count, channels)
    rstd_flat = pair_rstd.reshape(row_count * col_count, 1)
    offset = lax.axis_index("ch") * out_width
    grad_whole = lax.psum(d_flat.astype(jnp.bfloat16), "ch").astype(jnp.float32)
    grad_full = rstd_flat * (
        grad_whole
        - jnp.mean(grad_whole, -1, keepdims=True)
        - hat_all * jnp.mean(grad_whole * hat_all, -1, keepdims=True)
    )
    grad_pair = lax.dynamic_slice_in_dim(grad_full, offset, out_width, 1)
    grad_pair = grad_pair.astype(jnp.bfloat16).reshape(row_count, col_count, out_width)
    return (
        updated,
        grad_pair,
        summed[:, :hidden],
        summed[:, hidden : 2 * hidden],
        summed[:, 2 * hidden : 3 * hidden],
        summed[:, 3 * hidden :],
        head_grads[1],
        head_grads[0],
    )


everyone = ("col", "row", "ch")
f32, bf16 = jnp.float32, jnp.bfloat16


def dot(first, second, over):
    return lax.dot_general(
        first, second, (((over[0],), (over[1],)), ((), ())), preferred_element_type=f32
    )


def call(kernel, outs, args, scratch=(), far=(), outs_far=False, room=16):
    whole = pl.BlockSpec(memory_space=pltpu.VMEM)
    anywhere = pl.BlockSpec(memory_space=pl.ANY)
    return pl.pallas_call(
        kernel,
        out_shape=tuple(jax.ShapeDtypeStruct(*out) for out in outs),
        in_specs=[anywhere if at in far else whole for at in range(len(args))],
        out_specs=tuple(anywhere if outs_far else whole for _ in outs),
        scratch_shapes=scratch,
        compiler_params=pltpu.CompilerParams(vmem_limit_bytes=room * 2**20),
    )(*args)


def grouping(hidden, share):
    shape = (2 * hidden, 2 * hidden)
    rows = lax.broadcasted_iota(jnp.int32, shape, 0)
    columns = lax.broadcasted_iota(jnp.int32, shape, 1)
    group, within = rows // (2 * share), lax.rem(rows, 2 * share)
    side = within // share
    wanted = side * hidden + group * share + within - side * share
    return jnp.where(columns == wanted, 1.0, 0.0).astype(bf16)


def start_all(copies):
    for copy in copies:
        copy.start()


def wait_all(copies):
    for copy in copies:
        copy.wait()


def prepare(
    share, ga, pa, gb, pb, go, wo, pair_far, cotangent_far, out, normed, inverse, other,
    gates, values, last, pair, arrivals,
):
    hidden = go.shape[0]
    width = 2 * hidden
    count = pair.shape[0]
    core = lax.axis_index("ch")
    copies = []
    for at, (held, low, high) in enumerate(((gates, ga, gb), (values, pa, pb), (last, go, wo))):
        copies.append(pltpu.make_async_copy(low, held.at[0:hidden], arrivals.at[2 * at]))
        copies.append(pltpu.make_async_copy(high, held.at[hidden:width], arrivals.at[2 * at + 1]))
    fetch = pltpu.make_async_copy(pair_far.at[pl.ds(core * count, count)], pair, arrivals.at[6])
    cut = pltpu.make_async_copy(
        cotangent_far.at[pl.ds((1 - core) * count, count)], other, arrivals.at[7]
    )
    start_all(copies + [fetch, cut])
    order = grouping(hidden, share)
    wait_all(copies)
    out[:width] = dot(order, gates[...], (1, 0)).astype(bf16)
    out[width : 2 * width] = dot(order, values[...], (1, 0)).astype(bf16)
    out[2 * width :] = last[...]
    fetch.wait()
    hat, rstd = normalized(pair[...])
    normed[...] = hat.astype(bf16)
    inverse[...] = rstd
    cut.wait()


def rows_of(weights, start, count):
    return jnp.concatenate([weights[c, start : start + count] for c in range(weights.shape[0])], 0)


def normalized(pair):
    count, cols, channels = pair.shape
    values = pair.astype(f32).reshape(count * cols, channels).T
    centred = values - jnp.mean(values, 0, keepdims=True)
    rstd = lax.rsqrt(jnp.mean(centred * centred, 0, keepdims=True) + epsilon)
    return centred * rstd, rstd


def edges(width, normed, weights, send):
    gate = jax.nn.sigmoid(dot(rows_of(weights, 0, width), normed[...], (1, 0)))
    value = dot(rows_of(weights, width, width), normed[...], (1, 0))
    send[...] = (gate * value).reshape(send.shape).astype(bf16)


def spread_rows(block, cols, arrived, held):
    devices, q, flat = arrived.shape
    rows = flat // cols
    for s in range(devices):
        tile = arrived[s].astype(f32)
        for i in range(rows):
            start = (s * rows + i) * block
            held[start : start + q, 0:cols] = tile[:, i * cols : (i + 1) * cols]


def pack_rows(block, cols, held, send):
    devices, q, flat = send.shape
    rows = flat // cols
    for s in range(devices):
        starts = [(s * rows + i) * block for i in range(rows)]
        whole = jnp.concatenate([held[start : start + block, 0:cols] for start in starts], axis=1)
        send[s] = whole[:q].astype(bf16)


def square(block, parts, cols, held, e):
    tokens = parts * cols
    return jnp.concatenate(
        [
            held[pl.ds(p * tokens * block + e, tokens, stride=block), 0:cols]
            for p in range(parts)
        ],
        axis=1,
    ).astype(bf16)


def put_square(block, parts, cols, held, e, values):
    tokens = parts * cols
    for p in range(parts):
        held[pl.ds(p * tokens * block + e, tokens, stride=block), 0:cols] = values[
            :, p * cols : (p + 1) * cols
        ]


def mix(parts, cols, arrived, send, kept, held, result):
    block = 8
    q = arrived.shape[1]
    spread_rows(block, cols, arrived, held)
    for e in range(q // 2):
        left = square(block, parts, cols, held, e)
        right = square(block, parts, cols, held, q // 2 + e)
        kept[e] = left
        kept[q // 2 + e] = right
        put_square(block, parts, cols, result, e, dot(left, right, (1, 1)))
    pack_rows(block, cols, result, send)


def unmix(parts, cols, arrived, kept, send, held, result):
    block = 8
    q = arrived.shape[1]
    spread_rows(block, cols, arrived, held)
    for e in range(q):
        d_mixed = square(block, parts, cols, held, e)
        put_square(block, parts, cols, result, e, dot(d_mixed, kept[q + e], (1, 0)))
        put_square(block, parts, cols, result, q + e, dot(d_mixed, kept[e], (0, 0)))
    pack_rows(block, cols, result, send)


def split_rows(cols, values, own, other):
    hidden = values.shape[0] // 2
    first = lax.axis_index("ch") == 0
    low, high = values[:hidden], values[hidden:]
    mine = jnp.where(first, low, high)
    yours = jnp.where(first, high, low)
    for i in range(own.shape[0]):
        own[i] = mine[:, i * cols : (i + 1) * cols].astype(bf16)
        other[i] = yours[:, i * cols : (i + 1) * cols].astype(bf16)


def head(
    width, scale, arrived, weights, normed, cotangent, other,
    send, d_gate, terms, updated_own, updated_other,
    upstream,
):
    parts, total, _ = weights.shape
    hidden = (total - 2 * width) // 2
    devices, q, flat = arrived.shape
    count, _, cols = other.shape
    core = lax.axis_index("ch")
    mixed = jnp.concatenate([arrived[s].astype(f32) for s in range(devices)], 0)
    average = jnp.mean(mixed, 0, keepdims=True)
    spread = jnp.mean(mixed * mixed, 0, keepdims=True) - average * average
    inverse = lax.rsqrt(spread + epsilon)
    hat = (mixed - average) * inverse
    hat_rounded = hat.astype(bf16)
    w_out = rows_of(weights, 2 * width + hidden, hidden)
    proj = dot(w_out, hat_rounded, (1, 0))
    own = cotangent[pl.ds(core * count, count)]
    for part, side in ((own, core), (other[...], 1 - core)):
        upstream[pl.ds(pl.multiple_of(side * hidden, hidden), hidden)] = jnp.concatenate(
            [part[i].astype(f32) for i in range(count)], axis=1
        )
    gate = jax.nn.sigmoid(dot(rows_of(weights, 2 * width, hidden), normed[...], (1, 0)))
    up = upstream[...]
    d_proj = (up * gate).astype(bf16)
    d_gate[...] = (up * proj * gate * (1.0 - gate)).astype(bf16)
    d_norm = dot(w_out, d_proj, (0, 0))
    d_mixed = inverse * (
        d_norm
        - jnp.mean(d_norm, 0, keepdims=True)
        - hat * jnp.mean(d_norm * hat, 0, keepdims=True)
    )
    for s in range(devices):
        send[s] = d_mixed[s * q : (s + 1) * q].astype(bf16)
    by_gate = dot(d_gate[...], normed[...], (1, 1)) * scale
    by_out = dot(d_proj, hat_rounded, (1, 1)) * scale
    for c in range(parts):
        terms[c, :hidden] = by_gate[c * hidden : (c + 1) * hidden]
        terms[c, hidden:] = by_out[c * hidden : (c + 1) * hidden]
    split_rows(cols, gate * proj, updated_own, updated_other)


def tail(
    width, scale, cols, arrived, weights, pair_hat, inverse, d_gate, head_terms, updated_other,
    send, grad_own, others, whole,
):
    parts, total, channels = weights.shape
    hidden = (total - 2 * width) // 2
    devices, q, flat = arrived.shape
    others[0] = updated_other[...]
    normed = pair_hat[...]
    hat = normed.astype(f32)
    w_gate, w_value = rows_of(weights, 0, width), rows_of(weights, width, width)
    gate = jax.nn.sigmoid(dot(w_gate, normed, (1, 0)))
    value = dot(w_value, normed, (1, 0))
    grad = arrived[...].astype(f32).reshape(devices * q, flat)
    by_value = grad * gate
    by_gate = (by_value * (value * (1.0 - gate))).astype(bf16)
    by_value = by_value.astype(bf16)
    terms = [dot(by_gate, normed, (1, 1)) * scale, dot(by_value, normed, (1, 1)) * scale]
    for c in range(parts):
        for at, term in enumerate(terms):
            start = c * total + at * width
            whole[start : start + width] = term[c * width : (c + 1) * width]
        whole[c * total + 2 * width : (c + 1) * total] = head_terms[c]
    per = send.shape[1]
    for s in range(devices):
        send[s] = whole[s * per : (s + 1) * per].astype(bf16)
    d_input = dot(w_gate, by_gate, (0, 0)) + dot(w_value, by_value, (0, 0))
    d_input = d_input + dot(rows_of(weights, 2 * width, hidden), d_gate[...], (0, 0))
    back = inverse[...] * (
        d_input
        - jnp.mean(d_input, 0, keepdims=True)
        - hat * jnp.mean(d_input * hat, 0, keepdims=True)
    )
    split_rows(cols, back, grad_own, others.at[1])


def add_up(arrived, out):
    total = jnp.sum(arrived[...].astype(f32), 0).astype(bf16)
    for s in range(out.shape[0]):
        out[s] = total


def finish(share, sums, updated_own, grad_own, others, *refs):
    (updated, grad), outs, (whole, results, leaves) = refs[:2], refs[2:8], refs[8:]
    count = updated_own.shape[0]
    core = lax.axis_index("ch")
    here, there = pl.ds(core * count, count), pl.ds((1 - core) * count, count)
    joins = []
    for at, (own, out) in enumerate(((updated_own, updated), (grad_own, grad))):
        joins.append(pltpu.make_async_copy(own, out.at[here], leaves.at[2 * at]))
        joins.append(pltpu.make_async_copy(others.at[at], out.at[there], leaves.at[2 * at + 1]))
    start_all(joins)
    _, hidden, channels = results.shape
    width = 2 * hidden
    per = sums.shape[1]
    for s in range(sums.shape[0]):
        whole[s * per : (s + 1) * per] = sums[s].astype(f32)
    order = grouping(hidden, share)
    for at in range(2):
        both = dot(order, whole[at * width : (at + 1) * width].astype(bf16), (0, 0))
        results[at] = both[:hidden]
        results[2 + at] = both[hidden:]
    results[4] = whole[2 * width : 2 * width + hidden]
    results[5] = whole[2 * width + hidden :]
    copies = [
        pltpu.make_async_copy(results.at[at], out, leaves.at[4 + at]) for at, out in enumerate(outs)
    ]
    start_all(copies)
    wait_all(joins + copies)


def by_channels(pair, cotangent, w_gate_a, w_proj_a, w_gate_b, w_proj_b, w_gate_out, w_out):
    row_count, cols, channels = pair.shape
    hidden = w_gate_a.shape[1]
    parts, col_parts, row_parts = lax.axis_size("ch"), lax.axis_size("col"), lax.axis_size("row")
    devices = parts * col_parts * row_parts
    share = hidden * parts // devices
    width = 2 * hidden
    count = row_count // parts
    flat = count * cols
    tokens = cols * col_parts
    scale = 1.0 / tokens
    swap = [(c, parts - 1 - c) for c in range(parts)]
    weight = ((2 * width + 2 * hidden, channels), bf16)
    part = ((count, hidden, cols), bf16)
    own = jnp.swapaxes(cotangent, 1, 2)
    whole_weight = pltpu.VMEM((2 * hidden, channels), bf16)
    weights, normed, inverse, other = call(
        functools.partial(prepare, share),
        [weight, ((channels, flat), bf16), ((1, flat), f32), part],
        (w_gate_a.T, w_proj_a.T, w_gate_b.T, w_proj_b.T, w_gate_out.T, w_out.T, pair, own),
        (
            whole_weight,
            whole_weight,
            whole_weight,
            pltpu.VMEM((count, cols, channels), bf16),
            pltpu.SemaphoreType.DMA((8,)),
        ),
        far=range(8),
        room=60,
    )
    weights = lax.all_gather(weights, "ch")
    (send,) = call(
        functools.partial(edges, width), [((devices, 2 * share, flat), bf16)], (normed, weights)
    )
    arrived = lax.all_to_all(send, everyone, 0, 0)
    arrived, other = lax.optimization_barrier((arrived, other))
    other = lax.ppermute(other, "ch", swap)
    room = pltpu.VMEM((col_parts * tokens * 8, -(-cols // 128) * 128), f32)
    send, kept = call(
        functools.partial(mix, col_parts, cols),
        [((devices, share, flat), bf16), ((2 * share, tokens, tokens), bf16)],
        (arrived,),
        (room, room),
    )
    send, other = lax.optimization_barrier((send, other))
    arrived = lax.all_to_all(send, everyone, 0, 0)
    send, d_gate, head_terms, updated_own, updated_other = call(
        functools.partial(head, width, scale),
        [
            ((devices, share, flat), bf16),
            ((hidden * parts, flat), bf16),
            ((parts, 2 * hidden, channels), f32),
            part,
            part,
        ],
        (arrived, weights, normed, own, other),
        (pltpu.VMEM((hidden * parts, flat), f32),),
    )
    arrived = lax.all_to_all(send, everyone, 0, 0)
    (send,) = call(
        functools.partial(unmix, col_parts, cols),
        [((devices, 2 * share, flat), bf16)],
        (arrived, kept),
        (room, room),
    )
    arrived = lax.all_to_all(send, everyone, 0, 0)
    total = 2 * width + 2 * hidden
    per = total * parts // devices
    send, grad_own, others = call(
        functools.partial(tail, width, scale, cols),
        [((devices, per, channels), bf16), part, ((2, *part[0]), bf16)],
        (arrived, weights, normed, inverse, d_gate, head_terms, updated_other),
        (pltpu.VMEM((total * parts, channels), f32),),
    )
    arrived = lax.all_to_all(send, ("ch", "row", "col"), 0, 0)
    rest = devices // parts
    arrived, others = lax.optimization_barrier((arrived, others))
    (sums,) = call(add_up, [((rest, per, channels), bf16)], (arrived,))
    sums = lax.all_to_all(sums, ("row", "col"), 0, 0)
    updated, grad_pair, *grads = call(
        functools.partial(finish, share),
        [((row_count, hidden, cols), bf16)] * 2 + [((hidden, channels), f32)] * 6,
        (sums, updated_own, grad_own, lax.ppermute(others, "ch", swap)),
        (
            pltpu.VMEM((total, channels), f32),
            pltpu.VMEM((6, hidden, channels), f32),
            pltpu.SemaphoreType.DMA((10,)),
        ),
        (1, 2, 3),
        True,
    )
    return jnp.swapaxes(updated, 1, 2), jnp.swapaxes(grad_pair, 1, 2), *(g.T for g in grads)


def on_device(*arrays):
    row_count, cols, _ = arrays[0].shape
    parts, devices = lax.axis_size("ch"), lax.axis_size(everyone)
    hidden = arrays[2].shape[1]
    share = hidden * parts // devices
    fits = (
        share * devices == hidden * parts
        and parts == 2
        and 2 * share == 8
        and row_count % parts == 0
        and 6 * hidden * parts % devices == 0
        and arrays[1].shape[2] == hidden
        and cols % 16 == 0
    )
    return by_channels(*arrays) if fits else by_rows(*arrays)


def solution(mesh):
    in_specs = (
        P("row", "col", None),
        P("row", "col", "ch"),
        P(None, "ch"),
        P(None, "ch"),
        P(None, "ch"),
        P(None, "ch"),
        P(None, "ch"),
        P(None, "ch"),
    )
    out_specs = (
        P("row", "col", "ch"),
        P("row", "col", "ch"),
        P(None, "ch"),
        P(None, "ch"),
        P(None, "ch"),
        P(None, "ch"),
        P(None, "ch"),
        P(None, "ch"),
    )
    return jax.shard_map(
        on_device, mesh=mesh, in_specs=in_specs, out_specs=out_specs, check_vma=False
    )
```

```python
import functools

import jax
import jax.numpy as jnp
import numpy as np
from jax import lax
from jax.experimental import pallas as pl
from jax.experimental.pallas import tpu as pltpu
from jax.sharding import PartitionSpec as P

epsilon = 1e-05


def layer_norm(values):
    average = jnp.mean(values, -1, keepdims=True)
    centred = values - average
    spread = jnp.mean(centred * centred, -1, keepdims=True)
    inverse = lax.rsqrt(spread + epsilon)
    return (centred * inverse, inverse)


def matmul(first, second):
    return jnp.dot(first, second, preferred_element_type=jnp.float32)


def by_rows(pair, cotangent, w_gate_a, w_proj_a, w_gate_b, w_proj_b, w_gate_out, w_out):
    row_count, col_count, channels = pair.shape
    hidden = w_gate_a.shape[1]
    total_hidden = hidden * lax.axis_size("ch")
    out_width = cotangent.shape[2]
    length = row_count * lax.axis_size("row")
    grad_scale = 1.0 / length
    pair_hat, pair_rstd = layer_norm(pair.astype(jnp.float32))
    flat_norm = pair_hat.astype(jnp.bfloat16).reshape(row_count * col_count, channels)
    w_four = jnp.concatenate([w_gate_a, w_proj_a, w_gate_b, w_proj_b], axis=1)
    projected = matmul(flat_norm, w_four)
    gate_a = jax.nn.sigmoid(projected[:, :hidden])
    proj_a = projected[:, hidden : 2 * hidden]
    gate_b = jax.nn.sigmoid(projected[:, 2 * hidden : 3 * hidden])
    proj_b = projected[:, 3 * hidden :]
    left_edge = (gate_a * proj_a).astype(jnp.bfloat16).reshape(row_count, col_count, hidden)
    right_edge = (gate_b * proj_b).astype(jnp.bfloat16).reshape(row_count, col_count, hidden)
    right_all = lax.all_gather(right_edge, "row", axis=0, tiled=True)
    mixed_swap = lax.psum_scatter(
        jnp.einsum("jkh,ikh->jih", right_all, left_edge, preferred_element_type=jnp.float32).astype(
            jnp.bfloat16
        ),
        "col",
        scatter_dimension=0,
        tiled=True,
    ).astype(jnp.float32)
    mixed = jnp.swapaxes(mixed_swap, 0, 1).reshape(row_count * col_count, hidden)
    hidden_sums = lax.psum((jnp.sum(mixed, -1), jnp.sum(mixed * mixed, -1)), "ch")
    hidden_mean = (hidden_sums[0] / total_hidden)[:, None]
    hidden_var = (hidden_sums[1] / total_hidden)[:, None] - hidden_mean * hidden_mean
    hidden_rstd = lax.rsqrt(hidden_var + epsilon)
    mixed_hat = (mixed - hidden_mean) * hidden_rstd
    mixed_norm = mixed_hat.astype(jnp.bfloat16)
    norm_full = lax.all_gather(mixed_norm, "ch", axis=1, tiled=True)
    gate_out = jax.nn.sigmoid(matmul(flat_norm, w_gate_out))
    proj_out = matmul(norm_full, w_out)
    updated = (gate_out * proj_out).astype(jnp.bfloat16).reshape(row_count, col_count, out_width)
    upstream = cotangent.reshape(row_count * col_count, out_width).astype(jnp.float32)
    d_proj = (upstream * gate_out).astype(jnp.bfloat16)
    d_gate = (upstream * proj_out * gate_out * (1.0 - gate_out)).astype(jnp.bfloat16)
    head_grads = lax.psum(
        (matmul(norm_full.T, d_proj) * grad_scale, matmul(flat_norm.T, d_gate) * grad_scale),
        ("row", "col"),
    )
    d_norm = lax.psum_scatter(
        matmul(d_proj, w_out.T).astype(jnp.bfloat16), "ch", scatter_dimension=1, tiled=True
    ).astype(jnp.float32)
    back_sums = lax.psum((jnp.sum(d_norm, -1), jnp.sum(d_norm * mixed_hat, -1)), "ch")
    d_mixed = hidden_rstd * (
        d_norm
        - (back_sums[0] / total_hidden)[:, None]
        - mixed_hat * (back_sums[1] / total_hidden)[:, None]
    )
    d_mixed = d_mixed.astype(jnp.bfloat16).reshape(row_count, col_count, hidden)
    d_rows = lax.all_gather(d_mixed, "col", axis=1, tiled=True)
    right_back = lax.all_gather(right_edge, "row", axis=0, tiled=True)
    d_left = jnp.einsum("ijh,jkh->ikh", d_rows, right_back, preferred_element_type=jnp.float32)
    d_left = d_left.reshape(row_count * col_count, hidden)
    left_all = lax.all_gather(left_edge, "row", axis=0, tiled=True)
    d_columns = lax.all_to_all(d_rows, "row", split_axis=1, concat_axis=0, tiled=True)
    d_right = jnp.einsum("ijh,ikh->jkh", d_columns, left_all, preferred_element_type=jnp.float32)
    d_right = d_right.reshape(row_count * col_count, hidden)
    grad_pa = (d_left * gate_a).astype(jnp.bfloat16)
    grad_ga = (d_left * proj_a * gate_a * (1.0 - gate_a)).astype(jnp.bfloat16)
    grad_pb = (d_right * gate_b).astype(jnp.bfloat16)
    grad_gb = (d_right * proj_b * gate_b * (1.0 - gate_b)).astype(jnp.bfloat16)
    d_four = jnp.concatenate([grad_ga, grad_pa, grad_gb, grad_pb], axis=1)
    weight_terms = matmul(flat_norm.T, d_four) * grad_scale
    summed = lax.psum(weight_terms, ("row", "col"))
    d_flat = matmul(d_four, w_four.T) + matmul(d_gate, w_gate_out.T)
    hat_all = pair_hat.reshape(row_count * col_count, channels)
    rstd_flat = pair_rstd.reshape(row_count * col_count, 1)
    offset = lax.axis_index("ch") * out_width
    grad_whole = lax.psum(d_flat.astype(jnp.bfloat16), "ch").astype(jnp.float32)
    grad_full = rstd_flat * (
        grad_whole
        - jnp.mean(grad_whole, -1, keepdims=True)
        - hat_all * jnp.mean(grad_whole * hat_all, -1, keepdims=True)
    )
    grad_pair = lax.dynamic_slice_in_dim(grad_full, offset, out_width, 1)
    grad_pair = grad_pair.astype(jnp.bfloat16).reshape(row_count, col_count, out_width)
    return (
        updated,
        grad_pair,
        summed[:, :hidden],
        summed[:, hidden : 2 * hidden],
        summed[:, 2 * hidden : 3 * hidden],
        summed[:, 3 * hidden :],
        head_grads[1],
        head_grads[0],
    )


everyone = ("col", "row", "ch")
f32, bf16 = jnp.float32, jnp.bfloat16


def dot(first, second, over):
    return lax.dot_general(
        first, second, (((over[0],), (over[1],)), ((), ())), preferred_element_type=f32
    )


def call(kernel, outs, args, scratch=(), far=(), outs_far=False, room=16):
    whole = pl.BlockSpec(memory_space=pltpu.VMEM)
    anywhere = pl.BlockSpec(memory_space=pl.ANY)
    return pl.pallas_call(
        kernel,
        out_shape=tuple(jax.ShapeDtypeStruct(*out) for out in outs),
        in_specs=[anywhere if at in far else whole for at in range(len(args))],
        out_specs=tuple(anywhere if outs_far else whole for _ in outs),
        scratch_shapes=scratch,
        compiler_params=pltpu.CompilerParams(vmem_limit_bytes=room * 2**20),
    )(*args)


def grouping(hidden, share):
    shape = (2 * hidden, 2 * hidden)
    rows = lax.broadcasted_iota(jnp.int32, shape, 0)
    columns = lax.broadcasted_iota(jnp.int32, shape, 1)
    group, within = rows // (2 * share), lax.rem(rows, 2 * share)
    side = within // share
    wanted = side * hidden + group * share + within - side * share
    return jnp.where(columns == wanted, 1.0, 0.0).astype(bf16)


def start_all(copies):
    for copy in copies:
        copy.start()


def wait_all(copies):
    for copy in copies:
        copy.wait()


def prepare(
    share, ga, pa, gb, pb, go, wo, pair_far, cotangent_far, out, normed, inverse, other,
    gates, values, last, pair, arrivals,
):
    hidden = go.shape[0]
    width = 2 * hidden
    count = pair.shape[0]
    core = lax.axis_index("ch")
    copies = []
    for at, (held, low, high) in enumerate(((gates, ga, gb), (values, pa, pb), (last, go, wo))):
        copies.append(pltpu.make_async_copy(low, held.at[0:hidden], arrivals.at[2 * at]))
        copies.append(pltpu.make_async_copy(high, held.at[hidden:width], arrivals.at[2 * at + 1]))
    fetch = pltpu.make_async_copy(pair_far.at[pl.ds(core * count, count)], pair, arrivals.at[6])
    cut = pltpu.make_async_copy(
        cotangent_far.at[pl.ds((1 - core) * count, count)], other, arrivals.at[7]
    )
    start_all(copies + [fetch, cut])
    order = grouping(hidden, share)
    wait_all(copies)
    out[:width] = dot(order, gates[...], (1, 0)).astype(bf16)
    out[width : 2 * width] = dot(order, values[...], (1, 0)).astype(bf16)
    out[2 * width :] = last[...]
    fetch.wait()
    hat, rstd = normalized(pair[...])
    normed[...] = hat.astype(bf16)
    inverse[...] = rstd
    cut.wait()


def rows_of(weights, start, count):
    return jnp.concatenate([weights[c, start : start + count] for c in range(weights.shape[0])], 0)


def normalized(pair):
    count, cols, channels = pair.shape
    values = pair.astype(f32).reshape(count * cols, channels).T
    centred = values - jnp.mean(values, 0, keepdims=True)
    rstd = lax.rsqrt(jnp.mean(centred * centred, 0, keepdims=True) + epsilon)
    return centred * rstd, rstd


def edges(width, normed, weights, inverse, send, inverse_on):
    inverse_on[...] = inverse[...]
    gate = jax.nn.sigmoid(dot(rows_of(weights, 0, width), normed[...], (1, 0)))
    value = dot(rows_of(weights, width, width), normed[...], (1, 0))
    send[...] = (gate * value).reshape(send.shape).astype(bf16)


def spread_rows(block, cols, arrived, held):
    devices, q, flat = arrived.shape
    rows = flat // cols
    for s in range(devices):
        tile = arrived[s].astype(f32)
        for i in range(rows):
            start = (s * rows + i) * block
            held[start : start + q, 0:cols] = tile[:, i * cols : (i + 1) * cols]


def pack_rows(block, cols, held, send):
    devices, q, flat = send.shape
    rows = flat // cols
    for s in range(devices):
        starts = [(s * rows + i) * block for i in range(rows)]
        whole = jnp.concatenate([held[start : start + block, 0:cols] for start in starts], axis=1)
        send[s] = whole[:q].astype(bf16)


def square(block, parts, cols, held, e):
    tokens = parts * cols
    return jnp.concatenate(
        [
            held[pl.ds(p * tokens * block + e, tokens, stride=block), 0:cols]
            for p in range(parts)
        ],
        axis=1,
    ).astype(bf16)


def put_square(block, parts, cols, held, e, values):
    tokens = parts * cols
    for p in range(parts):
        held[pl.ds(p * tokens * block + e, tokens, stride=block), 0:cols] = values[
            :, p * cols : (p + 1) * cols
        ]


def mix(parts, cols, arrived, send, kept, held, result):
    block = 8
    q = arrived.shape[1]
    spread_rows(block, cols, arrived, held)
    for e in range(q // 2):
        left = square(block, parts, cols, held, e)
        right = square(block, parts, cols, held, q // 2 + e)
        kept[e] = left
        kept[q // 2 + e] = right
        put_square(block, parts, cols, result, e, dot(left, right, (1, 1)))
    pack_rows(block, cols, result, send)


def unmix(parts, cols, arrived, kept_far, send, held, result, kept, arrival):
    block = 8
    q = arrived.shape[1]
    copy = pltpu.make_async_copy(kept_far, kept, arrival)
    copy.start()
    spread_rows(block, cols, arrived, held)
    copy.wait()
    for e in range(q):
        d_mixed = square(block, parts, cols, held, e)
        put_square(block, parts, cols, result, e, dot(d_mixed, kept[q + e], (1, 0)))
        put_square(block, parts, cols, result, q + e, dot(d_mixed, kept[e], (0, 0)))
    pack_rows(block, cols, result, send)


def split_rows(cols, values, own, other):
    hidden = values.shape[0] // 2
    first = lax.axis_index("ch") == 0
    low, high = values[:hidden], values[hidden:]
    mine = jnp.where(first, low, high)
    yours = jnp.where(first, high, low)
    for i in range(own.shape[0]):
        own[i] = mine[:, i * cols : (i + 1) * cols].astype(bf16)
        other[i] = yours[:, i * cols : (i + 1) * cols].astype(bf16)


def head(
    width, scale, arrived, weights, normed, cotangent, other,
    send, d_gate, terms, updated_own, updated_other,
    upstream,
):
    parts, total, _ = weights.shape
    hidden = (total - 2 * width) // 2
    devices, q, flat = arrived.shape
    count, _, cols = other.shape
    core = lax.axis_index("ch")
    mixed = jnp.concatenate([arrived[s].astype(f32) for s in range(devices)], 0)
    average = jnp.mean(mixed, 0, keepdims=True)
    spread = jnp.mean(mixed * mixed, 0, keepdims=True) - average * average
    inverse = lax.rsqrt(spread + epsilon)
    hat = (mixed - average) * inverse
    hat_rounded = hat.astype(bf16)
    w_out = rows_of(weights, 2 * width + hidden, hidden)
    proj = dot(w_out, hat_rounded, (1, 0))
    own = cotangent[pl.ds(core * count, count)]
    for part, side in ((own, core), (other[...], 1 - core)):
        upstream[pl.ds(pl.multiple_of(side * hidden, hidden), hidden)] = jnp.concatenate(
            [part[i].astype(f32) for i in range(count)], axis=1
        )
    gate = jax.nn.sigmoid(dot(rows_of(weights, 2 * width, hidden), normed[...], (1, 0)))
    up = upstream[...]
    d_proj = (up * gate).astype(bf16)
    d_gate[...] = (up * proj * gate * (1.0 - gate)).astype(bf16)
    d_norm = dot(w_out, d_proj, (0, 0))
    d_mixed = inverse * (
        d_norm
        - jnp.mean(d_norm, 0, keepdims=True)
        - hat * jnp.mean(d_norm * hat, 0, keepdims=True)
    )
    for s in range(devices):
        send[s] = d_mixed[s * q : (s + 1) * q].astype(bf16)
    by_gate = dot(d_gate[...], normed[...], (1, 1)) * scale
    by_out = dot(d_proj, hat_rounded, (1, 1)) * scale
    for c in range(parts):
        terms[c, :hidden] = by_gate[c * hidden : (c + 1) * hidden]
        terms[c, hidden:] = by_out[c * hidden : (c + 1) * hidden]
    split_rows(cols, gate * proj, updated_own, updated_other)


def tail(
    width, scale, cols, arrived, weights, pair_hat, inverse, d_gate, head_terms, updated_other,
    send, grad_own, others, whole,
):
    parts, total, channels = weights.shape
    hidden = (total - 2 * width) // 2
    devices, q, flat = arrived.shape
    others[0] = updated_other[...]
    normed = pair_hat[...]
    hat = normed.astype(f32)
    w_gate, w_value = rows_of(weights, 0, width), rows_of(weights, width, width)
    gate = jax.nn.sigmoid(dot(w_gate, normed, (1, 0)))
    value = dot(w_value, normed, (1, 0))
    grad = arrived[...].astype(f32).reshape(devices * q, flat)
    by_value = grad * gate
    by_gate = (by_value * (value * (1.0 - gate))).astype(bf16)
    by_value = by_value.astype(bf16)
    terms = [dot(by_gate, normed, (1, 1)) * scale, dot(by_value, normed, (1, 1)) * scale]
    for c in range(parts):
        for at, term in enumerate(terms):
            start = c * total + at * width
            whole[start : start + width] = term[c * width : (c + 1) * width]
        whole[c * total + 2 * width : (c + 1) * total] = head_terms[c]
    per = send.shape[1]
    for s in range(devices):
        send[s] = whole[s * per : (s + 1) * per].astype(bf16)
    d_input = dot(w_gate, by_gate, (0, 0)) + dot(w_value, by_value, (0, 0))
    d_input = d_input + dot(rows_of(weights, 2 * width, hidden), d_gate[...], (0, 0))
    back = inverse[...] * (
        d_input
        - jnp.mean(d_input, 0, keepdims=True)
        - hat * jnp.mean(d_input * hat, 0, keepdims=True)
    )
    split_rows(cols, back, grad_own, others.at[1])


def add_up(arrived, out):
    total = jnp.sum(arrived[...].astype(f32), 0).astype(bf16)
    for s in range(out.shape[0]):
        out[s] = total


def finish(share, sums, updated_own, grad_own, others, *refs):
    (updated, grad), outs, (whole, results, leaves) = refs[:2], refs[2:8], refs[8:]
    count = updated_own.shape[0]
    core = lax.axis_index("ch")
    here, there = pl.ds(core * count, count), pl.ds((1 - core) * count, count)
    joins = []
    for at, (own, out) in enumerate(((updated_own, updated), (grad_own, grad))):
        joins.append(pltpu.make_async_copy(own, out.at[here], leaves.at[2 * at]))
        joins.append(pltpu.make_async_copy(others.at[at], out.at[there], leaves.at[2 * at + 1]))
    start_all(joins)
    _, hidden, channels = results.shape
    width = 2 * hidden
    per = sums.shape[1]
    for s in range(sums.shape[0]):
        whole[s * per : (s + 1) * per] = sums[s].astype(f32)
    order = grouping(hidden, share)
    for at in range(2):
        both = dot(order, whole[at * width : (at + 1) * width].astype(bf16), (0, 0))
        results[at] = both[:hidden]
        results[2 + at] = both[hidden:]
    results[4] = whole[2 * width : 2 * width + hidden]
    results[5] = whole[2 * width + hidden :]
    copies = [
        pltpu.make_async_copy(results.at[at], out, leaves.at[4 + at]) for at, out in enumerate(outs)
    ]
    start_all(copies)
    wait_all(joins + copies)


def by_channels(pair, cotangent, w_gate_a, w_proj_a, w_gate_b, w_proj_b, w_gate_out, w_out):
    row_count, cols, channels = pair.shape
    hidden = w_gate_a.shape[1]
    parts, col_parts, row_parts = lax.axis_size("ch"), lax.axis_size("col"), lax.axis_size("row")
    devices = parts * col_parts * row_parts
    share = hidden * parts // devices
    width = 2 * hidden
    count = row_count // parts
    flat = count * cols
    tokens = cols * col_parts
    scale = 1.0 / tokens
    swap = [(c, parts - 1 - c) for c in range(parts)]
    weight = ((2 * width + 2 * hidden, channels), bf16)
    part = ((count, hidden, cols), bf16)
    own = jnp.swapaxes(cotangent, 1, 2)
    whole_weight = pltpu.VMEM((2 * hidden, channels), bf16)
    weights, normed, inverse, other = call(
        functools.partial(prepare, share),
        [weight, ((channels, flat), bf16), ((1, flat), f32), part],
        (w_gate_a.T, w_proj_a.T, w_gate_b.T, w_proj_b.T, w_gate_out.T, w_out.T, pair, own),
        (
            whole_weight,
            whole_weight,
            whole_weight,
            pltpu.VMEM((count, cols, channels), bf16),
            pltpu.SemaphoreType.DMA((8,)),
        ),
        far=range(8),
        room=60,
    )
    weights = lax.all_gather(weights, "ch")
    send, inverse = call(
        functools.partial(edges, width),
        [((devices, 2 * share, flat), bf16), ((1, flat), f32)],
        (normed, weights, inverse),
    )
    arrived = lax.all_to_all(send, everyone, 0, 0)
    arrived, other = lax.optimization_barrier((arrived, other))
    other = lax.ppermute(other, "ch", swap)
    room = pltpu.VMEM((col_parts * tokens * 8, -(-cols // 128) * 128), f32)
    send, kept = call(
        functools.partial(mix, col_parts, cols),
        [((devices, share, flat), bf16), ((2 * share, tokens, tokens), bf16)],
        (arrived,),
        (room, room),
    )
    send, other = lax.optimization_barrier((send, other))
    arrived = lax.all_to_all(send, everyone, 0, 0)
    send, d_gate, head_terms, updated_own, updated_other = call(
        functools.partial(head, width, scale),
        [
            ((devices, share, flat), bf16),
            ((hidden * parts, flat), bf16),
            ((parts, 2 * hidden, channels), f32),
            part,
            part,
        ],
        (arrived, weights, normed, own, other),
        (pltpu.VMEM((hidden * parts, flat), f32),),
    )
    arrived = lax.all_to_all(send, everyone, 0, 0)
    (send,) = call(
        functools.partial(unmix, col_parts, cols),
        [((devices, 2 * share, flat), bf16)],
        (arrived, kept),
        (room, room, pltpu.VMEM(kept.shape, bf16), pltpu.SemaphoreType.DMA),
        far=(1,),
    )
    arrived = lax.all_to_all(send, everyone, 0, 0)
    total = 2 * width + 2 * hidden
    per = total * parts // devices
    send, grad_own, others = call(
        functools.partial(tail, width, scale, cols),
        [((devices, per, channels), bf16), part, ((2, *part[0]), bf16)],
        (arrived, weights, normed, inverse, d_gate, head_terms, updated_other),
        (pltpu.VMEM((total * parts, channels), f32),),
    )
    arrived = lax.all_to_all(send, ("ch", "row", "col"), 0, 0)
    rest = devices // parts
    arrived, others = lax.optimization_barrier((arrived, others))
    (sums,) = call(add_up, [((rest, per, channels), bf16)], (arrived,))
    sums = lax.all_to_all(sums, ("row", "col"), 0, 0)
    updated, grad_pair, *grads = call(
        functools.partial(finish, share),
        [((row_count, hidden, cols), bf16)] * 2 + [((hidden, channels), f32)] * 6,
        (sums, updated_own, grad_own, lax.ppermute(others, "ch", swap)),
        (
            pltpu.VMEM((total, channels), f32),
            pltpu.VMEM((6, hidden, channels), f32),
            pltpu.SemaphoreType.DMA((10,)),
        ),
        (1, 2, 3),
        True,
    )
    return jnp.swapaxes(updated, 1, 2), jnp.swapaxes(grad_pair, 1, 2), *(g.T for g in grads)


def on_device(*arrays):
    row_count, cols, _ = arrays[0].shape
    parts, devices = lax.axis_size("ch"), lax.axis_size(everyone)
    hidden = arrays[2].shape[1]
    share = hidden * parts // devices
    fits = (
        share * devices == hidden * parts
        and parts == 2
        and 2 * share == 8
        and row_count % parts == 0
        and 6 * hidden * parts % devices == 0
        and arrays[1].shape[2] == hidden
        and cols % 16 == 0
    )
    return by_channels(*arrays) if fits else by_rows(*arrays)


def solution(mesh):
    in_specs = (
        P("row", "col", None),
        P("row", "col", "ch"),
        P(None, "ch"),
        P(None, "ch"),
        P(None, "ch"),
        P(None, "ch"),
        P(None, "ch"),
        P(None, "ch"),
    )
    out_specs = (
        P("row", "col", "ch"),
        P("row", "col", "ch"),
        P(None, "ch"),
        P(None, "ch"),
        P(None, "ch"),
        P(None, "ch"),
        P(None, "ch"),
        P(None, "ch"),
    )
    return jax.shard_map(
        on_device, mesh=mesh, in_specs=in_specs, out_specs=out_specs, check_vma=False
    )
```

```python
import functools

import jax
import jax.numpy as jnp
import numpy as np
from jax import lax
from jax.experimental import pallas as pl
from jax.experimental.pallas import tpu as pltpu
from jax.sharding import PartitionSpec as P

epsilon = 1e-05


def layer_norm(values):
    average = jnp.mean(values, -1, keepdims=True)
    centred = values - average
    spread = jnp.mean(centred * centred, -1, keepdims=True)
    inverse = lax.rsqrt(spread + epsilon)
    return (centred * inverse, inverse)


def matmul(first, second):
    return jnp.dot(first, second, preferred_element_type=jnp.float32)


def by_rows(pair, cotangent, w_gate_a, w_proj_a, w_gate_b, w_proj_b, w_gate_out, w_out):
    row_count, col_count, channels = pair.shape
    hidden = w_gate_a.shape[1]
    total_hidden = hidden * lax.axis_size("ch")
    out_width = cotangent.shape[2]
    length = row_count * lax.axis_size("row")
    grad_scale = 1.0 / length
    pair_hat, pair_rstd = layer_norm(pair.astype(jnp.float32))
    flat_norm = pair_hat.astype(jnp.bfloat16).reshape(row_count * col_count, channels)
    w_four = jnp.concatenate([w_gate_a, w_proj_a, w_gate_b, w_proj_b], axis=1)
    projected = matmul(flat_norm, w_four)
    gate_a = jax.nn.sigmoid(projected[:, :hidden])
    proj_a = projected[:, hidden : 2 * hidden]
    gate_b = jax.nn.sigmoid(projected[:, 2 * hidden : 3 * hidden])
    proj_b = projected[:, 3 * hidden :]
    left_edge = (gate_a * proj_a).astype(jnp.bfloat16).reshape(row_count, col_count, hidden)
    right_edge = (gate_b * proj_b).astype(jnp.bfloat16).reshape(row_count, col_count, hidden)
    right_all = lax.all_gather(right_edge, "row", axis=0, tiled=True)
    mixed_swap = lax.psum_scatter(
        jnp.einsum("jkh,ikh->jih", right_all, left_edge, preferred_element_type=jnp.float32).astype(
            jnp.bfloat16
        ),
        "col",
        scatter_dimension=0,
        tiled=True,
    ).astype(jnp.float32)
    mixed = jnp.swapaxes(mixed_swap, 0, 1).reshape(row_count * col_count, hidden)
    hidden_sums = lax.psum((jnp.sum(mixed, -1), jnp.sum(mixed * mixed, -1)), "ch")
    hidden_mean = (hidden_sums[0] / total_hidden)[:, None]
    hidden_var = (hidden_sums[1] / total_hidden)[:, None] - hidden_mean * hidden_mean
    hidden_rstd = lax.rsqrt(hidden_var + epsilon)
    mixed_hat = (mixed - hidden_mean) * hidden_rstd
    mixed_norm = mixed_hat.astype(jnp.bfloat16)
    norm_full = lax.all_gather(mixed_norm, "ch", axis=1, tiled=True)
    gate_out = jax.nn.sigmoid(matmul(flat_norm, w_gate_out))
    proj_out = matmul(norm_full, w_out)
    updated = (gate_out * proj_out).astype(jnp.bfloat16).reshape(row_count, col_count, out_width)
    upstream = cotangent.reshape(row_count * col_count, out_width).astype(jnp.float32)
    d_proj = (upstream * gate_out).astype(jnp.bfloat16)
    d_gate = (upstream * proj_out * gate_out * (1.0 - gate_out)).astype(jnp.bfloat16)
    head_grads = lax.psum(
        (matmul(norm_full.T, d_proj) * grad_scale, matmul(flat_norm.T, d_gate) * grad_scale),
        ("row", "col"),
    )
    d_norm = lax.psum_scatter(
        matmul(d_proj, w_out.T).astype(jnp.bfloat16), "ch", scatter_dimension=1, tiled=True
    ).astype(jnp.float32)
    back_sums = lax.psum((jnp.sum(d_norm, -1), jnp.sum(d_norm * mixed_hat, -1)), "ch")
    d_mixed = hidden_rstd * (
        d_norm
        - (back_sums[0] / total_hidden)[:, None]
        - mixed_hat * (back_sums[1] / total_hidden)[:, None]
    )
    d_mixed = d_mixed.astype(jnp.bfloat16).reshape(row_count, col_count, hidden)
    d_rows = lax.all_gather(d_mixed, "col", axis=1, tiled=True)
    right_back = lax.all_gather(right_edge, "row", axis=0, tiled=True)
    d_left = jnp.einsum("ijh,jkh->ikh", d_rows, right_back, preferred_element_type=jnp.float32)
    d_left = d_left.reshape(row_count * col_count, hidden)
    left_all = lax.all_gather(left_edge, "row", axis=0, tiled=True)
    d_columns = lax.all_to_all(d_rows, "row", split_axis=1, concat_axis=0, tiled=True)
    d_right = jnp.einsum("ijh,ikh->jkh", d_columns, left_all, preferred_element_type=jnp.float32)
    d_right = d_right.reshape(row_count * col_count, hidden)
    grad_pa = (d_left * gate_a).astype(jnp.bfloat16)
    grad_ga = (d_left * proj_a * gate_a * (1.0 - gate_a)).astype(jnp.bfloat16)
    grad_pb = (d_right * gate_b).astype(jnp.bfloat16)
    grad_gb = (d_right * proj_b * gate_b * (1.0 - gate_b)).astype(jnp.bfloat16)
    d_four = jnp.concatenate([grad_ga, grad_pa, grad_gb, grad_pb], axis=1)
    weight_terms = matmul(flat_norm.T, d_four) * grad_scale
    summed = lax.psum(weight_terms, ("row", "col"))
    d_flat = matmul(d_four, w_four.T) + matmul(d_gate, w_gate_out.T)
    hat_all = pair_hat.reshape(row_count * col_count, channels)
    rstd_flat = pair_rstd.reshape(row_count * col_count, 1)
    offset = lax.axis_index("ch") * out_width
    grad_whole = lax.psum(d_flat.astype(jnp.bfloat16), "ch").astype(jnp.float32)
    grad_full = rstd_flat * (
        grad_whole
        - jnp.mean(grad_whole, -1, keepdims=True)
        - hat_all * jnp.mean(grad_whole * hat_all, -1, keepdims=True)
    )
    grad_pair = lax.dynamic_slice_in_dim(grad_full, offset, out_width, 1)
    grad_pair = grad_pair.astype(jnp.bfloat16).reshape(row_count, col_count, out_width)
    return (
        updated,
        grad_pair,
        summed[:, :hidden],
        summed[:, hidden : 2 * hidden],
        summed[:, 2 * hidden : 3 * hidden],
        summed[:, 3 * hidden :],
        head_grads[1],
        head_grads[0],
    )


everyone = ("col", "row", "ch")
f32, bf16 = jnp.float32, jnp.bfloat16


def dot(first, second, over):
    return lax.dot_general(
        first, second, (((over[0],), (over[1],)), ((), ())), preferred_element_type=f32
    )


def call(kernel, outs, args, scratch=(), far=(), outs_far=False, room=16):
    whole = pl.BlockSpec(memory_space=pltpu.VMEM)
    anywhere = pl.BlockSpec(memory_space=pl.ANY)
    return pl.pallas_call(
        kernel,
        out_shape=tuple(jax.ShapeDtypeStruct(*out) for out in outs),
        in_specs=[anywhere if at in far else whole for at in range(len(args))],
        out_specs=tuple(anywhere if outs_far else whole for _ in outs),
        scratch_shapes=scratch,
        compiler_params=pltpu.CompilerParams(vmem_limit_bytes=room * 2**20),
    )(*args)


def grouping(hidden, share):
    shape = (2 * hidden, 2 * hidden)
    rows = lax.broadcasted_iota(jnp.int32, shape, 0)
    columns = lax.broadcasted_iota(jnp.int32, shape, 1)
    group, within = rows // (2 * share), lax.rem(rows, 2 * share)
    side = within // share
    wanted = side * hidden + group * share + within - side * share
    return jnp.where(columns == wanted, 1.0, 0.0).astype(bf16)


def start_all(copies):
    for copy in copies:
        copy.start()


def wait_all(copies):
    for copy in copies:
        copy.wait()


def prepare(
    share, ga, pa, gb, pb, go, wo, pair_far, cotangent_far, out, normed, inverse, other,
    gates, values, last, pair, arrivals,
):
    hidden = go.shape[0]
    width = 2 * hidden
    count = pair.shape[0]
    core = lax.axis_index("ch")
    copies = []
    for at, (held, low, high) in enumerate(((gates, ga, gb), (values, pa, pb), (last, go, wo))):
        copies.append(pltpu.make_async_copy(low, held.at[0:hidden], arrivals.at[2 * at]))
        copies.append(pltpu.make_async_copy(high, held.at[hidden:width], arrivals.at[2 * at + 1]))
    fetch = pltpu.make_async_copy(pair_far.at[pl.ds(core * count, count)], pair, arrivals.at[6])
    cut = pltpu.make_async_copy(
        cotangent_far.at[pl.ds((1 - core) * count, count)], other, arrivals.at[7]
    )
    start_all(copies + [fetch, cut])
    order = grouping(hidden, share)
    wait_all(copies)
    out[:width] = dot(order, gates[...], (1, 0)).astype(bf16)
    out[width : 2 * width] = dot(order, values[...], (1, 0)).astype(bf16)
    out[2 * width :] = last[...]
    fetch.wait()
    hat, rstd = normalized(pair[...])
    normed[...] = hat.astype(bf16)
    inverse[...] = rstd
    cut.wait()


def rows_of(weights, start, count):
    return jnp.concatenate([weights[c, start : start + count] for c in range(weights.shape[0])], 0)


def normalized(pair):
    count, cols, channels = pair.shape
    values = pair.astype(f32).reshape(count * cols, channels).T
    centred = values - jnp.mean(values, 0, keepdims=True)
    rstd = lax.rsqrt(jnp.mean(centred * centred, 0, keepdims=True) + epsilon)
    return centred * rstd, rstd


def edges(width, normed, weights, send):
    gate = jax.nn.sigmoid(dot(rows_of(weights, 0, width), normed[...], (1, 0)))
    value = dot(rows_of(weights, width, width), normed[...], (1, 0))
    send[...] = (gate * value).reshape(send.shape).astype(bf16)


def spread_rows(block, cols, arrived, held):
    devices, q, flat = arrived.shape
    rows = flat // cols
    for s in range(devices):
        tile = arrived[s].astype(f32)
        for i in range(rows):
            start = (s * rows + i) * block
            held[start : start + q, 0:cols] = tile[:, i * cols : (i + 1) * cols]


def pack_rows(block, cols, held, send):
    devices, q, flat = send.shape
    rows = flat // cols
    for s in range(devices):
        starts = [(s * rows + i) * block for i in range(rows)]
        whole = jnp.concatenate([held[start : start + block, 0:cols] for start in starts], axis=1)
        send[s] = whole[:q].astype(bf16)


def square(block, parts, cols, held, e):
    tokens = parts * cols
    return jnp.concatenate(
        [
            held[pl.ds(p * tokens * block + e, tokens, stride=block), 0:cols]
            for p in range(parts)
        ],
        axis=1,
    ).astype(bf16)


def put_square(block, parts, cols, held, e, values):
    tokens = parts * cols
    for p in range(parts):
        held[pl.ds(p * tokens * block + e, tokens, stride=block), 0:cols] = values[
            :, p * cols : (p + 1) * cols
        ]


def mix(parts, cols, arrived, inverse, send, kept, inverse_on, held, result):
    inverse_on[...] = inverse[...]
    block = 8
    q = arrived.shape[1]
    spread_rows(block, cols, arrived, held)
    for e in range(q // 2):
        left = square(block, parts, cols, held, e)
        right = square(block, parts, cols, held, q // 2 + e)
        kept[e] = left
        kept[q // 2 + e] = right
        put_square(block, parts, cols, result, e, dot(left, right, (1, 1)))
    pack_rows(block, cols, result, send)


def unmix(parts, cols, arrived, kept_far, send, held, result, kept, arrival):
    block = 8
    q = arrived.shape[1]
    copy = pltpu.make_async_copy(kept_far, kept, arrival)
    copy.start()
    spread_rows(block, cols, arrived, held)
    copy.wait()
    for e in range(q):
        d_mixed = square(block, parts, cols, held, e)
        put_square(block, parts, cols, result, e, dot(d_mixed, kept[q + e], (1, 0)))
        put_square(block, parts, cols, result, q + e, dot(d_mixed, kept[e], (0, 0)))
    pack_rows(block, cols, result, send)


def split_rows(cols, values, own, other):
    hidden = values.shape[0] // 2
    first = lax.axis_index("ch") == 0
    low, high = values[:hidden], values[hidden:]
    mine = jnp.where(first, low, high)
    yours = jnp.where(first, high, low)
    for i in range(own.shape[0]):
        own[i] = mine[:, i * cols : (i + 1) * cols].astype(bf16)
        other[i] = yours[:, i * cols : (i + 1) * cols].astype(bf16)


def head(
    width, scale, arrived, weights, normed, cotangent, other,
    send, d_gate, terms, updated_own, updated_other,
    upstream,
):
    parts, total, _ = weights.shape
    hidden = (total - 2 * width) // 2
    devices, q, flat = arrived.shape
    count, _, cols = other.shape
    core = lax.axis_index("ch")
    mixed = jnp.concatenate([arrived[s].astype(f32) for s in range(devices)], 0)
    average = jnp.mean(mixed, 0, keepdims=True)
    spread = jnp.mean(mixed * mixed, 0, keepdims=True) - average * average
    inverse = lax.rsqrt(spread + epsilon)
    hat = (mixed - average) * inverse
    hat_rounded = hat.astype(bf16)
    w_out = rows_of(weights, 2 * width + hidden, hidden)
    proj = dot(w_out, hat_rounded, (1, 0))
    own = cotangent[pl.ds(core * count, count)]
    for part, side in ((own, core), (other[...], 1 - core)):
        upstream[pl.ds(pl.multiple_of(side * hidden, hidden), hidden)] = jnp.concatenate(
            [part[i].astype(f32) for i in range(count)], axis=1
        )
    gate = jax.nn.sigmoid(dot(rows_of(weights, 2 * width, hidden), normed[...], (1, 0)))
    up = upstream[...]
    d_proj = (up * gate).astype(bf16)
    d_gate[...] = (up * proj * gate * (1.0 - gate)).astype(bf16)
    d_norm = dot(w_out, d_proj, (0, 0))
    d_mixed = inverse * (
        d_norm
        - jnp.mean(d_norm, 0, keepdims=True)
        - hat * jnp.mean(d_norm * hat, 0, keepdims=True)
    )
    for s in range(devices):
        send[s] = d_mixed[s * q : (s + 1) * q].astype(bf16)
    by_gate = dot(d_gate[...], normed[...], (1, 1)) * scale
    by_out = dot(d_proj, hat_rounded, (1, 1)) * scale
    for c in range(parts):
        terms[c, :hidden] = by_gate[c * hidden : (c + 1) * hidden]
        terms[c, hidden:] = by_out[c * hidden : (c + 1) * hidden]
    split_rows(cols, gate * proj, updated_own, updated_other)


def tail(
    width, scale, cols, arrived, weights, pair_hat, inverse, d_gate, head_terms, updated_other,
    send, grad_own, others, whole,
):
    parts, total, channels = weights.shape
    hidden = (total - 2 * width) // 2
    devices, q, flat = arrived.shape
    others[0] = updated_other[...]
    normed = pair_hat[...]
    hat = normed.astype(f32)
    w_gate, w_value = rows_of(weights, 0, width), rows_of(weights, width, width)
    gate = jax.nn.sigmoid(dot(w_gate, normed, (1, 0)))
    value = dot(w_value, normed, (1, 0))
    grad = arrived[...].astype(f32).reshape(devices * q, flat)
    by_value = grad * gate
    by_gate = (by_value * (value * (1.0 - gate))).astype(bf16)
    by_value = by_value.astype(bf16)
    terms = [dot(by_gate, normed, (1, 1)) * scale, dot(by_value, normed, (1, 1)) * scale]
    for c in range(parts):
        for at, term in enumerate(terms):
            start = c * total + at * width
            whole[start : start + width] = term[c * width : (c + 1) * width]
        whole[c * total + 2 * width : (c + 1) * total] = head_terms[c]
    per = send.shape[1]
    for s in range(devices):
        send[s] = whole[s * per : (s + 1) * per].astype(bf16)
    d_input = dot(w_gate, by_gate, (0, 0)) + dot(w_value, by_value, (0, 0))
    d_input = d_input + dot(rows_of(weights, 2 * width, hidden), d_gate[...], (0, 0))
    back = inverse[...] * (
        d_input
        - jnp.mean(d_input, 0, keepdims=True)
        - hat * jnp.mean(d_input * hat, 0, keepdims=True)
    )
    split_rows(cols, back, grad_own, others.at[1])


def add_up(arrived, out):
    total = jnp.sum(arrived[...].astype(f32), 0).astype(bf16)
    for s in range(out.shape[0]):
        out[s] = total


def finish(share, sums, updated_own, grad_own, others, *refs):
    (updated, grad), outs, (whole, results, leaves) = refs[:2], refs[2:8], refs[8:]
    count = updated_own.shape[0]
    core = lax.axis_index("ch")
    here, there = pl.ds(core * count, count), pl.ds((1 - core) * count, count)
    joins = []
    for at, (own, out) in enumerate(((updated_own, updated), (grad_own, grad))):
        joins.append(pltpu.make_async_copy(own, out.at[here], leaves.at[2 * at]))
        joins.append(pltpu.make_async_copy(others.at[at], out.at[there], leaves.at[2 * at + 1]))
    start_all(joins)
    _, hidden, channels = results.shape
    width = 2 * hidden
    per = sums.shape[1]
    for s in range(sums.shape[0]):
        whole[s * per : (s + 1) * per] = sums[s].astype(f32)
    order = grouping(hidden, share)
    for at in range(2):
        both = dot(order, whole[at * width : (at + 1) * width].astype(bf16), (0, 0))
        results[at] = both[:hidden]
        results[2 + at] = both[hidden:]
    results[4] = whole[2 * width : 2 * width + hidden]
    results[5] = whole[2 * width + hidden :]
    copies = [
        pltpu.make_async_copy(results.at[at], out, leaves.at[4 + at]) for at, out in enumerate(outs)
    ]
    start_all(copies)
    wait_all(joins + copies)


def by_channels(pair, cotangent, w_gate_a, w_proj_a, w_gate_b, w_proj_b, w_gate_out, w_out):
    row_count, cols, channels = pair.shape
    hidden = w_gate_a.shape[1]
    parts, col_parts, row_parts = lax.axis_size("ch"), lax.axis_size("col"), lax.axis_size("row")
    devices = parts * col_parts * row_parts
    share = hidden * parts // devices
    width = 2 * hidden
    count = row_count // parts
    flat = count * cols
    tokens = cols * col_parts
    scale = 1.0 / tokens
    swap = [(c, parts - 1 - c) for c in range(parts)]
    weight = ((2 * width + 2 * hidden, channels), bf16)
    part = ((count, hidden, cols), bf16)
    own = jnp.swapaxes(cotangent, 1, 2)
    whole_weight = pltpu.VMEM((2 * hidden, channels), bf16)
    weights, normed, inverse, other = call(
        functools.partial(prepare, share),
        [weight, ((channels, flat), bf16), ((1, flat), f32), part],
        (w_gate_a.T, w_proj_a.T, w_gate_b.T, w_proj_b.T, w_gate_out.T, w_out.T, pair, own),
        (
            whole_weight,
            whole_weight,
            whole_weight,
            pltpu.VMEM((count, cols, channels), bf16),
            pltpu.SemaphoreType.DMA((8,)),
        ),
        far=range(8),
        room=60,
    )
    weights = lax.all_gather(weights, "ch")
    (send,) = call(
        functools.partial(edges, width), [((devices, 2 * share, flat), bf16)], (normed, weights)
    )
    arrived = lax.all_to_all(send, everyone, 0, 0)
    arrived, other = lax.optimization_barrier((arrived, other))
    other = lax.ppermute(other, "ch", swap)
    room = pltpu.VMEM((col_parts * tokens * 8, -(-cols // 128) * 128), f32)
    send, kept, inverse = call(
        functools.partial(mix, col_parts, cols),
        [
            ((devices, share, flat), bf16),
            ((2 * share, tokens, tokens), bf16),
            ((1, flat), f32),
        ],
        (arrived, inverse),
        (room, room),
    )
    send, other = lax.optimization_barrier((send, other))
    arrived = lax.all_to_all(send, everyone, 0, 0)
    send, d_gate, head_terms, updated_own, updated_other = call(
        functools.partial(head, width, scale),
        [
            ((devices, share, flat), bf16),
            ((hidden * parts, flat), bf16),
            ((parts, 2 * hidden, channels), f32),
            part,
            part,
        ],
        (arrived, weights, normed, own, other),
        (pltpu.VMEM((hidden * parts, flat), f32),),
    )
    arrived = lax.all_to_all(send, everyone, 0, 0)
    (send,) = call(
        functools.partial(unmix, col_parts, cols),
        [((devices, 2 * share, flat), bf16)],
        (arrived, kept),
        (room, room, pltpu.VMEM(kept.shape, bf16), pltpu.SemaphoreType.DMA),
        far=(1,),
    )
    arrived = lax.all_to_all(send, everyone, 0, 0)
    total = 2 * width + 2 * hidden
    per = total * parts // devices
    send, grad_own, others = call(
        functools.partial(tail, width, scale, cols),
        [((devices, per, channels), bf16), part, ((2, *part[0]), bf16)],
        (arrived, weights, normed, inverse, d_gate, head_terms, updated_other),
        (pltpu.VMEM((total * parts, channels), f32),),
    )
    arrived = lax.all_to_all(send, ("ch", "row", "col"), 0, 0)
    rest = devices // parts
    arrived, others = lax.optimization_barrier((arrived, others))
    (sums,) = call(add_up, [((rest, per, channels), bf16)], (arrived,))
    sums = lax.all_to_all(sums, ("row", "col"), 0, 0)
    updated, grad_pair, *grads = call(
        functools.partial(finish, share),
        [((row_count, hidden, cols), bf16)] * 2 + [((hidden, channels), f32)] * 6,
        (sums, updated_own, grad_own, lax.ppermute(others, "ch", swap)),
        (
            pltpu.VMEM((total, channels), f32),
            pltpu.VMEM((6, hidden, channels), f32),
            pltpu.SemaphoreType.DMA((10,)),
        ),
        (1, 2, 3),
        True,
    )
    return jnp.swapaxes(updated, 1, 2), jnp.swapaxes(grad_pair, 1, 2), *(g.T for g in grads)


def on_device(*arrays):
    row_count, cols, _ = arrays[0].shape
    parts, devices = lax.axis_size("ch"), lax.axis_size(everyone)
    hidden = arrays[2].shape[1]
    share = hidden * parts // devices
    fits = (
        share * devices == hidden * parts
        and parts == 2
        and 2 * share == 8
        and row_count % parts == 0
        and 6 * hidden * parts % devices == 0
        and arrays[1].shape[2] == hidden
        and cols % 16 == 0
    )
    return by_channels(*arrays) if fits else by_rows(*arrays)


def solution(mesh):
    in_specs = (
        P("row", "col", None),
        P("row", "col", "ch"),
        P(None, "ch"),
        P(None, "ch"),
        P(None, "ch"),
        P(None, "ch"),
        P(None, "ch"),
        P(None, "ch"),
    )
    out_specs = (
        P("row", "col", "ch"),
        P("row", "col", "ch"),
        P(None, "ch"),
        P(None, "ch"),
        P(None, "ch"),
        P(None, "ch"),
        P(None, "ch"),
        P(None, "ch"),
    )
    return jax.shard_map(
        on_device, mesh=mesh, in_specs=in_specs, out_specs=out_specs, check_vma=False
    )
```

```python
import functools

import jax
import jax.numpy as jnp
import numpy as np
from jax import lax
from jax.experimental import pallas as pl
from jax.experimental.pallas import tpu as pltpu
from jax.sharding import PartitionSpec as P

epsilon = 1e-05


def layer_norm(values):
    average = jnp.mean(values, -1, keepdims=True)
    centred = values - average
    spread = jnp.mean(centred * centred, -1, keepdims=True)
    inverse = lax.rsqrt(spread + epsilon)
    return (centred * inverse, inverse)


def matmul(first, second):
    return jnp.dot(first, second, preferred_element_type=jnp.float32)


def by_rows(pair, cotangent, w_gate_a, w_proj_a, w_gate_b, w_proj_b, w_gate_out, w_out):
    row_count, col_count, channels = pair.shape
    hidden = w_gate_a.shape[1]
    total_hidden = hidden * lax.axis_size("ch")
    out_width = cotangent.shape[2]
    length = row_count * lax.axis_size("row")
    grad_scale = 1.0 / length
    pair_hat, pair_rstd = layer_norm(pair.astype(jnp.float32))
    flat_norm = pair_hat.astype(jnp.bfloat16).reshape(row_count * col_count, channels)
    w_four = jnp.concatenate([w_gate_a, w_proj_a, w_gate_b, w_proj_b], axis=1)
    projected = matmul(flat_norm, w_four)
    gate_a = jax.nn.sigmoid(projected[:, :hidden])
    proj_a = projected[:, hidden : 2 * hidden]
    gate_b = jax.nn.sigmoid(projected[:, 2 * hidden : 3 * hidden])
    proj_b = projected[:, 3 * hidden :]
    left_edge = (gate_a * proj_a).astype(jnp.bfloat16).reshape(row_count, col_count, hidden)
    right_edge = (gate_b * proj_b).astype(jnp.bfloat16).reshape(row_count, col_count, hidden)
    right_all = lax.all_gather(right_edge, "row", axis=0, tiled=True)
    mixed_swap = lax.psum_scatter(
        jnp.einsum("jkh,ikh->jih", right_all, left_edge, preferred_element_type=jnp.float32).astype(
            jnp.bfloat16
        ),
        "col",
        scatter_dimension=0,
        tiled=True,
    ).astype(jnp.float32)
    mixed = jnp.swapaxes(mixed_swap, 0, 1).reshape(row_count * col_count, hidden)
    hidden_sums = lax.psum((jnp.sum(mixed, -1), jnp.sum(mixed * mixed, -1)), "ch")
    hidden_mean = (hidden_sums[0] / total_hidden)[:, None]
    hidden_var = (hidden_sums[1] / total_hidden)[:, None] - hidden_mean * hidden_mean
    hidden_rstd = lax.rsqrt(hidden_var + epsilon)
    mixed_hat = (mixed - hidden_mean) * hidden_rstd
    mixed_norm = mixed_hat.astype(jnp.bfloat16)
    norm_full = lax.all_gather(mixed_norm, "ch", axis=1, tiled=True)
    gate_out = jax.nn.sigmoid(matmul(flat_norm, w_gate_out))
    proj_out = matmul(norm_full, w_out)
    updated = (gate_out * proj_out).astype(jnp.bfloat16).reshape(row_count, col_count, out_width)
    upstream = cotangent.reshape(row_count * col_count, out_width).astype(jnp.float32)
    d_proj = (upstream * gate_out).astype(jnp.bfloat16)
    d_gate = (upstream * proj_out * gate_out * (1.0 - gate_out)).astype(jnp.bfloat16)
    head_grads = lax.psum(
        (matmul(norm_full.T, d_proj) * grad_scale, matmul(flat_norm.T, d_gate) * grad_scale),
        ("row", "col"),
    )
    d_norm = lax.psum_scatter(
        matmul(d_proj, w_out.T).astype(jnp.bfloat16), "ch", scatter_dimension=1, tiled=True
    ).astype(jnp.float32)
    back_sums = lax.psum((jnp.sum(d_norm, -1), jnp.sum(d_norm * mixed_hat, -1)), "ch")
    d_mixed = hidden_rstd * (
        d_norm
        - (back_sums[0] / total_hidden)[:, None]
        - mixed_hat * (back_sums[1] / total_hidden)[:, None]
    )
    d_mixed = d_mixed.astype(jnp.bfloat16).reshape(row_count, col_count, hidden)
    d_rows = lax.all_gather(d_mixed, "col", axis=1, tiled=True)
    right_back = lax.all_gather(right_edge, "row", axis=0, tiled=True)
    d_left = jnp.einsum("ijh,jkh->ikh", d_rows, right_back, preferred_element_type=jnp.float32)
    d_left = d_left.reshape(row_count * col_count, hidden)
    left_all = lax.all_gather(left_edge, "row", axis=0, tiled=True)
    d_columns = lax.all_to_all(d_rows, "row", split_axis=1, concat_axis=0, tiled=True)
    d_right = jnp.einsum("ijh,ikh->jkh", d_columns, left_all, preferred_element_type=jnp.float32)
    d_right = d_right.reshape(row_count * col_count, hidden)
    grad_pa = (d_left * gate_a).astype(jnp.bfloat16)
    grad_ga = (d_left * proj_a * gate_a * (1.0 - gate_a)).astype(jnp.bfloat16)
    grad_pb = (d_right * gate_b).astype(jnp.bfloat16)
    grad_gb = (d_right * proj_b * gate_b * (1.0 - gate_b)).astype(jnp.bfloat16)
    d_four = jnp.concatenate([grad_ga, grad_pa, grad_gb, grad_pb], axis=1)
    weight_terms = matmul(flat_norm.T, d_four) * grad_scale
    summed = lax.psum(weight_terms, ("row", "col"))
    d_flat = matmul(d_four, w_four.T) + matmul(d_gate, w_gate_out.T)
    hat_all = pair_hat.reshape(row_count * col_count, channels)
    rstd_flat = pair_rstd.reshape(row_count * col_count, 1)
    offset = lax.axis_index("ch") * out_width
    grad_whole = lax.psum(d_flat.astype(jnp.bfloat16), "ch").astype(jnp.float32)
    grad_full = rstd_flat * (
        grad_whole
        - jnp.mean(grad_whole, -1, keepdims=True)
        - hat_all * jnp.mean(grad_whole * hat_all, -1, keepdims=True)
    )
    grad_pair = lax.dynamic_slice_in_dim(grad_full, offset, out_width, 1)
    grad_pair = grad_pair.astype(jnp.bfloat16).reshape(row_count, col_count, out_width)
    return (
        updated,
        grad_pair,
        summed[:, :hidden],
        summed[:, hidden : 2 * hidden],
        summed[:, 2 * hidden : 3 * hidden],
        summed[:, 3 * hidden :],
        head_grads[1],
        head_grads[0],
    )


everyone = ("col", "row", "ch")
f32, bf16 = jnp.float32, jnp.bfloat16


def dot(first, second, over):
    return lax.dot_general(
        first, second, (((over[0],), (over[1],)), ((), ())), preferred_element_type=f32
    )


def call(kernel, outs, args, scratch=(), far=(), outs_far=False, room=16):
    whole = pl.BlockSpec(memory_space=pltpu.VMEM)
    anywhere = pl.BlockSpec(memory_space=pl.ANY)
    return pl.pallas_call(
        kernel,
        out_shape=tuple(jax.ShapeDtypeStruct(*out) for out in outs),
        in_specs=[anywhere if at in far else whole for at in range(len(args))],
        out_specs=tuple(anywhere if outs_far else whole for _ in outs),
        scratch_shapes=scratch,
        compiler_params=pltpu.CompilerParams(vmem_limit_bytes=room * 2**20),
    )(*args)


def grouping(hidden, share):
    shape = (2 * hidden, 2 * hidden)
    rows = lax.broadcasted_iota(jnp.int32, shape, 0)
    columns = lax.broadcasted_iota(jnp.int32, shape, 1)
    group, within = rows // (2 * share), lax.rem(rows, 2 * share)
    side = within // share
    wanted = side * hidden + group * share + within - side * share
    return jnp.where(columns == wanted, 1.0, 0.0).astype(bf16)


def start_all(copies):
    for copy in copies:
        copy.start()


def wait_all(copies):
    for copy in copies:
        copy.wait()


def prepare(
    share, ga, pa, gb, pb, go, wo, pair_far, cotangent_far, out, normed, inverse, other,
    gates, values, last, pair, arrivals,
):
    hidden = go.shape[0]
    width = 2 * hidden
    count = pair.shape[0]
    core = lax.axis_index("ch")
    copies = []
    for at, (held, low, high) in enumerate(((gates, ga, gb), (values, pa, pb), (last, go, wo))):
        copies.append(pltpu.make_async_copy(low, held.at[0:hidden], arrivals.at[2 * at]))
        copies.append(pltpu.make_async_copy(high, held.at[hidden:width], arrivals.at[2 * at + 1]))
    fetch = pltpu.make_async_copy(pair_far.at[pl.ds(core * count, count)], pair, arrivals.at[6])
    cut = pltpu.make_async_copy(
        cotangent_far.at[pl.ds((1 - core) * count, count)], other, arrivals.at[7]
    )
    start_all(copies + [fetch, cut])
    order = grouping(hidden, share)
    wait_all(copies)
    out[:width] = dot(order, gates[...], (1, 0)).astype(bf16)
    out[width : 2 * width] = dot(order, values[...], (1, 0)).astype(bf16)
    out[2 * width :] = last[...]
    fetch.wait()
    hat, rstd = normalized(pair[...])
    normed[...] = hat.astype(bf16)
    inverse[...] = rstd
    cut.wait()


def rows_of(weights, start, count):
    return jnp.concatenate([weights[c, start : start + count] for c in range(weights.shape[0])], 0)


def normalized(pair):
    count, cols, channels = pair.shape
    values = pair.astype(f32).reshape(count * cols, channels).T
    centred = values - jnp.mean(values, 0, keepdims=True)
    rstd = lax.rsqrt(jnp.mean(centred * centred, 0, keepdims=True) + epsilon)
    return centred * rstd, rstd


def edges(width, normed, weights, send):
    gate = jax.nn.sigmoid(dot(rows_of(weights, 0, width), normed[...], (1, 0)))
    value = dot(rows_of(weights, width, width), normed[...], (1, 0))
    send[...] = (gate * value).reshape(send.shape).astype(bf16)


def spread_rows(block, cols, arrived, held):
    devices, q, flat = arrived.shape
    rows = flat // cols
    for s in range(devices):
        tile = arrived[s].astype(f32)
        for i in range(rows):
            start = (s * rows + i) * block
            held[start : start + q, 0:cols] = tile[:, i * cols : (i + 1) * cols]


def pack_rows(block, cols, held, send):
    devices, q, flat = send.shape
    rows = flat // cols
    for s in range(devices):
        starts = [(s * rows + i) * block for i in range(rows)]
        whole = jnp.concatenate([held[start : start + block, 0:cols] for start in starts], axis=1)
        send[s] = whole[:q].astype(bf16)


def square(block, parts, cols, held, e):
    tokens = parts * cols
    return jnp.concatenate(
        [
            held[pl.ds(p * tokens * block + e, tokens, stride=block), 0:cols]
            for p in range(parts)
        ],
        axis=1,
    ).astype(bf16)


def put_square(block, parts, cols, held, e, values):
    tokens = parts * cols
    for p in range(parts):
        held[pl.ds(p * tokens * block + e, tokens, stride=block), 0:cols] = values[
            :, p * cols : (p + 1) * cols
        ]


def mix(parts, cols, arrived, inverse, send, kept, inverse_on, held, result):
    inverse_on[...] = inverse[...]
    block = 8
    q = arrived.shape[1]
    spread_rows(block, cols, arrived, held)
    for e in range(q // 2):
        left = square(block, parts, cols, held, e)
        right = square(block, parts, cols, held, q // 2 + e)
        kept[e] = left
        kept[q // 2 + e] = right
        put_square(block, parts, cols, result, e, dot(left, right, (1, 1)))
    pack_rows(block, cols, result, send)


def unmix(parts, cols, arrived, kept_far, send, held, result, kept, arrival):
    block = 8
    q = arrived.shape[1]
    copy = pltpu.make_async_copy(kept_far, kept, arrival)
    copy.start()
    spread_rows(block, cols, arrived, held)
    copy.wait()
    for e in range(q):
        d_mixed = square(block, parts, cols, held, e)
        put_square(block, parts, cols, result, e, dot(d_mixed, kept[q + e], (1, 0)))
        put_square(block, parts, cols, result, q + e, dot(d_mixed, kept[e], (0, 0)))
    pack_rows(block, cols, result, send)


def split_rows(cols, values, own, other):
    hidden = values.shape[0] // 2
    first = lax.axis_index("ch") == 0
    low, high = values[:hidden], values[hidden:]
    mine = jnp.where(first, low, high)
    yours = jnp.where(first, high, low)
    for i in range(own.shape[0]):
        own[i] = mine[:, i * cols : (i + 1) * cols].astype(bf16)
        other[i] = yours[:, i * cols : (i + 1) * cols].astype(bf16)


def head(
    width, scale, arrived, weights, normed, cotangent, other,
    send, d_gate, terms, updated_own, updated_other,
    upstream,
):
    parts, total, _ = weights.shape
    hidden = (total - 2 * width) // 2
    devices, q, flat = arrived.shape
    count, _, cols = other.shape
    core = lax.axis_index("ch")
    mixed = jnp.concatenate([arrived[s].astype(f32) for s in range(devices)], 0)
    average = jnp.mean(mixed, 0, keepdims=True)
    spread = jnp.mean(mixed * mixed, 0, keepdims=True) - average * average
    inverse = lax.rsqrt(spread + epsilon)
    hat = (mixed - average) * inverse
    hat_rounded = hat.astype(bf16)
    w_out = rows_of(weights, 2 * width + hidden, hidden)
    proj = dot(w_out, hat_rounded, (1, 0))
    own = cotangent[pl.ds(core * count, count)]
    for part, side in ((own, core), (other[...], 1 - core)):
        upstream[pl.ds(pl.multiple_of(side * hidden, hidden), hidden)] = jnp.concatenate(
            [part[i].astype(f32) for i in range(count)], axis=1
        )
    gate = jax.nn.sigmoid(dot(rows_of(weights, 2 * width, hidden), normed[...], (1, 0)))
    up = upstream[...]
    d_proj = (up * gate).astype(bf16)
    d_gate[...] = (up * proj * gate * (1.0 - gate)).astype(bf16)
    d_norm = dot(w_out, d_proj, (0, 0))
    d_mixed = inverse * (
        d_norm
        - jnp.mean(d_norm, 0, keepdims=True)
        - hat * jnp.mean(d_norm * hat, 0, keepdims=True)
    )
    for s in range(devices):
        send[s] = d_mixed[s * q : (s + 1) * q].astype(bf16)
    by_gate = dot(d_gate[...], normed[...], (1, 1)) * scale
    by_out = dot(d_proj, hat_rounded, (1, 1)) * scale
    for c in range(parts):
        terms[c, :hidden] = by_gate[c * hidden : (c + 1) * hidden]
        terms[c, hidden:] = by_out[c * hidden : (c + 1) * hidden]
    split_rows(cols, gate * proj, updated_own, updated_other)


def tail(
    width, scale, cols, arrived, weights, pair_hat, inverse, d_gate, head_terms, updated_other,
    send, grad_own, others, whole,
):
    parts, total, channels = weights.shape
    hidden = (total - 2 * width) // 2
    devices, q, flat = arrived.shape
    others[0] = updated_other[...]
    normed = pair_hat[...]
    hat = normed.astype(f32)
    w_gate, w_value = rows_of(weights, 0, width), rows_of(weights, width, width)
    gate = jax.nn.sigmoid(dot(w_gate, normed, (1, 0)))
    value = dot(w_value, normed, (1, 0))
    grad = arrived[...].astype(f32).reshape(devices * q, flat)
    by_value = grad * gate
    by_gate = (by_value * (value * (1.0 - gate))).astype(bf16)
    by_value = by_value.astype(bf16)
    terms = [dot(by_gate, normed, (1, 1)) * scale, dot(by_value, normed, (1, 1)) * scale]
    for c in range(parts):
        for at, term in enumerate(terms):
            start = c * total + at * width
            whole[start : start + width] = term[c * width : (c + 1) * width]
        whole[c * total + 2 * width : (c + 1) * total] = head_terms[c]
    per = send.shape[1]
    for s in range(devices):
        send[s] = whole[s * per : (s + 1) * per].astype(bf16)
    d_input = dot(w_gate, by_gate, (0, 0)) + dot(w_value, by_value, (0, 0))
    d_input = d_input + dot(rows_of(weights, 2 * width, hidden), d_gate[...], (0, 0))
    back = inverse[...] * (
        d_input
        - jnp.mean(d_input, 0, keepdims=True)
        - hat * jnp.mean(d_input * hat, 0, keepdims=True)
    )
    split_rows(cols, back, grad_own, others.at[1])


def add_up(arrived, out):
    total = jnp.sum(arrived[...].astype(f32), 0).astype(bf16)
    for s in range(out.shape[0]):
        out[s] = total


def finish(share, sums, updated_own, grad_own, others, *refs):
    (updated, grad), outs, (whole, results, leaves) = refs[:2], refs[2:8], refs[8:]
    count = updated_own.shape[0]
    core = lax.axis_index("ch")
    here, there = pl.ds(core * count, count), pl.ds((1 - core) * count, count)
    joins = []
    for at, (own, out) in enumerate(((updated_own, updated), (grad_own, grad))):
        joins.append(pltpu.make_async_copy(own, out.at[here], leaves.at[2 * at]))
        joins.append(pltpu.make_async_copy(others.at[at], out.at[there], leaves.at[2 * at + 1]))
    start_all(joins)
    _, hidden, channels = results.shape
    width = 2 * hidden
    per = sums.shape[1]
    for s in range(sums.shape[0]):
        whole[s * per : (s + 1) * per] = sums[s].astype(f32)
    order = grouping(hidden, share)
    for at in range(2):
        both = dot(order, whole[at * width : (at + 1) * width].astype(bf16), (0, 0))
        results[at] = both[:hidden]
        results[2 + at] = both[hidden:]
    results[4] = whole[2 * width : 2 * width + hidden]
    results[5] = whole[2 * width + hidden :]
    copies = [
        pltpu.make_async_copy(results.at[at], out, leaves.at[4 + at]) for at, out in enumerate(outs)
    ]
    start_all(copies)
    wait_all(joins + copies)


def by_channels(pair, cotangent, w_gate_a, w_proj_a, w_gate_b, w_proj_b, w_gate_out, w_out):
    row_count, cols, channels = pair.shape
    hidden = w_gate_a.shape[1]
    parts, col_parts, row_parts = lax.axis_size("ch"), lax.axis_size("col"), lax.axis_size("row")
    devices = parts * col_parts * row_parts
    share = hidden * parts // devices
    width = 2 * hidden
    count = row_count // parts
    flat = count * cols
    tokens = cols * col_parts
    scale = 1.0 / tokens
    swap = [(c, parts - 1 - c) for c in range(parts)]
    weight = ((2 * width + 2 * hidden, channels), bf16)
    part = ((count, hidden, cols), bf16)
    own = jnp.swapaxes(cotangent, 1, 2)
    whole_weight = pltpu.VMEM((2 * hidden, channels), bf16)
    weights, normed, inverse, other = call(
        functools.partial(prepare, share),
        [weight, ((channels, flat), bf16), ((1, flat), f32), part],
        (w_gate_a.T, w_proj_a.T, w_gate_b.T, w_proj_b.T, w_gate_out.T, w_out.T, pair, own),
        (
            whole_weight,
            whole_weight,
            whole_weight,
            pltpu.VMEM((count, cols, channels), bf16),
            pltpu.SemaphoreType.DMA((8,)),
        ),
        far=range(8),
        room=60,
    )
    weights = lax.all_gather(weights, "ch")
    (send,) = call(
        functools.partial(edges, width), [((devices, 2 * share, flat), bf16)], (normed, weights)
    )
    arrived = lax.all_to_all(send, everyone, 0, 0)
    arrived, other = lax.optimization_barrier((arrived, other))
    other = lax.ppermute(other, "ch", swap)
    room = pltpu.VMEM((col_parts * tokens * 8, -(-cols // 128) * 128), f32)
    send, kept, inverse = call(
        functools.partial(mix, col_parts, cols),
        [
            ((devices, share, flat), bf16),
            ((2 * share, tokens, tokens), bf16),
            ((1, flat), f32),
        ],
        (arrived, inverse),
        (room, room),
    )
    send, other = lax.optimization_barrier((send, other))
    arrived = lax.all_to_all(send, everyone, 0, 0)
    send, d_gate, head_terms, updated_own, updated_other = call(
        functools.partial(head, width, scale),
        [
            ((devices, share, flat), bf16),
            ((hidden * parts, flat), bf16),
            ((parts, 2 * hidden, channels), f32),
            part,
            part,
        ],
        (arrived, weights, normed, own, other),
        (pltpu.VMEM((hidden * parts, flat), f32),),
    )
    arrived = lax.all_to_all(send, everyone, 0, 0)
    (send,) = call(
        functools.partial(unmix, col_parts, cols),
        [((devices, 2 * share, flat), bf16)],
        (arrived, kept),
        (room, room, pltpu.VMEM(kept.shape, bf16), pltpu.SemaphoreType.DMA),
        far=(1,),
    )
    arrived = lax.all_to_all(send, everyone, 0, 0)
    total = 2 * width + 2 * hidden
    per = total * parts // devices
    send, grad_own, others = call(
        functools.partial(tail, width, scale, cols),
        [((devices, per, channels), bf16), part, ((2, *part[0]), bf16)],
        (arrived, weights, normed, inverse, d_gate, head_terms, updated_other),
        (pltpu.VMEM((total * parts, channels), f32),),
    )
    arrived = lax.all_to_all(send, ("ch", "col", "row"), 0, 0)
    rest = devices // parts
    arrived, others = lax.optimization_barrier((arrived, others))
    (sums,) = call(add_up, [((rest, per, channels), bf16)], (arrived,))
    sums = lax.all_to_all(sums, ("col", "row"), 0, 0)
    updated, grad_pair, *grads = call(
        functools.partial(finish, share),
        [((row_count, hidden, cols), bf16)] * 2 + [((hidden, channels), f32)] * 6,
        (sums, updated_own, grad_own, lax.ppermute(others, "ch", swap)),
        (
            pltpu.VMEM((total, channels), f32),
            pltpu.VMEM((6, hidden, channels), f32),
            pltpu.SemaphoreType.DMA((10,)),
        ),
        (1, 2, 3),
        True,
    )
    return jnp.swapaxes(updated, 1, 2), jnp.swapaxes(grad_pair, 1, 2), *(g.T for g in grads)


def on_device(*arrays):
    row_count, cols, _ = arrays[0].shape
    parts, devices = lax.axis_size("ch"), lax.axis_size(everyone)
    hidden = arrays[2].shape[1]
    share = hidden * parts // devices
    fits = (
        share * devices == hidden * parts
        and parts == 2
        and 2 * share == 8
        and row_count % parts == 0
        and 6 * hidden * parts % devices == 0
        and arrays[1].shape[2] == hidden
        and cols % 16 == 0
    )
    return by_channels(*arrays) if fits else by_rows(*arrays)


def solution(mesh):
    in_specs = (
        P("row", "col", None),
        P("row", "col", "ch"),
        P(None, "ch"),
        P(None, "ch"),
        P(None, "ch"),
        P(None, "ch"),
        P(None, "ch"),
        P(None, "ch"),
    )
    out_specs = (
        P("row", "col", "ch"),
        P("row", "col", "ch"),
        P(None, "ch"),
        P(None, "ch"),
        P(None, "ch"),
        P(None, "ch"),
        P(None, "ch"),
        P(None, "ch"),
    )
    return jax.shard_map(
        on_device, mesh=mesh, in_specs=in_specs, out_specs=out_specs, check_vma=False
    )
```

```python
import functools

import jax
import jax.numpy as jnp
import numpy as np
from jax import lax
from jax.experimental import pallas as pl
from jax.experimental.pallas import tpu as pltpu
from jax.sharding import PartitionSpec as P

epsilon = 1e-05


def layer_norm(values):
    average = jnp.mean(values, -1, keepdims=True)
    centred = values - average
    spread = jnp.mean(centred * centred, -1, keepdims=True)
    inverse = lax.rsqrt(spread + epsilon)
    return (centred * inverse, inverse)


def matmul(first, second):
    return jnp.dot(first, second, preferred_element_type=jnp.float32)


def by_rows(pair, cotangent, w_gate_a, w_proj_a, w_gate_b, w_proj_b, w_gate_out, w_out):
    row_count, col_count, channels = pair.shape
    hidden = w_gate_a.shape[1]
    total_hidden = hidden * lax.axis_size("ch")
    out_width = cotangent.shape[2]
    length = row_count * lax.axis_size("row")
    grad_scale = 1.0 / length
    pair_hat, pair_rstd = layer_norm(pair.astype(jnp.float32))
    flat_norm = pair_hat.astype(jnp.bfloat16).reshape(row_count * col_count, channels)
    w_four = jnp.concatenate([w_gate_a, w_proj_a, w_gate_b, w_proj_b], axis=1)
    projected = matmul(flat_norm, w_four)
    gate_a = jax.nn.sigmoid(projected[:, :hidden])
    proj_a = projected[:, hidden : 2 * hidden]
    gate_b = jax.nn.sigmoid(projected[:, 2 * hidden : 3 * hidden])
    proj_b = projected[:, 3 * hidden :]
    left_edge = (gate_a * proj_a).astype(jnp.bfloat16).reshape(row_count, col_count, hidden)
    right_edge = (gate_b * proj_b).astype(jnp.bfloat16).reshape(row_count, col_count, hidden)
    right_all = lax.all_gather(right_edge, "row", axis=0, tiled=True)
    mixed_swap = lax.psum_scatter(
        jnp.einsum("jkh,ikh->jih", right_all, left_edge, preferred_element_type=jnp.float32).astype(
            jnp.bfloat16
        ),
        "col",
        scatter_dimension=0,
        tiled=True,
    ).astype(jnp.float32)
    mixed = jnp.swapaxes(mixed_swap, 0, 1).reshape(row_count * col_count, hidden)
    hidden_sums = lax.psum((jnp.sum(mixed, -1), jnp.sum(mixed * mixed, -1)), "ch")
    hidden_mean = (hidden_sums[0] / total_hidden)[:, None]
    hidden_var = (hidden_sums[1] / total_hidden)[:, None] - hidden_mean * hidden_mean
    hidden_rstd = lax.rsqrt(hidden_var + epsilon)
    mixed_hat = (mixed - hidden_mean) * hidden_rstd
    mixed_norm = mixed_hat.astype(jnp.bfloat16)
    norm_full = lax.all_gather(mixed_norm, "ch", axis=1, tiled=True)
    gate_out = jax.nn.sigmoid(matmul(flat_norm, w_gate_out))
    proj_out = matmul(norm_full, w_out)
    updated = (gate_out * proj_out).astype(jnp.bfloat16).reshape(row_count, col_count, out_width)
    upstream = cotangent.reshape(row_count * col_count, out_width).astype(jnp.float32)
    d_proj = (upstream * gate_out).astype(jnp.bfloat16)
    d_gate = (upstream * proj_out * gate_out * (1.0 - gate_out)).astype(jnp.bfloat16)
    head_grads = lax.psum(
        (matmul(norm_full.T, d_proj) * grad_scale, matmul(flat_norm.T, d_gate) * grad_scale),
        ("row", "col"),
    )
    d_norm = lax.psum_scatter(
        matmul(d_proj, w_out.T).astype(jnp.bfloat16), "ch", scatter_dimension=1, tiled=True
    ).astype(jnp.float32)
    back_sums = lax.psum((jnp.sum(d_norm, -1), jnp.sum(d_norm * mixed_hat, -1)), "ch")
    d_mixed = hidden_rstd * (
        d_norm
        - (back_sums[0] / total_hidden)[:, None]
        - mixed_hat * (back_sums[1] / total_hidden)[:, None]
    )
    d_mixed = d_mixed.astype(jnp.bfloat16).reshape(row_count, col_count, hidden)
    d_rows = lax.all_gather(d_mixed, "col", axis=1, tiled=True)
    right_back = lax.all_gather(right_edge, "row", axis=0, tiled=True)
    d_left = jnp.einsum("ijh,jkh->ikh", d_rows, right_back, preferred_element_type=jnp.float32)
    d_left = d_left.reshape(row_count * col_count, hidden)
    left_all = lax.all_gather(left_edge, "row", axis=0, tiled=True)
    d_columns = lax.all_to_all(d_rows, "row", split_axis=1, concat_axis=0, tiled=True)
    d_right = jnp.einsum("ijh,ikh->jkh", d_columns, left_all, preferred_element_type=jnp.float32)
    d_right = d_right.reshape(row_count * col_count, hidden)
    grad_pa = (d_left * gate_a).astype(jnp.bfloat16)
    grad_ga = (d_left * proj_a * gate_a * (1.0 - gate_a)).astype(jnp.bfloat16)
    grad_pb = (d_right * gate_b).astype(jnp.bfloat16)
    grad_gb = (d_right * proj_b * gate_b * (1.0 - gate_b)).astype(jnp.bfloat16)
    d_four = jnp.concatenate([grad_ga, grad_pa, grad_gb, grad_pb], axis=1)
    weight_terms = matmul(flat_norm.T, d_four) * grad_scale
    summed = lax.psum(weight_terms, ("row", "col"))
    d_flat = matmul(d_four, w_four.T) + matmul(d_gate, w_gate_out.T)
    hat_all = pair_hat.reshape(row_count * col_count, channels)
    rstd_flat = pair_rstd.reshape(row_count * col_count, 1)
    offset = lax.axis_index("ch") * out_width
    grad_whole = lax.psum(d_flat.astype(jnp.bfloat16), "ch").astype(jnp.float32)
    grad_full = rstd_flat * (
        grad_whole
        - jnp.mean(grad_whole, -1, keepdims=True)
        - hat_all * jnp.mean(grad_whole * hat_all, -1, keepdims=True)
    )
    grad_pair = lax.dynamic_slice_in_dim(grad_full, offset, out_width, 1)
    grad_pair = grad_pair.astype(jnp.bfloat16).reshape(row_count, col_count, out_width)
    return (
        updated,
        grad_pair,
        summed[:, :hidden],
        summed[:, hidden : 2 * hidden],
        summed[:, 2 * hidden : 3 * hidden],
        summed[:, 3 * hidden :],
        head_grads[1],
        head_grads[0],
    )


everyone = ("col", "row", "ch")
f32, bf16 = jnp.float32, jnp.bfloat16


def dot(first, second, over):
    return lax.dot_general(
        first, second, (((over[0],), (over[1],)), ((), ())), preferred_element_type=f32
    )


def call(kernel, outs, args, scratch=(), far=(), outs_far=False, room=16):
    whole = pl.BlockSpec(memory_space=pltpu.VMEM)
    anywhere = pl.BlockSpec(memory_space=pl.ANY)
    return pl.pallas_call(
        kernel,
        out_shape=tuple(jax.ShapeDtypeStruct(*out) for out in outs),
        in_specs=[anywhere if at in far else whole for at in range(len(args))],
        out_specs=tuple(anywhere if outs_far else whole for _ in outs),
        scratch_shapes=scratch,
        compiler_params=pltpu.CompilerParams(vmem_limit_bytes=room * 2**20),
    )(*args)


def grouping(hidden, share):
    shape = (2 * hidden, 2 * hidden)
    rows = lax.broadcasted_iota(jnp.int32, shape, 0)
    columns = lax.broadcasted_iota(jnp.int32, shape, 1)
    group, within = rows // (2 * share), lax.rem(rows, 2 * share)
    side = within // share
    wanted = side * hidden + group * share + within - side * share
    return jnp.where(columns == wanted, 1.0, 0.0).astype(bf16)


def start_all(copies):
    for copy in copies:
        copy.start()


def wait_all(copies):
    for copy in copies:
        copy.wait()


def prepare(
    share, ga, pa, gb, pb, go, wo, pair_far, cotangent_far, out, normed, inverse, other,
    gates, values, last, pair, arrivals,
):
    hidden = go.shape[0]
    width = 2 * hidden
    count = pair.shape[0]
    core = lax.axis_index("ch")
    copies = []
    for at, (held, low, high) in enumerate(((gates, ga, gb), (values, pa, pb), (last, go, wo))):
        copies.append(pltpu.make_async_copy(low, held.at[0:hidden], arrivals.at[2 * at]))
        copies.append(pltpu.make_async_copy(high, held.at[hidden:width], arrivals.at[2 * at + 1]))
    fetch = pltpu.make_async_copy(pair_far.at[pl.ds(core * count, count)], pair, arrivals.at[6])
    cut = pltpu.make_async_copy(
        cotangent_far.at[pl.ds((1 - core) * count, count)], other, arrivals.at[7]
    )
    start_all(copies + [fetch, cut])
    order = grouping(hidden, share)
    wait_all(copies)
    out[:width] = dot(order, gates[...], (1, 0)).astype(bf16)
    out[width : 2 * width] = dot(order, values[...], (1, 0)).astype(bf16)
    out[2 * width :] = last[...]
    fetch.wait()
    hat, rstd = normalized(pair[...])
    normed[...] = hat.astype(bf16)
    inverse[...] = rstd
    cut.wait()


def rows_of(weights, start, count):
    return jnp.concatenate([weights[c, start : start + count] for c in range(weights.shape[0])], 0)


def normalized(pair):
    count, cols, channels = pair.shape
    values = pair.astype(f32).reshape(count * cols, channels).T
    centred = values - jnp.mean(values, 0, keepdims=True)
    rstd = lax.rsqrt(jnp.mean(centred * centred, 0, keepdims=True) + epsilon)
    return centred * rstd, rstd


def edges(width, normed, weights, send):
    gate = jax.nn.sigmoid(dot(rows_of(weights, 0, width), normed[...], (1, 0)))
    value = dot(rows_of(weights, width, width), normed[...], (1, 0))
    send[...] = (gate * value).reshape(send.shape).astype(bf16)


def spread_rows(block, cols, arrived, held):
    devices, q, flat = arrived.shape
    rows = flat // cols
    for s in range(devices):
        tile = arrived[s].astype(f32)
        for i in range(rows):
            start = (s * rows + i) * block
            held[start : start + q, 0:cols] = tile[:, i * cols : (i + 1) * cols]


def pack_rows(block, cols, held, send):
    devices, q, flat = send.shape
    rows = flat // cols
    for s in range(devices):
        starts = [(s * rows + i) * block for i in range(rows)]
        whole = jnp.concatenate([held[start : start + block, 0:cols] for start in starts], axis=1)
        send[s] = whole[:q].astype(bf16)


def square(block, parts, cols, held, e):
    tokens = parts * cols
    return jnp.concatenate(
        [
            held[pl.ds(p * tokens * block + e, tokens, stride=block), 0:cols]
            for p in range(parts)
        ],
        axis=1,
    ).astype(bf16)


def put_square(block, parts, cols, held, e, values):
    tokens = parts * cols
    for p in range(parts):
        held[pl.ds(p * tokens * block + e, tokens, stride=block), 0:cols] = values[
            :, p * cols : (p + 1) * cols
        ]


def mix(parts, cols, arrived, inverse, send, kept, inverse_on, held, result):
    inverse_on[...] = inverse[...]
    block = 8
    q = arrived.shape[1]
    spread_rows(block, cols, arrived, held)
    for e in range(q // 2):
        left = square(block, parts, cols, held, e)
        right = square(block, parts, cols, held, q // 2 + e)
        kept[e] = left
        kept[q // 2 + e] = right
        put_square(block, parts, cols, result, e, dot(left, right, (1, 1)))
    pack_rows(block, cols, result, send)


def unmix(parts, cols, arrived, kept_far, send, held, result, kept, arrival):
    block = 8
    q = arrived.shape[1]
    copy = pltpu.make_async_copy(kept_far, kept, arrival)
    copy.start()
    spread_rows(block, cols, arrived, held)
    copy.wait()
    for e in range(q):
        d_mixed = square(block, parts, cols, held, e)
        put_square(block, parts, cols, result, e, dot(d_mixed, kept[q + e], (1, 0)))
        put_square(block, parts, cols, result, q + e, dot(d_mixed, kept[e], (0, 0)))
    pack_rows(block, cols, result, send)


def split_rows(cols, values, own, other):
    hidden = values.shape[0] // 2
    first = lax.axis_index("ch") == 0
    low, high = values[:hidden], values[hidden:]
    mine = jnp.where(first, low, high)
    yours = jnp.where(first, high, low)
    for i in range(own.shape[0]):
        own[i] = mine[:, i * cols : (i + 1) * cols].astype(bf16)
        other[i] = yours[:, i * cols : (i + 1) * cols].astype(bf16)


def head(
    width, scale, arrived, weights, normed, cotangent, other,
    send, d_gate, terms, updated_own, updated_other,
    upstream,
):
    parts, total, _ = weights.shape
    hidden = (total - 2 * width) // 2
    devices, q, flat = arrived.shape
    count, _, cols = other.shape
    core = lax.axis_index("ch")
    mixed = jnp.concatenate([arrived[s].astype(f32) for s in range(devices)], 0)
    average = jnp.mean(mixed, 0, keepdims=True)
    spread = jnp.mean(mixed * mixed, 0, keepdims=True) - average * average
    inverse = lax.rsqrt(spread + epsilon)
    hat = (mixed - average) * inverse
    hat_rounded = hat.astype(bf16)
    w_out = rows_of(weights, 2 * width + hidden, hidden)
    proj = dot(w_out, hat_rounded, (1, 0))
    own = cotangent[pl.ds(core * count, count)]
    for part, side in ((own, core), (other[...], 1 - core)):
        upstream[pl.ds(pl.multiple_of(side * hidden, hidden), hidden)] = jnp.concatenate(
            [part[i].astype(f32) for i in range(count)], axis=1
        )
    gate = jax.nn.sigmoid(dot(rows_of(weights, 2 * width, hidden), normed[...], (1, 0)))
    up = upstream[...]
    d_proj = (up * gate).astype(bf16)
    d_gate[...] = (up * proj * gate * (1.0 - gate)).astype(bf16)
    d_norm = dot(w_out, d_proj, (0, 0))
    d_mixed = inverse * (
        d_norm
        - jnp.mean(d_norm, 0, keepdims=True)
        - hat * jnp.mean(d_norm * hat, 0, keepdims=True)
    )
    for s in range(devices):
        send[s] = d_mixed[s * q : (s + 1) * q].astype(bf16)
    by_gate = dot(d_gate[...], normed[...], (1, 1)) * scale
    by_out = dot(d_proj, hat_rounded, (1, 1)) * scale
    for c in range(parts):
        terms[c, :hidden] = by_gate[c * hidden : (c + 1) * hidden]
        terms[c, hidden:] = by_out[c * hidden : (c + 1) * hidden]
    split_rows(cols, gate * proj, updated_own, updated_other)


def tail(
    width, scale, cols, arrived, weights, pair_hat, inverse, d_gate, head_terms, updated_other,
    send, grad_own, others, whole,
):
    parts, total, channels = weights.shape
    hidden = (total - 2 * width) // 2
    devices, q, flat = arrived.shape
    others[0] = updated_other[...]
    normed = pair_hat[...]
    hat = normed.astype(f32)
    w_gate, w_value = rows_of(weights, 0, width), rows_of(weights, width, width)
    gate = jax.nn.sigmoid(dot(w_gate, normed, (1, 0)))
    value = dot(w_value, normed, (1, 0))
    grad = arrived[...].astype(f32).reshape(devices * q, flat)
    by_value = grad * gate
    by_gate = (by_value * (value * (1.0 - gate))).astype(bf16)
    by_value = by_value.astype(bf16)
    terms = [dot(by_gate, normed, (1, 1)) * scale, dot(by_value, normed, (1, 1)) * scale]
    for c in range(parts):
        for at, term in enumerate(terms):
            start = c * total + at * width
            whole[start : start + width] = term[c * width : (c + 1) * width]
        whole[c * total + 2 * width : (c + 1) * total] = head_terms[c]
    per = send.shape[1]
    for s in range(devices):
        send[s] = whole[s * per : (s + 1) * per].astype(bf16)
    d_input = dot(w_gate, by_gate, (0, 0)) + dot(w_value, by_value, (0, 0))
    d_input = d_input + dot(rows_of(weights, 2 * width, hidden), d_gate[...], (0, 0))
    back = inverse[...] * (
        d_input
        - jnp.mean(d_input, 0, keepdims=True)
        - hat * jnp.mean(d_input * hat, 0, keepdims=True)
    )
    split_rows(cols, back, grad_own, others.at[1])


def add_up(arrived, out):
    total = jnp.sum(arrived[...].astype(f32), 0).astype(bf16)
    for s in range(out.shape[0]):
        out[s] = total


def finish(share, sums, updated_own, grad_own, others, *refs):
    (updated, grad), outs, (whole, results, leaves) = refs[:2], refs[2:8], refs[8:]
    count = updated_own.shape[0]
    core = lax.axis_index("ch")
    here, there = pl.ds(core * count, count), pl.ds((1 - core) * count, count)
    joins = []
    for at, (own, out) in enumerate(((updated_own, updated), (grad_own, grad))):
        joins.append(pltpu.make_async_copy(own, out.at[here], leaves.at[2 * at]))
        joins.append(pltpu.make_async_copy(others.at[at], out.at[there], leaves.at[2 * at + 1]))
    start_all(joins)
    _, hidden, channels = results.shape
    width = 2 * hidden
    per = sums.shape[1]
    for s in range(sums.shape[0]):
        whole[s * per : (s + 1) * per] = sums[s].astype(f32)
    order = grouping(hidden, share)
    for at in range(2):
        both = dot(order, whole[at * width : (at + 1) * width].astype(bf16), (0, 0))
        results[at] = both[:hidden]
        results[2 + at] = both[hidden:]
    results[4] = whole[2 * width : 2 * width + hidden]
    results[5] = whole[2 * width + hidden :]
    copies = [
        pltpu.make_async_copy(results.at[at], out, leaves.at[4 + at]) for at, out in enumerate(outs)
    ]
    start_all(copies)
    wait_all(joins + copies)


def by_channels(pair, cotangent, w_gate_a, w_proj_a, w_gate_b, w_proj_b, w_gate_out, w_out):
    row_count, cols, channels = pair.shape
    hidden = w_gate_a.shape[1]
    parts, col_parts, row_parts = lax.axis_size("ch"), lax.axis_size("col"), lax.axis_size("row")
    devices = parts * col_parts * row_parts
    share = hidden * parts // devices
    width = 2 * hidden
    count = row_count // parts
    flat = count * cols
    tokens = cols * col_parts
    scale = 1.0 / tokens
    swap = [(c, parts - 1 - c) for c in range(parts)]
    weight = ((2 * width + 2 * hidden, channels), bf16)
    part = ((count, hidden, cols), bf16)
    own = jnp.swapaxes(cotangent, 1, 2)
    whole_weight = pltpu.VMEM((2 * hidden, channels), bf16)
    weights, normed, inverse, other = call(
        functools.partial(prepare, share),
        [weight, ((channels, flat), bf16), ((1, flat), f32), part],
        (w_gate_a.T, w_proj_a.T, w_gate_b.T, w_proj_b.T, w_gate_out.T, w_out.T, pair, own),
        (
            whole_weight,
            whole_weight,
            whole_weight,
            pltpu.VMEM((count, cols, channels), bf16),
            pltpu.SemaphoreType.DMA((8,)),
        ),
        far=range(8),
        room=50,
    )
    weights = lax.all_gather(weights, "ch")
    (send,) = call(
        functools.partial(edges, width), [((devices, 2 * share, flat), bf16)], (normed, weights)
    )
    arrived = lax.all_to_all(send, everyone, 0, 0)
    arrived, other = lax.optimization_barrier((arrived, other))
    other = lax.ppermute(other, "ch", swap)
    room = pltpu.VMEM((col_parts * tokens * 8, -(-cols // 128) * 128), f32)
    send, kept, inverse = call(
        functools.partial(mix, col_parts, cols),
        [
            ((devices, share, flat), bf16),
            ((2 * share, tokens, tokens), bf16),
            ((1, flat), f32),
        ],
        (arrived, inverse),
        (room, room),
    )
    send, other = lax.optimization_barrier((send, other))
    arrived = lax.all_to_all(send, everyone, 0, 0)
    send, d_gate, head_terms, updated_own, updated_other = call(
        functools.partial(head, width, scale),
        [
            ((devices, share, flat), bf16),
            ((hidden * parts, flat), bf16),
            ((parts, 2 * hidden, channels), f32),
            part,
            part,
        ],
        (arrived, weights, normed, own, other),
        (pltpu.VMEM((hidden * parts, flat), f32),),
    )
    arrived = lax.all_to_all(send, everyone, 0, 0)
    (send,) = call(
        functools.partial(unmix, col_parts, cols),
        [((devices, 2 * share, flat), bf16)],
        (arrived, kept),
        (room, room, pltpu.VMEM(kept.shape, bf16), pltpu.SemaphoreType.DMA),
        far=(1,),
    )
    arrived = lax.all_to_all(send, everyone, 0, 0)
    total = 2 * width + 2 * hidden
    per = total * parts // devices
    send, grad_own, others = call(
        functools.partial(tail, width, scale, cols),
        [((devices, per, channels), bf16), part, ((2, *part[0]), bf16)],
        (arrived, weights, normed, inverse, d_gate, head_terms, updated_other),
        (pltpu.VMEM((total * parts, channels), f32),),
    )
    arrived = lax.all_to_all(send, ("ch", "col", "row"), 0, 0)
    rest = devices // parts
    arrived, others = lax.optimization_barrier((arrived, others))
    (sums,) = call(add_up, [((rest, per, channels), bf16)], (arrived,))
    sums = lax.all_to_all(sums, ("col", "row"), 0, 0)
    updated, grad_pair, *grads = call(
        functools.partial(finish, share),
        [((row_count, hidden, cols), bf16)] * 2 + [((hidden, channels), f32)] * 6,
        (sums, updated_own, grad_own, lax.ppermute(others, "ch", swap)),
        (
            pltpu.VMEM((total, channels), f32),
            pltpu.VMEM((6, hidden, channels), f32),
            pltpu.SemaphoreType.DMA((10,)),
        ),
        (1, 2, 3),
        True,
    )
    return jnp.swapaxes(updated, 1, 2), jnp.swapaxes(grad_pair, 1, 2), *(g.T for g in grads)


def on_device(*arrays):
    row_count, cols, _ = arrays[0].shape
    parts, devices = lax.axis_size("ch"), lax.axis_size(everyone)
    hidden = arrays[2].shape[1]
    share = hidden * parts // devices
    fits = (
        share * devices == hidden * parts
        and parts == 2
        and 2 * share == 8
        and row_count % parts == 0
        and 6 * hidden * parts % devices == 0
        and arrays[1].shape[2] == hidden
        and cols % 16 == 0
    )
    return by_channels(*arrays) if fits else by_rows(*arrays)


def solution(mesh):
    in_specs = (
        P("row", "col", None),
        P("row", "col", "ch"),
        P(None, "ch"),
        P(None, "ch"),
        P(None, "ch"),
        P(None, "ch"),
        P(None, "ch"),
        P(None, "ch"),
    )
    out_specs = (
        P("row", "col", "ch"),
        P("row", "col", "ch"),
        P(None, "ch"),
        P(None, "ch"),
        P(None, "ch"),
        P(None, "ch"),
        P(None, "ch"),
        P(None, "ch"),
    )
    return jax.shard_map(
        on_device, mesh=mesh, in_specs=in_specs, out_specs=out_specs, check_vma=False
    )
```
